32 devices in a mesh: seq: 8 (over z, y), state: 4 (over x, core).
Axes of the slice: x: 2, y: 2, z: 4, core: 2. Of those that a mesh axis runs over, the one named last changes fastest.
Arguments:
- layer_input: bfloat16 [2048, 1024], P('seq'), may hold values from -6 to 6
- out_grad: bfloat16 [2048, 1024], P('seq'), may hold values from -6 to 6
- doc_starts: int32 [8], replicated, may hold values from 0 to 2047, as said below
- real_mask: int32 [2048], replicated, may hold values from 0 to 1, as said below
- norm_gain: float32 [1024], replicated, may hold values from 0.5 to 1.5
- attention_input_rows: bfloat16 [1024, 768], replicated, may hold values from -0.25 to 0.25
- mixer_in: bfloat16 [1024, 2, 1536], replicated, may hold values from -0.1875 to 0.1875
- state_in: bfloat16 [1024, 2, 128], P(None, None, 'state'), may hold values from -0.046875 to 0.046875
- step_in: bfloat16 [1024, 24], replicated, may hold values from -0.1875 to 0.1875
- conv_mixer: float32 [4, 1536], replicated, may hold values from -3 to 3
- conv_state: float32 [4, 2, 128], P(None, None, 'state'), may hold values from -3 to 3
- step_bias: float32 [24], replicated, may hold values from -1.5 to 0.5
- decay_rate: float32 [24], replicated, may hold values from 0 to 1, as said below
- skip_gain: float32 [24], replicated, may hold values from 0.5 to 1.5
- gated_gain: float32 [1536], replicated, may hold values from 0.5 to 1.5
- joint_out: bfloat16 [2048, 1024], replicated, may hold values from -0.15625 to 0.15625
- mlp_gain: float32 [1024], replicated, may hold values from 0.5 to 1.5
- gate_up: bfloat16 [1024, 2, 2048], P(None, None, 'state'), may hold values from -0.1875 to 0.1875
- down_weight: bfloat16 [1024, 2048], P(None, 'state'), may hold values from -0.125 to 0.125
Outputs:
- layer_output: bfloat16 [2048, 1024], P('seq')
- input_grad: float32 [2048, 1024], P('seq')
- grad_norm_gain: float32 [1024], P('seq')
- grad_attention_in: float32 [1024, 768], P('seq')
- grad_mixer_in: float32 [1024, 2, 1536], P('seq')
- grad_state_in: float32 [1024, 2, 128], P('seq', None, 'state')
- grad_step_in: float32 [1024, 24], P('seq')
- grad_conv_mixer: float32 [4, 1536], replicated
- grad_conv_state: float32 [4, 2, 128], P(None, None, 'state')
- grad_step_bias: float32 [24], replicated
- grad_decay_rate: float32 [24], replicated
- grad_skip_gain: float32 [24], replicated
- grad_gated_gain: float32 [1536], P('seq')
- grad_joint_out: float32 [2048, 1024], P('seq')
- grad_mlp_gain: float32 [1024], P('seq')
- grad_gate_up: float32 [1024, 2, 2048], P('seq', None, 'state')
- grad_down_weight: float32 [1024, 2048], P('seq', 'state')
The draws below stay inside these ranges and needn't reach their ends.
Inputs may be any that keep to these rules, and one draw needn't show every extreme that they name: doc_starts[0] is 0 and the entries rise strictly; document k covers doc_starts[k] up to the next entry, the last one up to 2048; entry 1 is at most 128 and entry 2 is at least 1792. `real_mask`: pad is the last 1 to 64 positions of the row, and in each document a tail of at most a quarter of its length; all other positions are real. `decay_rate`: positive rates.
All inputs are finite; a program needn't handle non-finite values.
Results may differ from the reference program's by a relative error of at most 0.015.
Values may be sent and summed in bfloat16 or wider, within the bound.
A program may use at most 320 MiB of HBM per device.

```python
import math
import jax
import jax.numpy as jnp
from jax import lax

MODEL_WIDTH = 1024
QUERY_HEADS = 8
KEY_VALUE_HEADS = 2
HEAD_SIZE = 64
NH = 24
HDM = 64
DS = 128
KC = 4
FF = 2048
TOK_DEV = 256
NDOC = 8
TOKENS = 2048
DM = 1536


def draw_doc_starts(key, part):
    key = jax.random.fold_in(key, 11)
    keys = jax.random.split(key, 3)
    head_len = jax.random.randint(keys[0], (), 1, TOK_DEV // 2 + 1)
    room = TOK_DEV // 2 + jax.random.randint(keys[1], (), 0, TOK_DEV // 4 + 1)
    tail_first = TOKENS - room
    tail_count = NDOC - 2
    steps = jnp.arange(tail_count, dtype=jnp.int32)
    spread = jnp.maximum(room // (2 * tail_count), 1)
    jitter = jax.random.randint(keys[2], (tail_count,), 0, 1 << 20) % spread
    tail_starts = tail_first + steps * room // tail_count + jitter
    return jnp.concatenate([jnp.zeros((1,), jnp.int32), head_len[None].astype(jnp.int32), tail_starts.astype(jnp.int32)])


def draw_real_mask(key, part):
    doc_firsts = draw_doc_starts(key, part)
    key = jax.random.fold_in(key, 23)
    keys = jax.random.split(key, 2)
    doc_ends = jnp.concatenate([doc_firsts[1:], jnp.full((1,), TOKENS, jnp.int32)])
    doc_lengths = doc_ends - doc_firsts
    doc_pads = jax.random.randint(keys[0], (NDOC,), 0, 1 << 20) % (doc_lengths // 4 + 1)
    row_pad = jax.random.randint(keys[1], (), 1, TOK_DEV // 4 + 1)
    places = jnp.arange(TOKENS, dtype=jnp.int32)
    inside = (doc_firsts[None, :] <= places[:, None]) & (places[:, None] < doc_ends[None, :])
    pad_from = jnp.sum(jnp.where(inside, (doc_ends - doc_pads)[None, :], 0), axis=1)
    real_flags = (places < pad_from) & (places < TOKENS - row_pad)
    return real_flags.astype(jnp.int32)


def draw_decay_rate(key, part):
    key = jax.random.fold_in(key, 37)
    keys = jax.random.split(key, 2)
    order = jax.random.permutation(keys[0], NH)
    fast_count = NH // 2
    uniform_part = jax.random.uniform(keys[1], (NH,), jnp.float32)
    slow_rate = 0.05 / TOKENS * jnp.exp(uniform_part * jnp.log(40.0))
    fast_rate = 0.005 * jnp.exp(uniform_part * jnp.log(12.0))
    return jnp.where(order < fast_count, fast_rate, slow_rate).astype(jnp.float32)


def raised(entries, own_key, source, target, shards_of, factor):
    def block_of(position):
        return (jnp.arange(entries.shape[position]) // (entries.shape[position] // shards_of)).reshape((-1,) + (1,) * (entries.ndim - 1 - position))

    first = jax.random.permutation(own_key, shards_of)[block_of(target)]
    second = (block_of(target) + shards_of // 2) % shards_of
    return jnp.where((block_of(source) == first) | (block_of(source) == second), factor * entries, entries)


def block_scale(own_key, dims, cuts, smallest, largest):
    level, own = 1.0, jax.random.fold_in(own_key, 6)
    for position, parts in cuts:
        steps = jnp.exp(jax.random.uniform(jax.random.fold_in(own, position), (parts,), jnp.float32, smallest / len(cuts), largest / len(cuts)))
        level = level * jnp.repeat(steps, dims[position] // parts).reshape([-1 if axis == position else 1 for axis in range(len(dims))])
    return level


def noise(rng, extent, scale, limit, cuts=(), held_as=jnp.bfloat16):
    values = scale * jax.random.normal(rng, extent, jnp.float32)
    if cuts:
        values = values * block_scale(rng, extent, cuts, -0.22, 0.18)
    return jnp.clip(values, -limit, limit).astype(held_as)


def bell_draw_with(rng, dims, deviation, most, shards, heavy, held_as=jnp.bfloat16):
    values = deviation * jax.random.normal(rng, dims, jnp.float32)
    if shards:
        values = values * block_scale(rng, dims, shards, -0.22, 0.18)
    return jnp.clip(raised(values, jax.random.fold_in(rng, 3), *heavy), -most, most).astype(held_as)


def setup_inputs(seed: int = 0) -> dict:
    streams_of = jax.random.split(jax.random.key(seed), 20)
    return {
        "layer_input": bell_draw_with(streams_of[0], (TOKENS, MODEL_WIDTH), 1.0, 6.0, ((0, 8),), (0, 1, 8, 2.0)),
        "out_grad": bell_draw_with(streams_of[1], (TOKENS, MODEL_WIDTH), 1.0, 6.0, ((0, 8),), (0, 1, 8, 2.0)),
        "doc_starts": draw_doc_starts(jax.random.fold_in(streams_of[19], 71), 0),
        "real_mask": draw_real_mask(jax.random.fold_in(streams_of[19], 71), 0),
        "norm_gain": jnp.clip(1.0 + 0.1 * jax.random.normal(streams_of[4], (MODEL_WIDTH,), jnp.float32), 0.5, 1.5),
        "attention_input_rows": noise(streams_of[5], (MODEL_WIDTH, (QUERY_HEADS + 2 * KEY_VALUE_HEADS) * HEAD_SIZE), (MODEL_WIDTH // 2) ** -0.5, 0.25),
        "mixer_in": noise(streams_of[6], (MODEL_WIDTH, 2, DM), MODEL_WIDTH ** -0.5, 0.1875),
        "state_in": noise(streams_of[7], (MODEL_WIDTH, 2, DS), (16 * MODEL_WIDTH) ** -0.5, 0.046875, ((2, 4),)),
        "step_in": noise(streams_of[8], (MODEL_WIDTH, NH), MODEL_WIDTH ** -0.5, 0.1875),
        "conv_mixer": noise(streams_of[9], (KC, DM), KC ** -0.5, 3.0, (), jnp.float32),
        "conv_state": noise(streams_of[10], (KC, 2, DS), KC ** -0.5, 3.0, ((2, 4),), jnp.float32),
        "step_bias": jnp.clip(jax.random.uniform(streams_of[11], (NH,), jnp.float32, -1.5, 0.5), -1.5, 0.5),
        "decay_rate": draw_decay_rate(jax.random.fold_in(streams_of[19], 71), 0),
        "skip_gain": jnp.clip(jax.random.uniform(streams_of[13], (NH,), jnp.float32, 0.5, 1.5), 0.5, 1.5),
        "gated_gain": jnp.clip(1.0 + 0.1 * jax.random.normal(streams_of[14], (DM,), jnp.float32), 0.5, 1.5),
        "joint_out": noise(streams_of[15], (QUERY_HEADS * HEAD_SIZE + DM, MODEL_WIDTH), DM ** -0.5, 0.15625),
        "mlp_gain": jnp.clip(1.0 + 0.1 * jax.random.normal(streams_of[16], (MODEL_WIDTH,), jnp.float32), 0.5, 1.5),
        "gate_up": noise(streams_of[17], (MODEL_WIDTH, 2, FF), MODEL_WIDTH ** -0.5, 0.1875, ((2, 4),)),
        "down_weight": noise(streams_of[18], (MODEL_WIDTH, FF), FF ** -0.5, 0.125, ((1, 4),)),
    }


EPSILON = 1e-05
ROPE_BASE = 10000.0
HIGHEST = lax.Precision.HIGHEST

@jax.custom_vjp
def low(v):
    return lax.optimization_barrier(v.astype(jnp.bfloat16)).astype(jnp.float32)

@jax.custom_vjp
def low_back(v):
    return v

def low_keep(v):
    return (low(v), None)

def low_pass(kept, grad):
    return (grad,)

def back_keep(v):
    return (v, None)

def back_low(kept, grad):
    return (low(grad),)
low.defvjp(low_keep, low_pass)
low_back.defvjp(back_keep, back_low)

def rms_apply(values, gain_vec):
    inverse = lax.rsqrt(lax.optimization_barrier(jnp.mean(values * values, axis=-1, keepdims=True)) + EPSILON)
    return values * inverse * gain_vec

def doc_lookup(doc_starts, positions):
    hit_table = doc_starts[None, :] <= positions[:, None]
    doc_ids = lax.optimization_barrier(jnp.sum(hit_table.astype(jnp.int32), axis=1)) - 1
    firsts = lax.optimization_barrier(jnp.max(jnp.where(hit_table, doc_starts[None, :], 0), axis=1))
    return (doc_ids.astype(jnp.int32), (positions - firsts).astype(jnp.int32))

def apply_rotation(vectors, row_offset_list, direction):
    half_size = vectors.shape[-1] // 2
    powers = jnp.arange(half_size, dtype=jnp.float32) * (2.0 / vectors.shape[-1])
    angles = direction * row_offset_list.astype(jnp.float32)[:, None] * jnp.exp(-math.log(ROPE_BASE) * powers)[None, :]
    cosine = jnp.cos(angles)[:, None, :]
    sine_part = jnp.sin(angles)[:, None, :]
    first_half = vectors[..., :half_size]
    second_half = vectors[..., half_size:]
    return jnp.concatenate([first_half * cosine - second_half * sine_part, second_half * cosine + first_half * sine_part], axis=-1)

def causal_conv(extended, weight, ext_ids):
    length = extended.shape[0] - KC + 1
    own_ids = ext_ids[KC - 1:]
    result = jnp.zeros((length, extended.shape[1]), jnp.float32)
    for tap_index in range(KC):
        same_doc = (ext_ids[tap_index:tap_index + length] == own_ids).astype(jnp.float32)
        result = result + extended[tap_index:tap_index + length] * weight[tap_index][None, :] * same_doc[:, None]
    return result

def ssd_parts(inputs, write_vecs, read_vecs, step_size, decay_rates, real_flags, doc_ids, prior_doc):
    log_decay = -step_size * decay_rates[None, :]
    cumulative = jnp.cumsum(log_decay, axis=0)
    places = jnp.arange(inputs.shape[0])
    linked = (doc_ids[:, None] == doc_ids[None, :]) & (places[:, None] >= places[None, :])
    log_gaps = jnp.where(linked[:, :, None], cumulative[:, None, :] - cumulative[None, :, :], 0.0)
    inflow = step_size * real_flags[:, None]
    intersection = jnp.dot(read_vecs, write_vecs.T, precision=HIGHEST)
    mixing = jnp.where(linked[:, :, None], jnp.exp(log_gaps), 0.0) * inflow[None, :, :] * intersection[:, :, None]
    inner_out = jnp.einsum('tsh,shp->thp', mixing, inputs, precision=HIGHEST)
    alive_flags = (doc_ids == prior_doc).astype(jnp.float32)
    reach_weight = alive_flags[:, None] * jnp.exp(cumulative)
    final_log = cumulative[-1]
    tail_weight = jnp.where((doc_ids == doc_ids[-1])[:, None], jnp.exp(final_log[None, :] - cumulative), 0.0) * inflow
    state_part = jnp.einsum('sh,shp,sn->hpn', tail_weight, inputs, write_vecs, precision=HIGHEST)
    through = alive_flags[-1] * jnp.exp(final_log)
    return (inner_out, reach_weight, through, state_part)

def ssd_sequence(inputs, write_vecs, read_vecs, step_size, decay_rates, real_flags, doc_ids):
    overall_row_count = inputs.shape[0]
    block_extent = min(256, overall_row_count)
    block_count = overall_row_count // block_extent

    def advance(running, pieces):
        state_now, prior_doc = running
        piece_in, piece_write, piece_read, piece_step, piece_real, piece_ids = pieces
        inner_out, reach_weight, through, state_part = ssd_parts(piece_in, piece_write, piece_read, piece_step, decay_rates, piece_real, piece_ids, prior_doc)
        outputs = inner_out + jnp.einsum('th,tn,hpn->thp', reach_weight, piece_read, state_now, precision=HIGHEST)
        return ((through[:, None, None] * state_now + state_part, piece_ids[-1]), outputs)
    start_state = jnp.zeros((inputs.shape[1], inputs.shape[2], write_vecs.shape[1]), jnp.float32)
    pieces = tuple((member.reshape((block_count, block_extent) + member.shape[1:]) for member in (inputs, write_vecs, read_vecs, step_size, real_flags, doc_ids)))
    final_running, outputs = lax.scan(jax.checkpoint(advance), (start_state, jnp.int32(-1)), pieces)
    return outputs.reshape(inputs.shape)

def attention(query_rows, every_key_row, every_value_row, doc_ids, real_flags):
    overall_row_count = query_rows.shape[0]
    block_extent = min(512, overall_row_count)
    query_group_count = QUERY_HEADS // KEY_VALUE_HEADS
    score_scale = 1.0 / math.sqrt(HEAD_SIZE)
    positions = jnp.arange(overall_row_count, dtype=jnp.int32)
    grouped_queries = query_rows.reshape(overall_row_count // block_extent, block_extent, KEY_VALUE_HEADS, query_group_count, HEAD_SIZE)

    def one_block(pieces):
        query_block, query_pos, query_ids = pieces
        scores = low_back(jnp.einsum('qhgd,khd->hgqk', query_block, every_key_row, precision=HIGHEST) * score_scale)
        allowed = (query_ids[:, None] == doc_ids[None, :]) & (positions[None, :] <= query_pos[:, None]) & ((real_flags[None, :] > 0.0) | (positions[None, :] == query_pos[:, None]))
        scores = jnp.where(allowed, scores, -1e+30)
        weights = jax.nn.softmax(scores, axis=-1)
        return jnp.einsum('hgqk,khd->qhgd', low(weights), every_value_row, precision=HIGHEST)
    outputs = lax.map(jax.checkpoint(one_block), (grouped_queries, positions.reshape(-1, block_extent), doc_ids.reshape(-1, block_extent)))
    return outputs.reshape(overall_row_count, QUERY_HEADS * HEAD_SIZE)

def reference(layer_input, out_grad, doc_starts, real_mask, norm_gain, attention_input_rows, mixer_in, state_in, step_in, conv_mixer, conv_state, step_bias, decay_rate, skip_gain, gated_gain, joint_out, mlp_gain, gate_up, down_weight):
    overall_row_count = layer_input.shape[0]
    positions = jnp.arange(overall_row_count, dtype=jnp.int32)
    doc_ids, row_offset_list = doc_lookup(doc_starts, positions)
    real_flags = real_mask.astype(jnp.float32)
    ext_ids = jnp.concatenate([jnp.full((KC - 1,), -1, jnp.int32), doc_ids])

    def forward(hidden_in, norm_gain, attention_input_rows, mixer_in, state_in, step_in, conv_mixer, conv_state, step_bias, decay_rate, skip_gain, gated_gain, joint_out, mlp_gain, gate_up, down_weight):
        normed = low(rms_apply(hidden_in, norm_gain))
        projected_rows = low_back(jnp.dot(normed, attention_input_rows, precision=HIGHEST))
        query_rows = projected_rows[:, :QUERY_HEADS * HEAD_SIZE].reshape(overall_row_count, QUERY_HEADS, HEAD_SIZE)
        every_key_row = projected_rows[:, QUERY_HEADS * HEAD_SIZE:(QUERY_HEADS + KEY_VALUE_HEADS) * HEAD_SIZE].reshape(overall_row_count, KEY_VALUE_HEADS, HEAD_SIZE)
        every_value_row = projected_rows[:, (QUERY_HEADS + KEY_VALUE_HEADS) * HEAD_SIZE:].reshape(overall_row_count, KEY_VALUE_HEADS, HEAD_SIZE)
        query_rows = low(apply_rotation(query_rows, row_offset_list, 1.0))
        every_key_row = low(apply_rotation(every_key_row, row_offset_list, 1.0))
        every_value_row = low(every_value_row)
        attended = low_back(low(attention(query_rows, every_key_row, every_value_row, doc_ids, real_flags)))
        mixed_proj = low_back(jnp.einsum('td,dcm->tcm', normed, mixer_in, precision=HIGHEST))
        gate_z = mixed_proj[:, 0]
        inner_pre = low(mixed_proj[:, 1])
        state_pre = low(low_back(jnp.einsum('td,dcn->tcn', normed, state_in, precision=HIGHEST))).reshape(overall_row_count, -1)
        step_raw = low_back(jnp.dot(normed, step_in, precision=HIGHEST))
        step_size = jax.nn.softplus(step_raw + step_bias)
        inner_conv = jax.nn.silu(causal_conv(jnp.concatenate([jnp.zeros((KC - 1, inner_pre.shape[1]), jnp.float32), inner_pre]), conv_mixer, ext_ids))
        state_conv = jax.nn.silu(causal_conv(jnp.concatenate([jnp.zeros((KC - 1, state_pre.shape[1]), jnp.float32), state_pre]), conv_state.reshape(KC, -1), ext_ids))
        half_state = state_conv.shape[1] // 2
        inner_heads = inner_conv.reshape(overall_row_count, NH, HDM)
        ssd_out = ssd_sequence(inner_heads, state_conv[:, :half_state], state_conv[:, half_state:], step_size, decay_rate, real_flags, doc_ids)
        full_mix = (ssd_out + skip_gain[None, :, None] * inner_heads).reshape(overall_row_count, NH * HDM)
        gated_out = full_mix * jax.nn.silu(gate_z)
        gated_norm = low(rms_apply(gated_out, gated_gain))
        joined = jnp.concatenate([attended, gated_norm], axis=1)
        branch = low_back(jnp.dot(joined, joint_out, precision=HIGHEST))
        residual = hidden_in + branch
        normed_two = low(rms_apply(residual, mlp_gain))
        gate_and_up = low_back(jnp.einsum('td,dcf->tcf', normed_two, gate_up, precision=HIGHEST))
        hidden_mlp = low(jax.nn.silu(gate_and_up[:, 0]) * gate_and_up[:, 1])
        mlp_out = low_back(jnp.einsum('tf,df->td', hidden_mlp, down_weight, precision=HIGHEST))
        return residual + mlp_out
    primals = tuple((member.astype(jnp.float32) for member in (layer_input, norm_gain, attention_input_rows, mixer_in, state_in, step_in, conv_mixer, conv_state, step_bias, decay_rate, skip_gain, gated_gain, joint_out, mlp_gain, gate_up, down_weight)))
    result, pullback = jax.vjp(forward, *primals)
    gradients = pullback(out_grad.astype(jnp.float32))
    return (result.astype(jnp.bfloat16), gradients[0], gradients[1], gradients[2], gradients[3], gradients[4], gradients[5], gradients[6], gradients[7], gradients[8], gradients[9], gradients[10], gradients[11], gradients[12], gradients[13], gradients[14], gradients[15])
```

```python
import math

import jax
import jax.numpy as jnp
from jax import lax
from jax.sharding import PartitionSpec as P

QUERY_HEADS = 8
KEY_VALUE_HEADS = 2
HEAD_SIZE = 64
NH = 24
HDM = 64
KC = 4
EPSILON = 1e-05
ROPE_BASE = 10000.0
HI = lax.Precision.HIGHEST
F32 = jnp.float32
BF16 = jnp.bfloat16
LANES = 128
HALO = 16
FAR = -1e30


def nn(a, b, p=None):
    return lax.dot_general(a, b, (((1,), (0,)), ((), ())), precision=p, preferred_element_type=F32)


def nt(a, b, p=None):
    return lax.dot_general(a, b, (((1,), (1,)), ((), ())), precision=p, preferred_element_type=F32)


def tn(a, b, p=None):
    return lax.dot_general(a, b, (((0,), (0,)), ((), ())), precision=p, preferred_element_type=F32)


def sigmoid(v):
    return 1.0 / (1.0 + jnp.exp(-v))


def silu(v):
    return v * sigmoid(v)


def silu_slope(v):
    s = sigmoid(v)
    return s * (1.0 + v * (1.0 - s))


def softplus(v):
    return jnp.maximum(v, 0.0) + jnp.log1p(jnp.exp(-jnp.abs(v)))


def iota(shape, dim):
    return lax.broadcasted_iota(jnp.int32, shape, dim)


def doc_of(starts, pos):
    found = jnp.full(pos.shape, -1, jnp.int32)
    for start in starts:
        found = found + (pos >= start).astype(jnp.int32)
    return found


def roll(v, shift):
    return jnp.roll(v, shift, axis=1)


def rope(v, cosine, sine, direction):
    first = (iota(v.shape, 1) % HEAD_SIZE) < HEAD_SIZE // 2
    half = HEAD_SIZE // 2
    partner = jnp.where(first, -roll(v, v.shape[1] - half), roll(v, half))
    return v * cosine + partner * (direction * sine)


def expander(width):
    return (iota((LANES, width), 1) // HDM == iota((LANES, width), 0)).astype(F32)


def conv_fwd(ext, taps, masks):
    rows = ext.shape[0] - HALO
    total = 0.0
    for k in range(KC):
        at = HALO - KC + 1 + k
        total = total + ext[at : at + rows] * taps[k : k + 1] * masks[k]
    return total


def conv_bwd(ext, taps, masks, up):
    rows = up.shape[0]
    total, weights = 0.0, []
    for k in range(KC):
        at = HALO - KC + 1 + k
        masked = up * masks[k]
        weights.append(jnp.sum(masked * ext[at : at + rows], axis=0, keepdims=True))
        parts = [jnp.zeros((at, up.shape[1]), F32), masked * taps[k : k + 1]]
        if KC - 1 - k:
            parts.append(jnp.zeros((KC - 1 - k, up.shape[1]), F32))
        total = total + jnp.concatenate(parts, axis=0)
    return total, jnp.concatenate(weights, axis=0)


def masks_of(starts, first_row, rows):
    pos = first_row + iota((rows, 1), 0)
    doc = doc_of(starts, pos)
    masks = [(doc_of(starts, pos - (KC - 1 - k)) == doc).astype(F32) for k in range(KC)]
    return doc, masks


def local(
    layer_input,
    out_grad,
    doc_starts,
    real_mask,
    norm_gain,
    attention_input_rows,
    mixer_in,
    state_in,
    step_in,
    conv_mixer,
    conv_state,
    step_bias,
    decay_rate,
    skip_gain,
    gated_gain,
    joint_out,
    mlp_gain,
    gate_up,
    down_weight,
):
    T, D = layer_input.shape
    NS, n = lax.axis_size("state"), lax.axis_size("seq")
    t, s = lax.axis_index("state"), lax.axis_index("seq")
    HL = NH // NS
    C = HL * HDM
    QC = QUERY_HEADS * HEAD_SIZE // NS
    TO = T // NS
    DM = NH * HDM
    NW = state_in.shape[2]
    AQ = QUERY_HEADS * HEAD_SIZE
    KW = KEY_VALUE_HEADS * HEAD_SIZE
    kvh = t * KEY_VALUE_HEADS // NS
    first_row = s * T
    starts = [doc_starts[k] for k in range(doc_starts.shape[0])]
    dsl = lax.dynamic_slice_in_dim

    w_q = dsl(attention_input_rows, QC * t, QC, 1)
    w_k = dsl(attention_input_rows, AQ + HEAD_SIZE * kvh, HEAD_SIZE, 1)
    w_v = dsl(attention_input_rows, AQ + KW + HEAD_SIZE * kvh, HEAD_SIZE, 1)
    w_qkv = jnp.concatenate([w_q, w_k, w_v], axis=1)
    w_mix = dsl(mixer_in, C * t, C, 2)
    w_mix = jnp.concatenate([w_mix[:, 0], w_mix[:, 1]], axis=1)
    w_step = jnp.pad(dsl(step_in, HL * t, HL, 1), ((0, 0), (0, LANES - HL)))
    pad_row = lambda v: jnp.pad(dsl(v, HL * t, HL, 0), (0, LANES - HL))[None, :]
    bias_row, rate_row = pad_row(step_bias), pad_row(decay_rate)
    skip_row = jnp.repeat(dsl(skip_gain, HL * t, HL, 0), HDM)[None, :]
    taps_mix = dsl(conv_mixer, C * t, C, 1)
    ggain_row = dsl(gated_gain, C * t, C, 0)[None, :]
    w_joint = jnp.concatenate([dsl(joint_out, QC * t, QC, 0), dsl(joint_out, AQ + C * t, C, 0)], axis=0)
    st_own = jnp.transpose(state_in, (1, 2, 0))
    taps_own = conv_state.reshape(KC, 2 * NW)
    w_gu = jnp.concatenate([gate_up[:, 0], gate_up[:, 1]], axis=1)
    F = gate_up.shape[2]
    ngain, mgain = norm_gain[None, :], mlp_gain[None, :]
    real_f = real_mask.astype(F32)
    real_col = dsl(real_f, first_row, T, 0)[:, None]
    all_doc = doc_of(starts, jnp.arange(n * T, dtype=jnp.int32)[None, :])[0]
    codes = jnp.where(real_mask > 0, all_doc, -7).reshape(n, 1, T)
    pos = first_row + jnp.arange(T, dtype=jnp.int32)
    firsts = jnp.max(jnp.where(doc_starts[None, :] <= pos[:, None], doc_starts[None, :], 0), axis=1)
    powers = (jnp.arange(LANES) % (HEAD_SIZE // 2)).astype(F32) * (2.0 / HEAD_SIZE)
    angles = (pos - firsts).astype(F32)[:, None] * jnp.exp(-math.log(ROPE_BASE) * powers)[None, :]
    cosine, sine = jnp.cos(angles), jnp.sin(angles)

    halo = lax.ppermute(layer_input[T - HALO :], "seq", [(i, (i + 1) % n) for i in range(n)])
    st_all = lax.all_gather(st_own, "state", axis=1, tiled=True).reshape(-1, D)
    taps_all = lax.all_gather(conv_state, "state", axis=2, tiled=True).reshape(KC, -1)

    doc, masks = masks_of(starts, first_row, T)
    x_ext = jnp.concatenate([halo, layer_input]).astype(F32)
    inv1 = lax.rsqrt(jnp.mean(x_ext * x_ext, axis=1, keepdims=True) + EPSILON)
    normed = (x_ext * inv1 * ngain).astype(BF16)
    main = normed[HALO:]
    qkv = nn(main, w_qkv)
    scale = 1.0 / math.sqrt(HEAD_SIZE)
    q = (rope(qkv[:, :QC], cosine, sine, 1.0).astype(BF16) * scale).astype(BF16)
    lane = iota((T, LANES), 1)
    is_k = lane < HEAD_SIZE
    kcos, ksin = jnp.where(is_k, cosine, 1.0), jnp.where(is_k, sine, 0.0)
    kv = rope(qkv[:, QC:], kcos, ksin, 1.0).astype(BF16)
    z = nn(main, w_mix[:, :C])
    inner_ext = nn(normed, w_mix[:, C:]).astype(BF16).astype(F32)
    state_ext = nt(normed, st_all).astype(BF16).astype(F32)
    step_raw = nn(main, w_step)
    inner_lin = conv_fwd(inner_ext, taps_mix, masks)
    inner = silu(inner_lin)
    state_conv = silu(conv_fwd(state_ext, taps_all, masks))
    N = state_conv.shape[1] // 2
    write, read = state_conv[:, :N], state_conv[:, N:]
    step = softplus(step_raw + bias_row)
    tri = (iota((T, T), 0) >= iota((T, T), 1)).astype(F32)
    cum = nn(tri, -step * rate_row, HI)
    cum_t = cum.T
    doc_row = doc.T
    linked = (doc == doc_row) & (iota((T, T), 0) >= iota((T, T), 1))
    inflow = step * real_col
    E = expander(C)
    g_mat = nt(read, write, HI)
    in_x = inner * nn(inflow, E, HI)

    def link(h):
        return jnp.exp(jnp.where(linked, cum[:, h : h + 1] - cum_t[h : h + 1, :], FAR))

    y = []
    for p in range(C // LANES):
        xp = in_x[:, LANES * p : LANES * (p + 1)]
        y0 = nn(link(2 * p) * g_mat, xp, HI)
        y1 = nn(link(2 * p + 1) * g_mat, xp, HI)
        y.append(jnp.where(is_k, y0, y1))
    y_intra = jnp.concatenate(y, axis=1)
    doc_last = doc[T - 1 : T]
    cum_last = cum[T - 1 : T]
    tail = jnp.where(doc == doc_last, jnp.exp(cum_last - cum), 0.0)
    tail_e = nn(tail, E, HI)
    state_part = tn(tail_e * in_x, write, HI)
    prior = doc_of(starts, jnp.full((1, 1), first_row - 1, jnp.int32))
    alive = (doc == prior).astype(F32)
    through = alive[T - 1 : T] * jnp.exp(cum_last)
    reach_e = nn(alive * jnp.exp(cum), E, HI)
    thr_col = tn(E, through.T, HI)

    def carry(value, direction):
        thr, total = thr_col, value
        move = lambda v, d: lax.ppermute(
            v, "seq", [(i, i + d * direction) for i in range(n) if 0 <= i + d * direction < n]
        )
        thr, total = move(thr, 1), move(total, 1)
        d = 1
        while d < n:
            thr_e, total_e = move(thr, d), move(total, d)
            total = total + thr * total_e
            thr = thr * thr_e
            d *= 2
        return total

    s_in = carry(state_part, 1)
    kv_all = lax.all_gather(kv, "seq")
    head0 = lane < HEAD_SIZE
    qf = q.astype(F32)
    q2 = jnp.where(
        jnp.concatenate([head0, head0]), jnp.concatenate([qf, roll(qf, HEAD_SIZE)]), 0.0
    ).astype(BF16)
    doc2 = jnp.concatenate([doc, doc])
    row2 = jnp.concatenate([iota((T, T), 0), iota((T, T), 0)])
    col2 = iota((2 * T, T), 1)

    def allowed_at(j):
        code = codes[j]
        return ((code == doc2) & ((j < s) | (col2 <= row2))) | ((j == s) & (col2 == row2))

    def attend(j, carried):
        m, l, acc = carried
        scores = jnp.where(allowed_at(j), nt(q2, kv_all[j]), FAR)
        m_new = jnp.maximum(m, jnp.max(scores, axis=1, keepdims=True))
        shrink = jnp.exp(m - m_new)
        p = jnp.exp(scores - m_new)
        return m_new, l * shrink + jnp.sum(p, axis=1, keepdims=True), acc * shrink + nn(
            p.astype(BF16), kv_all[j]
        )

    begin = attend(
        s, (jnp.full((2 * T, 1), FAR), jnp.zeros((2 * T, 1)), jnp.zeros((2 * T, LANES)))
    )
    m, l, acc = lax.fori_loop(0, s, attend, begin)
    out2 = acc / l
    lse = m + jnp.log(l)
    attended_f = jnp.where(head0, roll(out2[:T], HEAD_SIZE), out2[T:])
    attended = attended_f.astype(BF16)

    y_inter = reach_e * nt(read, s_in, HI)
    ssd = y_intra + y_inter
    full_mix = ssd + skip_row * inner
    gated = full_mix * silu(z)
    sumsq = lax.psum(jnp.sum(gated * gated, axis=1, keepdims=True), "state")
    inv_g = lax.rsqrt(sumsq / DM + EPSILON)
    joined = jnp.concatenate([attended, (gated * inv_g * ggain_row).astype(BF16)], axis=1)
    part = nn(joined, w_joint).astype(BF16)

    def rs_state(v):
        return lax.psum_scatter(v.astype(F32), "state", scatter_dimension=0, tiled=True)

    def ag_state(v):
        return lax.all_gather(v, "state", axis=0, tiled=True)

    x_own = dsl(layer_input, TO * t, TO, 0).astype(F32)
    res = x_own + rs_state(part)
    inv2 = lax.rsqrt(jnp.mean(res * res, axis=1, keepdims=True) + EPSILON)
    n2 = ag_state((res * inv2 * mgain).astype(BF16))

    gu = nn(n2, w_gu)
    gate, up = gu[:, :F], gu[:, F:]
    dh = nn(out_grad, down_weight)
    sig = sigmoid(gate)
    act = gate * sig
    hidden = (act * up).astype(BF16)
    d_gu = jnp.concatenate(
        [dh * up * (sig * (1.0 + gate * (1.0 - sig))), dh * act], axis=1
    ).astype(BF16)
    mlp_part = nt(hidden, down_weight).astype(BF16)
    dn2_part = nt(d_gu, w_gu).astype(BF16)
    gw_down = tn(out_grad, hidden).astype(BF16)
    gw_gu = tn(n2, d_gu).astype(BF16)
    layer_output = ag_state((res + rs_state(mlp_part)).astype(BF16))
    dn2 = rs_state(dn2_part)
    g_own = dsl(out_grad, TO * t, TO, 0).astype(F32)
    scaled = dn2 * mgain
    d_res = g_own + inv2 * scaled - res * inv2**3 * jnp.mean(scaled * res, axis=1, keepdims=True)
    g_mgain = jnp.sum(dn2 * res * inv2, axis=0, keepdims=True)
    d_branch = ag_state(d_res.astype(BF16))

    d_joined = nt(d_branch, w_joint)
    gw_joint = tn(joined, d_branch).astype(BF16)
    d_att = d_joined[:, :QC].astype(BF16).astype(F32)
    d_gn = d_joined[:, QC:]
    scaled_g = d_gn * ggain_row
    row_dot = lax.psum(jnp.sum(scaled_g * gated, axis=1, keepdims=True), "state") / DM
    d_gated = inv_g * scaled_g - gated * inv_g**3 * row_dot
    g_ggain = jnp.sum(d_gn * gated * inv_g, axis=0, keepdims=True)
    sig_z = sigmoid(z)
    dy = d_gated * z * sig_z
    d_z = d_gated * full_mix * (sig_z * (1.0 + z * (1.0 - sig_z)))
    g_skip = jnp.sum(dy * inner, axis=0, keepdims=True)
    direct = tn(reach_e * dy, read, HI)
    later = carry(direct, -1)

    dout2 = jnp.where(
        jnp.concatenate([head0, head0]), 0.0, jnp.concatenate([roll(d_att, HEAD_SIZE), d_att])
    )
    delta = jnp.sum(dout2 * out2, axis=1, keepdims=True)
    dout2 = dout2.astype(BF16)

    def attend_back(j, carried):
        dq2, dkv = carried
        scores = jnp.where(allowed_at(j), nt(q2, kv_all[j]), FAR)
        p = jnp.exp(scores - lse)
        ds = (p * (nt(dout2, kv_all[j]) - delta)).astype(BF16)
        dkv = lax.dynamic_update_index_in_dim(dkv, tn(ds, q2) + tn(p.astype(BF16), dout2), j, 0)
        return dq2 + nn(ds, kv_all[j]), dkv

    dq2, dkv_all = lax.fori_loop(
        0, s + 1, attend_back, (jnp.zeros((2 * T, LANES)), jnp.zeros((n, T, LANES)))
    )
    dq = jnp.where(head0, dq2[:T], roll(dq2[T:], HEAD_SIZE)) * scale
    d_q = rope(dq, cosine, sine, -1.0).astype(BF16)
    dkv = lax.psum_scatter(dkv_all, "seq", scatter_dimension=0, tiled=False)
    pair = NS // KEY_VALUE_HEADS
    groups = [[g * pair + i for i in range(pair)] for g in range(KEY_VALUE_HEADS)]
    dkv = lax.psum(dkv, "state", axis_index_groups=groups)
    d_kv = rope(dkv, kcos, ksin, -1.0).astype(BF16)

    w_r = nt(write, later, HI)
    tail_r = tail_e * w_r
    d_g = 0.0
    ws = []
    for p in range(C // LANES):
        xp = in_x[:, LANES * p : LANES * (p + 1)]
        dyp = dy[:, LANES * p : LANES * (p + 1)]
        halves = []
        for k in range(2):
            lk = link(2 * p + k)
            mine = is_k if k == 0 else ~is_k
            halves.append(tn(lk * g_mat, dyp, HI))
            d_g = d_g + lk * nt(jnp.where(mine, dyp, 0.0), xp, HI)
        ws.append(jnp.where(is_k, halves[0], halves[1]))
    w_intra = jnp.concatenate(ws, axis=1)
    w_tot = w_intra + tail_r
    ET = E.T
    inflow_e = nn(inflow, E, HI)
    u = nn(inner * w_tot, ET, HI)
    tl = nn(in_x * tail_r, ET, HI)
    dx = inflow_e * w_tot
    thr_s = nn(jnp.sum((later * s_in), axis=1, keepdims=True).T, ET, HI) * through
    d_cum = nn(dy * ssd, ET, HI) - inflow * u
    last = iota((T, LANES), 0) == T - 1
    d_cum = d_cum + jnp.where(last, jnp.sum(tl, axis=0, keepdims=True) + thr_s, 0.0)
    d_ld = tn(tri, d_cum, HI)
    d_step = real_col * u - rate_row * d_ld
    g_rate = -jnp.sum(step * d_ld, axis=0, keepdims=True)
    d_read = nn(d_g, write, HI) + nn(reach_e * dy, s_in, HI)
    d_write = tn(d_g, read, HI) + nn(tail_e * in_x, later, HI)
    d_step_f = d_step * sigmoid(step_raw + bias_row)
    g_bias = jnp.sum(d_step_f, axis=0, keepdims=True)
    d_step_b = d_step_f.astype(BF16)
    d_inner_lin = (dx + skip_row * dy) * silu_slope(inner_lin)
    d_inner_ext, g_taps_mix = conv_bwd(inner_ext, taps_mix, masks, d_inner_lin)
    wr_t = jnp.concatenate([d_write.T, d_read.T], axis=0).reshape(2, NS, NW, T).transpose(1, 0, 2, 3)
    wr_own = lax.psum_scatter(wr_t, "state", scatter_dimension=0, tiled=False).reshape(2 * NW, T).T
    st_ext_own = nt(normed, st_own.reshape(-1, D)).astype(BF16).astype(F32)
    d_st_lin = wr_own * silu_slope(conv_fwd(st_ext_own, taps_own, masks))
    d_st_ext, g_taps_st = conv_bwd(st_ext_own, taps_own, masks, d_st_lin)
    d_st_ext = d_st_ext.astype(BF16)
    d_inner_ext = d_inner_ext.astype(BF16)
    d_z = d_z.astype(BF16)
    gw_mix = jnp.concatenate([tn(main, d_z), tn(normed, d_inner_ext)], axis=1).astype(BF16)
    gw_st = tn(normed, d_st_ext).astype(BF16)
    gw_step = tn(main, d_step_b).astype(BF16)
    odd = t % pair
    d_kv_mine = jnp.where(is_k == (odd == 0), d_kv, jnp.zeros_like(d_kv))
    gw_q = tn(main, d_q).astype(BF16)
    gw_kv = tn(main, d_kv).astype(BF16)
    gw_kv = jnp.where(odd == 0, gw_kv[:, :HEAD_SIZE], gw_kv[:, HEAD_SIZE:])
    halo_part = nt(d_inner_ext[:HALO], w_mix[:, C:]) + nn(d_st_ext[:HALO], st_own.reshape(-1, D))
    back = lax.ppermute(halo_part, "seq", [((i + 1) % n, i) for i in range(n)])
    d_n = (
        nt(jnp.concatenate([d_q, d_kv_mine], axis=1), w_qkv)
        + nt(jnp.concatenate([d_z, d_inner_ext[HALO:]], axis=1), w_mix)
        + nn(d_st_ext[HALO:], st_own.reshape(-1, D))
        + nt(d_step_b, w_step)
    )
    d_n = jnp.concatenate([d_n[: T - HALO], d_n[T - HALO :] + back])
    d_n = rs_state(d_n.astype(BF16))
    inv1_own = dsl(inv1, HALO + TO * t, TO, 0)
    scaled_n = d_n * ngain
    in_g = d_res + inv1_own * scaled_n - x_own * inv1_own**3 * jnp.mean(
        scaled_n * x_own, axis=1, keepdims=True
    )
    g_ngain = jnp.sum(d_n * x_own * inv1_own, axis=0, keepdims=True)
    input_grad = ag_state(in_g)

    def rs_seq(v):
        return lax.psum_scatter(v, "seq", scatter_dimension=0, tiled=True)

    r_down, r_gu = rs_seq(gw_down), rs_seq(gw_gu)
    r_a = rs_seq(jnp.concatenate([gw_q, gw_kv, gw_mix, gw_step[:, :HL], gw_st], axis=1))
    rows = D // n
    gj = lax.all_gather(gw_joint, "state", axis=0)
    gj = jnp.concatenate([gj[:, :QC].reshape(AQ, D), gj[:, QC:].reshape(DM, D)], axis=0)
    r_joint = lax.psum_scatter(gj, "seq", scatter_dimension=0, tiled=True)
    W = QC + HEAD_SIZE + 2 * C + HL
    ga = lax.all_gather(r_a[:, :W], "state", axis=1)
    g_att = jnp.concatenate(
        [ga[:, :, :QC].reshape(rows, AQ)]
        + [ga[:, h * pair + k, QC : QC + HEAD_SIZE] for k in range(2) for h in range(KEY_VALUE_HEADS)],
        axis=1,
    )
    o = QC + HEAD_SIZE
    g_mix = jnp.stack(
        [ga[:, :, o : o + C].reshape(rows, DM), ga[:, :, o + C : o + 2 * C].reshape(rows, DM)], axis=1
    )
    g_step = ga[:, :, o + 2 * C :].reshape(rows, NH)
    g_st = r_a[:, W:].reshape(rows, 2, NW)
    sums = lax.psum((g_ngain, g_mgain), ("seq", "state"))
    small = lax.psum(
        (g_ggain, g_taps_mix, g_taps_st, g_bias[:, :HL], g_rate[:, :HL], g_skip), "seq"
    )
    s_ggain, s_taps, s_st, s_bias, s_rate, s_skip = small
    s_skip = jnp.sum(s_skip.reshape(1, HL, HDM), axis=2)
    cat = lambda v: lax.all_gather(v, "state", axis=1, tiled=True)
    s_ggain, s_taps, s_bias, s_rate, s_skip = map(cat, (s_ggain, s_taps, s_bias, s_rate, s_skip))
    take = lambda v: dsl(v[0], s * (v.shape[1] // n), v.shape[1] // n, 0)
    f = lambda v: v.astype(F32)
    return (
        layer_output,
        input_grad,
        take(sums[0]),
        f(g_att),
        f(g_mix),
        f(g_st),
        f(g_step),
        s_taps,
        s_st.reshape(KC, 2, NW),
        s_bias[0],
        s_rate[0],
        s_skip[0],
        take(s_ggain),
        f(r_joint),
        take(sums[1]),
        f(r_gu).reshape(rows, 2, F),
        f(r_down),
    )


def solution(mesh):
    rep = P()
    in_specs = (
        P("seq", None),
        P("seq", None),
        rep,
        rep,
        rep,
        rep,
        rep,
        P(None, None, "state"),
        rep,
        rep,
        P(None, None, "state"),
        rep,
        rep,
        rep,
        rep,
        rep,
        rep,
        P(None, None, "state"),
        P(None, "state"),
    )
    out_specs = (
        P("seq", None),
        P("seq", None),
        P("seq"),
        P("seq", None),
        P("seq", None, None),
        P("seq", None, "state"),
        P("seq", None),
        rep,
        P(None, None, "state"),
        rep,
        rep,
        rep,
        P("seq"),
        P("seq", None),
        P("seq"),
        P("seq", None, "state"),
        P("seq", "state"),
    )
    return jax.shard_map(local, mesh=mesh, in_specs=in_specs, out_specs=out_specs, check_vma=False)
```

```python
import functools
import math

import jax
import jax.numpy as jnp
from jax import lax
from jax.experimental import pallas as pl
from jax.experimental.pallas import tpu as pltpu
from jax.sharding import PartitionSpec as P

QUERY_HEADS = 8
KEY_VALUE_HEADS = 2
HEAD_SIZE = 64
NH = 24
HDM = 64
KC = 4
EPSILON = 1e-05
ROPE_BASE = 10000.0
HI = lax.Precision.HIGHEST
F32 = jnp.float32
BF16 = jnp.bfloat16
LANES = 128
HALO = 16
FAR = -1e30
MESH = pl.DeviceIdType.MESH
VMEM_LIMIT = 60 << 20


def nn(a, b, p=None):
    return lax.dot_general(a, b, (((1,), (0,)), ((), ())), precision=p, preferred_element_type=F32)


def nt(a, b, p=None):
    return lax.dot_general(a, b, (((1,), (1,)), ((), ())), precision=p, preferred_element_type=F32)


def tn(a, b, p=None):
    return lax.dot_general(a, b, (((0,), (0,)), ((), ())), precision=p, preferred_element_type=F32)


def sigmoid(v):
    return 1.0 / (1.0 + jnp.exp(-v))


def silu(v):
    return v * sigmoid(v)


def silu_slope(v):
    s = sigmoid(v)
    return s * (1.0 + v * (1.0 - s))


def softplus(v):
    return jnp.maximum(v, 0.0) + jnp.log1p(jnp.exp(-jnp.abs(v)))


def iota(shape, dim):
    return lax.broadcasted_iota(jnp.int32, shape, dim)


def doc_of(starts, pos):
    found = jnp.full(pos.shape, -1, jnp.int32)
    for start in starts:
        found = found + (pos >= start).astype(jnp.int32)
    return found


def roll(v, shift):
    return pltpu.roll(v, shift, 1)


def rope(v, cosine, sine, direction):
    first = (iota(v.shape, 1) % HEAD_SIZE) < HEAD_SIZE // 2
    half = HEAD_SIZE // 2
    partner = jnp.where(first, -roll(v, v.shape[1] - half), roll(v, half))
    return v * cosine + partner * (direction * sine)


def expander(width):
    return (iota((LANES, width), 1) // HDM == iota((LANES, width), 0)).astype(F32)


def conv_fwd(ext, taps, masks):
    rows = ext.shape[0] - HALO
    total = 0.0
    for k in range(KC):
        at = HALO - KC + 1 + k
        total = total + ext[at : at + rows] * taps[k : k + 1] * masks[k]
    return total


def conv_bwd(ext, taps, masks, up):
    rows = up.shape[0]
    total, weights = 0.0, []
    for k in range(KC):
        at = HALO - KC + 1 + k
        masked = up * masks[k]
        weights.append(jnp.sum(masked * ext[at : at + rows], axis=0, keepdims=True))
        parts = [jnp.zeros((at, up.shape[1]), F32), masked * taps[k : k + 1]]
        if KC - 1 - k:
            parts.append(jnp.zeros((KC - 1 - k, up.shape[1]), F32))
        total = total + jnp.concatenate(parts, axis=0)
    return total, jnp.concatenate(weights, axis=0)


def masks_of(starts, first_row, rows):
    pos = first_row + iota((rows, 1), 0)
    doc = doc_of(starts, pos)
    masks = [(doc_of(starts, pos - (KC - 1 - k)) == doc).astype(F32) for k in range(KC)]
    return doc, masks


def push(src, dst, send_sem, recv_sem, device):
    copy = pltpu.make_async_remote_copy(
        src_ref=src,
        dst_ref=dst,
        send_sem=send_sem,
        recv_sem=recv_sem,
        device_id=device,
        device_id_type=MESH,
    )
    copy.start()
    return copy


def greet(n, ns, s, t):
    barrier = pltpu.get_barrier_semaphore()

    def seq_turn(k, carried):
        pl.semaphore_signal(
            barrier, inc=1, device_id={"seq": lax.rem(s + k, n)}, device_id_type=MESH
        )
        return carried

    lax.fori_loop(1, n, seq_turn, 0)
    for k in range(1, ns):
        pl.semaphore_signal(
            barrier, inc=1, device_id={"state": lax.rem(t + k, ns)}, device_id_type=MESH
        )
    pl.semaphore_wait(barrier, n - 1 + ns - 1)


def spread(ref, ns, t, src, send, recv):
    return [
        push(src, ref, send.at[k - 1], recv.at[k - 1], {"state": lax.rem(t + k, ns)})
        for k in range(1, ns)
    ]


def conv_ref(ext_ref, taps, masks, rows):
    total = 0.0
    for k in range(KC):
        at = HALO - KC + 1 + k
        total = total + ext_ref[at : at + rows, :] * taps[k : k + 1] * masks[k]
    return total


class Carry:
    def __init__(self, n, s, direction, tx, rx, thr_tx, thr_rx, sems):
        self.n, self.s, self.direction = n, s, direction
        self.tx, self.rx, self.thr_tx, self.thr_rx = tx, rx, thr_tx, thr_rx
        self.send, self.recv, self.thr_send, self.thr_recv = sems
        self.steps = carry_steps(n)

    def copies(self, slot):
        d, source = self.steps[slot]
        to = lax.rem(self.s + self.direction * d + self.n, self.n)
        make = lambda src, dst, a, b: pltpu.make_async_remote_copy(
            src_ref=src,
            dst_ref=dst,
            send_sem=a,
            recv_sem=b,
            device_id={"seq": to},
            device_id_type=MESH,
        )
        return (
            make(self.tx.at[source], self.rx.at[slot], self.send.at[slot], self.recv.at[slot]),
            make(
                self.thr_tx.at[source],
                self.thr_rx.at[slot],
                self.thr_send.at[slot],
                self.thr_recv.at[slot],
            ),
        )

    def sends(self, slot):
        to = self.s + self.direction * self.steps[slot][0]
        return (to >= 0) & (to < self.n)

    def gets(self, slot):
        source = self.s - self.direction * self.steps[slot][0]
        return (source >= 0) & (source < self.n)

    def start(self, slot):
        @pl.when(self.sends(slot))
        def _():
            for copy in self.copies(slot):
                copy.start()

    def finish(self, slot):
        @pl.when(self.sends(slot))
        def _():
            for copy in self.copies(slot):
                copy.wait_send()

    def arrive(self, slot):
        @pl.when(self.gets(slot))
        def _():
            for copy in self.copies(slot):
                copy.wait_recv()

        @pl.when(jnp.logical_not(self.gets(slot)))
        def _():
            self.rx[slot] = jnp.zeros(self.rx.shape[1:], self.rx.dtype)
            self.thr_rx[slot] = jnp.zeros(self.thr_rx.shape[1:], F32)

        return self.rx[slot].astype(F32), self.thr_rx[slot]

    def begin(self, part, thr):
        self.tx[0] = part.astype(BF16)
        self.thr_tx[0] = thr
        self.start(0)
        if len(self.steps) > 1:
            self.start(1)

    def put(self, source, part, thr):
        self.tx[source] = part.astype(BF16)
        self.thr_tx[source] = thr


def carry_steps(n):
    steps = [(1, 0)]
    if n > 2:
        steps.append((2, 0))
    d, source = 2, 1
    while 2 * d < n + 1 and d < n - 1:
        steps.append((d, source))
        d, source = 2 * d, source + 1
    return steps


def expand_rows(width):
    return (iota((width, LANES), 0) // HDM == iota((width, LANES), 1)).astype(F32)


def link_of(linked, cum, cum_t, h):
    return jnp.exp(jnp.where(linked, cum[:, h : h + 1] - cum_t[h : h + 1, :], FAR))


def forward_kernel(
    n, ns, x, w_qkv, w_mix, w_step, st_own, taps_st, taps_mix, ngain, bias_row, rate_row, skip_row,
    ggain_row, w_joint, mgain, real_col, codes, cosine, sine, doc_starts,
    n2, res, inv2, normed, inv1, q2_out, kv_out, out2, lse, z_out, inner_ext, state_ext, step_raw,
    ssd_out, s_in_out, inv_g_out, joined,
    halo, st_all, taps_all, kv_all, ext_f, ext_s, m_ref, l_ref, acc_ref,
    carry_tx, carry_rx, thr_tx, thr_rx, sq_tx, sq_rx, rs_tx, rs_rx, n2_all,
    halo_sem, st_send, st_recv, taps_send, taps_recv, kv_send, kv_recv,
    c_send, c_recv, ct_send, ct_recv, sq_send, sq_recv, rs_send, rs_recv, ag_send, ag_recv,
):
    T, D = x.shape
    t, s = lax.axis_index("state"), lax.axis_index("seq")
    C = taps_mix.shape[1]
    QC = 2 * HEAD_SIZE
    NW = st_own.shape[1]
    N = NW * ns
    TO = T // ns
    DM = C * ns
    scale = 1.0 / math.sqrt(HEAD_SIZE)
    greet(n, ns, s, t)
    halo_copy = push(
        x.at[pl.ds(T - HALO, HALO)], halo, halo_sem.at[0], halo_sem.at[1], {"seq": lax.rem(s + 1, n)}
    )
    mine = pl.ds(pl.multiple_of(NW * t, NW), NW)
    st_copies = spread(st_all.at[:, mine, :], ns, t, st_own, st_send, st_recv)
    taps_copies = spread(taps_all.at[:, mine, :], ns, t, taps_st, taps_send, taps_recv)
    st_all[:, mine, :] = st_own[...]
    taps_all[:, mine, :] = taps_st[...]

    first_row = s * T
    starts = [doc_starts[k] for k in range(doc_starts.shape[0])]
    doc, masks = masks_of(starts, first_row, T)
    doc_row = doc_of(starts, first_row + iota((1, T), 1))
    lane = iota((T, LANES), 1)
    low = lane < HEAD_SIZE

    xf = x[...].astype(F32)
    inv = lax.rsqrt(jnp.mean(xf * xf, axis=1, keepdims=True) + EPSILON)
    inv1[HALO:, :] = inv
    normed[HALO:, :] = (xf * inv * ngain[...]).astype(BF16)
    main = normed[HALO:, :]
    qkv = nn(main, w_qkv[...])
    q = (rope(qkv[:, :QC], cosine[...], sine[...], 1.0).astype(BF16) * scale).astype(F32)
    kcos, ksin = jnp.where(low, cosine[...], 1.0), jnp.where(low, sine[...], 0.0)
    kv = rope(qkv[:, QC:], kcos, ksin, 1.0).astype(BF16)
    kv_all[s] = kv
    kv_out[s] = kv

    def kv_copy(k, to):
        return pltpu.make_async_remote_copy(
            src_ref=kv_all.at[s],
            dst_ref=kv_all.at[s],
            send_sem=kv_send.at[k - 1],
            recv_sem=kv_recv.at[k - 1],
            device_id={"seq": to},
            device_id_type=MESH,
        )

    def kv_turn(k, carried):
        kv_copy(k, lax.rem(s + k, n)).start()
        return carried

    lax.fori_loop(1, n - s, kv_turn, 0)
    q2_out[:T, :] = jnp.where(low, q, 0.0).astype(BF16)
    q2_out[T:, :] = jnp.where(low, roll(q, HEAD_SIZE), 0.0).astype(BF16)
    z_out[...] = nn(main, w_mix[:, :C])
    raw = nn(main, w_step[...])
    step_raw[...] = raw

    halo_copy.wait_recv()
    hf = halo[...].astype(F32)
    inv_h = lax.rsqrt(jnp.mean(hf * hf, axis=1, keepdims=True) + EPSILON)
    inv1[:HALO, :] = inv_h
    normed[:HALO, :] = (hf * inv_h * ngain[...]).astype(BF16)
    ext = nn(normed[...], w_mix[:, C:]).astype(BF16)
    inner_ext[...] = ext
    ext_f[...] = ext.astype(F32)
    inner = silu(conv_ref(ext_f, taps_mix[...], masks, T))
    for copy in st_copies + taps_copies:
        copy.wait_recv()
    state_conv = []
    for c in range(2):
        ext = nt(normed[...], st_all[c]).astype(BF16)
        state_ext[:, N * c : N * (c + 1)] = ext
        ext_s[...] = ext.astype(F32)
        taps = taps_all[c].T
        state_conv.append(silu(conv_ref(ext_s, taps, masks, T)))
    write, read = state_conv
    step = softplus(raw + bias_row[...])
    causal = iota((T, T), 0) >= iota((T, T), 1)
    cum = nn(causal.astype(F32), -step * rate_row[...], HI)
    cum_t = cum.T
    linked = (doc == doc_row) & causal
    E = expander(C)
    in_x = inner * nn(step * real_col[...], E, HI)
    cum_last = cum[T - 1 : T]
    last = first_row + T - 1
    doc_last = doc_of(starts, jnp.full((T, 1), last, jnp.int32))
    prior = doc_of(starts, jnp.full((T, 1), first_row - 1, jnp.int32))
    tail = jnp.where(doc == doc_last, jnp.exp(cum_last - cum), 0.0)
    state_part = tn(nn(tail, E, HI) * in_x, write, HI)
    alive = (doc == prior).astype(F32)
    alive_last = (doc_last == prior).astype(F32)[:8]
    thr = alive_last * jnp.exp(jnp.broadcast_to(cum_last, (8, LANES)))
    carry = Carry(
        n, s, 1, carry_tx, carry_rx, thr_tx, thr_rx, (c_send, c_recv, ct_send, ct_recv)
    )
    carry.begin(state_part, thr)
    steps = len(carry.steps)
    rows_e = expand_rows(C)
    window = [None]

    def advance(slot):
        total, thr_got = carry.arrive(slot)
        if slot == 0:
            window[0] = (total, thr_got)
        else:
            now, thr_now = window[0]
            window[0] = (now + nt(rows_e, thr_now, HI)[:, :1] * total, thr_now * thr_got)
        if slot >= 1 and slot + 1 < steps:
            carry.put(carry.steps[slot + 1][1], *window[0])
            carry.start(slot + 1)

    g_mat = nt(read, write, HI)
    for p in range(C // LANES):
        at = slice(LANES * p, LANES * (p + 1))
        y0 = nn(link_of(linked, cum, cum_t, 2 * p) * g_mat, in_x[:, at], HI)
        y1 = nn(link_of(linked, cum, cum_t, 2 * p + 1) * g_mat, in_x[:, at], HI)
        ssd_out[:, at] = jnp.where(low, y0, y1)
        if p == 0:
            advance(0)
            if steps > 1:
                advance(1)
        elif p + 1 < steps:
            advance(p + 1)
    done = max(2, C // LANES + 1)

    q2 = q2_out[...]
    doc2 = jnp.concatenate([doc, doc], axis=0)
    m_ref[...] = jnp.full(m_ref.shape, FAR, F32)
    l_ref[...] = jnp.zeros(l_ref.shape, F32)
    acc_ref[...] = jnp.zeros(acc_ref.shape, F32)

    def attend(j, diagonal):
        block = kv_all[j]
        allowed = codes[j] == doc2
        if diagonal:
            rows2 = jnp.concatenate([iota((T, T), 0)] * 2, axis=0)
            cols2 = iota((2 * T, T), 1)
            allowed = (allowed & (cols2 <= rows2)) | (cols2 == rows2)
        scores = jnp.where(allowed, nt(q2, block), FAR)
        m = m_ref[...]
        m_new = jnp.maximum(m, jnp.max(scores, axis=1, keepdims=True))
        shrink = jnp.exp(m - m_new)
        p = jnp.exp(scores - m_new)
        l_ref[...] = l_ref[...] * shrink + jnp.sum(p, axis=1, keepdims=True)
        acc_ref[...] = acc_ref[...] * shrink + nn(p.astype(BF16), block)
        m_ref[...] = m_new

    attend(s, True)

    def attend_turn(k, carried):
        kv_copy(k, lax.rem(s + k, n)).wait_recv()
        attend(s - k, False)
        kv_out[s - k] = kv_all[s - k]
        return carried

    lax.fori_loop(1, s + 1, attend_turn, 0)
    lse[...] = m_ref[...] + jnp.log(l_ref[...])
    out = acc_ref[...] / l_ref[...]
    out2[...] = out
    joined[:, :QC] = jnp.where(low, roll(out[:T], HEAD_SIZE), out[T:]).astype(BF16)

    for slot in range(done, steps):
        advance(slot)
    s_in = window[0][0]
    s_in_out[...] = s_in
    ssd = ssd_out[...] + nn(alive * jnp.exp(cum), E, HI) * nt(read, s_in, HI)
    ssd_out[...] = ssd
    gated = (ssd + skip_row[...] * inner) * silu(z_out[...])
    sq_tx[...] = nt(jnp.ones((8, C), F32), gated * gated, HI)
    sq_copies = [
        push(
            sq_tx, sq_rx.at[k - 1], sq_send.at[k - 1], sq_recv.at[k - 1],
            {"state": lax.rem(t + k, ns)},
        )
        for k in range(1, ns)
    ]
    total = sq_tx[...]
    for k in range(1, ns):
        sq_copies[k - 1].wait_recv()
        total = total + sq_rx[k - 1]
    inv_row = lax.rsqrt(total / DM + EPSILON)
    first = (iota((8, LANES), 0) == 0).astype(F32)
    inv_g = tn(inv_row, first, HI)[:, :1]
    inv_g_out[...] = inv_g
    joined[:, QC:] = (gated * inv_g * ggain_row[...]).astype(BF16)
    part = nn(joined[...], w_joint[...]).astype(BF16)
    for k in range(ns):
        rs_tx[k] = part[TO * k : TO * (k + 1)]
    rs_copies = []
    for k in range(1, ns):
        p = lax.rem(t + k, ns)
        rs_copies.append(
            push(rs_tx.at[p], rs_rx.at[k - 1], rs_send.at[k - 1], rs_recv.at[k - 1], {"state": p})
        )
    total = x[pl.ds(pl.multiple_of(TO * t, TO), TO), :].astype(F32) + rs_tx[t].astype(F32)
    for k in range(1, ns):
        rs_copies[k - 1].wait_recv()
        total = total + rs_rx[k - 1].astype(F32)
    res[...] = total
    inv = lax.rsqrt(jnp.mean(total * total, axis=1, keepdims=True) + EPSILON)
    inv2[...] = inv
    n2_all[t] = (total * inv * mgain[...]).astype(BF16)
    ag_copies = spread(n2_all.at[t], ns, t, n2_all.at[t], ag_send, ag_recv)
    for copy in ag_copies:
        copy.wait_recv()
    for k in range(ns):
        n2[TO * k : TO * (k + 1), :] = n2_all[k]
    for copy in [halo_copy] + st_copies + taps_copies + sq_copies + rs_copies + ag_copies:
        copy.wait_send()
    for slot in range(steps):
        carry.finish(slot)

    def kv_end(k, carried):
        kv_copy(k, lax.rem(s + k, n)).wait_send()
        return carried

    lax.fori_loop(1, n - s, kv_end, 0)


def forward(n, ns, args):
    x, w_qkv, w_mix, w_step, st_own = args[:5]
    T, D = x.shape
    C = w_mix.shape[1] // 2
    NW = st_own.shape[1]
    N, TO = NW * ns, T // ns
    steps = len(carry_steps(n))
    sd = jax.ShapeDtypeStruct
    outs = (
        sd((T, D), BF16), sd((TO, D), F32), sd((TO, 1), F32), sd((T + HALO, D), BF16),
        sd((T + HALO, 1), F32), sd((2 * T, LANES), BF16), sd((n, T, LANES), BF16),
        sd((2 * T, LANES), F32), sd((2 * T, 1), F32), sd((T, C), F32), sd((T + HALO, C), BF16),
        sd((T + HALO, 2 * N), BF16), sd((T, LANES), F32), sd((T, C), F32), sd((C, N), F32),
        sd((T, 1), F32), sd((T, 2 * HEAD_SIZE + C), BF16),
    )
    vm, dma = pltpu.VMEM, lambda k: pltpu.SemaphoreType.DMA((k,))
    scratch = [
        vm((HALO, D), BF16), vm((2, N, D), BF16), vm((2, N, LANES), F32), vm((n, T, LANES), BF16),
        vm((T + HALO, C), F32), vm((T + HALO, N), F32), vm((2 * T, 1), F32), vm((2 * T, 1), F32),
        vm((2 * T, LANES), F32),
        vm((steps, C, N), BF16), vm((steps, C, N), BF16), vm((steps, 8, LANES), F32),
        vm((steps, 8, LANES), F32), vm((8, T), F32), vm((ns - 1, 8, T), F32),
        vm((ns, TO, D), BF16), vm((ns - 1, TO, D), BF16), vm((ns, TO, D), BF16),
        dma(2), dma(ns - 1), dma(ns - 1), dma(ns - 1), dma(ns - 1), dma(n - 1), dma(n - 1),
        dma(steps), dma(steps), dma(steps), dma(steps), dma(ns - 1), dma(ns - 1), dma(ns - 1),
        dma(ns - 1), dma(ns - 1), dma(ns - 1),
    ]
    whole = pl.BlockSpec(memory_space=pltpu.VMEM)
    return pl.pallas_call(
        functools.partial(forward_kernel, n, ns),
        out_shape=outs,
        in_specs=[whole] * (len(args) - 1) + [pl.BlockSpec(memory_space=pltpu.SMEM)],
        out_specs=(whole,) * len(outs),
        scratch_shapes=scratch,
        name="forward",
        compiler_params=pltpu.CompilerParams(
            collective_id=1, has_side_effects=True, vmem_limit_bytes=VMEM_LIMIT
        ),
    )(*args)


def rope_x(v, cosine, sine, direction):
    first = (iota(v.shape, 1) % HEAD_SIZE) < HEAD_SIZE // 2
    half = HEAD_SIZE // 2
    partner = jnp.where(first, -jnp.roll(v, -half, axis=1), jnp.roll(v, half, axis=1))
    return v * cosine + partner * (direction * sine)


def local(
    layer_input,
    out_grad,
    doc_starts,
    real_mask,
    norm_gain,
    attention_input_rows,
    mixer_in,
    state_in,
    step_in,
    conv_mixer,
    conv_state,
    step_bias,
    decay_rate,
    skip_gain,
    gated_gain,
    joint_out,
    mlp_gain,
    gate_up,
    down_weight,
):
    T, D = layer_input.shape
    NS, n = lax.axis_size("state"), lax.axis_size("seq")
    t, s = lax.axis_index("state"), lax.axis_index("seq")
    HL = NH // NS
    C = HL * HDM
    QC = QUERY_HEADS * HEAD_SIZE // NS
    TO = T // NS
    DM = NH * HDM
    NW = state_in.shape[2]
    AQ = QUERY_HEADS * HEAD_SIZE
    KW = KEY_VALUE_HEADS * HEAD_SIZE
    kvh = t * KEY_VALUE_HEADS // NS
    first_row = s * T
    starts = [doc_starts[k] for k in range(doc_starts.shape[0])]
    dsl = lax.dynamic_slice_in_dim

    w_q = dsl(attention_input_rows, QC * t, QC, 1)
    w_k = dsl(attention_input_rows, AQ + HEAD_SIZE * kvh, HEAD_SIZE, 1)
    w_v = dsl(attention_input_rows, AQ + KW + HEAD_SIZE * kvh, HEAD_SIZE, 1)
    w_qkv = jnp.concatenate([w_q, w_k, w_v], axis=1)
    w_mix = dsl(mixer_in, C * t, C, 2)
    w_mix = jnp.concatenate([w_mix[:, 0], w_mix[:, 1]], axis=1)
    w_step = jnp.pad(dsl(step_in, HL * t, HL, 1), ((0, 0), (0, LANES - HL)))
    pad_row = lambda v: jnp.pad(dsl(v, HL * t, HL, 0), (0, LANES - HL))[None, :]
    bias_row, rate_row = pad_row(step_bias), pad_row(decay_rate)
    skip_row = jnp.repeat(dsl(skip_gain, HL * t, HL, 0), HDM)[None, :]
    taps_mix = dsl(conv_mixer, C * t, C, 1)
    ggain_row = dsl(gated_gain, C * t, C, 0)[None, :]
    w_joint = jnp.concatenate([dsl(joint_out, QC * t, QC, 0), dsl(joint_out, AQ + C * t, C, 0)], axis=0)
    st_own = jnp.transpose(state_in, (1, 2, 0))
    taps_own = conv_state.reshape(KC, 2 * NW)
    w_gu = jnp.concatenate([gate_up[:, 0], gate_up[:, 1]], axis=1)
    F = gate_up.shape[2]
    ngain, mgain = norm_gain[None, :], mlp_gain[None, :]
    real_f = real_mask.astype(F32)
    real_col = dsl(real_f, first_row, T, 0)[:, None]
    all_doc = doc_of(starts, jnp.arange(n * T, dtype=jnp.int32)[None, :])[0]
    codes = jnp.where(real_mask > 0, all_doc, -7).reshape(n, 1, T)
    pos = first_row + jnp.arange(T, dtype=jnp.int32)
    firsts = jnp.max(jnp.where(doc_starts[None, :] <= pos[:, None], doc_starts[None, :], 0), axis=1)
    powers = (jnp.arange(LANES) % (HEAD_SIZE // 2)).astype(F32) * (2.0 / HEAD_SIZE)
    angles = (pos - firsts).astype(F32)[:, None] * jnp.exp(-math.log(ROPE_BASE) * powers)[None, :]
    cosine, sine = jnp.cos(angles), jnp.sin(angles)

    taps_rows = jnp.pad(jnp.transpose(conv_state, (1, 2, 0)), ((0, 0), (0, 0), (0, LANES - KC)))
    (
        n2, res, inv2, normed, inv1, q2, kv_all, out2, lse, z, inner_ext, state_ext, step_raw, ssd,
        s_in, inv_g, joined,
    ) = forward(
        n,
        NS,
        (
            layer_input, w_qkv, w_mix, w_step, st_own, taps_rows, taps_mix, ngain, bias_row,
            rate_row, skip_row, ggain_row, w_joint, mgain, real_col, codes, cosine, sine, doc_starts,
        ),
    )

    doc, masks = masks_of(starts, first_row, T)
    main = normed[HALO:]
    scale = 1.0 / math.sqrt(HEAD_SIZE)
    lane = iota((T, LANES), 1)
    is_k = lane < HEAD_SIZE
    kcos, ksin = jnp.where(is_k, cosine, 1.0), jnp.where(is_k, sine, 0.0)
    inner_ext, state_ext = inner_ext.astype(F32), state_ext.astype(F32)
    inner_lin = conv_fwd(inner_ext, taps_mix, masks)
    inner = silu(inner_lin)
    taps_all = lax.all_gather(conv_state, "state", axis=2, tiled=True).reshape(KC, -1)
    state_conv = silu(conv_fwd(state_ext, taps_all, masks))
    N = state_conv.shape[1] // 2
    write, read = state_conv[:, :N], state_conv[:, N:]
    step = softplus(step_raw + bias_row)
    tri = (iota((T, T), 0) >= iota((T, T), 1)).astype(F32)
    cum = nn(tri, -step * rate_row, HI)
    cum_t = cum.T
    doc_row = doc.T
    linked = (doc == doc_row) & (iota((T, T), 0) >= iota((T, T), 1))
    inflow = step * real_col
    E = expander(C)
    g_mat = nt(read, write, HI)
    in_x = inner * nn(inflow, E, HI)

    def link(h):
        return jnp.exp(jnp.where(linked, cum[:, h : h + 1] - cum_t[h : h + 1, :], FAR))

    doc_last = doc[T - 1 : T]
    cum_last = cum[T - 1 : T]
    tail = jnp.where(doc == doc_last, jnp.exp(cum_last - cum), 0.0)
    tail_e = nn(tail, E, HI)
    prior = doc_of(starts, jnp.full((1, 1), first_row - 1, jnp.int32))
    alive = (doc == prior).astype(F32)
    through = alive[T - 1 : T] * jnp.exp(cum_last)
    reach_e = nn(alive * jnp.exp(cum), E, HI)
    thr_col = tn(E, through.T, HI)

    def carry(value, direction):
        thr, total = thr_col, value
        move = lambda v, d: lax.ppermute(
            v, "seq", [(i, i + d * direction) for i in range(n) if 0 <= i + d * direction < n]
        )
        thr, total = move(thr, 1), move(total, 1)
        d = 1
        while d < n:
            thr_e, total_e = move(thr, d), move(total, d)
            total = total + thr * total_e
            thr = thr * thr_e
            d *= 2
        return total

    head0 = lane < HEAD_SIZE
    doc2 = jnp.concatenate([doc, doc])
    row2 = jnp.concatenate([iota((T, T), 0), iota((T, T), 0)])
    col2 = iota((2 * T, T), 1)

    def allowed_at(j):
        code = codes[j]
        return ((code == doc2) & ((j < s) | (col2 <= row2))) | ((j == s) & (col2 == row2))

    full_mix = ssd + skip_row * inner
    gated = full_mix * silu(z)
    x_own = dsl(layer_input, TO * t, TO, 0).astype(F32)

    def rs_state(v):
        return lax.psum_scatter(v.astype(F32), "state", scatter_dimension=0, tiled=True)

    def ag_state(v):
        return lax.all_gather(v, "state", axis=0, tiled=True)

    gu = nn(n2, w_gu)
    gate, up = gu[:, :F], gu[:, F:]
    dh = nn(out_grad, down_weight)
    sig = sigmoid(gate)
    act = gate * sig
    hidden = (act * up).astype(BF16)
    d_gu = jnp.concatenate(
        [dh * up * (sig * (1.0 + gate * (1.0 - sig))), dh * act], axis=1
    ).astype(BF16)
    mlp_part = nt(hidden, down_weight).astype(BF16)
    dn2_part = nt(d_gu, w_gu).astype(BF16)
    gw_down = tn(out_grad, hidden).astype(BF16)
    gw_gu = tn(n2, d_gu).astype(BF16)
    layer_output = ag_state((res + rs_state(mlp_part)).astype(BF16))
    dn2 = rs_state(dn2_part)
    g_own = dsl(out_grad, TO * t, TO, 0).astype(F32)
    scaled = dn2 * mgain
    d_res = g_own + inv2 * scaled - res * inv2**3 * jnp.mean(scaled * res, axis=1, keepdims=True)
    g_mgain = jnp.sum(dn2 * res * inv2, axis=0, keepdims=True)
    d_branch = ag_state(d_res.astype(BF16))

    d_joined = nt(d_branch, w_joint)
    gw_joint = tn(joined, d_branch).astype(BF16)
    d_att = d_joined[:, :QC].astype(BF16).astype(F32)
    d_gn = d_joined[:, QC:]
    scaled_g = d_gn * ggain_row
    row_dot = lax.psum(jnp.sum(scaled_g * gated, axis=1, keepdims=True), "state") / DM
    d_gated = inv_g * scaled_g - gated * inv_g**3 * row_dot
    g_ggain = jnp.sum(d_gn * gated * inv_g, axis=0, keepdims=True)
    sig_z = sigmoid(z)
    dy = d_gated * z * sig_z
    d_z = d_gated * full_mix * (sig_z * (1.0 + z * (1.0 - sig_z)))
    g_skip = jnp.sum(dy * inner, axis=0, keepdims=True)
    direct = tn(reach_e * dy, read, HI)
    later = carry(direct, -1)

    dout2 = jnp.where(
        jnp.concatenate([head0, head0]), 0.0, jnp.concatenate([jnp.roll(d_att, HEAD_SIZE, axis=1), d_att])
    )
    delta = jnp.sum(dout2 * out2, axis=1, keepdims=True)
    dout2 = dout2.astype(BF16)

    def attend_back(j, carried):
        dq2, dkv = carried
        scores = jnp.where(allowed_at(j), nt(q2, kv_all[j]), FAR)
        p = jnp.exp(scores - lse)
        ds = (p * (nt(dout2, kv_all[j]) - delta)).astype(BF16)
        dkv = lax.dynamic_update_index_in_dim(dkv, tn(ds, q2) + tn(p.astype(BF16), dout2), j, 0)
        return dq2 + nn(ds, kv_all[j]), dkv

    dq2, dkv_all = lax.fori_loop(
        0, s + 1, attend_back, (jnp.zeros((2 * T, LANES)), jnp.zeros((n, T, LANES)))
    )
    dq = jnp.where(head0, dq2[:T], jnp.roll(dq2[T:], HEAD_SIZE, axis=1)) * scale
    d_q = rope_x(dq, cosine, sine, -1.0).astype(BF16)
    dkv = lax.psum_scatter(dkv_all, "seq", scatter_dimension=0, tiled=False)
    pair = NS // KEY_VALUE_HEADS
    groups = [[g * pair + i for i in range(pair)] for g in range(KEY_VALUE_HEADS)]
    dkv = lax.psum(dkv, "state", axis_index_groups=groups)
    d_kv = rope_x(dkv, kcos, ksin, -1.0).astype(BF16)

    w_r = nt(write, later, HI)
    tail_r = tail_e * w_r
    d_g = 0.0
    ws = []
    for p in range(C // LANES):
        xp = in_x[:, LANES * p : LANES * (p + 1)]
        dyp = dy[:, LANES * p : LANES * (p + 1)]
        halves = []
        for k in range(2):
            lk = link(2 * p + k)
            mine = is_k if k == 0 else ~is_k
            halves.append(tn(lk * g_mat, dyp, HI))
            d_g = d_g + lk * nt(jnp.where(mine, dyp, 0.0), xp, HI)
        ws.append(jnp.where(is_k, halves[0], halves[1]))
    w_intra = jnp.concatenate(ws, axis=1)
    w_tot = w_intra + tail_r
    ET = E.T
    inflow_e = nn(inflow, E, HI)
    u = nn(inner * w_tot, ET, HI)
    tl = nn(in_x * tail_r, ET, HI)
    dx = inflow_e * w_tot
    thr_s = nn(jnp.sum((later * s_in), axis=1, keepdims=True).T, ET, HI) * through
    d_cum = nn(dy * ssd, ET, HI) - inflow * u
    last = iota((T, LANES), 0) == T - 1
    d_cum = d_cum + jnp.where(last, jnp.sum(tl, axis=0, keepdims=True) + thr_s, 0.0)
    d_ld = tn(tri, d_cum, HI)
    d_step = real_col * u - rate_row * d_ld
    g_rate = -jnp.sum(step * d_ld, axis=0, keepdims=True)
    d_read = nn(d_g, write, HI) + nn(reach_e * dy, s_in, HI)
    d_write = tn(d_g, read, HI) + nn(tail_e * in_x, later, HI)
    d_step_f = d_step * sigmoid(step_raw + bias_row)
    g_bias = jnp.sum(d_step_f, axis=0, keepdims=True)
    d_step_b = d_step_f.astype(BF16)
    d_inner_lin = (dx + skip_row * dy) * silu_slope(inner_lin)
    d_inner_ext, g_taps_mix = conv_bwd(inner_ext, taps_mix, masks, d_inner_lin)
    wr_t = jnp.concatenate([d_write.T, d_read.T], axis=0).reshape(2, NS, NW, T).transpose(1, 0, 2, 3)
    wr_own = lax.psum_scatter(wr_t, "state", scatter_dimension=0, tiled=False).reshape(2 * NW, T).T
    st_ext_own = nt(normed, st_own.reshape(-1, D)).astype(BF16).astype(F32)
    d_st_lin = wr_own * silu_slope(conv_fwd(st_ext_own, taps_own, masks))
    d_st_ext, g_taps_st = conv_bwd(st_ext_own, taps_own, masks, d_st_lin)
    d_st_ext = d_st_ext.astype(BF16)
    d_inner_ext = d_inner_ext.astype(BF16)
    d_z = d_z.astype(BF16)
    gw_mix = jnp.concatenate([tn(main, d_z), tn(normed, d_inner_ext)], axis=1).astype(BF16)
    gw_st = tn(normed, d_st_ext).astype(BF16)
    gw_step = tn(main, d_step_b).astype(BF16)
    odd = t % pair
    d_kv_mine = jnp.where(is_k == (odd == 0), d_kv, jnp.zeros_like(d_kv))
    gw_q = tn(main, d_q).astype(BF16)
    gw_kv = tn(main, d_kv).astype(BF16)
    gw_kv = jnp.where(odd == 0, gw_kv[:, :HEAD_SIZE], gw_kv[:, HEAD_SIZE:])
    halo_part = nt(d_inner_ext[:HALO], w_mix[:, C:]) + nn(d_st_ext[:HALO], st_own.reshape(-1, D))
    back = lax.ppermute(halo_part, "seq", [((i + 1) % n, i) for i in range(n)])
    d_n = (
        nt(jnp.concatenate([d_q, d_kv_mine], axis=1), w_qkv)
        + nt(jnp.concatenate([d_z, d_inner_ext[HALO:]], axis=1), w_mix)
        + nn(d_st_ext[HALO:], st_own.reshape(-1, D))
        + nt(d_step_b, w_step)
    )
    d_n = jnp.concatenate([d_n[: T - HALO], d_n[T - HALO :] + back])
    d_n = rs_state(d_n.astype(BF16))
    inv1_own = dsl(inv1, HALO + TO * t, TO, 0)
    scaled_n = d_n * ngain
    in_g = d_res + inv1_own * scaled_n - x_own * inv1_own**3 * jnp.mean(
        scaled_n * x_own, axis=1, keepdims=True
    )
    g_ngain = jnp.sum(d_n * x_own * inv1_own, axis=0, keepdims=True)
    input_grad = ag_state(in_g)

    def rs_seq(v):
        return lax.psum_scatter(v, "seq", scatter_dimension=0, tiled=True)

    r_down, r_gu = rs_seq(gw_down), rs_seq(gw_gu)
    r_a = rs_seq(jnp.concatenate([gw_q, gw_kv, gw_mix, gw_step[:, :HL], gw_st], axis=1))
    rows = D // n
    gj = lax.all_gather(gw_joint, "state", axis=0)
    gj = jnp.concatenate([gj[:, :QC].reshape(AQ, D), gj[:, QC:].reshape(DM, D)], axis=0)
    r_joint = lax.psum_scatter(gj, "seq", scatter_dimension=0, tiled=True)
    W = QC + HEAD_SIZE + 2 * C + HL
    ga = lax.all_gather(r_a[:, :W], "state", axis=1)
    g_att = jnp.concatenate(
        [ga[:, :, :QC].reshape(rows, AQ)]
        + [ga[:, h * pair + k, QC : QC + HEAD_SIZE] for k in range(2) for h in range(KEY_VALUE_HEADS)],
        axis=1,
    )
    o = QC + HEAD_SIZE
    g_mix = jnp.stack(
        [ga[:, :, o : o + C].reshape(rows, DM), ga[:, :, o + C : o + 2 * C].reshape(rows, DM)], axis=1
    )
    g_step = ga[:, :, o + 2 * C :].reshape(rows, NH)
    g_st = r_a[:, W:].reshape(rows, 2, NW)
    sums = lax.psum((g_ngain, g_mgain), ("seq", "state"))
    small = lax.psum(
        (g_ggain, g_taps_mix, g_taps_st, g_bias[:, :HL], g_rate[:, :HL], g_skip), "seq"
    )
    s_ggain, s_taps, s_st, s_bias, s_rate, s_skip = small
    s_skip = jnp.sum(s_skip.reshape(1, HL, HDM), axis=2)
    cat = lambda v: lax.all_gather(v, "state", axis=1, tiled=True)
    s_ggain, s_taps, s_bias, s_rate, s_skip = map(cat, (s_ggain, s_taps, s_bias, s_rate, s_skip))
    take = lambda v: dsl(v[0], s * (v.shape[1] // n), v.shape[1] // n, 0)
    f = lambda v: v.astype(F32)
    return (
        layer_output,
        input_grad,
        take(sums[0]),
        f(g_att),
        f(g_mix),
        f(g_st),
        f(g_step),
        s_taps,
        s_st.reshape(KC, 2, NW),
        s_bias[0],
        s_rate[0],
        s_skip[0],
        take(s_ggain),
        f(r_joint),
        take(sums[1]),
        f(r_gu).reshape(rows, 2, F),
        f(r_down),
    )


def solution(mesh):
    rep = P()
    in_specs = (
        P("seq", None),
        P("seq", None),
        rep,
        rep,
        rep,
        rep,
        rep,
        P(None, None, "state"),
        rep,
        rep,
        P(None, None, "state"),
        rep,
        rep,
        rep,
        rep,
        rep,
        rep,
        P(None, None, "state"),
        P(None, "state"),
    )
    out_specs = (
        P("seq", None),
        P("seq", None),
        P("seq"),
        P("seq", None),
        P("seq", None, None),
        P("seq", None, "state"),
        P("seq", None),
        rep,
        P(None, None, "state"),
        rep,
        rep,
        rep,
        P("seq"),
        P("seq", None),
        P("seq"),
        P("seq", None, "state"),
        P("seq", "state"),
    )
    return jax.shard_map(local, mesh=mesh, in_specs=in_specs, out_specs=out_specs, check_vma=False)
```

```python
import functools
import math
import types

import jax
import jax.numpy as jnp
from jax import lax
from jax.experimental import pallas as pl
from jax.experimental.pallas import tpu as pltpu
from jax.sharding import PartitionSpec as P

QUERY_HEADS = 8
KEY_VALUE_HEADS = 2
HEAD_SIZE = 64
NH = 24
HDM = 64
KC = 4
EPSILON = 1e-05
ROPE_BASE = 10000.0
HI = lax.Precision.HIGHEST
F32 = jnp.float32
BF16 = jnp.bfloat16
LANES = 128
HALO = 16
FAR = -1e30
MESH = pl.DeviceIdType.MESH
VMEM_LIMIT = 60 << 20


def nn(a, b, p=None):
    return lax.dot_general(a, b, (((1,), (0,)), ((), ())), precision=p, preferred_element_type=F32)


def nt(a, b, p=None):
    return lax.dot_general(a, b, (((1,), (1,)), ((), ())), precision=p, preferred_element_type=F32)


def tn(a, b, p=None):
    return lax.dot_general(a, b, (((0,), (0,)), ((), ())), precision=p, preferred_element_type=F32)


def sigmoid(v):
    return 1.0 / (1.0 + jnp.exp(-v))


def silu(v):
    return v * sigmoid(v)


def silu_slope(v):
    s = sigmoid(v)
    return s * (1.0 + v * (1.0 - s))


def softplus(v):
    return jnp.maximum(v, 0.0) + jnp.log1p(jnp.exp(-jnp.abs(v)))


def iota(shape, dim):
    return lax.broadcasted_iota(jnp.int32, shape, dim)


def doc_of(starts, pos):
    found = jnp.full(pos.shape, -1, jnp.int32)
    for start in starts:
        found = found + (pos >= start).astype(jnp.int32)
    return found


def roll(v, shift):
    return pltpu.roll(v, shift, 1)


def rope(v, cosine, sine, direction):
    first = (iota(v.shape, 1) % HEAD_SIZE) < HEAD_SIZE // 2
    half = HEAD_SIZE // 2
    partner = jnp.where(first, -roll(v, v.shape[1] - half), roll(v, half))
    return v * cosine + partner * (direction * sine)


def expander(width):
    return (iota((LANES, width), 1) // HDM == iota((LANES, width), 0)).astype(F32)


def conv_fwd(ext, taps, masks):
    rows = ext.shape[0] - HALO
    total = 0.0
    for k in range(KC):
        at = HALO - KC + 1 + k
        total = total + ext[at : at + rows] * taps[k : k + 1] * masks[k]
    return total


def conv_bwd(ext, taps, masks, up):
    rows = up.shape[0]
    total, weights = 0.0, []
    for k in range(KC):
        at = HALO - KC + 1 + k
        masked = up * masks[k]
        weights.append(jnp.sum(masked * ext[at : at + rows], axis=0, keepdims=True))
        parts = [jnp.zeros((at, up.shape[1]), F32), masked * taps[k : k + 1]]
        if KC - 1 - k:
            parts.append(jnp.zeros((KC - 1 - k, up.shape[1]), F32))
        total = total + jnp.concatenate(parts, axis=0)
    return total, jnp.concatenate(weights, axis=0)


def masks_of(starts, first_row, rows):
    pos = first_row + iota((rows, 1), 0)
    doc = doc_of(starts, pos)
    masks = [(doc_of(starts, pos - (KC - 1 - k)) == doc).astype(F32) for k in range(KC)]
    return doc, masks


def push(src, dst, send_sem, recv_sem, device):
    copy = pltpu.make_async_remote_copy(
        src_ref=src,
        dst_ref=dst,
        send_sem=send_sem,
        recv_sem=recv_sem,
        device_id=device,
        device_id_type=MESH,
    )
    copy.start()
    return copy


def greet(n, ns, s, t):
    barrier = pltpu.get_barrier_semaphore()

    def seq_turn(k, carried):
        pl.semaphore_signal(
            barrier, inc=1, device_id={"seq": lax.rem(s + k, n)}, device_id_type=MESH
        )
        return carried

    lax.fori_loop(1, n, seq_turn, 0)
    for k in range(1, ns):
        pl.semaphore_signal(
            barrier, inc=1, device_id={"state": lax.rem(t + k, ns)}, device_id_type=MESH
        )
    pl.semaphore_wait(barrier, n - 1 + ns - 1)


def spread(ref, ns, t, src, send, recv):
    return [
        push(src, ref, send.at[k - 1], recv.at[k - 1], {"state": lax.rem(t + k, ns)})
        for k in range(1, ns)
    ]


def conv_ref(ext_ref, taps, masks, rows):
    total = 0.0
    for k in range(KC):
        at = HALO - KC + 1 + k
        total = total + ext_ref[at : at + rows, :] * taps[k : k + 1] * masks[k]
    return total


class Carry:
    def __init__(self, n, s, direction, tx, rx, thr_tx, thr_rx, sems):
        self.n, self.s, self.direction = n, s, direction
        self.tx, self.rx, self.thr_tx, self.thr_rx = tx, rx, thr_tx, thr_rx
        self.send, self.recv, self.thr_send, self.thr_recv = sems
        self.steps = carry_steps(n)

    def copies(self, slot):
        d, source = self.steps[slot]
        to = lax.rem(self.s + self.direction * d + self.n, self.n)
        make = lambda src, dst, a, b: pltpu.make_async_remote_copy(
            src_ref=src,
            dst_ref=dst,
            send_sem=a,
            recv_sem=b,
            device_id={"seq": to},
            device_id_type=MESH,
        )
        return (
            make(self.tx.at[source], self.rx.at[slot], self.send.at[slot], self.recv.at[slot]),
            make(
                self.thr_tx.at[source],
                self.thr_rx.at[slot],
                self.thr_send.at[slot],
                self.thr_recv.at[slot],
            ),
        )

    def sends(self, slot):
        to = self.s + self.direction * self.steps[slot][0]
        return (to >= 0) & (to < self.n)

    def gets(self, slot):
        source = self.s - self.direction * self.steps[slot][0]
        return (source >= 0) & (source < self.n)

    def start(self, slot):
        @pl.when(self.sends(slot))
        def _():
            for copy in self.copies(slot):
                copy.start()

    def finish(self, slot):
        @pl.when(self.sends(slot))
        def _():
            for copy in self.copies(slot):
                copy.wait_send()

    def arrive(self, slot):
        @pl.when(self.gets(slot))
        def _():
            for copy in self.copies(slot):
                copy.wait_recv()

        @pl.when(jnp.logical_not(self.gets(slot)))
        def _():
            self.rx[slot] = jnp.zeros(self.rx.shape[1:], self.rx.dtype)
            self.thr_rx[slot] = jnp.zeros(self.thr_rx.shape[1:], F32)

        return self.rx[slot].astype(F32), self.thr_rx[slot]

    def begin(self, part, thr):
        self.tx[0] = part.astype(BF16)
        self.thr_tx[0] = thr
        self.start(0)
        if len(self.steps) > 1:
            self.start(1)

    def put(self, source, part, thr):
        self.tx[source] = part.astype(BF16)
        self.thr_tx[source] = thr


def carry_steps(n):
    steps = [(1, 0)]
    if n > 2:
        steps.append((2, 0))
    d, source = 2, 1
    while 2 * d < n + 1 and d < n - 1:
        steps.append((d, source))
        d, source = 2 * d, source + 1
    return steps


def expand_rows(width):
    return (iota((width, LANES), 0) // HDM == iota((width, LANES), 1)).astype(F32)


def link_of(linked, cum, cum_t, h):
    return jnp.exp(jnp.where(linked, cum[:, h : h + 1] - cum_t[h : h + 1, :], FAR))


def send_to(refs, name, k, src, dst, device):
    send, recv = getattr(refs, name)
    return push(src, dst, send.at[k], recv.at[k], device)


def row_sums(values):
    return nt(jnp.ones((8, values.shape[1]), F32), values, HI)


def as_column(row):
    first = (iota((8, LANES), 0) == 0).astype(F32)
    return tn(row, first, HI)[:, :1]


def share_rows(refs, name, ns, t, row):
    tx, rx = getattr(refs, name + "_tx"), getattr(refs, name + "_rx")
    tx[...] = row
    copies = [
        send_to(refs, name, k - 1, tx, rx.at[k - 1], {"state": lax.rem(t + k, ns)})
        for k in range(1, ns)
    ]

    def wait():
        total = tx[...]
        for k in range(1, ns):
            copies[k - 1].wait_recv()
            total = total + rx[k - 1]
        return total

    return copies, wait


def scatter_rows(refs, name, ns, t, part):
    tx, rx = getattr(refs, name + "_tx"), getattr(refs, name + "_rx")
    rows = tx.shape[1]
    part = part.astype(BF16)
    for k in range(ns):
        tx[k] = part[rows * k : rows * (k + 1)]
    copies = []
    for k in range(1, ns):
        p = lax.rem(t + k, ns)
        copies.append(send_to(refs, name, k - 1, tx.at[p], rx.at[k - 1], {"state": p}))

    def wait():
        total = tx[t].astype(F32)
        for k in range(1, ns):
            copies[k - 1].wait_recv()
            total = total + rx[k - 1].astype(F32)
        return total

    return copies, wait


def gather_rows(refs, name, ns, t, own):
    every = getattr(refs, name + "_all")
    every[t] = own
    return [
        send_to(refs, name, k - 1, every.at[t], every.at[t], {"state": lax.rem(t + k, ns)})
        for k in range(1, ns)
    ]


def layer_kernel(n, ns, names, *flat):
    refs = types.SimpleNamespace()
    at = 0
    for name, count in names:
        setattr(refs, name, flat[at] if count == 1 else flat[at : at + count])
        at += count
    x, normed, inv1, joined = refs.x, refs.normed, refs.inv1, refs.joined
    w_mix, w_qkv, w_joint, w_gu, down = refs.w_mix, refs.w_qkv, refs.w_joint, refs.w_gu, refs.down
    T, D = x.shape
    t, s = lax.axis_index("state"), lax.axis_index("seq")
    C = refs.taps_mix.shape[1]
    QC = 2 * HEAD_SIZE
    NW = refs.st_own.shape[1]
    N = NW * ns
    TO = T // ns
    DM = C * ns
    F = down.shape[1]
    pairs = C // LANES
    scale = 1.0 / math.sqrt(HEAD_SIZE)
    state_peer = lambda k: {"state": lax.rem(t + k, ns)}
    greet(n, ns, s, t)
    sent = []
    halo_copy = send_to(refs, "halo", 0, x.at[pl.ds(T - HALO, HALO)], refs.halo_rx, {"seq": lax.rem(s + 1, n)})
    mine = pl.ds(pl.multiple_of(NW * t, NW), NW)
    arriving = []
    for k in range(1, ns):
        arriving.append(send_to(refs, "st", k - 1, refs.st_own, refs.st_all.at[:, mine, :], state_peer(k)))
        arriving.append(send_to(refs, "taps", k - 1, refs.taps_st, refs.taps_all.at[:, mine, :], state_peer(k)))
    sent += [halo_copy] + arriving
    refs.st_all[:, mine, :] = refs.st_own[...]
    refs.taps_all[:, mine, :] = refs.taps_st[...]

    first_row = s * T
    starts = [refs.doc_starts[k] for k in range(refs.doc_starts.shape[0])]
    doc, masks = masks_of(starts, first_row, T)
    doc_row = doc_of(starts, first_row + iota((1, T), 1))
    lane = iota((T, LANES), 1)
    low = lane < HEAD_SIZE
    ngain = refs.ngain[...]

    xf = x[...].astype(F32)
    inv = lax.rsqrt(jnp.mean(xf * xf, axis=1, keepdims=True) + EPSILON)
    inv1[...] = inv
    normed[HALO:, :] = (xf * inv * ngain).astype(BF16)
    main = normed[HALO:, :]
    qkv = nn(main, w_qkv[...])
    cosine, sine = refs.cosine[...], refs.sine[...]
    q = (rope(qkv[:, :QC], cosine, sine, 1.0).astype(BF16) * scale).astype(F32)
    kcos, ksin = jnp.where(low, cosine, 1.0), jnp.where(low, sine, 0.0)
    kv_all = refs.kv_all
    kv_all[s] = rope(qkv[:, QC:], kcos, ksin, 1.0).astype(BF16)

    def kv_copy(k, to):
        return pltpu.make_async_remote_copy(
            src_ref=kv_all.at[s],
            dst_ref=kv_all.at[s],
            send_sem=refs.kv[0].at[k - 1],
            recv_sem=refs.kv[1].at[k - 1],
            device_id={"seq": to},
            device_id_type=MESH,
        )

    def kv_turn(k, carried):
        kv_copy(k, lax.rem(s + k, n)).start()
        return carried

    lax.fori_loop(1, n - s, kv_turn, 0)
    refs.q2[:T, :] = jnp.where(low, q, 0.0).astype(BF16)
    refs.q2[T:, :] = jnp.where(low, roll(q, HEAD_SIZE), 0.0).astype(BF16)
    refs.z[...] = nn(main, w_mix[:, :C])
    raw = nn(main, refs.w_step[...]) + refs.bias_row[...]

    halo_copy.wait_recv()
    hf = refs.halo_rx[...].astype(F32)
    inv_h = lax.rsqrt(jnp.mean(hf * hf, axis=1, keepdims=True) + EPSILON)
    normed[:HALO, :] = (hf * inv_h * ngain).astype(BF16)
    ext_f, ext_s, ext_o = refs.ext_f, refs.ext_s, refs.ext_o
    ext_f[...] = nn(normed[...], w_mix[:, C:]).astype(BF16).astype(F32)
    taps_mix = refs.taps_mix[...]
    inner_lin = conv_ref(ext_f, taps_mix, masks, T)
    refs.inner_lin[...] = inner_lin
    inner = silu(inner_lin)
    for copy in arriving:
        copy.wait_recv()
    for c in range(2):
        ext_s[...] = nt(normed[...], refs.st_all[c]).astype(BF16).astype(F32)
        taps = refs.taps_all[c].T
        refs.wr[c] = silu(conv_ref(ext_s, taps, masks, T))
    write, read = refs.wr[0], refs.wr[1]
    step = softplus(raw)
    causal = iota((T, T), 0) >= iota((T, T), 1)
    tri = causal.astype(F32)
    rate_row = refs.rate_row[...]
    cum = nn(tri, -step * rate_row, HI)
    cum_t = cum.T
    linked = (doc == doc_row) & causal
    E = expander(C)
    rows_e = expand_rows(C)
    real_col = refs.real_col[...]
    inflow = step * real_col
    inflow_e = nn(inflow, E, HI)
    in_x = inner * inflow_e
    refs.in_x[...] = in_x
    cum_last = cum[T - 1 : T]
    last = first_row + T - 1
    doc_last = doc_of(starts, jnp.full((T, 1), last, jnp.int32))
    prior = doc_of(starts, jnp.full((T, 1), first_row - 1, jnp.int32))
    tail = jnp.where(doc == doc_last, jnp.exp(cum_last - cum), 0.0)
    refs.tail_e[...] = nn(tail, E, HI)
    state_part = tn(refs.tail_e[...] * in_x, write, HI)
    alive = (doc == prior).astype(F32)
    alive_last = (doc_last == prior).astype(F32)[:8]
    thr = alive_last * jnp.exp(jnp.broadcast_to(cum_last, (8, LANES)))
    steps = len(carry_steps(n))

    def make_carry(direction, name):
        send, recv = getattr(refs, name)
        thr_send, thr_recv = getattr(refs, name + "_thr")
        carry = Carry(
            n, s, direction, getattr(refs, name + "_tx"), getattr(refs, name + "_rx"),
            getattr(refs, name + "_thr_tx"), getattr(refs, name + "_thr_rx"),
            (send, recv, thr_send, thr_recv),
        )
        window = [None]

        def advance(slot):
            total, thr_got = carry.arrive(slot)
            if slot == 0:
                window[0] = (total, thr_got)
            else:
                now, thr_now = window[0]
                window[0] = (now + nt(rows_e, thr_now, HI)[:, :1] * total, thr_now * thr_got)
            if slot >= 1 and slot + 1 < steps:
                carry.put(carry.steps[slot + 1][1], *window[0])
                carry.start(slot + 1)

        return carry, window, advance

    carry, window, advance = make_carry(1, "fc")
    carry.begin(state_part, thr)
    done = max(2, pairs + 1)

    def between(advance, p):
        if p == 0:
            advance(0)
            if steps > 1:
                advance(1)
        elif p + 1 < steps:
            advance(p + 1)

    g_mat = nt(read, write, HI)
    for p in range(pairs):
        cols = slice(LANES * p, LANES * (p + 1))
        ys = []
        for h in (2 * p, 2 * p + 1):
            link = link_of(linked, cum, cum_t, h)
            refs.link[h] = link
            ys.append(nn(link * g_mat, in_x[:, cols], HI))
        refs.ssd[:, cols] = jnp.where(low, ys[0], ys[1])
        between(advance, p)
    refs.g_mat[...] = g_mat

    doc2 = jnp.concatenate([doc, doc], axis=0)
    m_ref, l_ref, acc_ref = refs.m_acc, refs.l_acc, refs.o_acc
    m_ref[...] = jnp.full(m_ref.shape, FAR, F32)
    l_ref[...] = jnp.zeros(l_ref.shape, F32)
    acc_ref[...] = jnp.zeros(acc_ref.shape, F32)

    def allowed_at(j, diagonal):
        allowed = refs.codes[j] == doc2
        if diagonal:
            rows2 = jnp.concatenate([iota((T, T), 0)] * 2, axis=0)
            cols2 = iota((2 * T, T), 1)
            allowed = (allowed & (cols2 <= rows2)) | (cols2 == rows2)
        return allowed

    def attend(j, diagonal):
        block = kv_all[j]
        scores = jnp.where(allowed_at(j, diagonal), nt(refs.q2[...], block), FAR)
        m = m_ref[...]
        m_new = jnp.maximum(m, jnp.max(scores, axis=1, keepdims=True))
        shrink = jnp.exp(m - m_new)
        p = jnp.exp(scores - m_new)
        l_ref[...] = l_ref[...] * shrink + jnp.sum(p, axis=1, keepdims=True)
        acc_ref[...] = acc_ref[...] * shrink + nn(p.astype(BF16), block)
        m_ref[...] = m_new

    attend(s, True)

    def attend_turn(k, carried):
        kv_copy(k, lax.rem(s + k, n)).wait_recv()
        attend(s - k, False)
        return carried

    lax.fori_loop(1, s + 1, attend_turn, 0)
    out = acc_ref[...] / l_ref[...]
    acc_ref[...] = out
    m_ref[...] = m_ref[...] + jnp.log(l_ref[...])
    joined[:, :QC] = jnp.where(low, roll(out[:T], HEAD_SIZE), out[T:]).astype(BF16)

    for slot in range(done, steps):
        advance(slot)
    s_in = window[0][0]
    refs.s_in[...] = s_in
    refs.reach_e[...] = nn(alive * jnp.exp(cum), E, HI)
    ssd = refs.ssd[...] + refs.reach_e[...] * nt(read, s_in, HI)
    refs.ssd[...] = ssd
    z = refs.z[...]
    skip_row, ggain_row = refs.skip_row[...], refs.ggain_row[...]
    full_mix = ssd + skip_row * inner
    refs.full_mix[...] = full_mix
    gated = full_mix * silu(z)
    refs.gated[...] = gated
    copies, wait = share_rows(refs, "sq", ns, t, row_sums(gated * gated))
    sent += copies
    inv_g = as_column(lax.rsqrt(wait() / DM + EPSILON))
    joined[:, QC:] = (gated * inv_g * ggain_row).astype(BF16)
    copies, wait = scatter_rows(refs, "rs1", ns, t, nn(joined[...], w_joint[...]))
    sent += copies
    own_rows = pl.ds(pl.multiple_of(TO * t, TO), TO)
    dh = nn(refs.g[...], down[...])
    x_own = x[own_rows, :].astype(F32)
    res = x_own + wait()
    inv2 = lax.rsqrt(jnp.mean(res * res, axis=1, keepdims=True) + EPSILON)
    mgain = refs.mgain[...]
    ag = gather_rows(refs, "ag1", ns, t, (res * inv2 * mgain).astype(BF16))
    sent += ag
    for copy in ag:
        copy.wait_recv()

    n2 = jnp.concatenate([refs.ag1_all[k] for k in range(ns)], axis=0)
    gu = nn(n2, w_gu[...])
    gate, up = gu[:, :F], gu[:, F:]
    sig = sigmoid(gate)
    act = gate * sig
    hidden = (act * up).astype(BF16)
    d_gu = jnp.concatenate(
        [dh * up * (sig * (1.0 + gate * (1.0 - sig))), dh * act], axis=1
    ).astype(BF16)
    copies, wait_dn2 = scatter_rows(refs, "rs2", ns, t, nt(d_gu, w_gu[...]))
    sent += copies
    copies, wait_mlp = scatter_rows(refs, "rs3", ns, t, nt(hidden, down[...]))
    sent += copies
    refs.gw_down[...] = tn(refs.g[...], hidden).astype(BF16)
    for k in range(2):
        refs.gw_gu[:, F * k : F * (k + 1)] = tn(n2, d_gu[:, F * k : F * (k + 1)]).astype(BF16)
    dn2 = wait_dn2()
    scaled = dn2 * mgain
    d_res = (
        refs.g[own_rows, :].astype(F32)
        + inv2 * scaled
        - res * inv2 * inv2 * inv2 * jnp.mean(scaled * res, axis=1, keepdims=True)
    )
    ag2 = gather_rows(refs, "ag2", ns, t, d_res.astype(BF16))
    refs.g_mgain[...] = jnp.sum(dn2 * res * inv2, axis=0, keepdims=True)
    ag3 = gather_rows(refs, "ag3", ns, t, (res + wait_mlp()).astype(BF16))
    sent += ag2 + ag3
    for copy in ag2:
        copy.wait_recv()

    d_branch = jnp.concatenate([refs.ag2_all[k] for k in range(ns)], axis=0)
    d_joined = nt(d_branch, w_joint[...])
    d_gn = d_joined[:, QC:]
    scaled = d_gn * ggain_row
    copies, wait = share_rows(refs, "dot", ns, t, row_sums(scaled * gated))
    sent += copies
    refs.gw_joint[...] = tn(joined[...], d_branch).astype(BF16)
    refs.g_ggain[...] = jnp.sum(d_gn * gated * inv_g, axis=0, keepdims=True)
    d_att = d_joined[:, :QC].astype(BF16).astype(F32)
    dout2 = jnp.concatenate(
        [jnp.where(low, 0.0, roll(d_att, HEAD_SIZE)), jnp.where(low, 0.0, d_att)], axis=0
    )
    delta = jnp.sum(dout2 * acc_ref[...], axis=1, keepdims=True)
    l_ref[...] = delta
    refs.dout2[...] = dout2.astype(BF16)
    dot = as_column(wait() / DM)
    d_gated = inv_g * scaled - gated * (inv_g * inv_g * inv_g * dot)
    sig = sigmoid(z)
    dy = d_gated * z * sig
    refs.dy[...] = dy
    refs.d_z[...] = (d_gated * full_mix * (sig * (1.0 + z * (1.0 - sig)))).astype(BF16)
    refs.g_skip[...] = jnp.sum(dy * inner, axis=0, keepdims=True)
    reach_dy = refs.reach_e[...] * dy
    carry_b, window, advance = make_carry(-1, "bc")
    carry_b.begin(tn(reach_dy, read, HI), thr)
    d_g = jnp.zeros((T, T), F32)
    for p in range(pairs):
        cols = slice(LANES * p, LANES * (p + 1))
        xp, dyp = in_x[:, cols], dy[:, cols]
        halves = []
        for k in range(2):
            link = refs.link[2 * p + k]
            halves.append(tn(link * g_mat, dyp, HI))
            own = low if k == 0 else jnp.logical_not(low)
            d_g = d_g + link * nt(jnp.where(own, dyp, 0.0), xp, HI)
        refs.w_tot[:, cols] = jnp.where(low, halves[0], halves[1])
        between(advance, p)
    refs.d_g[...] = d_g

    refs.dq2[...] = jnp.zeros(refs.dq2.shape, F32)

    def attend_back(j, diagonal):
        block = kv_all[j]
        q2, dout2 = refs.q2[...], refs.dout2[...]
        scores = jnp.where(allowed_at(j, diagonal), nt(q2, block), FAR)
        p = jnp.exp(scores - m_ref[...])
        ds = (p * (nt(dout2, block) - l_ref[...])).astype(BF16)
        refs.dq2[...] += nn(ds, block)
        return tn(ds, q2) + tn(p.astype(BF16), dout2)

    def dkv_copy(k, to, source):
        return pltpu.make_async_remote_copy(
            src_ref=source,
            dst_ref=refs.dkv_rx.at[k - 1],
            send_sem=refs.dkv[0].at[k - 1],
            recv_sem=refs.dkv[1].at[k - 1],
            device_id={"seq": to},
            device_id_type=MESH,
        )

    def back_turn(k, carried):
        kv_all[s - k] = attend_back(s - k, False).astype(BF16)
        dkv_copy(k, lax.rem(s - k + n, n), kv_all.at[s - k]).start()
        return carried

    lax.fori_loop(1, s + 1, back_turn, 0)
    refs.dkv_sum[...] = attend_back(s, True)

    for slot in range(done, steps):
        advance(slot)
    later = window[0][0]
    tail_e = refs.tail_e[...]
    tail_r = tail_e * nt(write, later, HI)
    w_tot = refs.w_tot[...] + tail_r
    d_write = tn(refs.d_g[...], read, HI) + nn(tail_e * in_x, later, HI)
    d_read = nn(refs.d_g[...], write, HI) + nn(reach_dy, s_in, HI)
    refs.dwr_tx[0] = d_write.T.astype(BF16)
    refs.dwr_tx[1] = d_read.T.astype(BF16)
    dwr = []
    for k in range(1, ns):
        p = lax.rem(t + k, ns)
        theirs = pl.ds(pl.multiple_of(NW * p, NW), NW)
        dwr.append(
            send_to(refs, "dwr", k - 1, refs.dwr_tx.at[:, theirs, :], refs.dwr_rx.at[k - 1], {"state": p})
        )
    sent += dwr
    u = nt(inner * w_tot, E, HI)
    tl = nt(in_x * tail_r, E, HI)
    thr_s = jnp.sum(tn(later * s_in, rows_e, HI), axis=0, keepdims=True) * thr[:1]
    d_cum = nt(dy * ssd, E, HI) - inflow * u
    at_last = iota((T, LANES), 0) == T - 1
    d_cum = d_cum + jnp.where(at_last, jnp.sum(tl, axis=0, keepdims=True) + thr_s, 0.0)
    d_ld = tn(tri, d_cum, HI)
    d_step = real_col * u - rate_row * d_ld
    refs.g_rate[...] = -jnp.sum(step * d_ld, axis=0, keepdims=True)
    d_step = d_step * sigmoid(raw)
    refs.g_bias[...] = jnp.sum(d_step, axis=0, keepdims=True)
    d_step = d_step.astype(BF16)
    d_lin = (inflow_e * w_tot + skip_row * dy) * silu_slope(inner_lin)

    def conv_back(ext, grad, taps, up, g_taps):
        grad[...] = jnp.zeros(grad.shape, F32)
        for k in range(KC):
            at = HALO - KC + 1 + k
            masked = up * masks[k]
            g_taps[k : k + 1, :] = jnp.sum(masked * ext[at : at + T, :], axis=0, keepdims=True)
            grad[at : at + T, :] += masked * taps[k : k + 1]
        return grad[...].astype(BF16)

    d_ext = conv_back(ext_f, refs.grad_f, taps_mix, d_lin, refs.g_taps_mix)
    st64 = refs.st_own[...].reshape(2 * NW, D)
    taps_own = refs.taps_st[...].reshape(2 * NW, LANES).T
    ext_o[...] = nt(normed[...], st64).astype(BF16).astype(F32)
    slope_o = silu_slope(conv_ref(ext_o, taps_own, masks, T))
    for copy in dwr:
        copy.wait_recv()
    d_wr = refs.dwr_tx[:, mine, :].astype(F32)
    for k in range(1, ns):
        d_wr = d_wr + refs.dwr_rx[k - 1].astype(F32)
    d_st = conv_back(ext_o, refs.grad_o, taps_own, d_wr.reshape(2 * NW, T).T * slope_o, refs.g_taps_st)
    refs.back_tx[...] = (nt(d_ext[:HALO], w_mix[:, C:]) + nn(d_st[:HALO], st64)).astype(BF16)
    back = send_to(refs, "back", 0, refs.back_tx, refs.back_rx, {"seq": lax.rem(s + n - 1, n)})
    sent.append(back)
    def dkv_turn(k, carried):
        dkv_copy(k, lax.rem(s - k + n, n), refs.dkv_rx.at[k - 1]).wait_recv()
        refs.dkv_sum[...] += refs.dkv_rx[k - 1].astype(F32)
        return carried

    lax.fori_loop(1, n - s, dkv_turn, 0)
    refs.pair_tx[...] = refs.dkv_sum[...].astype(BF16)
    odd = lax.rem(t, 2)
    pair = send_to(refs, "pair", 0, refs.pair_tx, refs.pair_rx, {"state": t + 1 - 2 * odd})
    sent.append(pair)
    d_z = refs.d_z[...]
    refs.gw_mix[:, :C] = tn(main, d_z).astype(BF16)
    refs.gw_mix[:, C:] = tn(normed[...], d_ext).astype(BF16)
    refs.gw_st[...] = tn(normed[...], d_st).astype(BF16)
    refs.gw_step[...] = tn(main, d_step).astype(BF16)
    dq2 = refs.dq2[...]
    dq = jnp.where(low, dq2[:T], roll(dq2[T:], HEAD_SIZE)) * scale
    d_q = rope(dq, cosine, sine, -1.0).astype(BF16)
    d_n = (
        nt(jnp.concatenate([d_z, d_ext[HALO:]], axis=1), w_mix[...])
        + nn(d_st[HALO:], st64)
        + nt(d_step, refs.w_step[...])
    )
    pair.wait_recv()
    d_kv = rope(refs.dkv_sum[...] + refs.pair_rx[...].astype(F32), kcos, ksin, -1.0)
    d_kv = jnp.where(low == (odd == 0), d_kv, 0.0).astype(BF16)
    d_qkv = jnp.concatenate([d_q, d_kv], axis=1)
    refs.gw_qkv[...] = tn(main, d_qkv).astype(BF16)
    d_n = d_n + nt(d_qkv, w_qkv[...])
    back.wait_recv()
    tail_rows = d_n[T - HALO :] + refs.back_rx[...].astype(F32)
    d_n = jnp.concatenate([d_n[: T - HALO], tail_rows], axis=0)
    copies, wait = scatter_rows(refs, "rs4", ns, t, d_n)
    sent += copies
    inv_own = inv1[own_rows, :]
    d_n = wait()
    scaled = d_n * ngain
    in_g = (
        d_res
        + inv_own * scaled
        - x_own * inv_own * inv_own * inv_own * jnp.mean(scaled * x_own, axis=1, keepdims=True)
    )
    ag4 = gather_rows(refs, "ag4", ns, t, in_g.astype(BF16))
    sent += ag4
    refs.g_ngain[...] = jnp.sum(d_n * x_own * inv_own, axis=0, keepdims=True)
    for copy in ag3:
        copy.wait_recv()
    for k in range(ns):
        refs.layer_output[TO * k : TO * (k + 1), :] = refs.ag3_all[k]
    for copy in ag4:
        copy.wait_recv()
    for k in range(ns):
        refs.input_grad[TO * k : TO * (k + 1), :] = refs.ag4_all[k]
    for copy in sent:
        copy.wait_send()
    for slot in range(steps):
        carry.finish(slot)
        carry_b.finish(slot)

    def kv_end(k, carried):
        kv_copy(k, lax.rem(s + k, n)).wait_send()
        return carried

    lax.fori_loop(1, n - s, kv_end, 0)

    def dkv_end(k, carried):
        dkv_copy(k, lax.rem(s - k + n, n), kv_all.at[s - k]).wait_send()
        return carried

    lax.fori_loop(1, s + 1, dkv_end, 0)


def layer(n, ns, inputs):
    T, D = inputs["x"].shape
    C = inputs["w_mix"].shape[1] // 2
    NW = inputs["st_own"].shape[1]
    F = inputs["down"].shape[1]
    N, TO, H = NW * ns, T // ns, NH // ns
    steps = len(carry_steps(n))
    sd = jax.ShapeDtypeStruct
    J = 2 * HEAD_SIZE + C
    outs = {
        "layer_output": sd((T, D), BF16),
        "input_grad": sd((T, D), BF16),
        "gw_down": sd((D, F), BF16),
        "gw_gu": sd((D, 2 * F), BF16),
        "gw_joint": sd((J, D), BF16),
        "gw_mix": sd((D, 2 * C), BF16),
        "gw_qkv": sd((D, 4 * HEAD_SIZE), BF16),
        "gw_st": sd((D, 2 * NW), BF16),
        "gw_step": sd((D, LANES), BF16),
        "g_mgain": sd((1, D), F32),
        "g_ngain": sd((1, D), F32),
        "g_ggain": sd((1, C), F32),
        "g_skip": sd((1, C), F32),
        "g_rate": sd((1, LANES), F32),
        "g_bias": sd((1, LANES), F32),
        "g_taps_mix": sd((KC, C), F32),
        "g_taps_st": sd((KC, 2 * NW), F32),
    }
    vm = pltpu.VMEM
    dma = lambda k: (pltpu.SemaphoreType.DMA((k,)), pltpu.SemaphoreType.DMA((k,)))
    scratch = {
        "halo_rx": vm((HALO, D), BF16),
        "st_all": vm((2, N, D), BF16),
        "taps_all": vm((2, N, LANES), F32),
        "kv_all": vm((n, T, LANES), BF16),
        "normed": vm((T + HALO, D), BF16),
        "inv1": vm((T, 1), F32),
        "q2": vm((2 * T, LANES), BF16),
        "z": vm((T, C), F32),
        "ext_f": vm((T + HALO, C), F32),
        "ext_s": vm((T + HALO, N), F32),
        "ext_o": vm((T + HALO, 2 * NW), F32),
        "grad_f": vm((T + HALO, C), F32),
        "grad_o": vm((T + HALO, 2 * NW), F32),
        "inner_lin": vm((T, C), F32),
        "wr": vm((2, T, N), F32),
        "in_x": vm((T, C), F32),
        "tail_e": vm((T, C), F32),
        "reach_e": vm((T, C), F32),
        "link": vm((H, T, T), F32),
        "g_mat": vm((T, T), F32),
        "d_g": vm((T, T), F32),
        "ssd": vm((T, C), F32),
        "full_mix": vm((T, C), F32),
        "gated": vm((T, C), F32),
        "dy": vm((T, C), F32),
        "w_tot": vm((T, C), F32),
        "d_z": vm((T, C), BF16),
        "s_in": vm((C, N), F32),
        "joined": vm((T, J), BF16),
        "m_acc": vm((2 * T, 1), F32),
        "l_acc": vm((2 * T, 1), F32),
        "o_acc": vm((2 * T, LANES), F32),
        "dout2": vm((2 * T, LANES), BF16),
        "dq2": vm((2 * T, LANES), F32),
        "dkv_rx": vm((n, T, LANES), BF16),
        "dkv_sum": vm((T, LANES), F32),
        "pair_tx": vm((T, LANES), BF16),
        "pair_rx": vm((T, LANES), BF16),
        "back_tx": vm((HALO, D), BF16),
        "back_rx": vm((HALO, D), BF16),
        "dwr_tx": vm((2, N, T), BF16),
        "dwr_rx": vm((ns - 1, 2, NW, T), BF16),
        "halo": dma(1),
        "st": dma(ns - 1),
        "taps": dma(ns - 1),
        "kv": dma(n - 1),
        "dkv": dma(n - 1),
        "pair": dma(1),
        "back": dma(1),
        "dwr": dma(ns - 1),
    }
    for name in ("fc", "bc"):
        scratch[name + "_tx"] = vm((steps, C, N), BF16)
        scratch[name + "_rx"] = vm((steps, C, N), BF16)
        scratch[name + "_thr_tx"] = vm((steps, 8, LANES), F32)
        scratch[name + "_thr_rx"] = vm((steps, 8, LANES), F32)
        scratch[name] = dma(steps)
        scratch[name + "_thr"] = dma(steps)
    for name in ("sq", "dot"):
        scratch[name + "_tx"] = vm((8, T), F32)
        scratch[name + "_rx"] = vm((ns - 1, 8, T), F32)
        scratch[name] = dma(ns - 1)
    for name in ("rs1", "rs2", "rs3", "rs4"):
        scratch[name + "_tx"] = vm((ns, TO, D), BF16)
        scratch[name + "_rx"] = vm((ns - 1, TO, D), BF16)
        scratch[name] = dma(ns - 1)
    for name in ("ag1", "ag2", "ag3", "ag4"):
        scratch[name + "_all"] = vm((ns, TO, D), BF16)
        scratch[name] = dma(ns - 1)
    names, flat = [], []
    for group in (inputs, outs, scratch):
        for name, item in group.items():
            names.append((name, len(item) if isinstance(item, tuple) else 1))
    for item in scratch.values():
        flat += list(item) if isinstance(item, tuple) else [item]
    whole = pl.BlockSpec(memory_space=pltpu.VMEM)
    small = pl.BlockSpec(memory_space=pltpu.SMEM)
    got = pl.pallas_call(
        functools.partial(layer_kernel, n, ns, names),
        out_shape=tuple(outs.values()),
        in_specs=[small if name == "doc_starts" else whole for name in inputs],
        out_specs=(whole,) * len(outs),
        scratch_shapes=flat,
        name="layer",
        compiler_params=pltpu.CompilerParams(
            collective_id=1, has_side_effects=True, vmem_limit_bytes=VMEM_LIMIT
        ),
    )(*inputs.values())
    return types.SimpleNamespace(**dict(zip(outs, got)))


def local(
    layer_input,
    out_grad,
    doc_starts,
    real_mask,
    norm_gain,
    attention_input_rows,
    mixer_in,
    state_in,
    step_in,
    conv_mixer,
    conv_state,
    step_bias,
    decay_rate,
    skip_gain,
    gated_gain,
    joint_out,
    mlp_gain,
    gate_up,
    down_weight,
):
    T, D = layer_input.shape
    NS, n = lax.axis_size("state"), lax.axis_size("seq")
    t, s = lax.axis_index("state"), lax.axis_index("seq")
    HL = NH // NS
    C = HL * HDM
    QC = QUERY_HEADS * HEAD_SIZE // NS
    TO = T // NS
    DM = NH * HDM
    NW = state_in.shape[2]
    AQ = QUERY_HEADS * HEAD_SIZE
    KW = KEY_VALUE_HEADS * HEAD_SIZE
    kvh = t * KEY_VALUE_HEADS // NS
    first_row = s * T
    starts = [doc_starts[k] for k in range(doc_starts.shape[0])]
    dsl = lax.dynamic_slice_in_dim

    w_q = dsl(attention_input_rows, QC * t, QC, 1)
    w_k = dsl(attention_input_rows, AQ + HEAD_SIZE * kvh, HEAD_SIZE, 1)
    w_v = dsl(attention_input_rows, AQ + KW + HEAD_SIZE * kvh, HEAD_SIZE, 1)
    w_qkv = jnp.concatenate([w_q, w_k, w_v], axis=1)
    w_mix = dsl(mixer_in, C * t, C, 2)
    w_mix = jnp.concatenate([w_mix[:, 0], w_mix[:, 1]], axis=1)
    w_step = jnp.pad(dsl(step_in, HL * t, HL, 1), ((0, 0), (0, LANES - HL)))
    pad_row = lambda v: jnp.pad(dsl(v, HL * t, HL, 0), (0, LANES - HL))[None, :]
    bias_row, rate_row = pad_row(step_bias), pad_row(decay_rate)
    skip_row = jnp.repeat(dsl(skip_gain, HL * t, HL, 0), HDM)[None, :]
    taps_mix = dsl(conv_mixer, C * t, C, 1)
    ggain_row = dsl(gated_gain, C * t, C, 0)[None, :]
    w_joint = jnp.concatenate([dsl(joint_out, QC * t, QC, 0), dsl(joint_out, AQ + C * t, C, 0)], axis=0)
    st_own = jnp.transpose(state_in, (1, 2, 0))
    taps_own = conv_state.reshape(KC, 2 * NW)
    w_gu = jnp.concatenate([gate_up[:, 0], gate_up[:, 1]], axis=1)
    F = gate_up.shape[2]
    ngain, mgain = norm_gain[None, :], mlp_gain[None, :]
    real_f = real_mask.astype(F32)
    real_col = dsl(real_f, first_row, T, 0)[:, None]
    all_doc = doc_of(starts, jnp.arange(n * T, dtype=jnp.int32)[None, :])[0]
    codes = jnp.where(real_mask > 0, all_doc, -7).reshape(n, 1, T)
    pos = first_row + jnp.arange(T, dtype=jnp.int32)
    firsts = jnp.max(jnp.where(doc_starts[None, :] <= pos[:, None], doc_starts[None, :], 0), axis=1)
    powers = (jnp.arange(LANES) % (HEAD_SIZE // 2)).astype(F32) * (2.0 / HEAD_SIZE)
    angles = (pos - firsts).astype(F32)[:, None] * jnp.exp(-math.log(ROPE_BASE) * powers)[None, :]
    cosine, sine = jnp.cos(angles), jnp.sin(angles)

    taps_rows = jnp.pad(jnp.transpose(conv_state, (1, 2, 0)), ((0, 0), (0, 0), (0, LANES - KC)))
    o = layer(
        n,
        NS,
        {
            "x": layer_input,
            "g": out_grad,
            "w_qkv": w_qkv,
            "w_mix": w_mix,
            "w_step": w_step,
            "st_own": st_own,
            "taps_st": taps_rows,
            "taps_mix": taps_mix,
            "ngain": ngain,
            "bias_row": bias_row,
            "rate_row": rate_row,
            "skip_row": skip_row,
            "ggain_row": ggain_row,
            "w_joint": w_joint,
            "mgain": mgain,
            "w_gu": w_gu,
            "down": down_weight,
            "real_col": real_col,
            "codes": codes,
            "cosine": cosine,
            "sine": sine,
            "doc_starts": doc_starts,
        },
    )
    pair = NS // KEY_VALUE_HEADS
    odd = t % pair
    gw_q, gw_kv = o.gw_qkv[:, :QC], o.gw_qkv[:, QC:]
    gw_kv = jnp.where(odd == 0, gw_kv[:, :HEAD_SIZE], gw_kv[:, HEAD_SIZE:])
    gw_down, gw_gu, gw_joint, gw_mix, gw_step, gw_st = (
        o.gw_down, o.gw_gu, o.gw_joint, o.gw_mix, o.gw_step, o.gw_st
    )
    layer_output, input_grad = o.layer_output, o.input_grad.astype(F32)
    g_ngain, g_mgain, g_ggain, g_skip = o.g_ngain, o.g_mgain, o.g_ggain, o.g_skip
    g_taps_mix, g_taps_st, g_bias, g_rate = o.g_taps_mix, o.g_taps_st, o.g_bias, o.g_rate

    def rs_seq(v):
        return lax.psum_scatter(v, "seq", scatter_dimension=0, tiled=True)

    r_down, r_gu = rs_seq(gw_down), rs_seq(gw_gu)
    r_a = rs_seq(jnp.concatenate([gw_q, gw_kv, gw_mix, gw_step[:, :HL], gw_st], axis=1))
    rows = D // n
    gj = lax.all_gather(gw_joint, "state", axis=0)
    gj = jnp.concatenate([gj[:, :QC].reshape(AQ, D), gj[:, QC:].reshape(DM, D)], axis=0)
    r_joint = lax.psum_scatter(gj, "seq", scatter_dimension=0, tiled=True)
    W = QC + HEAD_SIZE + 2 * C + HL
    ga = lax.all_gather(r_a[:, :W], "state", axis=1)
    g_att = jnp.concatenate(
        [ga[:, :, :QC].reshape(rows, AQ)]
        + [ga[:, h * pair + k, QC : QC + HEAD_SIZE] for k in range(2) for h in range(KEY_VALUE_HEADS)],
        axis=1,
    )
    o = QC + HEAD_SIZE
    g_mix = jnp.stack(
        [ga[:, :, o : o + C].reshape(rows, DM), ga[:, :, o + C : o + 2 * C].reshape(rows, DM)], axis=1
    )
    g_step = ga[:, :, o + 2 * C :].reshape(rows, NH)
    g_st = r_a[:, W:].reshape(rows, 2, NW)
    sums = lax.psum((g_ngain, g_mgain), ("seq", "state"))
    small = lax.psum(
        (g_ggain, g_taps_mix, g_taps_st, g_bias[:, :HL], g_rate[:, :HL], g_skip), "seq"
    )
    s_ggain, s_taps, s_st, s_bias, s_rate, s_skip = small
    s_skip = jnp.sum(s_skip.reshape(1, HL, HDM), axis=2)
    cat = lambda v: lax.all_gather(v, "state", axis=1, tiled=True)
    s_ggain, s_taps, s_bias, s_rate, s_skip = map(cat, (s_ggain, s_taps, s_bias, s_rate, s_skip))
    take = lambda v: dsl(v[0], s * (v.shape[1] // n), v.shape[1] // n, 0)
    f = lambda v: v.astype(F32)
    return (
        layer_output,
        input_grad,
        take(sums[0]),
        f(g_att),
        f(g_mix),
        f(g_st),
        f(g_step),
        s_taps,
        s_st.reshape(KC, 2, NW),
        s_bias[0],
        s_rate[0],
        s_skip[0],
        take(s_ggain),
        f(r_joint),
        take(sums[1]),
        f(r_gu).reshape(rows, 2, F),
        f(r_down),
    )


def solution(mesh):
    rep = P()
    in_specs = (
        P("seq", None),
        P("seq", None),
        rep,
        rep,
        rep,
        rep,
        rep,
        P(None, None, "state"),
        rep,
        rep,
        P(None, None, "state"),
        rep,
        rep,
        rep,
        rep,
        rep,
        rep,
        P(None, None, "state"),
        P(None, "state"),
    )
    out_specs = (
        P("seq", None),
        P("seq", None),
        P("seq"),
        P("seq", None),
        P("seq", None, None),
        P("seq", None, "state"),
        P("seq", None),
        rep,
        P(None, None, "state"),
        rep,
        rep,
        rep,
        P("seq"),
        P("seq", None),
        P("seq"),
        P("seq", None, "state"),
        P("seq", "state"),
    )
    return jax.shard_map(local, mesh=mesh, in_specs=in_specs, out_specs=out_specs, check_vma=False)
```

```python
import functools
import math
import types

import jax
import jax.numpy as jnp
from jax import lax
from jax.experimental import pallas as pl
from jax.experimental.pallas import tpu as pltpu
from jax.sharding import PartitionSpec as P

QUERY_HEADS = 8
KEY_VALUE_HEADS = 2
HEAD_SIZE = 64
NH = 24
HDM = 64
KC = 4
EPSILON = 1e-05
ROPE_BASE = 10000.0
HI = lax.Precision.HIGHEST
F32 = jnp.float32
BF16 = jnp.bfloat16
LANES = 128
HALO = 16
FAR = -1e30
MESH = pl.DeviceIdType.MESH
SEQ, STATE = "seq", "state"
VMEM_LIMIT = 61 << 20


def nn(a, b, p=None):
    return lax.dot_general(a, b, (((1,), (0,)), ((), ())), precision=p, preferred_element_type=F32)


def nt(a, b, p=None):
    return lax.dot_general(a, b, (((1,), (1,)), ((), ())), precision=p, preferred_element_type=F32)


def tn(a, b, p=None):
    return lax.dot_general(a, b, (((0,), (0,)), ((), ())), precision=p, preferred_element_type=F32)


def sigmoid(v):
    return 1.0 / (1.0 + jnp.exp(-v))


def silu(v):
    return v * sigmoid(v)


def silu_slope(v):
    s = sigmoid(v)
    return s * (1.0 + v * (1.0 - s))


def softplus(v):
    return jnp.maximum(v, 0.0) + jnp.log1p(jnp.exp(-jnp.abs(v)))


def iota(shape, dim):
    return lax.broadcasted_iota(jnp.int32, shape, dim)


def doc_of(starts, pos):
    found = jnp.full(pos.shape, -1, jnp.int32)
    for start in starts:
        found = found + (pos >= start).astype(jnp.int32)
    return found


def roll(v, shift):
    return pltpu.roll(v, shift, 1)


def rope(v, cosine, sine, direction):
    first = (iota(v.shape, 1) % HEAD_SIZE) < HEAD_SIZE // 2
    half = HEAD_SIZE // 2
    partner = jnp.where(first, -roll(v, v.shape[1] - half), roll(v, half))
    return v * cosine + partner * (direction * sine)


def expander(width):
    return (iota((LANES, width), 1) // HDM == iota((LANES, width), 0)).astype(F32)


def masks_of(starts, first_row, rows):
    pos = first_row + iota((rows, 1), 0)
    doc = doc_of(starts, pos)
    masks = [(doc_of(starts, pos - (KC - 1 - k)) == doc).astype(F32) for k in range(KC)]
    return doc, masks


def push(src, dst, send_sem, recv_sem, device):
    copy = pltpu.make_async_remote_copy(
        src_ref=src,
        dst_ref=dst,
        send_sem=send_sem,
        recv_sem=recv_sem,
        device_id=device,
        device_id_type=MESH,
    )
    copy.start()
    return copy


def greet(n, ns, s, t):
    barrier = pltpu.get_barrier_semaphore()

    def seq_turn(k, carried):
        pl.semaphore_signal(
            barrier, inc=1, device_id={SEQ: lax.rem(s + k, n)}, device_id_type=MESH
        )
        return carried

    lax.fori_loop(1, n, seq_turn, 0)
    for k in range(1, ns):
        pl.semaphore_signal(
            barrier, inc=1, device_id={STATE: lax.rem(t + k, ns)}, device_id_type=MESH
        )
    pl.semaphore_wait(barrier, n - 1 + ns - 1)


def conv_ref(ext_ref, taps, masks, rows):
    total = 0.0
    for k in range(KC):
        at = HALO - KC + 1 + k
        total = total + ext_ref[at : at + rows, :] * taps[k : k + 1] * masks[k]
    return total


class Carry:
    def __init__(self, refs, window, n, s, direction, rows_e):
        self.n, self.s, self.direction, self.rows_e = n, s, direction, rows_e
        self.tx, self.rx, self.thr_tx, self.thr_rx = refs.tx, refs.rx, refs.thr_tx, refs.thr_rx
        self.send, self.recv = refs.sem
        self.thr_send, self.thr_recv = refs.thr_sem
        self.total, self.thr = window
        self.count = carry_steps(n)

    def place(self, slot):
        return (1, 0) if slot == 0 else (2, 0) if slot == 1 else (1 << (slot - 1), slot - 1)

    def copies(self, slot, d, source):
        to = lax.rem(self.s + self.direction * d + self.n, self.n)
        make = lambda src, dst, a, b: pltpu.make_async_remote_copy(
            src_ref=src,
            dst_ref=dst,
            send_sem=a,
            recv_sem=b,
            device_id={SEQ: to},
            device_id_type=MESH,
        )
        return (
            make(self.tx.at[source], self.rx.at[slot], self.send.at[slot], self.recv.at[slot]),
            make(
                self.thr_tx.at[source],
                self.thr_rx.at[slot],
                self.thr_send.at[slot],
                self.thr_recv.at[slot],
            ),
        )

    def inside(self, index):
        return (index >= 0) & (index < self.n)

    def start(self, slot, d, source):
        @pl.when(self.inside(self.s + self.direction * d))
        def _():
            for copy in self.copies(slot, d, source):
                copy.start()

    def finish(self):
        for slot in range(self.count):
            d, source = self.place(slot)

            @pl.when(self.inside(self.s + self.direction * d))
            def _():
                for copy in self.copies(slot, d, source):
                    copy.wait_send()

    def begin(self, part, thr):
        self.tx[0] = part.astype(BF16)
        self.thr_tx[0] = thr
        self.total[...] = jnp.zeros(self.total.shape, F32)
        self.thr[...] = jnp.ones(self.thr.shape, F32)
        for slot in range(min(2, self.count)):
            self.start(slot, *self.place(slot))

    def join(self, slot, d, source):
        @pl.when(self.inside(self.s - self.direction * d))
        def _():
            for copy in self.copies(slot, d, source):
                copy.wait_recv()
            column = nt(self.rows_e, self.thr[...], HI)[:, :1]
            self.total[...] += column * self.rx[slot].astype(F32)
            self.thr[...] = self.thr[...] * self.thr_rx[slot]

        @pl.when(jnp.logical_not(self.inside(self.s - self.direction * d)))
        def _():
            self.thr[...] = jnp.zeros(self.thr.shape, F32)

    def pass_on(self, slot, d):
        self.tx[slot - 1] = self.total[...].astype(BF16)
        self.thr_tx[slot - 1] = self.thr[...]
        self.start(slot, d, slot - 1)

    def advance(self, slot):
        self.join(slot, *self.place(slot))
        if 1 <= slot < self.count - 1:
            self.pass_on(slot + 1, 1 << slot)

    def rest(self, first):
        if first >= self.count:
            return
        for slot in range(first, min(2, self.count)):
            self.advance(slot)
        first = max(first, 2)

        def turn(slot, d):
            self.join(slot, d, slot - 1)
            self.pass_on(slot + 1, 2 * d)
            return 2 * d

        if first < self.count:
            lax.fori_loop(first, self.count - 1, turn, 1 << (first - 1))
            self.join(self.count - 1, 1 << (self.count - 2), self.count - 2)


def carry_steps(n):
    return 1 if n <= 2 else 1 + (n - 2).bit_length()


def expand_rows(width):
    return (iota((width, LANES), 0) // HDM == iota((width, LANES), 1)).astype(F32)


def link_of(linked, cum, cum_t, h):
    return jnp.exp(jnp.where(linked, cum[:, h : h + 1] - cum_t[h : h + 1, :], FAR))


def send_to(sems, k, src, dst, device):
    send, recv = sems
    return push(src, dst, send.at[k], recv.at[k], device)


def row_sums(values):
    return nt(jnp.ones((8, values.shape[1]), F32), values, HI)


def as_column(row):
    first = (iota((8, LANES), 0) == 0).astype(F32)
    return tn(row, first, HI)[:, :1]


def share_rows(refs, ns, t, row):
    tx, rx = refs.tx, refs.rx
    tx[...] = row
    copies = [
        send_to(refs.sem, k - 1, tx, rx.at[k - 1], {STATE: lax.rem(t + k, ns)})
        for k in range(1, ns)
    ]

    def wait():
        total = tx[...]
        for k in range(1, ns):
            copies[k - 1].wait_recv()
            total = total + rx[k - 1]
        return total

    return copies, wait


class RowScatter:
    def __init__(self, refs, sem, t):
        self.sem, self.t = sem, t
        self.tx, self.rx, self.mid = refs.tx, refs.rx, refs.mid
        self.odd, self.far = lax.rem(t, 2), t // 2
        self.copies = []

    def start(self, part):
        rows = self.tx.shape[1]
        part = part.astype(BF16)
        for k in range(4):
            self.tx[(k % 2) * 2 + k // 2] = part[rows * k : rows * (k + 1)]
        theirs = self.tx.at[pl.ds(2 - 2 * self.odd, 2)]
        self.copies.append(
            send_to(self.sem, 0, theirs, self.rx.at[pl.ds(0, 2)], {STATE: sibling(self.t)})
        )

    def middle(self):
        self.copies[0].wait_recv()
        away = 1 - self.far
        self.mid[...] = (
            self.tx[2 * self.odd + away].astype(F32) + self.rx[away].astype(F32)
        ).astype(BF16)
        self.copies.append(
            send_to(self.sem, 1, self.mid, self.rx.at[2], {STATE: lax.rem(self.t + 2, 4)})
        )

    def finish(self):
        total = self.tx[2 * self.odd + self.far].astype(F32) + self.rx[self.far].astype(F32)
        self.copies[1].wait_recv()
        return total + self.rx[2].astype(F32)


class Gather:
    def __init__(self, every, sem, t, own):
        self.every, self.sem, self.t = every, sem, t
        every[t] = own
        block = self.every.at[t]
        self.copies = [
            send_to(sem, 0, block, block, {STATE: sibling(t)}),
            send_to(sem, 1, block, block, {STATE: lax.rem(t + 2, 4)}),
        ]

    def middle(self):
        self.copies[1].wait_recv()
        block = self.every.at[lax.rem(self.t + 2, 4)]
        self.copies.append(send_to(self.sem, 2, block, block, {STATE: sibling(self.t)}))

    def finish(self):
        self.copies[0].wait_recv()
        self.copies[2].wait_recv()


def sibling(t):
    return t + 1 - 2 * lax.rem(t, 2)


def levels_of(n):
    return n.bit_length() - 1


def bits_of(n, swapped):
    order = list(range(levels_of(n)))
    if swapped and len(order) > 1:
        order[0], order[1] = order[1], order[0]
    return order


class HalvingSum:
    def __init__(self, refs, n, s, swapped=False):
        self.sem, self.n, self.s = refs.sem, n, s
        self.bits = bits_of(n, swapped)
        self.src, self.rx = refs.src, refs.rx
        self.copies = []

    def owner(self, p):
        top = len(self.bits) - 1
        return sum(((p >> (top - level)) & 1) << bit for level, bit in enumerate(self.bits))

    def block_of(self, index):
        top = len(self.bits) - 1
        return sum(((index >> bit) & 1) << (top - level) for level, bit in enumerate(self.bits))

    def fill(self, column, values):
        rows = self.src.shape[1]
        width = values.shape[1]
        for p in range(self.n):
            at = rows * self.owner(p)
            self.src[p, :, column : column + width] = values[at : at + rows]

    def parts(self, level):
        half = self.n >> (level + 1)
        mine = lax.rem(self.s // (1 << self.bits[level]), 2)
        if level == 0:
            return self.src, 0, half, mine
        return self.rx, self.n - (self.n >> (level - 1)), half, mine

    def start(self, level=0):
        buffer, base, half, mine = self.parts(level)
        to = self.s + (1 - 2 * mine) * (1 << self.bits[level])
        here = self.n - (self.n >> level)
        self.copies.append(
            send_to(
                self.sem,
                level,
                buffer.at[pl.ds(base + (1 - mine) * half, half)],
                self.rx.at[pl.ds(here, half)],
                {SEQ: to},
            )
        )

    def step(self, level):
        buffer, base, half, mine = self.parts(level)
        self.copies[level].wait_recv()
        here = self.n - (self.n >> level)

        def turn(i, carried):
            kept = buffer[base + mine * half + i].astype(F32)
            self.rx[here + i] = (kept + self.rx[here + i].astype(F32)).astype(BF16)
            return carried

        lax.fori_loop(0, half, turn, 0)
        if level + 1 < len(self.bits):
            self.start(level + 1)

    def result(self):
        return self.rx[self.n - 2]


def named(value):
    if isinstance(value, dict):
        return types.SimpleNamespace(**{key: named(item) for key, item in value.items()})
    return value


def layer_kernel(n, ns, trees, *flat):
    refs, at = types.SimpleNamespace(), 0
    for tree in trees:
        part = jax.tree.unflatten(tree, flat[at : at + tree.num_leaves])
        at += tree.num_leaves
        refs.__dict__.update(named(part).__dict__)
    x, normed, inv1 = refs.x, refs.normed, refs.inv1
    w_mix, w_qkv, w_joint, w_gu, down = refs.w_mix, refs.w_qkv, refs.w_joint, refs.w_gu, refs.down
    grad = refs.grad
    w_step = refs.w_step
    T, D = x.shape
    t, s = lax.axis_index(STATE), lax.axis_index(SEQ)
    joined = refs.jall_all.at[t]
    C = w_mix.shape[2]
    QC = 2 * HEAD_SIZE
    AQ = QUERY_HEADS * HEAD_SIZE
    NW = refs.st_own.shape[1]
    HL = NH // ns
    N = NW * ns
    TO = T // ns
    DM = C * ns
    F = down.shape[1]
    pairs = C // LANES
    scale = 1.0 / math.sqrt(HEAD_SIZE)
    state_peer = lambda k: {STATE: lax.rem(t + k, ns)}
    own_c = pl.ds(pl.multiple_of(C * t, LANES), C)
    loads = [
        pltpu.make_async_copy(src, dst, refs.load[k])
        for k, (src, dst) in enumerate(
            [
                (refs.w_att.at[:, pl.ds(pl.multiple_of(QC * t, LANES), QC)], w_qkv.at[:, pl.ds(0, QC)]),
                (refs.w_att.at[:, pl.ds(AQ, 2 * QC)], w_qkv.at[:, pl.ds(QC, 2 * QC)]),
                (refs.w_mix_in, w_mix),
                (refs.joint.at[pl.ds(pl.multiple_of(QC * t, QC), QC)], w_joint.at[pl.ds(0, QC)]),
                (refs.joint.at[pl.ds(pl.multiple_of(AQ + C * t, LANES), C)], w_joint.at[pl.ds(QC, C)]),
                (refs.g, grad),
                (refs.down_in, down),
                (refs.w_gu_in, w_gu),
            ]
        )
    ]
    for load in loads:
        load.start()
    lanes_row = iota((1, LANES), 1)
    blank = jnp.zeros((1, LANES), F32)
    bias_row, rate_row = blank, blank
    skip_row = jnp.zeros((1, C), F32)
    heads_row = iota((1, C), 1) // HDM
    for h in range(HL):
        bias_row = jnp.where(lanes_row == h, refs.step_bias[HL * t + h], bias_row)
        rate_row = jnp.where(lanes_row == h, refs.decay_rate[HL * t + h], rate_row)
        skip_row = jnp.where(heads_row == h, refs.skip_gain[HL * t + h], skip_row)
    taps_mix = refs.conv_mixer[:, own_c]
    ggain_row = refs.ggain[:, own_c]
    pick = (iota((NH, LANES), 0) == HL * t + iota((NH, LANES), 1)) & (iota((NH, LANES), 1) < HL)
    pick = pick.astype(F32)
    refs.taps8[...] = jnp.zeros(refs.taps8.shape, F32)
    refs.taps8[:KC, : 2 * NW] = refs.conv_state[...]
    eye8 = (iota((8, LANES), 0) == iota((8, LANES), 1)).astype(F32)
    taps_cols = tn(refs.taps8[...], eye8, HI)
    for c in range(2):
        refs.taps_st[c] = taps_cols[NW * c : NW * (c + 1)]
    greet(n, ns, s, t)
    sent = []
    halo_copy = send_to(refs.halo, 0, x.at[pl.ds(T - HALO, HALO)], refs.halo_rx, {SEQ: lax.rem(s + 1, n)})
    mine = pl.ds(pl.multiple_of(NW * t, NW), NW)
    arriving = []
    for k in range(1, ns):
        arriving.append(send_to(refs.st, k - 1, refs.st_own, refs.st_all.at[:, mine, :], state_peer(k)))
        arriving.append(send_to(refs.taps, k - 1, refs.taps_st, refs.taps_all.at[:, mine, :], state_peer(k)))
    sent += [halo_copy] + arriving
    refs.st_all[:, mine, :] = refs.st_own[...]
    refs.taps_all[:, mine, :] = refs.taps_st[...]

    first_row = s * T
    starts = [refs.doc_starts[k] for k in range(refs.doc_starts.shape[0])]
    doc, masks = masks_of(starts, first_row, T)
    tiles = T // LANES

    def code_turn(j, carried):
        for i in range(tiles):
            real = refs.real[pl.ds(tiles * j + i, 1), :]
            ids = doc_of(starts, j * T + i * LANES + iota((1, LANES), 1))
            refs.codes[j, :, LANES * i : LANES * (i + 1)] = jnp.where(real > 0, ids, -7)
        return carried

    lax.fori_loop(0, n, code_turn, 0)
    real_col = as_column(jnp.broadcast_to((refs.codes[s] >= 0).astype(F32), (8, T)))
    firsts = jnp.zeros((T, 1), jnp.int32)
    places = first_row + iota((T, 1), 0)
    for start in starts:
        firsts = jnp.where(places >= start, start, firsts)
    powers = (iota((1, LANES), 1) % (HEAD_SIZE // 2)).astype(F32) * (2.0 / HEAD_SIZE)
    angles = (places - firsts).astype(F32) * jnp.exp(-math.log(ROPE_BASE) * powers)
    cosine, sine = jnp.cos(angles), jnp.sin(angles)
    doc_row = doc_of(starts, first_row + iota((1, T), 1))
    lane = iota((T, LANES), 1)
    low = lane < HEAD_SIZE
    ngain = refs.ngain[...]

    xf = x[...].astype(F32)
    inv = lax.rsqrt(jnp.mean(xf * xf, axis=1, keepdims=True) + EPSILON)
    inv1[...] = inv
    normed[HALO:, :] = (xf * inv * ngain).astype(BF16)
    main = normed[HALO:, :]
    loads[0].wait()
    loads[1].wait()
    qkv = nn(main, w_qkv[...])
    q = (rope(qkv[:, :QC], cosine, sine, 1.0).astype(BF16) * scale).astype(F32)
    kcos, ksin = jnp.where(low, cosine, 1.0), jnp.where(low, sine, 0.0)
    kv_all = refs.kv_all
    group = t // 2
    both_k, both_v = qkv[:, QC : 2 * QC], qkv[:, 2 * QC :]
    own_kv = jnp.where(
        low,
        jnp.where(group == 0, both_k, roll(both_k, HEAD_SIZE)),
        jnp.where(group == 0, roll(both_v, HEAD_SIZE), both_v),
    )
    kv_all[s] = rope(own_kv, kcos, ksin, 1.0).astype(BF16)

    def kv_copy(k, to):
        return pltpu.make_async_remote_copy(
            src_ref=kv_all.at[s],
            dst_ref=kv_all.at[s],
            send_sem=refs.kv[0].at[k - 1],
            recv_sem=refs.kv[1].at[k - 1],
            device_id={SEQ: to},
            device_id_type=MESH,
        )

    def kv_turn(k, carried):
        kv_copy(k, lax.rem(s + k, n)).start()
        return carried

    lax.fori_loop(1, n - s, kv_turn, 0)
    refs.q2[:T, :] = jnp.where(low, q, 0.0).astype(BF16)
    refs.q2[T:, :] = jnp.where(low, roll(q, HEAD_SIZE), 0.0).astype(BF16)
    loads[2].wait()
    refs.z[...] = nn(main, w_mix[0])
    raw = nn(nt(main, w_step[...]), pick, HI) + bias_row

    halo_copy.wait_recv()
    hf = refs.halo_rx[...].astype(F32)
    inv_h = lax.rsqrt(jnp.mean(hf * hf, axis=1, keepdims=True) + EPSILON)
    normed[:HALO, :] = (hf * inv_h * ngain).astype(BF16)
    ext_f, ext_s, ext_o = refs.ext_f, refs.ext_s, refs.ext_o
    ext_f[...] = nn(normed[...], w_mix[1]).astype(BF16).astype(F32)
    inner_lin = conv_ref(ext_f, taps_mix, masks, T)
    inner = silu(inner_lin)
    for copy in arriving:
        copy.wait_recv()
    for c in range(2):
        ext_s[...] = nt(normed[...], refs.st_all[c]).astype(BF16).astype(F32)
        taps = refs.taps_all[c].T
        refs.wr[c] = silu(conv_ref(ext_s, taps, masks, T))
    write, read = refs.wr[0], refs.wr[1]
    step = softplus(raw)
    causal = iota((T, T), 0) >= iota((T, T), 1)
    tri = causal.astype(F32)
    cum = nn(tri, -step * rate_row, HI)
    cum_t = cum.T
    linked = (doc == doc_row) & causal
    E = expander(C)
    rows_e = expand_rows(C)
    inflow = step * real_col
    inflow_e = nn(inflow, E, HI)
    in_x = inner * inflow_e
    cum_last = cum[T - 1 : T]
    last = first_row + T - 1
    doc_last = doc_of(starts, jnp.full((T, 1), last, jnp.int32))
    prior = doc_of(starts, jnp.full((T, 1), first_row - 1, jnp.int32))
    tail = jnp.where(doc == doc_last, jnp.exp(cum_last - cum), 0.0)
    refs.tail_e[...] = nn(tail, E, HI)
    state_part = tn(refs.tail_e[...] * in_x, write, HI)
    alive = (doc == prior).astype(F32)
    alive_last = (doc_last == prior).astype(F32)[:8]
    thr = alive_last * jnp.exp(jnp.broadcast_to(cum_last, (8, LANES)))
    steps = carry_steps(n)

    carry = Carry(refs.fc, (refs.window, refs.window_thr), n, s, 1, rows_e)
    carry.begin(state_part, thr)

    def between(carry, p):
        slots = (0, 1) if p == 0 else (p + 1,)
        for slot in slots:
            if slot < steps:
                carry.advance(slot)

    g_mat = nt(read, write, HI)
    for p in range(pairs):
        cols = slice(LANES * p, LANES * (p + 1))
        ys = []
        for h in (2 * p, 2 * p + 1):
            link = link_of(linked, cum, cum_t, h)
            ys.append(nn(link * g_mat, in_x[:, cols], HI))
        refs.ssd[:, cols] = jnp.where(low, ys[0], ys[1])
        between(carry, p)

    doc2 = jnp.concatenate([doc, doc], axis=0)
    m_ref, l_ref, acc_ref = refs.m_acc, refs.l_acc, refs.o_acc
    m_ref[...] = jnp.full(m_ref.shape, FAR, F32)
    l_ref[...] = jnp.zeros(l_ref.shape, F32)
    acc_ref[...] = jnp.zeros(acc_ref.shape, F32)

    def allowed_at(j, diagonal):
        allowed = refs.codes[j] == doc2
        if diagonal:
            rows2 = jnp.concatenate([iota((T, T), 0)] * 2, axis=0)
            cols2 = iota((2 * T, T), 1)
            allowed = (allowed & (cols2 <= rows2)) | (cols2 == rows2)
        return allowed

    def attend(j, diagonal):
        block = kv_all[j]
        scores = jnp.where(allowed_at(j, diagonal), nt(refs.q2[...], block), FAR)
        m = m_ref[...]
        m_new = jnp.maximum(m, jnp.max(scores, axis=1, keepdims=True))
        shrink = jnp.exp(m - m_new)
        p = jnp.exp(scores - m_new)
        l_ref[...] = l_ref[...] * shrink + jnp.sum(p, axis=1, keepdims=True)
        acc_ref[...] = acc_ref[...] * shrink + nn(p.astype(BF16), block)
        m_ref[...] = m_new

    attend(s, True)

    def attend_turn(k, carried):
        kv_copy(k, lax.rem(s + k, n)).wait_recv()
        attend(s - k, False)
        return carried

    lax.fori_loop(1, s + 1, attend_turn, 0)
    out = acc_ref[...] / l_ref[...]
    acc_ref[...] = out
    m_ref[...] = m_ref[...] + jnp.log(l_ref[...])
    joined[:, :QC] = jnp.where(low, roll(out[:T], HEAD_SIZE), out[T:]).astype(BF16)

    carry.rest(pairs + 1)
    s_in = refs.window[...]
    refs.reach_e[...] = nn(alive * jnp.exp(cum), E, HI)
    ssd = refs.ssd[...] + refs.reach_e[...] * nt(read, s_in, HI)
    refs.ssd[...] = ssd
    z = refs.z[...]
    full_mix = ssd + skip_row * inner
    gated = full_mix * silu(z)
    copies, wait = share_rows(refs.sq, ns, t, row_sums(gated * gated))
    sent += copies
    inv_g = as_column(lax.rsqrt(wait() / DM + EPSILON))
    joined[:, QC:] = (gated * inv_g * ggain_row).astype(BF16)
    loads[3].wait()
    loads[4].wait()
    rs1 = RowScatter(refs.rs1, refs.rs1_sem, t)
    rs1.start(nn(joined[...], w_joint[...]))
    own_rows = pl.ds(pl.multiple_of(TO * t, TO), TO)
    loads[5].wait()
    loads[6].wait()
    dh = nn(grad[...], down[...])
    x_own = x[own_rows, :].astype(F32)
    rs1.middle()
    res = x_own + rs1.finish()
    inv2 = lax.rsqrt(jnp.mean(res * res, axis=1, keepdims=True) + EPSILON)
    mgain = refs.mgain[...]
    ag1 = Gather(refs.ag1_all, refs.ag1_sem, t, (res * inv2 * mgain).astype(BF16))
    ag1.middle()
    ag1.finish()

    n2 = jnp.concatenate([refs.ag1_all[k] for k in range(ns)], axis=0)
    loads[7].wait()
    gate, up = nn(n2, w_gu[0]), nn(n2, w_gu[1])
    sig = sigmoid(gate)
    act = gate * sig
    hidden = (act * up).astype(BF16)
    d_gate = (dh * up * (sig * (1.0 + gate * (1.0 - sig)))).astype(BF16)
    d_up = (dh * act).astype(BF16)
    rs2 = RowScatter(refs.rs2, refs.rs2_sem, t)
    rs2.start(nt(d_gate, w_gu[0]) + nt(d_up, w_gu[1]))
    for copy in rs1.copies + ag1.copies:
        copy.wait_send()
    rs3 = RowScatter(refs.rs1, refs.rs3_sem, t)
    rs3.start(nt(hidden, down[...]))
    rs2.middle()
    def weight_sum(stream, parts, swapped=False):
        total = HalvingSum(stream, n, s, swapped)
        column = 0
        for lhs, rhs in parts:
            width = rhs.shape[1]
            for c in range(0, width, 256):
                piece = rhs[:, c : min(c + 256, width)]
                total.fill(column + c, tn(lhs, piece).astype(BF16))
            column += width
        total.start()
        return total

    sum_w_gu = weight_sum(refs.w_gu_g, [(n2, d_gate), (n2, d_up)], True)
    rs3.middle()
    sum_down = weight_sum(refs.down_g, [(grad[...], hidden)])
    dn2 = rs2.finish()
    scaled = dn2 * mgain
    d_res = (
        grad[own_rows, :].astype(F32)
        + inv2 * scaled
        - res * inv2 * inv2 * inv2 * jnp.mean(scaled * res, axis=1, keepdims=True)
    )
    ag2 = Gather(refs.ag2_all, refs.ag2_sem, t, d_res.astype(BF16))

    def put_small(row, values):
        for k in range(0, values.shape[1], LANES):
            piece = values[:, k : k + LANES]
            refs.small_tx[row : row + 1, : piece.shape[1]] = piece
            row += 1

    refs.small_tx[...] = jnp.zeros(refs.small_tx.shape, F32)
    put_small(8, jnp.sum(dn2 * res * inv2, axis=0, keepdims=True))
    ag2.middle()
    ag3 = Gather(refs.ag1_all, refs.ag3_sem, t, (res + rs3.finish()).astype(BF16))
    ag2.finish()
    joined_copies = [
        send_to(refs.jall, k - 1, joined, joined, state_peer(k)) for k in range(1, ns)
    ]
    sent += joined_copies

    d_branch = jnp.concatenate([refs.ag2_all[k] for k in range(ns)], axis=0)
    d_joined = nt(d_branch, w_joint[...])
    d_gn = d_joined[:, QC:]
    scaled = d_gn * ggain_row
    copies, wait = share_rows(refs.dot, ns, t, row_sums(scaled * gated))
    sent += copies
    put_small(16, jnp.sum(d_gn * gated * inv_g, axis=0, keepdims=True))
    d_att = d_joined[:, :QC].astype(BF16).astype(F32)
    dout2 = jnp.concatenate(
        [jnp.where(low, 0.0, roll(d_att, HEAD_SIZE)), jnp.where(low, 0.0, d_att)], axis=0
    )
    delta = jnp.sum(dout2 * acc_ref[...], axis=1, keepdims=True)
    l_ref[...] = delta
    refs.dout2[...] = dout2.astype(BF16)
    dot = as_column(wait() / DM)
    d_gated = inv_g * scaled - gated * (inv_g * inv_g * inv_g * dot)
    sig = sigmoid(z)
    dy = d_gated * z * sig
    refs.d_z[...] = (d_gated * full_mix * (sig * (1.0 + z * (1.0 - sig)))).astype(BF16)
    put_small(19, nt(jnp.broadcast_to(jnp.sum(dy * inner, axis=0, keepdims=True), (8, C)), E, HI)[:1])
    reach_dy = refs.reach_e[...] * dy
    carry_b = Carry(refs.bc, (refs.window, refs.window_thr), n, s, -1, rows_e)
    carry_b.begin(tn(reach_dy, read, HI), thr)
    sum_z = weight_sum(refs.z_g, [(main, refs.d_z[...])])
    ag3.middle()
    ag3.finish()
    for k in range(ns):
        refs.layer_output[TO * k : TO * (k + 1), :] = refs.ag1_all[k]
    d_g = jnp.zeros((T, T), F32)
    for p in range(pairs):
        cols = slice(LANES * p, LANES * (p + 1))
        xp, dyp = in_x[:, cols], dy[:, cols]
        halves = []
        for k in range(2):
            link = link_of(linked, cum, cum_t, 2 * p + k)
            halves.append(tn(link * g_mat, dyp, HI))
            own = low if k == 0 else jnp.logical_not(low)
            d_g = d_g + link * nt(jnp.where(own, dyp, 0.0), xp, HI)
        refs.w_tot[:, cols] = jnp.where(low, halves[0], halves[1])
        between(carry_b, p)

    refs.dq2[...] = jnp.zeros(refs.dq2.shape, F32)

    def attend_back(j, diagonal):
        block = kv_all[j]
        q2, dout2 = refs.q2[...], refs.dout2[...]
        scores = jnp.where(allowed_at(j, diagonal), nt(q2, block), FAR)
        p = jnp.exp(scores - m_ref[...])
        ds = (p * (nt(dout2, block) - l_ref[...])).astype(BF16)
        refs.dq2[...] += nn(ds, block)
        return tn(ds, q2) + tn(p.astype(BF16), dout2)

    def dkv_copy(k, to, source):
        return pltpu.make_async_remote_copy(
            src_ref=source,
            dst_ref=refs.dkv_rx.at[k - 1],
            send_sem=refs.dkv[0].at[k - 1],
            recv_sem=refs.dkv[1].at[k - 1],
            device_id={SEQ: to},
            device_id_type=MESH,
        )

    def back_turn(k, carried):
        kv_all[s - k] = attend_back(s - k, False).astype(BF16)
        dkv_copy(k, lax.rem(s - k + n, n), kv_all.at[s - k]).start()
        return carried

    lax.fori_loop(1, s + 1, back_turn, 0)
    refs.dkv_sum[...] = attend_back(s, True)
    sum_w_gu.step(0)
    sum_down.step(0)
    for copy in joined_copies:
        copy.wait_recv()
    own_d = pl.ds(pl.multiple_of((D // ns) * t, LANES), D // ns)
    d_cols = jnp.concatenate([refs.ag2_all[k, :, own_d] for k in range(ns)], axis=0)
    sum_joint = joint = HalvingSum(refs.joint_g, n, s)
    rows_j = joint.src.shape[1]
    piece = min(rows_j, LANES)
    for k in range(ns):
        values = tn(refs.jall_all[k], d_cols).astype(BF16)
        for at in range(0, QC + C, piece):
            row = QC * k + at if at < QC else AQ + C * k + at - QC
            offset = row % rows_j
            joint.src[joint.block_of(row // rows_j), offset : offset + piece, :] = values[at : at + piece]
    joint.start()

    carry_b.rest(pairs + 1)
    later = refs.window[...]
    tail_e = refs.tail_e[...]
    tail_r = tail_e * nt(write, later, HI)
    w_tot = refs.w_tot[...] + tail_r
    d_write = tn(d_g, read, HI) + nn(tail_e * in_x, later, HI)
    d_read = nn(d_g, write, HI) + nn(reach_dy, s_in, HI)
    refs.dwr_tx[0] = d_write.T.astype(BF16)
    refs.dwr_tx[1] = d_read.T.astype(BF16)
    dwr = []
    for k in range(1, ns):
        p = lax.rem(t + k, ns)
        theirs = pl.ds(pl.multiple_of(NW * p, NW), NW)
        dwr.append(
            send_to(refs.dwr, k - 1, refs.dwr_tx.at[:, theirs, :], refs.dwr_rx.at[k - 1], {STATE: p})
        )
    sent += dwr
    u = nt(inner * w_tot, E, HI)
    tl = nt(in_x * tail_r, E, HI)
    thr_s = jnp.sum(tn(later * s_in, rows_e, HI), axis=0, keepdims=True) * thr[:1]
    d_cum = nt(dy * ssd, E, HI) - inflow * u
    at_last = iota((T, LANES), 0) == T - 1
    d_cum = d_cum + jnp.where(at_last, jnp.sum(tl, axis=0, keepdims=True) + thr_s, 0.0)
    d_ld = tn(tri, d_cum, HI)
    d_step = real_col * u - rate_row * d_ld
    put_small(20, -jnp.sum(step * d_ld, axis=0, keepdims=True))
    d_step = d_step * sigmoid(raw)
    put_small(21, jnp.sum(d_step, axis=0, keepdims=True))
    d_step = d_step.astype(BF16)
    sum_z.step(0)
    d_lin = (inflow_e * w_tot + skip_row * dy) * silu_slope(inner_lin)

    def conv_back(ext, grad, taps, up, row, rows):
        grad[...] = jnp.zeros(grad.shape, F32)
        for k in range(KC):
            at = HALO - KC + 1 + k
            masked = up * masks[k]
            put_small(row + rows * k, jnp.sum(masked * ext[at : at + T, :], axis=0, keepdims=True))
            grad[at : at + T, :] += masked * taps[k : k + 1]
        return grad[...].astype(BF16)

    d_ext = conv_back(ext_f, refs.grad_f, taps_mix, d_lin, 22, C // LANES)
    st64 = refs.st_own[...].reshape(2 * NW, D)
    taps_own = refs.taps_st[...].reshape(2 * NW, LANES).T
    ext_o[...] = nt(normed[...], st64).astype(BF16).astype(F32)
    slope_o = silu_slope(conv_ref(ext_o, taps_own, masks, T))
    for copy in dwr:
        copy.wait_recv()
    d_wr = refs.dwr_tx[:, mine, :].astype(F32)
    for k in range(1, ns):
        d_wr = d_wr + refs.dwr_rx[k - 1].astype(F32)
    sum_inner = weight_sum(refs.inner_g, [(normed[...], d_ext)])
    sum_w_gu.step(1)
    sum_down.step(1)
    row_st = 22 + KC * (C // LANES)
    d_st = conv_back(ext_o, refs.grad_o, taps_own, d_wr.reshape(2 * NW, T).T * slope_o, row_st, 1)
    refs.back_tx[...] = (nt(d_ext[:HALO], w_mix[1]) + nn(d_st[:HALO], st64)).astype(BF16)
    back = send_to(refs.back, 0, refs.back_tx, refs.back_rx, {SEQ: lax.rem(s + n - 1, n)})
    sent.append(back)
    def dkv_turn(k, carried):
        dkv_copy(k, lax.rem(s - k + n, n), refs.dkv_rx.at[k - 1]).wait_recv()
        refs.dkv_sum[...] += refs.dkv_rx[k - 1].astype(F32)
        return carried

    lax.fori_loop(1, n - s, dkv_turn, 0)
    refs.pair_tx[...] = refs.dkv_sum[...].astype(BF16)
    odd = lax.rem(t, 2)
    pair = send_to(refs.pair, 0, refs.pair_tx, refs.pair_rx, {STATE: t + 1 - 2 * odd})
    sent.append(pair)
    d_z = refs.d_z[...]
    sum_joint.step(0)
    sum_z.step(1)
    dq2 = refs.dq2[...]
    dq = jnp.where(low, dq2[:T], roll(dq2[T:], HEAD_SIZE)) * scale
    d_q = rope(dq, cosine, sine, -1.0).astype(BF16)
    d_n = (
        nt(d_z, w_mix[0])
        + nt(d_ext[HALO:], w_mix[1])
        + nn(d_st[HALO:], st64)
        + nn(nt(d_step, pick.astype(BF16)).astype(BF16), w_step[...])
    )
    pair.wait_recv()
    d_kv = rope(refs.dkv_sum[...] + refs.pair_rx[...].astype(F32), kcos, ksin, -1.0)
    d_kv = jnp.where(low == (odd == 0), d_kv, 0.0)
    other = roll(d_kv, HEAD_SIZE)
    d_k = jnp.where(low, jnp.where(group == 0, d_kv, 0.0), jnp.where(group == 0, 0.0, other))
    d_v = jnp.where(low, jnp.where(group == 0, other, 0.0), jnp.where(group == 0, 0.0, d_kv))
    d_kv_b = d_kv.astype(BF16)
    d_qkv = jnp.concatenate([d_q, jnp.where(odd == 0, d_k, d_v).astype(BF16)], axis=1)
    mine_kv = jnp.where(odd == 0, d_kv, other).astype(BF16)
    pad_st = jnp.concatenate([jnp.zeros((T + HALO, HEAD_SIZE), F32), d_st.astype(F32)], axis=1)
    mine_kv = jnp.concatenate([jnp.zeros((HALO, LANES), F32), mine_kv.astype(F32)], axis=0)
    mixed = jnp.where(iota((T + HALO, LANES), 1) < HEAD_SIZE, mine_kv, pad_st).astype(BF16)
    sum_rest = weight_sum(refs.rest_g, [(main, d_q), (normed[...], mixed), (main, d_step)])
    w_kv = jnp.where(odd == 0, w_qkv[:, QC : 2 * QC], w_qkv[:, 2 * QC :])
    d_n = d_n + nt(d_qkv, jnp.concatenate([w_qkv[:, :QC], w_kv], axis=1))
    back.wait_recv()
    tail_rows = d_n[T - HALO :] + refs.back_rx[...].astype(F32)
    d_n = jnp.concatenate([d_n[: T - HALO], tail_rows], axis=0)
    for copy in rs2.copies + ag3.copies:
        copy.wait_send()
    rs4 = RowScatter(refs.rs2, refs.rs4_sem, t)
    rs4.start(d_n)
    sum_inner.step(0)
    rs4.middle()
    sum_w_gu.step(2)
    sum_down.step(2)
    inv_own = inv1[own_rows, :]
    d_n = rs4.finish()
    scaled = d_n * ngain
    in_g = (
        d_res
        + inv_own * scaled
        - x_own * inv_own * inv_own * inv_own * jnp.mean(scaled * x_own, axis=1, keepdims=True)
    )
    ag4 = Gather(refs.ag1_all, refs.ag4_sem, t, in_g.astype(BF16))
    put_small(0, jnp.sum(d_n * x_own * inv_own, axis=0, keepdims=True))

    def small_copy(k, source):
        return pltpu.make_async_remote_copy(
            src_ref=source,
            dst_ref=refs.small_rx.at[s],
            send_sem=refs.small[0].at[k - 1],
            recv_sem=refs.small[1].at[k - 1],
            device_id={SEQ: lax.rem(s + k, n)},
            device_id_type=MESH,
        )

    refs.small_rx[s] = refs.small_tx[...]

    def small_turn(k, carried):
        small_copy(k, refs.small_tx).start()
        return carried

    lax.fori_loop(1, n, small_turn, 0)
    last_level = len(bits_of(n, False)) - 1

    def steps_of(total, first, stop):
        for level in range(first, stop):
            total.step(level)

    steps_of(sum_joint, 1, 2)
    steps_of(sum_z, 2, last_level + 1)
    gz = Gather(refs.gz_all, refs.gz_sem, t, sum_z.result())
    steps_of(sum_inner, 1, 2)
    steps_of(sum_rest, 0, 1)
    ag4.middle()
    steps_of(sum_joint, 2, last_level + 1)
    gj = Gather(refs.gj_all, refs.gj_sem, t, sum_joint.result())
    steps_of(sum_inner, 2, last_level + 1)
    gi = Gather(refs.gi_all, refs.gi_sem, t, sum_inner.result())
    steps_of(sum_rest, 1, 2)
    ag4.finish()
    for k in range(ns):
        refs.input_grad[TO * k : TO * (k + 1), :] = refs.ag1_all[k]
    gz.middle()

    def small_end(k, carried):
        small_copy(k, refs.small_tx).wait_recv()
        return carried

    lax.fori_loop(1, n, small_end, 0)

    def small_sum(j, total):
        return total + refs.small_rx[j]

    small = Gather(refs.sm_all, refs.sm_sem, t, lax.fori_loop(0, n, small_sum, jnp.zeros(refs.small_tx.shape, F32))
    )
    steps_of(sum_rest, 2, last_level + 1)
    gr = Gather(refs.gr_all, refs.gr_sem, t, sum_rest.result())
    gj.middle()
    gi.middle()
    small.middle()
    steps_of(sum_w_gu, 3, last_level + 1)
    steps_of(sum_down, 3, last_level + 1)
    refs.o_gu[...] = sum_w_gu.result()
    refs.o_down[...] = sum_down.result()
    gz.finish()
    gj.finish()
    gi.finish()
    gr.middle()
    for k in range(ns):
        refs.o_mix[0, :, C * k : C * (k + 1)] = refs.gz_all[k]
        refs.o_mix[1, :, C * k : C * (k + 1)] = refs.gi_all[k]
        refs.o_joint[:, (D // ns) * k : (D // ns) * (k + 1)] = refs.gj_all[k]
    small.finish()
    total = refs.sm_all[0, :16, :]
    for k in range(1, ns):
        total = total + refs.sm_all[k, :16, :]
    refs.o_gains[...] = total
    refs.o_small[...] = refs.sm_all[:, 16:, :]
    gr.finish()
    rows = refs.gr_all.shape[1]
    half = iota((rows, LANES), 1) < HEAD_SIZE
    g_step = 0.0
    for k in range(ns):
        refs.o_att[:, QC * k : QC * (k + 1)] = refs.gr_all[k, :, :QC]
        chosen = (iota((NH, LANES), 0) == HL * k + iota((NH, LANES), 1)) & (iota((NH, LANES), 1) < HL)
        g_step = g_step + nt(refs.gr_all[k, :, 2 * QC :].astype(F32), chosen.astype(F32), HI)
    refs.o_step[...] = g_step
    for c in range(2):
        first = refs.gr_all[c, :, QC : 2 * QC].astype(F32)
        second = refs.gr_all[2 + c, :, QC : 2 * QC].astype(F32)
        refs.o_att[:, AQ + QC * c : AQ + QC * (c + 1)] = jnp.where(
            half, first, roll(second, HEAD_SIZE)
        ).astype(BF16)
    refs.o_st[...] = refs.gr_all[t, :, QC : 2 * QC]

    def small_sent(k, carried):
        small_copy(k, refs.small_tx).wait_send()
        return carried

    lax.fori_loop(1, n, small_sent, 0)
    for group_of in (rs3, rs4, ag2, ag4, gz, gj, gi, gr, small, sum_w_gu, sum_down, sum_z, sum_joint, sum_inner, sum_rest):
        sent += group_of.copies
    for copy in sent:
        copy.wait_send()
    carry.finish()
    carry_b.finish()

    def kv_end(k, carried):
        kv_copy(k, lax.rem(s + k, n)).wait_send()
        return carried

    lax.fori_loop(1, n - s, kv_end, 0)

    def dkv_end(k, carried):
        dkv_copy(k, lax.rem(s - k + n, n), kv_all.at[s - k]).wait_send()
        return carried

    lax.fori_loop(1, s + 1, dkv_end, 0)


def layer(n, ns, arrays):
    inputs = types.SimpleNamespace(**arrays)
    T, D = inputs.x.shape
    C = inputs.w_mix_in.shape[2]
    NW = inputs.st_own.shape[1]
    F = inputs.down_in.shape[1]
    N, TO, H = NW * ns, T // ns, NH // ns
    KJ = inputs.joint.shape[0]
    QC = 2 * HEAD_SIZE
    R, RJ = D // n, KJ // n
    steps = carry_steps(n)
    levels = levels_of(n)
    sd = jax.ShapeDtypeStruct
    J = QC + C
    SMALL = -(-(22 + KC * (C // LANES) + KC) // 8) * 8
    outs = dict(
        layer_output=sd((T, D), BF16),
        input_grad=sd((T, D), BF16),
        o_down=sd((R, F), BF16),
        o_gu=sd((R, 2 * F), BF16),
        o_mix=sd((2, R, ns * C), BF16),
        o_joint=sd((RJ, D), BF16),
        o_att=sd((R, inputs.w_att.shape[1]), BF16),
        o_step=sd((R, NH), F32),
        o_st=sd((R, LANES), BF16),
        o_gains=sd((16, LANES), F32),
        o_small=sd((ns, SMALL - 16, LANES), F32),
    )
    vm = pltpu.VMEM
    dma = lambda k: (pltpu.SemaphoreType.DMA((k,)), pltpu.SemaphoreType.DMA((k,)))
    blocks = lambda *shape: vm((ns,) + shape, BF16)

    def scan():
        return dict(
            tx=vm((steps, C, N), BF16),
            rx=vm((steps, C, N), BF16),
            thr_tx=vm((steps, 8, LANES), F32),
            thr_rx=vm((steps, 8, LANES), F32),
            sem=dma(steps),
            thr_sem=dma(steps),
        )

    def rows():
        return dict(tx=vm((8, T), F32), rx=vm((ns - 1, 8, T), F32), sem=dma(ns - 1))

    def scatter():
        return dict(tx=blocks(TO, D), rx=vm((3, TO, D), BF16), mid=vm((TO, D), BF16))

    def stream(*shape):
        return dict(src=vm((n,) + shape, BF16), rx=vm((n - 1,) + shape, BF16), sem=dma(levels))

    scratch = dict(
        w_qkv=vm((D, 3 * QC), BF16),
        w_joint=vm((J, D), BF16),
        w_mix=vm((2, D, C), BF16),
        w_gu=vm((2, D, F), BF16),
        down=vm((D, F), BF16),
        grad=vm((T, D), BF16),
        load=tuple(pltpu.SemaphoreType.DMA for _ in range(8)),
        taps8=vm((8, LANES), F32),
        taps_st=vm((2, NW, LANES), F32),
        codes=vm((n, 1, T), jnp.int32),
        halo_rx=vm((HALO, D), BF16),
        st_all=vm((2, N, D), BF16),
        taps_all=vm((2, N, LANES), F32),
        kv_all=vm((n, T, LANES), BF16),
        normed=vm((T + HALO, D), BF16),
        inv1=vm((T, 1), F32),
        q2=vm((2 * T, LANES), BF16),
        z=vm((T, C), F32),
        ext_f=vm((T + HALO, C), F32),
        ext_s=vm((T + HALO, N), F32),
        ext_o=vm((T + HALO, 2 * NW), F32),
        grad_f=vm((T + HALO, C), F32),
        grad_o=vm((T + HALO, 2 * NW), F32),
        wr=vm((2, T, N), F32),
        tail_e=vm((T, C), F32),
        reach_e=vm((T, C), F32),
        ssd=vm((T, C), F32),
        w_tot=vm((T, C), F32),
        d_z=vm((T, C), BF16),
        jall_all=vm((ns, T, J), BF16),
        window=vm((C, N), F32),
        window_thr=vm((8, LANES), F32),
        m_acc=vm((2 * T, 1), F32),
        l_acc=vm((2 * T, 1), F32),
        o_acc=vm((2 * T, LANES), F32),
        dout2=vm((2 * T, LANES), BF16),
        dq2=vm((2 * T, LANES), F32),
        dkv_rx=vm((n, T, LANES), BF16),
        dkv_sum=vm((T, LANES), F32),
        pair_tx=vm((T, LANES), BF16),
        pair_rx=vm((T, LANES), BF16),
        back_tx=vm((HALO, D), BF16),
        back_rx=vm((HALO, D), BF16),
        dwr_tx=vm((2, N, T), BF16),
        dwr_rx=vm((ns - 1, 2, NW, T), BF16),
        small_tx=vm((SMALL, LANES), F32),
        small_rx=vm((n, SMALL, LANES), F32),
        halo=dma(1),
        st=dma(ns - 1),
        taps=dma(ns - 1),
        kv=dma(n - 1),
        dkv=dma(n - 1),
        jall=dma(ns - 1),
        pair=dma(1),
        back=dma(1),
        dwr=dma(ns - 1),
        small=dma(n - 1),
        sm_all=vm((ns, SMALL, LANES), F32),
        fc=scan(),
        bc=scan(),
        sq=rows(),
        dot=rows(),
        rs1=scatter(),
        rs2=scatter(),
        rs1_sem=dma(2),
        rs2_sem=dma(2),
        rs3_sem=dma(2),
        rs4_sem=dma(2),
        ag1_all=blocks(TO, D),
        ag2_all=blocks(TO, D),
        gz_all=blocks(R, C),
        gi_all=blocks(R, C),
        gr_all=blocks(R, 3 * LANES),
        gj_all=blocks(RJ, D // ns),
        ag1_sem=dma(3),
        ag2_sem=dma(3),
        ag3_sem=dma(3),
        ag4_sem=dma(3),
        gz_sem=dma(3),
        gi_sem=dma(3),
        gr_sem=dma(3),
        gj_sem=dma(3),
        sm_sem=dma(3),
        w_gu_g=stream(R, 2 * F),
        down_g=stream(R, F),
        z_g=stream(R, C),
        inner_g=stream(R, C),
        rest_g=stream(R, 3 * LANES),
        joint_g=stream(RJ, D // ns),
    )
    whole = pl.BlockSpec(memory_space=pltpu.VMEM)
    small = pl.BlockSpec(memory_space=pltpu.SMEM)
    far = pl.BlockSpec(memory_space=pl.ANY)
    specs = {key: whole for key in arrays}
    specs.update(doc_starts=small, step_bias=small, decay_rate=small, skip_gain=small)
    specs.update(w_att=far, joint=far, g=far, w_mix_in=far, w_gu_in=far, down_in=far)
    flat = [jax.tree.flatten(group) for group in (arrays, outs, scratch)]
    got = pl.pallas_call(
        functools.partial(layer_kernel, n, ns, [tree for _, tree in flat]),
        out_shape=flat[1][0],
        in_specs=jax.tree.flatten(specs)[0],
        out_specs=[whole] * len(outs),
        scratch_shapes=flat[2][0],
        name="layer",
        compiler_params=pltpu.CompilerParams(
            collective_id=1, has_side_effects=True, vmem_limit_bytes=VMEM_LIMIT
        ),
    )(*flat[0][0])
    return types.SimpleNamespace(**jax.tree.unflatten(flat[1][1], got))


def local(
    layer_input,
    out_grad,
    doc_starts,
    real_mask,
    norm_gain,
    attention_input_rows,
    mixer_in,
    state_in,
    step_in,
    conv_mixer,
    conv_state,
    step_bias,
    decay_rate,
    skip_gain,
    gated_gain,
    joint_out,
    mlp_gain,
    gate_up,
    down_weight,
):
    T, D = layer_input.shape
    NS, n = lax.axis_size(STATE), lax.axis_size(SEQ)
    t, s = lax.axis_index(STATE), lax.axis_index(SEQ)
    HL = NH // NS
    C = HL * HDM
    DM = NH * HDM
    NW = state_in.shape[2]
    F = gate_up.shape[2]
    w_mix = jnp.transpose(lax.dynamic_slice_in_dim(mixer_in, C * t, C, 2), (1, 0, 2))
    o = layer(
        n,
        NS,
        dict(
            x=layer_input,
            g=out_grad,
            w_att=attention_input_rows,
            w_mix_in=w_mix,
            w_step=step_in.T,
            st_own=jnp.transpose(state_in, (1, 2, 0)),
            conv_state=conv_state.reshape(KC, 2 * NW),
            conv_mixer=conv_mixer,
            ngain=norm_gain[None, :],
            ggain=gated_gain[None, :],
            mgain=mlp_gain[None, :],
            joint=joint_out,
            w_gu_in=jnp.transpose(gate_up, (1, 0, 2)),
            down_in=down_weight,
            real=real_mask.reshape(-1, LANES),
            step_bias=step_bias,
            decay_rate=decay_rate,
            skip_gain=skip_gain,
            doc_starts=doc_starts,
        ),
    )
    R = D // n
    f = lambda v: v.astype(F32)
    take = lambda v, count: lax.dynamic_slice_in_dim(v.reshape(-1), s * count, count, 0)
    per = C // LANES
    small = o.o_small
    taps = small[:, 6 : 6 + KC * per].reshape(NS, KC, C).transpose(1, 0, 2).reshape(KC, DM)
    row_st = 6 + KC * per
    taps_st = lax.dynamic_index_in_dim(small, t, 0, False)[row_st : row_st + KC, : 2 * NW]
    return (
        o.layer_output,
        f(o.input_grad),
        take(o.o_gains[:8], R),
        f(o.o_att),
        f(o.o_mix.transpose(1, 0, 2)),
        f(o.o_st[:, HEAD_SIZE:]).reshape(R, 2, NW),
        o.o_step,
        taps,
        taps_st.reshape(KC, 2, NW),
        small[:, 5, :HL].reshape(-1),
        small[:, 4, :HL].reshape(-1),
        small[:, 3, :HL].reshape(-1),
        take(small[:, :3], DM // n),
        f(o.o_joint),
        take(o.o_gains[8:], R),
        f(o.o_gu).reshape(R, 2, F),
        f(o.o_down),
    )


def solution(mesh):
    rep = P()
    in_specs = (
        P(SEQ, None),
        P(SEQ, None),
        rep,
        rep,
        rep,
        rep,
        rep,
        P(None, None, STATE),
        rep,
        rep,
        P(None, None, STATE),
        rep,
        rep,
        rep,
        rep,
        rep,
        rep,
        P(None, None, STATE),
        P(None, STATE),
    )
    out_specs = (
        P(SEQ, None),
        P(SEQ, None),
        P(SEQ),
        P(SEQ, None),
        P(SEQ, None, None),
        P(SEQ, None, STATE),
        P(SEQ, None),
        rep,
        P(None, None, STATE),
        rep,
        rep,
        rep,
        P(SEQ),
        P(SEQ, None),
        P(SEQ),
        P(SEQ, None, STATE),
        P(SEQ, STATE),
    )
    return jax.shard_map(local, mesh=mesh, in_specs=in_specs, out_specs=out_specs, check_vma=False)
```

```python
import functools
import math
import types

import jax
import jax.numpy as jnp
from jax import lax
from jax.experimental import pallas as pl
from jax.experimental.pallas import tpu as pltpu
from jax.sharding import PartitionSpec as P

QUERY_HEADS = 8
KEY_VALUE_HEADS = 2
HEAD_SIZE = 64
NH = 24
HDM = 64
KC = 4
EPSILON = 1e-05
ROPE_BASE = 10000.0
HI = lax.Precision.HIGHEST
F32 = jnp.float32
BF16 = jnp.bfloat16
LANES = 128
HALO = 16
FAR = -1e30
MESH = pl.DeviceIdType.MESH
SEQ, STATE = "seq", "state"
VMEM_LIMIT = 62 << 20


def nn(a, b, p=None):
    return lax.dot_general(a, b, (((1,), (0,)), ((), ())), precision=p, preferred_element_type=F32)


def nt(a, b, p=None):
    return lax.dot_general(a, b, (((1,), (1,)), ((), ())), precision=p, preferred_element_type=F32)


def tn(a, b, p=None):
    return lax.dot_general(a, b, (((0,), (0,)), ((), ())), precision=p, preferred_element_type=F32)


def sigmoid(v):
    return 1.0 / (1.0 + jnp.exp(-v))


def silu(v):
    return v * sigmoid(v)


def silu_slope(v):
    s = sigmoid(v)
    return s * (1.0 + v * (1.0 - s))


def softplus(v):
    return jnp.maximum(v, 0.0) + jnp.log1p(jnp.exp(-jnp.abs(v)))


def iota(shape, dim):
    return lax.broadcasted_iota(jnp.int32, shape, dim)


def doc_of(starts, pos):
    found = jnp.full(pos.shape, -1, jnp.int32)
    for start in starts:
        found = found + (pos >= start).astype(jnp.int32)
    return found


def roll(v, shift):
    return pltpu.roll(v, shift, 1)


def rope(v, cosine, sine, direction):
    first = (iota(v.shape, 1) % HEAD_SIZE) < HEAD_SIZE // 2
    half = HEAD_SIZE // 2
    partner = jnp.where(first, -roll(v, v.shape[1] - half), roll(v, half))
    return v * cosine + partner * (direction * sine)


def expander(width):
    return (iota((LANES, width), 1) // HDM == iota((LANES, width), 0)).astype(F32)


def masks_of(starts, first_row, rows):
    pos = first_row + iota((rows, 1), 0)
    doc = doc_of(starts, pos)
    masks = [(doc_of(starts, pos - (KC - 1 - k)) == doc).astype(F32) for k in range(KC)]
    return doc, masks


def push(src, dst, send_sem, recv_sem, device):
    copy = pltpu.make_async_remote_copy(
        src_ref=src,
        dst_ref=dst,
        send_sem=send_sem,
        recv_sem=recv_sem,
        device_id=device,
        device_id_type=MESH,
    )
    copy.start()
    return copy


def greet(n, ns, s, t):
    barrier = pltpu.get_barrier_semaphore()

    def seq_turn(k, carried):
        pl.semaphore_signal(barrier, inc=1, device_id={SEQ: lax.rem(s + k, n)}, device_id_type=MESH)
        return carried

    lax.fori_loop(1, n, seq_turn, 0)
    for k in range(1, ns):
        pl.semaphore_signal(
            barrier, inc=1, device_id={STATE: lax.rem(t + k, ns)}, device_id_type=MESH
        )
    return lambda: pl.semaphore_wait(barrier, n - 1 + ns - 1)


def conv_ref(ext_ref, taps, masks, rows):
    total = 0.0
    for k in range(KC):
        at = HALO - KC + 1 + k
        total = total + ext_ref[at : at + rows, :] * taps[k : k + 1] * masks[k]
    return total


class Carry:
    def __init__(self, refs, window, n, s, direction, rows_e):
        self.n, self.s, self.direction, self.rows_e = n, s, direction, rows_e
        self.tx, self.rx, self.thr_tx, self.thr_rx = refs.tx, refs.rx, refs.thr_tx, refs.thr_rx
        self.send, self.recv = refs.sem
        self.thr_send, self.thr_recv = refs.thr_sem
        self.total, self.thr = window
        self.count = carry_steps(n)

    def place(self, slot):
        return (1, 0) if slot == 0 else (2, 0) if slot == 1 else (1 << (slot - 1), slot - 1)

    def copies(self, slot, d, source):
        to = lax.rem(self.s + self.direction * d + self.n, self.n)
        make = lambda src, dst, a, b: pltpu.make_async_remote_copy(
            src_ref=src,
            dst_ref=dst,
            send_sem=a,
            recv_sem=b,
            device_id={SEQ: to},
            device_id_type=MESH,
        )
        return (
            make(self.tx.at[source], self.rx.at[slot], self.send.at[slot], self.recv.at[slot]),
            make(
                self.thr_tx.at[source],
                self.thr_rx.at[slot],
                self.thr_send.at[slot],
                self.thr_recv.at[slot],
            ),
        )

    def inside(self, index):
        return (index >= 0) & (index < self.n)

    def start(self, slot, d, source):
        @pl.when(self.inside(self.s + self.direction * d))
        def _():
            for copy in self.copies(slot, d, source):
                copy.start()

    def finish(self):
        for slot in range(self.count):
            d, source = self.place(slot)

            @pl.when(self.inside(self.s + self.direction * d))
            def _():
                for copy in self.copies(slot, d, source):
                    copy.wait_send()

    def begin(self, part, thr):
        self.tx[0] = part.astype(BF16)
        self.thr_tx[0] = thr
        self.total[...] = jnp.zeros(self.total.shape, F32)
        self.thr[...] = jnp.ones(self.thr.shape, F32)
        for slot in range(min(2, self.count)):
            self.start(slot, *self.place(slot))

    def join(self, slot, d, source):
        @pl.when(self.inside(self.s - self.direction * d))
        def _():
            for copy in self.copies(slot, d, source):
                copy.wait_recv()
            column = nt(self.rows_e, self.thr[...], HI)[:, :1]
            self.total[...] += column * self.rx[slot].astype(F32)
            self.thr[...] = self.thr[...] * self.thr_rx[slot]

        @pl.when(jnp.logical_not(self.inside(self.s - self.direction * d)))
        def _():
            self.thr[...] = jnp.zeros(self.thr.shape, F32)

    def pass_on(self, slot, d):
        self.tx[slot - 1] = self.total[...].astype(BF16)
        self.thr_tx[slot - 1] = self.thr[...]
        self.start(slot, d, slot - 1)

    def advance(self, slot):
        self.join(slot, *self.place(slot))
        if 1 <= slot < self.count - 1:
            self.pass_on(slot + 1, 1 << slot)

    def rest(self, first):
        if first >= self.count:
            return
        for slot in range(first, min(2, self.count)):
            self.advance(slot)
        first = max(first, 2)

        def turn(slot, d):
            self.join(slot, d, slot - 1)
            self.pass_on(slot + 1, 2 * d)
            return 2 * d

        if first < self.count:
            lax.fori_loop(first, self.count - 1, turn, 1 << (first - 1))
            self.join(self.count - 1, 1 << (self.count - 2), self.count - 2)


def carry_steps(n):
    return 1 if n <= 2 else 1 + (n - 2).bit_length()


def expand_rows(width):
    return (iota((width, LANES), 0) // HDM == iota((width, LANES), 1)).astype(F32)


def link_of(linked, cum, cum_t, h):
    return jnp.exp(jnp.where(linked, cum[:, h : h + 1] - cum_t[h : h + 1, :], FAR))


def send_to(sems, k, src, dst, device):
    send, recv = sems
    return push(src, dst, send.at[k], recv.at[k], device)


def row_sums(values):
    return nt(jnp.ones((8, values.shape[1]), F32), values, HI)


def as_column(row):
    first = (iota((8, LANES), 0) == 0).astype(F32)
    return tn(row, first, HI)[:, :1]


def share_rows(refs, ns, t, row):
    tx, rx = refs.tx, refs.rx
    tx[...] = row
    copies = [
        send_to(refs.sem, k - 1, tx, rx.at[k - 1], {STATE: lax.rem(t + k, ns)})
        for k in range(1, ns)
    ]

    def wait():
        total = tx[...]
        for k in range(1, ns):
            copies[k - 1].wait_recv()
            total = total + rx[k - 1]
        return total

    return copies, wait


class RowScatter:
    def __init__(self, refs, sem, t):
        self.sem, self.t = sem, t
        self.tx, self.rx, self.mid = refs.tx, refs.rx, refs.mid
        self.odd, self.far = lax.rem(t, 2), t // 2
        self.copies = []

    def start(self, part):
        rows = self.tx.shape[1]
        part = part.astype(BF16)
        for k in range(4):
            self.tx[(k % 2) * 2 + k // 2] = part[rows * k : rows * (k + 1)]
        theirs = self.tx.at[pl.ds(2 - 2 * self.odd, 2)]
        self.copies.append(
            send_to(self.sem, 0, theirs, self.rx.at[pl.ds(0, 2)], {STATE: sibling(self.t)})
        )

    def middle(self):
        self.copies[0].wait_recv()
        away = 1 - self.far
        self.mid[...] = (
            self.tx[2 * self.odd + away].astype(F32) + self.rx[away].astype(F32)
        ).astype(BF16)
        self.copies.append(
            send_to(self.sem, 1, self.mid, self.rx.at[2], {STATE: lax.rem(self.t + 2, 4)})
        )

    def finish(self):
        total = self.tx[2 * self.odd + self.far].astype(F32) + self.rx[self.far].astype(F32)
        self.copies[1].wait_recv()
        return total + self.rx[2].astype(F32)


class Gather:
    def __init__(self, block, sem, t):
        self.block, self.sem, self.t = block, sem, t
        own = block(t)
        self.copies = [
            send_to(sem, 0, own, own, {STATE: sibling(t)}),
            send_to(sem, 1, own, own, {STATE: lax.rem(t + 2, 4)}),
        ]

    def middle(self):
        self.copies[1].wait_recv()
        block = self.block(lax.rem(self.t + 2, 4))
        self.copies.append(send_to(self.sem, 2, block, block, {STATE: sibling(self.t)}))

    def finish(self):
        self.copies[0].wait_recv()
        self.copies[2].wait_recv()


def gather(every, sem, t, own):
    every[t] = own
    return Gather(lambda index: every.at[index], sem, t)


def sibling(t):
    return t + 1 - 2 * lax.rem(t, 2)


def levels_of(n):
    return n.bit_length() - 1


def bits_of(n, swapped):
    order = list(range(levels_of(n)))
    if swapped and len(order) > 1:
        order[0], order[1] = order[1], order[0]
    return order


class HalvingSum:
    def __init__(self, refs, n, s, swapped=False):
        self.sem, self.n, self.s = refs.sem, n, s
        self.bits = bits_of(n, swapped)
        self.src, self.rx = refs.src, refs.rx
        self.copies = []

    def owner(self, p):
        top = len(self.bits) - 1
        return sum(((p >> (top - level)) & 1) << bit for level, bit in enumerate(self.bits))

    def block_of(self, index):
        top = len(self.bits) - 1
        return sum(((index >> bit) & 1) << (top - level) for level, bit in enumerate(self.bits))

    def fill(self, column, values):
        rows = self.src.shape[1]
        width = values.shape[1]
        for p in range(self.n):
            at = rows * self.owner(p)
            self.src[p, :, column : column + width] = values[at : at + rows]

    def parts(self, level):
        half = self.n >> (level + 1)
        mine = lax.rem(self.s // (1 << self.bits[level]), 2)
        if level == 0:
            return self.src, 0, half, mine
        return self.rx, self.n - (self.n >> (level - 1)), half, mine

    def start(self, level=0):
        buffer, base, half, mine = self.parts(level)
        to = self.s + (1 - 2 * mine) * (1 << self.bits[level])
        here = self.n - (self.n >> level)
        self.copies.append(
            send_to(
                self.sem,
                level,
                buffer.at[pl.ds(base + (1 - mine) * half, half)],
                self.rx.at[pl.ds(here, half)],
                {SEQ: to},
            )
        )

    def step(self, level):
        buffer, base, half, mine = self.parts(level)
        self.copies[level].wait_recv()
        here = self.n - (self.n >> level)

        def turn(i, carried):
            kept = buffer[base + mine * half + i].astype(F32)
            self.rx[here + i] = (kept + self.rx[here + i].astype(F32)).astype(BF16)
            return carried

        lax.fori_loop(0, half, turn, 0)
        if level + 1 < len(self.bits):
            self.start(level + 1)

    def result(self):
        return self.rx[self.n - 2]


def named(value):
    if isinstance(value, dict):
        return types.SimpleNamespace(**{key: named(item) for key, item in value.items()})
    return value


def layer_kernel(n, ns, trees, *flat):
    refs, at = types.SimpleNamespace(), 0
    for tree in trees:
        part = jax.tree.unflatten(tree, flat[at : at + tree.num_leaves])
        at += tree.num_leaves
        refs.__dict__.update(named(part).__dict__)
    x, normed, inv1 = refs.x, refs.normed, refs.inv1
    w_mix, w_qkv, w_joint, w_gu, down = refs.w_mix, refs.w_qkv, refs.w_joint, refs.w_gu, refs.down
    grad = refs.grad
    w_step = refs.w_step
    T, D = x.shape
    t, s = lax.axis_index(STATE), lax.axis_index(SEQ)
    joined = refs.jall_all.at[t]
    C = w_mix.shape[2]
    QC = 2 * HEAD_SIZE
    AQ = QUERY_HEADS * HEAD_SIZE
    NW = refs.st_own.shape[1]
    HL = NH // ns
    N = NW * ns
    TO = T // ns
    DM = C * ns
    F = down.shape[1]
    pairs = C // LANES
    scale = 1.0 / math.sqrt(HEAD_SIZE)
    state_peer = lambda k: {STATE: lax.rem(t + k, ns)}
    own_c = pl.ds(pl.multiple_of(C * t, LANES), C)
    loads = [
        pltpu.make_async_copy(src, dst, refs.load[k])
        for k, (src, dst) in enumerate(
            [
                (refs.w_att.at[:, pl.ds(pl.multiple_of(QC * t, LANES), QC)], w_qkv.at[:, pl.ds(0, QC)]),
                (refs.w_att.at[:, pl.ds(AQ, 2 * QC)], w_qkv.at[:, pl.ds(QC, 2 * QC)]),
                (refs.w_mix_in, w_mix),
                (refs.joint.at[pl.ds(pl.multiple_of(QC * t, QC), QC)], w_joint.at[pl.ds(0, QC)]),
                (refs.joint.at[pl.ds(pl.multiple_of(AQ + C * t, LANES), C)], w_joint.at[pl.ds(QC, C)]),
                (refs.g, grad),
                (refs.down_in, down),
                (refs.w_gu_in, w_gu),
            ]
        )
    ]
    for load in loads:
        load.start()
    lanes_row = iota((1, LANES), 1)
    blank = jnp.zeros((1, LANES), F32)
    met = greet(n, ns, s, t)
    bias_row, rate_row = blank, blank
    skip_row = jnp.zeros((1, C), F32)
    heads_row = iota((1, C), 1) // HDM
    for h in range(HL):
        bias_row = jnp.where(lanes_row == h, refs.step_bias[HL * t + h], bias_row)
        rate_row = jnp.where(lanes_row == h, refs.decay_rate[HL * t + h], rate_row)
        skip_row = jnp.where(heads_row == h, refs.skip_gain[HL * t + h], skip_row)
    taps_mix = refs.conv_mixer[:, own_c]
    ggain_row = refs.ggain[:, own_c]
    pick = (iota((NH, LANES), 0) == HL * t + iota((NH, LANES), 1)) & (iota((NH, LANES), 1) < HL)
    pick = pick.astype(F32)
    refs.taps8[...] = jnp.zeros(refs.taps8.shape, F32)
    refs.taps8[:KC, : 2 * NW] = refs.conv_state[...]
    eye8 = (iota((8, LANES), 0) == iota((8, LANES), 1)).astype(F32)
    taps_cols = tn(refs.taps8[...], eye8, HI)
    for c in range(2):
        refs.taps_st[c] = taps_cols[NW * c : NW * (c + 1)]
    sent = []
    mine = pl.ds(pl.multiple_of(NW * t, NW), NW)
    refs.st_all[:, mine, :] = refs.st_own[...]
    refs.taps_all[:, mine, :] = refs.taps_st[...]

    first_row = s * T
    starts = [refs.doc_starts[k] for k in range(refs.doc_starts.shape[0])]
    doc, masks = masks_of(starts, first_row, T)
    tiles = T // LANES

    def code_turn(j, carried):
        for i in range(tiles):
            real = refs.real[pl.ds(tiles * j + i, 1), :]
            ids = doc_of(starts, j * T + i * LANES + iota((1, LANES), 1))
            refs.codes[pl.ds(tiles * j + i, 1), :] = jnp.where(real > 0, ids, -7)
        return carried

    lax.fori_loop(0, n, code_turn, 0)

    def code_of(j):
        return jnp.concatenate([refs.codes[pl.ds(tiles * j + i, 1), :] for i in range(tiles)], axis=1)

    real_col = as_column(jnp.broadcast_to((code_of(s) >= 0).astype(F32), (8, T)))
    firsts = jnp.zeros((T, 1), jnp.int32)
    places = first_row + iota((T, 1), 0)
    for start in starts:
        firsts = jnp.where(places >= start, start, firsts)
    powers = (iota((1, LANES), 1) % (HEAD_SIZE // 2)).astype(F32) * (2.0 / HEAD_SIZE)
    angles = (places - firsts).astype(F32) * jnp.exp(-math.log(ROPE_BASE) * powers)
    cosine, sine = jnp.cos(angles), jnp.sin(angles)
    doc_row = doc_of(starts, first_row + iota((1, T), 1))
    lane = iota((T, LANES), 1)
    low = lane < HEAD_SIZE
    ngain = refs.ngain[...]

    met()
    halo_copy = pltpu.make_async_remote_copy(
        src_ref=x.at[pl.ds(T - HALO, HALO)],
        dst_ref=refs.halo_rx,
        send_sem=refs.halo[0].at[0],
        recv_sem=refs.halo[1].at[0],
        device_id={SEQ: lax.rem(s + 1, n)},
        device_id_type=MESH,
    )

    @pl.when(s + 1 < n)
    def _():
        halo_copy.start()

    columns = lambda every: lambda i: every.at[:, pl.ds(pl.multiple_of(NW * i, NW), NW), :]
    st_gather = Gather(columns(refs.st_all), refs.st, t)
    taps_gather = Gather(columns(refs.taps_all), refs.taps, t)
    xf = x[...].astype(F32)
    inv = lax.rsqrt(jnp.mean(xf * xf, axis=1, keepdims=True) + EPSILON)
    inv1[...] = inv
    normed[HALO:, :] = (xf * inv * ngain).astype(BF16)
    main = normed[HALO:, :]
    loads[0].wait()
    loads[1].wait()
    qkv = nn(main, w_qkv[...])
    q = (rope(qkv[:, :QC], cosine, sine, 1.0).astype(BF16) * scale).astype(F32)
    kcos, ksin = jnp.where(low, cosine, 1.0), jnp.where(low, sine, 0.0)
    kv_all = refs.kv_all
    group = t // 2
    both_k, both_v = qkv[:, QC : 2 * QC], qkv[:, 2 * QC :]
    own_kv = jnp.where(
        low,
        jnp.where(group == 0, both_k, roll(both_k, HEAD_SIZE)),
        jnp.where(group == 0, roll(both_v, HEAD_SIZE), both_v),
    )
    kv_all[s] = rope(own_kv, kcos, ksin, 1.0).astype(BF16)

    core = lax.rem(t, 2)
    H2 = T // 2
    own_half = pl.ds(pl.multiple_of(H2 * core, H2), H2)
    other_half = pl.ds(pl.multiple_of(H2 * (1 - core), H2), H2)

    def kv_copy(k):
        return pltpu.make_async_remote_copy(
            src_ref=kv_all.at[s, own_half],
            dst_ref=kv_all.at[s, own_half],
            send_sem=refs.kv[0].at[k - 1],
            recv_sem=refs.kv[1].at[k - 1],
            device_id={SEQ: lax.rem(s + k, n)},
            device_id_type=MESH,
        )

    def kv_pair(k):
        block = kv_all.at[s - k, own_half]
        return pltpu.make_async_remote_copy(
            src_ref=block,
            dst_ref=block,
            send_sem=refs.kv_fwd[0].at[k - 1],
            recv_sem=refs.kv_fwd[1].at[k - 1],
            device_id={STATE: sibling(t)},
            device_id_type=MESH,
        )

    def kv_turn(k, carried):
        kv_copy(k).start()
        return carried

    lax.fori_loop(1, n - s, kv_turn, 0)
    refs.q2[:T, :] = jnp.where(low, q, 0.0).astype(BF16)
    refs.q2[T:, :] = jnp.where(low, roll(q, HEAD_SIZE), 0.0).astype(BF16)
    loads[2].wait()
    refs.z[...] = nn(main, w_mix[0])
    raw = nn(nt(main, w_step[...]), pick, HI) + bias_row

    doc2 = jnp.concatenate([doc, doc], axis=0)
    m_ref, l_ref, acc_ref = refs.m_acc, refs.l_acc, refs.o_acc
    m_ref[...] = jnp.full(m_ref.shape, FAR, F32)
    l_ref[...] = jnp.zeros(l_ref.shape, F32)
    acc_ref[...] = jnp.zeros(acc_ref.shape, F32)

    def allowed_at(j, diagonal):
        allowed = code_of(j) == doc2
        if diagonal:
            rows2 = jnp.concatenate([iota((T, T), 0)] * 2, axis=0)
            cols2 = iota((2 * T, T), 1)
            allowed = (allowed & (cols2 <= rows2)) | (cols2 == rows2)
        return allowed

    def attend(j, diagonal):
        block = kv_all[j]
        scores = jnp.where(allowed_at(j, diagonal), nt(refs.q2[...], block), FAR)
        m = m_ref[...]
        m_new = jnp.maximum(m, jnp.max(scores, axis=1, keepdims=True))
        shrink = jnp.exp(m - m_new)
        p = jnp.exp(scores - m_new)
        l_ref[...] = l_ref[...] * shrink + jnp.sum(p, axis=1, keepdims=True)
        acc_ref[...] = acc_ref[...] * shrink + nn(p.astype(BF16), block)
        m_ref[...] = m_new

    def attend_turn(k, carried):
        @pl.when(k < s)
        def _():
            kv_copy(k + 1).wait_recv()
            kv_pair(k + 1).start()

        kv_pair(k).wait_recv()
        attend(s - k, False)
        return carried

    def attend_some(first, stop):
        lax.fori_loop(first, stop, attend_turn, 0)

    cut1, cut2 = 1 + (s + 1) // 3, 1 + (2 * s + 1) // 3
    attend(s, True)
    taps_gather.middle()
    st_gather.middle()

    @pl.when(s > 0)
    def _():
        halo_copy.wait_recv()

    @pl.when(s == 0)
    def _():
        refs.halo_rx[...] = jnp.zeros(refs.halo_rx.shape, BF16)

    hf = refs.halo_rx[...].astype(F32)
    inv_h = lax.rsqrt(jnp.mean(hf * hf, axis=1, keepdims=True) + EPSILON)
    normed[:HALO, :] = (hf * inv_h * ngain).astype(BF16)
    ext_f, ext_s, ext_o = refs.ext_f, refs.ext_s, refs.ext_o
    ext_f[...] = nn(normed[...], w_mix[1]).astype(BF16).astype(F32)
    inner_lin = conv_ref(ext_f, taps_mix, masks, T)
    inner = silu(inner_lin)
    taps_gather.finish()
    st_gather.finish()
    for c in range(2):
        ext_s[...] = nt(normed[...], refs.st_all[c]).astype(BF16).astype(F32)
        taps = refs.taps_all[c].T
        refs.wr[c] = silu(conv_ref(ext_s, taps, masks, T))
    write, read = refs.wr[0], refs.wr[1]
    step = softplus(raw)
    causal = iota((T, T), 0) >= iota((T, T), 1)
    tri = causal.astype(F32)
    cum = nn(tri, -step * rate_row, HI)
    cum_t = cum.T
    linked = (doc == doc_row) & causal
    E = expander(C)
    rows_e = expand_rows(C)
    inflow = step * real_col
    inflow_e = nn(inflow, E, HI)
    in_x = inner * inflow_e
    cum_last = cum[T - 1 : T]
    last = first_row + T - 1
    doc_last = doc_of(starts, jnp.full((T, 1), last, jnp.int32))
    prior = doc_of(starts, jnp.full((T, 1), first_row - 1, jnp.int32))
    tail = jnp.where(doc == doc_last, jnp.exp(cum_last - cum), 0.0)
    refs.tail_e[...] = nn(tail, E, HI)
    state_part = tn(refs.tail_e[...] * in_x, write, HI)
    alive = (doc == prior).astype(F32)
    alive_last = (doc_last == prior).astype(F32)[:8]
    thr = alive_last * jnp.exp(jnp.broadcast_to(cum_last, (8, LANES)))
    steps = carry_steps(n)

    carry = Carry(refs.fc, (refs.window, refs.window_thr), n, s, 1, rows_e)
    carry.begin(state_part, thr)

    g_mat = nt(read, write, HI)
    for p in range(pairs):
        cols = slice(LANES * p, LANES * (p + 1))
        ys = []
        for h in (2 * p, 2 * p + 1):
            link = link_of(linked, cum, cum_t, h)
            ys.append(nn(link * g_mat, in_x[:, cols], HI))
        refs.ssd[:, cols] = jnp.where(low, ys[0], ys[1])

    for slot in range(min(2, steps)):
        carry.advance(slot)

    @pl.when(s > 0)
    def _():
        kv_copy(1).wait_recv()
        kv_pair(1).start()

    attend_some(1, cut1)
    if steps > 2:
        carry.advance(2)
    attend_some(cut1, cut2)
    carry.rest(3)
    s_in = refs.window[...]
    refs.reach_e[...] = nn(alive * jnp.exp(cum), E, HI)
    ssd = refs.ssd[...] + refs.reach_e[...] * nt(read, s_in, HI)
    refs.ssd[...] = ssd
    z = refs.z[...]
    full_mix = ssd + skip_row * inner
    gated = full_mix * silu(z)
    copies, wait = share_rows(refs.sq, ns, t, row_sums(gated * gated))
    sent += copies
    attend_some(cut2, s + 1)
    out = acc_ref[...] / l_ref[...]
    acc_ref[...] = out
    m_ref[...] = m_ref[...] + jnp.log(l_ref[...])
    joined[:, :QC] = jnp.where(low, roll(out[:T], HEAD_SIZE), out[T:]).astype(BF16)
    loads[3].wait()
    loads[4].wait()
    loads[5].wait()
    loads[6].wait()
    dh = nn(grad[...], down[...])
    inv_g = as_column(lax.rsqrt(wait() / DM + EPSILON))
    joined[:, QC:] = (gated * inv_g * ggain_row).astype(BF16)
    rs1 = RowScatter(refs.rs1, refs.rs1_sem, t)
    rs1.start(nn(joined[...], w_joint[...]))
    own_rows = pl.ds(pl.multiple_of(TO * t, TO), TO)
    x_own = x[own_rows, :].astype(F32)
    rs1.middle()
    res = x_own + rs1.finish()
    inv2 = lax.rsqrt(jnp.mean(res * res, axis=1, keepdims=True) + EPSILON)
    mgain = refs.mgain[...]
    ag1 = gather(refs.ag1_all, refs.ag1_sem, t, (res * inv2 * mgain).astype(BF16))
    ag1.middle()
    jall = Gather(lambda index: refs.jall_all.at[index], refs.jall, t)
    ag1.finish()

    n2 = jnp.concatenate([refs.ag1_all[k] for k in range(ns)], axis=0)
    loads[7].wait()
    gate, up = nn(n2, w_gu[0]), nn(n2, w_gu[1])
    sig = sigmoid(gate)
    act = gate * sig
    hidden = (act * up).astype(BF16)
    d_gate = (dh * up * (sig * (1.0 + gate * (1.0 - sig)))).astype(BF16)
    d_up = (dh * act).astype(BF16)
    rs2 = RowScatter(refs.rs2, refs.rs2_sem, t)
    rs2.start(nt(d_gate, w_gu[0]) + nt(d_up, w_gu[1]))
    for copy in rs1.copies + ag1.copies:
        copy.wait_send()
    rs3 = RowScatter(refs.rs1, refs.rs3_sem, t)
    rs3.start(nt(hidden, down[...]))
    rs2.middle()

    def weight_sum(stream, parts, swapped=False):
        total = HalvingSum(stream, n, s, swapped)
        column = 0
        for lhs, rhs in parts:
            width = rhs.shape[1]
            for c in range(0, width, 256):
                piece = rhs[:, c : min(c + 256, width)]
                total.fill(column + c, tn(lhs, piece).astype(BF16))
            column += width
        return total

    sum_gate = weight_sum(refs.gate_g, [(n2, d_gate)], True)
    sum_gate.start()
    rs3.middle()
    sum_down = weight_sum(refs.down_g, [(grad[...], hidden)])
    sum_down.start()
    sum_up = weight_sum(refs.up_g, [(n2, d_up)])
    dn2 = rs2.finish()
    scaled = dn2 * mgain
    d_res = (
        grad[own_rows, :].astype(F32)
        + inv2 * scaled
        - res * inv2 * inv2 * inv2 * jnp.mean(scaled * res, axis=1, keepdims=True)
    )
    ag2 = gather(refs.ag2_all, refs.ag2_sem, t, d_res.astype(BF16))

    def put_small(row, values):
        for k in range(0, values.shape[1], LANES):
            piece = values[:, k : k + LANES]
            refs.small_tx[row : row + 1, : piece.shape[1]] = piece
            row += 1

    refs.small_tx[...] = jnp.zeros(refs.small_tx.shape, F32)
    refs.small_src[...] = jnp.zeros(refs.small_src.shape, F32)
    put_small(8, jnp.sum(dn2 * res * inv2, axis=0, keepdims=True))
    ag2.middle()
    ag3 = gather(refs.ag1_all, refs.ag3_sem, t, (res + rs3.finish()).astype(BF16))
    ag2.finish()
    d_branch = jnp.concatenate([refs.ag2_all[k] for k in range(ns)], axis=0)
    d_joined = nt(d_branch, w_joint[...])
    d_gn = d_joined[:, QC:]
    scaled = d_gn * ggain_row
    copies, wait = share_rows(refs.dot, ns, t, row_sums(scaled * gated))
    sent += copies
    put_small(16, jnp.sum(d_gn * gated * inv_g, axis=0, keepdims=True))
    d_att = d_joined[:, :QC].astype(BF16).astype(F32)
    dout2 = jnp.concatenate(
        [jnp.where(low, 0.0, roll(d_att, HEAD_SIZE)), jnp.where(low, 0.0, d_att)], axis=0
    )
    delta = jnp.sum(dout2 * acc_ref[...], axis=1, keepdims=True)
    l_ref[...] = delta
    refs.dout2[...] = dout2.astype(BF16)
    jall.middle()
    sum_down.step(0)
    sum_gate.step(0)
    jall.finish()
    own_d = pl.ds(pl.multiple_of((D // ns) * t, LANES), D // ns)
    d_cols = jnp.concatenate([refs.ag2_all[k, :, own_d] for k in range(ns)], axis=0)
    sum_joint = joint = HalvingSum(refs.joint_g, n, s)
    rows_j = joint.src.shape[1]
    piece = min(rows_j, LANES)
    for k in range(ns):
        values = tn(refs.jall_all[k], d_cols).astype(BF16)
        for at in range(0, QC + C, piece):
            row = QC * k + at if at < QC else AQ + C * k + at - QC
            offset = row % rows_j
            joint.src[joint.block_of(row // rows_j), offset : offset + piece, :] = values[at : at + piece]
    dot = as_column(wait() / DM)
    d_gated = inv_g * scaled - gated * (inv_g * inv_g * inv_g * dot)
    sig = sigmoid(z)
    dy = d_gated * z * sig
    refs.d_z[...] = (d_gated * full_mix * (sig * (1.0 + z * (1.0 - sig)))).astype(BF16)
    put_small(19, nt(jnp.broadcast_to(jnp.sum(dy * inner, axis=0, keepdims=True), (8, C)), E, HI)[:1])
    reach_dy = refs.reach_e[...] * dy
    carry_b = Carry(refs.bc, (refs.window, refs.window_thr), n, s, -1, rows_e)
    carry_b.begin(tn(reach_dy, read, HI), thr)
    sum_up.start()
    joint.start()
    sum_z = weight_sum(refs.z_g, [(main, refs.d_z[...])], True)
    ag3.middle()
    d_g = jnp.zeros((T, T), F32)
    for p in range(pairs):
        cols = slice(LANES * p, LANES * (p + 1))
        xp, dyp = in_x[:, cols], dy[:, cols]
        halves = []
        for k in range(2):
            link = link_of(linked, cum, cum_t, 2 * p + k)
            halves.append(tn(link * g_mat, dyp, HI))
            own = low if k == 0 else jnp.logical_not(low)
            d_g = d_g + link * nt(jnp.where(own, dyp, 0.0), xp, HI)
        refs.w_tot[:, cols] = jnp.where(low, halves[0], halves[1])

    refs.dq2[...] = jnp.zeros(refs.dq2.shape, F32)

    def attend_back(j, diagonal):
        block = kv_all[j]
        q2, dout2 = refs.q2[...], refs.dout2[...]
        scores = jnp.where(allowed_at(j, diagonal), nt(q2, block), FAR)
        p = jnp.exp(scores - m_ref[...])
        ds = (p * (nt(dout2, block) - l_ref[...])).astype(BF16)
        refs.dq2[...] += nn(ds, block)
        return tn(ds, q2) + tn(p.astype(BF16), dout2)

    def dkv_copy(k):
        return pltpu.make_async_remote_copy(
            src_ref=refs.dkv_mid.at[k - 1],
            dst_ref=refs.dkv_rx.at[k - 1],
            send_sem=refs.dkv[0].at[k - 1],
            recv_sem=refs.dkv[1].at[k - 1],
            device_id={SEQ: lax.rem(s - k + n, n)},
            device_id_type=MESH,
        )

    def dkv_pair(k):
        return pltpu.make_async_remote_copy(
            src_ref=kv_all.at[s - k, other_half],
            dst_ref=refs.dkv_mid.at[lax.rem(k + n - 1, n)],
            send_sem=refs.dkv_fwd[0].at[k],
            recv_sem=refs.dkv_fwd[1].at[k],
            device_id={STATE: sibling(t)},
            device_id_type=MESH,
        )

    def dkv_on(k):
        dkv_pair(k).wait_recv()
        both = refs.dkv_mid[k - 1].astype(F32) + kv_all[s - k, own_half].astype(F32)
        refs.dkv_mid[k - 1] = both.astype(BF16)
        dkv_copy(k).start()

    def back_turn(k, carried):
        kv_all[s - k] = attend_back(s - k, False).astype(BF16)
        dkv_pair(k).start()

        @pl.when(k > 1)
        def _():
            dkv_on(k - 1)

        return carried

    def back_some(first, stop):
        lax.fori_loop(first, stop, back_turn, 0)

    def kv_end(k, carried):
        kv_copy(k).wait_send()
        return carried

    def pair_end(k, carried):
        kv_pair(k).wait_send()
        return carried

    lax.fori_loop(1, n - s, kv_end, 0)
    lax.fori_loop(1, s + 1, pair_end, 0)
    for slot in range(min(2, steps)):
        carry_b.advance(slot)
    back_some(1, cut1)
    if steps > 2:
        carry_b.advance(2)
    back_some(cut1, cut2)
    carry_b.rest(3)
    sum_z.start()
    back_some(cut2, s + 1)
    diagonal = attend_back(s, True)
    refs.dkv_sum[...] = diagonal
    kv_all[s] = diagonal.astype(BF16)
    dkv_pair(0).start()

    @pl.when(s > 0)
    def _():
        dkv_on(s)

    ag3.finish()
    for k in range(ns):
        refs.layer_output[TO * k : TO * (k + 1), :] = refs.ag1_all[k]
    sum_down.step(1)
    sum_gate.step(1)
    sum_up.step(0)
    later = refs.window[...]
    tail_e = refs.tail_e[...]
    tail_r = tail_e * nt(write, later, HI)
    w_tot = refs.w_tot[...] + tail_r
    d_write = tn(d_g, read, HI) + nn(tail_e * in_x, later, HI)
    d_read = nn(d_g, write, HI) + nn(reach_dy, s_in, HI)
    refs.dwr_tx[0] = d_write.T.astype(BF16)
    refs.dwr_tx[1] = d_read.T.astype(BF16)
    dwr = []
    for k in range(1, ns):
        p = lax.rem(t + k, ns)
        theirs = pl.ds(pl.multiple_of(NW * p, NW), NW)
        dwr.append(
            send_to(refs.dwr, k - 1, refs.dwr_tx.at[:, theirs, :], refs.dwr_rx.at[k - 1], {STATE: p})
        )
    sent += dwr
    u = nt(inner * w_tot, E, HI)
    tl = nt(in_x * tail_r, E, HI)
    thr_s = jnp.sum(tn(later * s_in, rows_e, HI), axis=0, keepdims=True) * thr[:1]
    d_cum = nt(dy * ssd, E, HI) - inflow * u
    at_last = iota((T, LANES), 0) == T - 1
    d_cum = d_cum + jnp.where(at_last, jnp.sum(tl, axis=0, keepdims=True) + thr_s, 0.0)
    d_ld = tn(tri, d_cum, HI)
    d_step = real_col * u - rate_row * d_ld
    put_small(20, -jnp.sum(step * d_ld, axis=0, keepdims=True))
    d_step = d_step * sigmoid(raw)
    put_small(21, jnp.sum(d_step, axis=0, keepdims=True))
    d_step = d_step.astype(BF16)
    d_lin = (inflow_e * w_tot + skip_row * dy) * silu_slope(inner_lin)

    def conv_back(ext, grad, taps, up, row, rows):
        grad[...] = jnp.zeros(grad.shape, F32)
        for k in range(KC):
            at = HALO - KC + 1 + k
            masked = up * masks[k]
            put_small(row + rows * k, jnp.sum(masked * ext[at : at + T, :], axis=0, keepdims=True))
            grad[at : at + T, :] += masked * taps[k : k + 1]
        return grad[...].astype(BF16)

    d_ext = conv_back(ext_f, refs.grad_f, taps_mix, d_lin, 22, C // LANES)
    st64 = refs.st_own[...].reshape(2 * NW, D)
    taps_own = refs.taps_st[...].reshape(2 * NW, LANES).T
    ext_o[...] = nt(normed[...], st64).astype(BF16).astype(F32)
    slope_o = silu_slope(conv_ref(ext_o, taps_own, masks, T))
    for copy in dwr:
        copy.wait_recv()
    d_wr = refs.dwr_tx[:, mine, :].astype(F32)
    for k in range(1, ns):
        d_wr = d_wr + refs.dwr_rx[k - 1].astype(F32)
    row_st = 22 + KC * (C // LANES)
    d_st = conv_back(ext_o, refs.grad_o, taps_own, d_wr.reshape(2 * NW, T).T * slope_o, row_st, 1)
    refs.back_tx[...] = (nt(d_ext[:HALO], w_mix[1]) + nn(d_st[:HALO], st64)).astype(BF16)
    back = pltpu.make_async_remote_copy(
        src_ref=refs.back_tx,
        dst_ref=refs.back_rx,
        send_sem=refs.back[0].at[0],
        recv_sem=refs.back[1].at[0],
        device_id={SEQ: lax.rem(s + n - 1, n)},
        device_id_type=MESH,
    )

    @pl.when(s > 0)
    def _():
        back.start()

    sum_inner = weight_sum(refs.inner_g, [(normed[...], d_ext)])
    sum_inner.start()
    def dkv_turn(k, carried):
        dkv_copy(k).wait_recv()
        refs.dkv_half[...] += refs.dkv_rx[k - 1].astype(F32)
        return carried

    dkv_pair(0).wait_recv()
    refs.dkv_half[...] = refs.dkv_sum[own_half, :] + refs.dkv_mid[n - 1].astype(F32)
    lax.fori_loop(1, n - s, dkv_turn, 0)
    refs.pair_tx[...] = refs.dkv_half[...].astype(BF16)
    odd = core
    pair = send_to(refs.pair, 0, refs.pair_tx, refs.pair_rx, {STATE: sibling(t)})
    sent.append(pair)
    d_z = refs.d_z[...]
    dq2 = refs.dq2[...]
    dq = jnp.where(low, dq2[:T], roll(dq2[T:], HEAD_SIZE)) * scale
    d_q = rope(dq, cosine, sine, -1.0).astype(BF16)
    d_n = (
        nt(d_z, w_mix[0])
        + nt(d_ext[HALO:], w_mix[1])
        + nn(d_st[HALO:], st64)
        + nn(nt(d_step, pick.astype(BF16)).astype(BF16), w_step[...])
    )
    pair.wait_recv()
    refs.dkv_sum[own_half, :] = refs.pair_tx[...].astype(F32)
    refs.dkv_sum[other_half, :] = refs.pair_rx[...].astype(F32)
    d_kv = rope(refs.dkv_sum[...], kcos, ksin, -1.0)
    d_kv = jnp.where(low == (odd == 0), d_kv, 0.0)
    other = roll(d_kv, HEAD_SIZE)
    d_k = jnp.where(low, jnp.where(group == 0, d_kv, 0.0), jnp.where(group == 0, 0.0, other))
    d_v = jnp.where(low, jnp.where(group == 0, other, 0.0), jnp.where(group == 0, 0.0, d_kv))
    d_kv_b = d_kv.astype(BF16)
    d_qkv = jnp.concatenate([d_q, jnp.where(odd == 0, d_k, d_v).astype(BF16)], axis=1)
    mine_kv = jnp.where(odd == 0, d_kv, other).astype(BF16)
    pad_st = jnp.concatenate([jnp.zeros((T + HALO, HEAD_SIZE), F32), d_st.astype(F32)], axis=1)
    mine_kv = jnp.concatenate([jnp.zeros((HALO, LANES), F32), mine_kv.astype(F32)], axis=0)
    mixed = jnp.where(iota((T + HALO, LANES), 1) < HEAD_SIZE, mine_kv, pad_st).astype(BF16)
    sum_rest = weight_sum(refs.rest_g, [(main, d_q), (normed[...], mixed)])
    sum_rest.start()
    w_kv = jnp.where(odd == 0, w_qkv[:, QC : 2 * QC], w_qkv[:, 2 * QC :])
    d_n = d_n + nt(d_qkv, jnp.concatenate([w_qkv[:, :QC], w_kv], axis=1))
    @pl.when(s + 1 < n)
    def _():
        back.wait_recv()

    @pl.when(s + 1 == n)
    def _():
        refs.back_rx[...] = jnp.zeros(refs.back_rx.shape, BF16)

    tail_rows = d_n[T - HALO :] + refs.back_rx[...].astype(F32)
    d_n = jnp.concatenate([d_n[: T - HALO], tail_rows], axis=0)
    for copy in rs2.copies + ag3.copies:
        copy.wait_send()
    rs4 = RowScatter(refs.rs2, refs.rs4_sem, t)
    rs4.start(d_n)
    sum_joint.step(0)
    rs4.middle()
    sum_z.step(0)
    inv_own = inv1[own_rows, :]
    d_n = rs4.finish()
    scaled = d_n * ngain
    in_g = (
        d_res
        + inv_own * scaled
        - x_own * inv_own * inv_own * inv_own * jnp.mean(scaled * x_own, axis=1, keepdims=True)
    )
    ag4 = gather(refs.ag1_all, refs.ag4_sem, t, in_g.astype(BF16))
    put_small(0, jnp.sum(d_n * x_own * inv_own, axis=0, keepdims=True))

    def small_copy(k):
        return pltpu.make_async_remote_copy(
            src_ref=refs.small_src.at[lax.rem(s + k, n)],
            dst_ref=refs.small_rx.at[s],
            send_sem=refs.small[0].at[k - 1],
            recv_sem=refs.small[1].at[k - 1],
            device_id={SEQ: lax.rem(s + k, n)},
            device_id_type=MESH,
        )

    step_rows = tn(d_step, main)[:8]
    common = refs.small_tx[...]
    rows_c, rows_d = common.shape[0], D // n
    for k in range(n):
        refs.small_src[k, :rows_c, :] = common
        refs.small_src[k, rows_c:, :rows_d] = step_rows[:, rows_d * k : rows_d * (k + 1)]
    refs.small_rx[s] = refs.small_src[s]

    def small_turn(k, carried):
        small_copy(k).start()
        return carried

    lax.fori_loop(1, n, small_turn, 0)
    last_level = len(bits_of(n, False)) - 1

    def steps_of(total, first, stop):
        for level in range(first, stop):
            total.step(level)

    sum_up.step(1)
    ag4.middle()
    sum_inner.step(0)
    sum_joint.step(1)
    sum_z.step(1)
    sum_rest.step(0)
    steps_of(sum_down, 2, last_level + 1)
    steps_of(sum_gate, 2, last_level + 1)

    def small_end(k, carried):
        small_copy(k).wait_recv()
        return carried

    lax.fori_loop(1, n, small_end, 0)

    def small_sum(j, total):
        return total + refs.small_rx[j]

    small = gather(
        refs.sm_all, refs.sm_sem, t,
        lax.fori_loop(0, n, small_sum, jnp.zeros(refs.small_rx.shape[1:], F32)),
    )
    ag4.finish()
    for k in range(ns):
        refs.input_grad[TO * k : TO * (k + 1), :] = refs.ag1_all[k]
    sum_inner.step(1)
    sum_rest.step(1)
    small.middle()
    steps_of(sum_up, 2, last_level + 1)
    steps_of(sum_z, 2, last_level + 1)
    gz = gather(refs.gz_all, refs.gz_sem, t, sum_z.result())
    steps_of(sum_joint, 2, last_level + 1)
    gj = gather(refs.gj_all, refs.gj_sem, t, sum_joint.result())
    steps_of(sum_inner, 2, last_level + 1)
    gi = gather(refs.gi_all, refs.gi_sem, t, sum_inner.result())
    steps_of(sum_rest, 2, last_level + 1)
    gr = gather(refs.gr_all, refs.gr_sem, t, sum_rest.result())
    gz.middle()
    gj.middle()
    gi.middle()
    refs.o_gu[0] = sum_gate.result()
    refs.o_gu[1] = sum_up.result()
    refs.o_down[...] = sum_down.result()
    gz.finish()
    gj.finish()
    gi.finish()
    gr.middle()
    for k in range(ns):
        refs.o_mix[0, :, C * k : C * (k + 1)] = refs.gz_all[k]
        refs.o_mix[1, :, C * k : C * (k + 1)] = refs.gi_all[k]
        refs.o_joint[:, (D // ns) * k : (D // ns) * (k + 1)] = refs.gj_all[k]
    small.finish()
    total = refs.sm_all[0, :16, :]
    for k in range(1, ns):
        total = total + refs.sm_all[k, :16, :]
    refs.o_gains[...] = total
    refs.o_small[...] = refs.sm_all[:, 16:rows_c, :]
    gr.finish()
    rows = refs.gr_all.shape[1]
    half = iota((rows, LANES), 1) < HEAD_SIZE
    g_step = 0.0
    for k in range(ns):
        refs.o_att[:, QC * k : QC * (k + 1)] = refs.gr_all[k, :, :QC]
        chosen = (iota((8, NH), 1) == HL * k + iota((8, NH), 0)) & (iota((8, NH), 0) < HL)
        g_step = g_step + tn(refs.sm_all[k, rows_c:, :], chosen.astype(F32), HI)
    refs.o_step[...] = g_step[:rows]
    for c in range(2):
        first = refs.gr_all[c, :, QC : 2 * QC].astype(F32)
        second = refs.gr_all[2 + c, :, QC : 2 * QC].astype(F32)
        refs.o_att[:, AQ + QC * c : AQ + QC * (c + 1)] = jnp.where(
            half, first, roll(second, HEAD_SIZE)
        ).astype(BF16)
    refs.o_st[...] = refs.gr_all[t, :, QC : 2 * QC]

    def small_sent(k, carried):
        small_copy(k).wait_send()
        return carried

    lax.fori_loop(1, n, small_sent, 0)
    for group_of in (
        st_gather, taps_gather, jall, rs3, rs4, ag2, ag4, gz, gj, gi, gr, small,
        sum_gate, sum_up, sum_down, sum_z, sum_joint, sum_inner, sum_rest,
    ):
        sent += group_of.copies
    for copy in sent:
        copy.wait_send()

    @pl.when(s + 1 < n)
    def _():
        halo_copy.wait_send()

    @pl.when(s > 0)
    def _():
        back.wait_send()

    carry.finish()
    carry_b.finish()

    def dkv_end(k, carried):
        dkv_copy(k).wait_send()
        return carried

    def dkv_pair_end(k, carried):
        dkv_pair(k).wait_send()
        return carried

    lax.fori_loop(1, s + 1, dkv_end, 0)
    lax.fori_loop(0, s + 1, dkv_pair_end, 0)


def layer(n, ns, arrays):
    inputs = types.SimpleNamespace(**arrays)
    T, D = inputs.x.shape
    C = inputs.w_mix_in.shape[2]
    NW = inputs.st_own.shape[1]
    F = inputs.down_in.shape[1]
    N, TO, H = NW * ns, T // ns, NH // ns
    KJ = inputs.joint.shape[0]
    QC = 2 * HEAD_SIZE
    R, RJ = D // n, KJ // n
    steps = carry_steps(n)
    levels = levels_of(n)
    sd = jax.ShapeDtypeStruct
    J = QC + C
    SMALL = -(-(22 + KC * (C // LANES) + KC) // 8) * 8
    outs = dict(
        layer_output=sd((T, D), BF16),
        input_grad=sd((T, D), BF16),
        o_down=sd((R, F), BF16),
        o_gu=sd((2, R, F), BF16),
        o_mix=sd((2, R, ns * C), BF16),
        o_joint=sd((RJ, D), BF16),
        o_att=sd((R, inputs.w_att.shape[1]), BF16),
        o_step=sd((R, NH), F32),
        o_st=sd((R, LANES), BF16),
        o_gains=sd((16, LANES), F32),
        o_small=sd((ns, SMALL - 16, LANES), F32),
    )
    vm = pltpu.VMEM
    dma = lambda k: (pltpu.SemaphoreType.DMA((k,)), pltpu.SemaphoreType.DMA((k,)))
    blocks = lambda *shape: vm((ns,) + shape, BF16)

    def scan():
        return dict(
            tx=vm((max(1, steps - 1), C, N), BF16),
            rx=vm((steps, C, N), BF16),
            thr_tx=vm((max(1, steps - 1), 8, LANES), F32),
            thr_rx=vm((steps, 8, LANES), F32),
            sem=dma(steps),
            thr_sem=dma(steps),
        )

    def rows():
        return dict(tx=vm((8, T), F32), rx=vm((ns - 1, 8, T), F32), sem=dma(ns - 1))

    def scatter():
        return dict(tx=blocks(TO, D), rx=vm((3, TO, D), BF16), mid=vm((TO, D), BF16))

    def stream(*shape):
        return dict(src=vm((n,) + shape, BF16), rx=vm((n - 1,) + shape, BF16), sem=dma(levels))

    scratch = dict(
        w_qkv=vm((D, 3 * QC), BF16),
        w_joint=vm((J, D), BF16),
        w_mix=vm((2, D, C), BF16),
        w_gu=vm((2, D, F), BF16),
        down=vm((D, F), BF16),
        grad=vm((T, D), BF16),
        load=tuple(pltpu.SemaphoreType.DMA for _ in range(8)),
        taps8=vm((8, LANES), F32),
        taps_st=vm((2, NW, LANES), F32),
        codes=vm((n * T // LANES, LANES), jnp.int32),
        halo_rx=vm((HALO, D), BF16),
        st_all=vm((2, N, D), BF16),
        taps_all=vm((2, N, LANES), F32),
        kv_all=vm((n, T, LANES), BF16),
        normed=vm((T + HALO, D), BF16),
        inv1=vm((T, 1), F32),
        q2=vm((2 * T, LANES), BF16),
        z=vm((T, C), F32),
        ext_f=vm((T + HALO, C), F32),
        ext_s=vm((T + HALO, N), F32),
        ext_o=vm((T + HALO, 2 * NW), F32),
        grad_f=vm((T + HALO, C), F32),
        grad_o=vm((T + HALO, 2 * NW), F32),
        wr=vm((2, T, N), F32),
        tail_e=vm((T, C), F32),
        reach_e=vm((T, C), F32),
        ssd=vm((T, C), F32),
        w_tot=vm((T, C), F32),
        d_z=vm((T, C), BF16),
        jall_all=vm((ns, T, J), BF16),
        window=vm((C, N), F32),
        window_thr=vm((8, LANES), F32),
        m_acc=vm((2 * T, 1), F32),
        l_acc=vm((2 * T, 1), F32),
        o_acc=vm((2 * T, LANES), F32),
        dout2=vm((2 * T, LANES), BF16),
        dq2=vm((2 * T, LANES), F32),
        dkv_rx=vm((n, T // 2, LANES), BF16),
        dkv_mid=vm((n, T // 2, LANES), BF16),
        dkv_half=vm((T // 2, LANES), F32),
        dkv_sum=vm((T, LANES), F32),
        pair_tx=vm((T // 2, LANES), BF16),
        pair_rx=vm((T // 2, LANES), BF16),
        back_tx=vm((HALO, D), BF16),
        back_rx=vm((HALO, D), BF16),
        dwr_tx=vm((2, N, T), BF16),
        dwr_rx=vm((ns - 1, 2, NW, T), BF16),
        small_tx=vm((SMALL, LANES), F32),
        small_src=vm((n, SMALL + 8, LANES), F32),
        small_rx=vm((n, SMALL + 8, LANES), F32),
        halo=dma(1),
        st=dma(3),
        taps=dma(3),
        kv=dma(n - 1),
        kv_fwd=dma(n - 1),
        dkv=dma(n - 1),
        dkv_fwd=dma(n),
        jall=dma(3),
        pair=dma(1),
        back=dma(1),
        dwr=dma(ns - 1),
        small=dma(n - 1),
        sm_all=vm((ns, SMALL + 8, LANES), F32),
        fc=scan(),
        bc=scan(),
        sq=rows(),
        dot=rows(),
        rs1=scatter(),
        rs2=scatter(),
        rs1_sem=dma(2),
        rs2_sem=dma(2),
        rs3_sem=dma(2),
        rs4_sem=dma(2),
        ag1_all=blocks(TO, D),
        ag2_all=blocks(TO, D),
        gz_all=blocks(R, C),
        gi_all=blocks(R, C),
        gr_all=blocks(R, 2 * LANES),
        gj_all=blocks(RJ, D // ns),
        ag1_sem=dma(3),
        ag2_sem=dma(3),
        ag3_sem=dma(3),
        ag4_sem=dma(3),
        gz_sem=dma(3),
        gi_sem=dma(3),
        gr_sem=dma(3),
        gj_sem=dma(3),
        sm_sem=dma(3),
        gate_g=stream(R, F),
        up_g=stream(R, F),
        down_g=stream(R, F),
        z_g=stream(R, C),
        inner_g=stream(R, C),
        rest_g=stream(R, 2 * LANES),
        joint_g=stream(RJ, D // ns),
    )
    whole = pl.BlockSpec(memory_space=pltpu.VMEM)
    small = pl.BlockSpec(memory_space=pltpu.SMEM)
    far = pl.BlockSpec(memory_space=pl.ANY)
    specs = {key: whole for key in arrays}
    specs.update(doc_starts=small, step_bias=small, decay_rate=small, skip_gain=small)
    specs.update(w_att=far, joint=far, g=far, w_mix_in=far, w_gu_in=far, down_in=far)
    flat = [jax.tree.flatten(group) for group in (arrays, outs, scratch)]
    got = pl.pallas_call(
        functools.partial(layer_kernel, n, ns, [tree for _, tree in flat]),
        out_shape=flat[1][0],
        in_specs=jax.tree.flatten(specs)[0],
        out_specs=[whole] * len(outs),
        scratch_shapes=flat[2][0],
        name="layer",
        compiler_params=pltpu.CompilerParams(
            collective_id=1, has_side_effects=True, vmem_limit_bytes=VMEM_LIMIT
        ),
    )(*flat[0][0])
    return types.SimpleNamespace(**jax.tree.unflatten(flat[1][1], got))


def local(
    layer_input,
    out_grad,
    doc_starts,
    real_mask,
    norm_gain,
    attention_input_rows,
    mixer_in,
    state_in,
    step_in,
    conv_mixer,
    conv_state,
    step_bias,
    decay_rate,
    skip_gain,
    gated_gain,
    joint_out,
    mlp_gain,
    gate_up,
    down_weight,
):
    T, D = layer_input.shape
    NS, n = lax.axis_size(STATE), lax.axis_size(SEQ)
    t, s = lax.axis_index(STATE), lax.axis_index(SEQ)
    HL = NH // NS
    C = HL * HDM
    DM = NH * HDM
    NW = state_in.shape[2]
    F = gate_up.shape[2]
    w_mix = jnp.transpose(lax.dynamic_slice_in_dim(mixer_in, C * t, C, 2), (1, 0, 2))
    o = layer(
        n,
        NS,
        dict(
            x=layer_input,
            g=out_grad,
            w_att=attention_input_rows,
            w_mix_in=w_mix,
            w_step=step_in.T,
            st_own=jnp.transpose(state_in, (1, 2, 0)),
            conv_state=conv_state.reshape(KC, 2 * NW),
            conv_mixer=conv_mixer,
            ngain=norm_gain[None, :],
            ggain=gated_gain[None, :],
            mgain=mlp_gain[None, :],
            joint=joint_out,
            w_gu_in=jnp.transpose(gate_up, (1, 0, 2)),
            down_in=down_weight,
            real=real_mask.reshape(-1, LANES),
            step_bias=step_bias,
            decay_rate=decay_rate,
            skip_gain=skip_gain,
            doc_starts=doc_starts,
        ),
    )
    R = D // n
    f = lambda v: v.astype(F32)
    take = lambda v, count: lax.dynamic_slice_in_dim(v.reshape(-1), s * count, count, 0)
    per = C // LANES
    small = o.o_small
    taps = small[:, 6 : 6 + KC * per].reshape(NS, KC, C).transpose(1, 0, 2).reshape(KC, DM)
    row_st = 6 + KC * per
    taps_st = lax.dynamic_index_in_dim(small, t, 0, False)[row_st : row_st + KC, : 2 * NW]
    return (
        o.layer_output,
        f(o.input_grad),
        take(o.o_gains[:8], R),
        f(o.o_att),
        f(o.o_mix.transpose(1, 0, 2)),
        f(o.o_st[:, HEAD_SIZE:]).reshape(R, 2, NW),
        o.o_step,
        taps,
        taps_st.reshape(KC, 2, NW),
        small[:, 5, :HL].reshape(-1),
        small[:, 4, :HL].reshape(-1),
        small[:, 3, :HL].reshape(-1),
        take(small[:, :3], DM // n),
        f(o.o_joint),
        take(o.o_gains[8:], R),
        f(o.o_gu.transpose(1, 0, 2)),
        f(o.o_down),
    )


def solution(mesh):
    rep = P()
    in_specs = (
        P(SEQ, None),
        P(SEQ, None),
        rep,
        rep,
        rep,
        rep,
        rep,
        P(None, None, STATE),
        rep,
        rep,
        P(None, None, STATE),
        rep,
        rep,
        rep,
        rep,
        rep,
        rep,
        P(None, None, STATE),
        P(None, STATE),
    )
    out_specs = (
        P(SEQ, None),
        P(SEQ, None),
        P(SEQ),
        P(SEQ, None),
        P(SEQ, None, None),
        P(SEQ, None, STATE),
        P(SEQ, None),
        rep,
        P(None, None, STATE),
        rep,
        rep,
        rep,
        P(SEQ),
        P(SEQ, None),
        P(SEQ),
        P(SEQ, None, STATE),
        P(SEQ, STATE),
    )
    return jax.shard_map(local, mesh=mesh, in_specs=in_specs, out_specs=out_specs, check_vma=False)
```

```python
import functools
import math
import types

import jax
import jax.numpy as jnp
from jax import lax
from jax.experimental import pallas as pl
from jax.experimental.pallas import tpu as pltpu
from jax.sharding import PartitionSpec as P

QUERY_HEADS = 8
KEY_VALUE_HEADS = 2
HEAD_SIZE = 64
NH = 24
HDM = 64
KC = 4
EPSILON = 1e-05
ROPE_BASE = 10000.0
HI = lax.Precision.HIGHEST
F32 = jnp.float32
BF16 = jnp.bfloat16
LANES = 128
HALO = 16
FAR = -1e30
MESH = pl.DeviceIdType.MESH
SEQ, STATE = "seq", "state"
VMEM_LIMIT = 63 << 20


def nn(a, b, p=None):
    return lax.dot_general(a, b, (((1,), (0,)), ((), ())), precision=p, preferred_element_type=F32)


def nt(a, b, p=None):
    return lax.dot_general(a, b, (((1,), (1,)), ((), ())), precision=p, preferred_element_type=F32)


def tn(a, b, p=None):
    return lax.dot_general(a, b, (((0,), (0,)), ((), ())), precision=p, preferred_element_type=F32)


def sigmoid(v):
    return 1.0 / (1.0 + jnp.exp(-v))


def silu(v):
    return v * sigmoid(v)


def silu_slope(v):
    s = sigmoid(v)
    return s * (1.0 + v * (1.0 - s))


def softplus(v):
    return jnp.maximum(v, 0.0) + jnp.log1p(jnp.exp(-jnp.abs(v)))


def iota(shape, dim):
    return lax.broadcasted_iota(jnp.int32, shape, dim)


def doc_of(starts, pos):
    found = jnp.full(pos.shape, -1, jnp.int32)
    for start in starts:
        found = found + (pos >= start).astype(jnp.int32)
    return found


def roll(v, shift):
    return pltpu.roll(v, shift, 1)


def rope(v, cosine, sine, direction):
    first = (iota(v.shape, 1) % HEAD_SIZE) < HEAD_SIZE // 2
    half = HEAD_SIZE // 2
    partner = jnp.where(first, -roll(v, v.shape[1] - half), roll(v, half))
    return v * cosine + partner * (direction * sine)


def expander(width):
    return (iota((LANES, width), 1) // HDM == iota((LANES, width), 0)).astype(F32)


def masks_of(starts, first_row, rows):
    pos = first_row + iota((rows, 1), 0)
    doc = doc_of(starts, pos)
    masks = [(doc_of(starts, pos - (KC - 1 - k)) == doc).astype(F32) for k in range(KC)]
    return doc, masks


def push(src, dst, send_sem, recv_sem, device):
    copy = pltpu.make_async_remote_copy(
        src_ref=src,
        dst_ref=dst,
        send_sem=send_sem,
        recv_sem=recv_sem,
        device_id=device,
        device_id_type=MESH,
    )
    copy.start()
    return copy


def greet(n, ns, s, t):
    barrier = pltpu.get_barrier_semaphore()

    def seq_turn(k, carried):
        pl.semaphore_signal(barrier, inc=1, device_id={SEQ: lax.rem(s + k, n)}, device_id_type=MESH)
        return carried

    lax.fori_loop(1, n, seq_turn, 0)
    for k in range(1, ns):
        pl.semaphore_signal(
            barrier, inc=1, device_id={STATE: lax.rem(t + k, ns)}, device_id_type=MESH
        )
    return lambda: pl.semaphore_wait(barrier, n - 1 + ns - 1)


def conv_ref(ext_ref, taps, masks, rows):
    total = 0.0
    for k in range(KC):
        at = HALO - KC + 1 + k
        total = total + ext_ref[at : at + rows, :] * taps[k : k + 1] * masks[k]
    return total


class Carry:
    def __init__(self, refs, window, n, s, direction, rows_e):
        self.n, self.s, self.direction, self.rows_e = n, s, direction, rows_e
        self.tx, self.rx, self.thr_tx, self.thr_rx = refs.tx, refs.rx, refs.thr_tx, refs.thr_rx
        self.send, self.recv = refs.sem
        self.thr_send, self.thr_recv = refs.thr_sem
        self.total, self.thr = window
        self.count = carry_steps(n)

    def place(self, slot):
        return (1, 0) if slot == 0 else (2, 0) if slot == 1 else (1 << (slot - 1), slot - 1)

    def copies(self, slot, d, source):
        to = lax.rem(self.s + self.direction * d + self.n, self.n)
        make = lambda src, dst, a, b: pltpu.make_async_remote_copy(
            src_ref=src,
            dst_ref=dst,
            send_sem=a,
            recv_sem=b,
            device_id={SEQ: to},
            device_id_type=MESH,
        )
        return (
            make(self.tx.at[source], self.rx.at[slot], self.send.at[slot], self.recv.at[slot]),
            make(
                self.thr_tx.at[source],
                self.thr_rx.at[slot],
                self.thr_send.at[slot],
                self.thr_recv.at[slot],
            ),
        )

    def inside(self, index):
        return (index >= 0) & (index < self.n)

    def start(self, slot, d, source):
        @pl.when(self.inside(self.s + self.direction * d))
        def _():
            for copy in self.copies(slot, d, source):
                copy.start()

    def finish(self):
        for slot in range(self.count):
            d, source = self.place(slot)

            @pl.when(self.inside(self.s + self.direction * d))
            def _():
                for copy in self.copies(slot, d, source):
                    copy.wait_send()

    def begin(self, part, thr):
        self.tx[0] = part.astype(BF16)
        self.thr_tx[0] = thr
        self.total[...] = jnp.zeros(self.total.shape, F32)
        self.thr[...] = jnp.ones(self.thr.shape, F32)
        for slot in range(min(2, self.count)):
            self.start(slot, *self.place(slot))

    def join(self, slot, d, source):
        @pl.when(self.inside(self.s - self.direction * d))
        def _():
            for copy in self.copies(slot, d, source):
                copy.wait_recv()
            column = nt(self.rows_e, self.thr[...], HI)[:, :1]
            self.total[...] += column * self.rx[slot].astype(F32)
            self.thr[...] = self.thr[...] * self.thr_rx[slot]

        @pl.when(jnp.logical_not(self.inside(self.s - self.direction * d)))
        def _():
            self.thr[...] = jnp.zeros(self.thr.shape, F32)

    def pass_on(self, slot, d):
        self.tx[slot - 1] = self.total[...].astype(BF16)
        self.thr_tx[slot - 1] = self.thr[...]
        self.start(slot, d, slot - 1)

    def advance(self, slot):
        self.join(slot, *self.place(slot))
        if 1 <= slot < self.count - 1:
            self.pass_on(slot + 1, 1 << slot)

    def rest(self, first):
        if first >= self.count:
            return
        for slot in range(first, min(2, self.count)):
            self.advance(slot)
        first = max(first, 2)

        def turn(slot, d):
            self.join(slot, d, slot - 1)
            self.pass_on(slot + 1, 2 * d)
            return 2 * d

        if first < self.count:
            lax.fori_loop(first, self.count - 1, turn, 1 << (first - 1))
            self.join(self.count - 1, 1 << (self.count - 2), self.count - 2)


def carry_steps(n):
    return 1 if n <= 2 else 1 + (n - 2).bit_length()


def expand_rows(width):
    return (iota((width, LANES), 0) // HDM == iota((width, LANES), 1)).astype(F32)


def link_of(linked, cum, cum_t, h):
    return jnp.exp(jnp.where(linked, cum[:, h : h + 1] - cum_t[h : h + 1, :], FAR))


def send_to(sems, k, src, dst, device):
    send, recv = sems
    return push(src, dst, send.at[k], recv.at[k], device)


def row_sums(values):
    return nt(jnp.ones((8, values.shape[1]), F32), values, HI)


def as_column(row):
    first = (iota((8, LANES), 0) == 0).astype(F32)
    return tn(row, first, HI)[:, :1]


def share_rows(refs, ns, t, row):
    tx, rx = refs.tx, refs.rx
    tx[...] = row
    copies = [
        send_to(refs.sem, k - 1, tx, rx.at[k - 1], {STATE: lax.rem(t + k, ns)})
        for k in range(1, ns)
    ]

    def wait():
        total = tx[...]
        for k in range(1, ns):
            copies[k - 1].wait_recv()
            total = total + rx[k - 1]
        return total

    return copies, wait


class RowScatter:
    def __init__(self, refs, sem, t):
        self.sem, self.t = sem, t
        self.tx, self.rx, self.mid = refs.tx, refs.rx, refs.mid
        self.odd, self.far = lax.rem(t, 2), t // 2
        self.copies = []

    def start(self, part):
        rows = self.tx.shape[1]
        part = part.astype(BF16)
        for k in range(4):
            self.tx[(k % 2) * 2 + k // 2] = part[rows * k : rows * (k + 1)]
        theirs = self.tx.at[pl.ds(2 - 2 * self.odd, 2)]
        self.copies.append(
            send_to(self.sem, 0, theirs, self.rx.at[pl.ds(0, 2)], {STATE: sibling(self.t)})
        )

    def middle(self):
        self.copies[0].wait_recv()
        away = 1 - self.far
        self.mid[...] = (
            self.tx[2 * self.odd + away].astype(F32) + self.rx[away].astype(F32)
        ).astype(BF16)
        self.copies.append(
            send_to(self.sem, 1, self.mid, self.rx.at[2], {STATE: lax.rem(self.t + 2, 4)})
        )

    def finish(self):
        total = self.tx[2 * self.odd + self.far].astype(F32) + self.rx[self.far].astype(F32)
        self.copies[1].wait_recv()
        return total + self.rx[2].astype(F32)


class Gather:
    def __init__(self, block, sem, t):
        self.block, self.sem, self.t = block, sem, t
        own = block(t)
        self.copies = [
            send_to(sem, 0, own, own, {STATE: sibling(t)}),
            send_to(sem, 1, own, own, {STATE: lax.rem(t + 2, 4)}),
        ]

    def middle(self):
        self.copies[1].wait_recv()
        block = self.block(lax.rem(self.t + 2, 4))
        self.copies.append(send_to(self.sem, 2, block, block, {STATE: sibling(self.t)}))

    def finish(self):
        self.copies[0].wait_recv()
        self.copies[2].wait_recv()


def gather(every, sem, t, own):
    every[t] = own
    return Gather(lambda index: every.at[index], sem, t)


def sibling(t):
    return t + 1 - 2 * lax.rem(t, 2)


def levels_of(n):
    return n.bit_length() - 1


def bits_of(n, swapped):
    order = list(range(levels_of(n)))
    if swapped and len(order) > 1:
        order[0], order[1] = order[1], order[0]
    return order


class HalvingSum:
    def __init__(self, refs, n, s, swapped=False):
        self.sem, self.n, self.s = refs.sem, n, s
        self.bits = bits_of(n, swapped)
        self.src, self.rx = refs.src, refs.rx
        self.copies = []

    def owner(self, p):
        top = len(self.bits) - 1
        return sum(((p >> (top - level)) & 1) << bit for level, bit in enumerate(self.bits))

    def block_of(self, index):
        top = len(self.bits) - 1
        return sum(((index >> bit) & 1) << (top - level) for level, bit in enumerate(self.bits))

    def fill(self, column, values):
        rows = self.src.shape[1]
        width = values.shape[1]
        for p in range(self.n):
            at = rows * self.owner(p)
            self.src[p, :, column : column + width] = values[at : at + rows]

    def parts(self, level):
        half = self.n >> (level + 1)
        mine = lax.rem(self.s // (1 << self.bits[level]), 2)
        if level == 0:
            return self.src, 0, half, mine
        return self.rx, self.n - (self.n >> (level - 1)), half, mine

    def start(self, level=0):
        buffer, base, half, mine = self.parts(level)
        to = self.s + (1 - 2 * mine) * (1 << self.bits[level])
        here = self.n - (self.n >> level)
        self.copies.append(
            send_to(
                self.sem,
                level,
                buffer.at[pl.ds(base + (1 - mine) * half, half)],
                self.rx.at[pl.ds(here, half)],
                {SEQ: to},
            )
        )

    def step(self, level):
        buffer, base, half, mine = self.parts(level)
        self.copies[level].wait_recv()
        here = self.n - (self.n >> level)

        def turn(i, carried):
            kept = buffer[base + mine * half + i].astype(F32)
            self.rx[here + i] = (kept + self.rx[here + i].astype(F32)).astype(BF16)
            return carried

        lax.fori_loop(0, half, turn, 0)
        if level + 1 < len(self.bits):
            self.start(level + 1)

    def result(self):
        return self.rx[self.n - 2]


def named(value):
    if isinstance(value, dict):
        return types.SimpleNamespace(**{key: named(item) for key, item in value.items()})
    return value


def layer_kernel(n, ns, trees, *flat):
    refs, at = types.SimpleNamespace(), 0
    for tree in trees:
        part = jax.tree.unflatten(tree, flat[at : at + tree.num_leaves])
        at += tree.num_leaves
        refs.__dict__.update(named(part).__dict__)
    x, normed, inv1 = refs.x, refs.normed, refs.inv1
    w_mix, w_qkv, w_joint, w_gu, down = refs.w_mix, refs.w_qkv, refs.w_joint, refs.w_gu, refs.down
    grad = refs.grad
    w_step = refs.w_step
    T, D = x.shape
    t, s = lax.axis_index(STATE), lax.axis_index(SEQ)
    joined = refs.jall_all.at[t]
    C = w_mix.shape[2]
    QC = 2 * HEAD_SIZE
    AQ = QUERY_HEADS * HEAD_SIZE
    NW = refs.st_own.shape[1]
    HL = NH // ns
    N = NW * ns
    TO = T // ns
    DM = C * ns
    F = down.shape[1]
    pairs = C // LANES
    scale = 1.0 / math.sqrt(HEAD_SIZE)
    state_peer = lambda k: {STATE: lax.rem(t + k, ns)}
    own_c = pl.ds(pl.multiple_of(C * t, LANES), C)
    loads = [
        pltpu.make_async_copy(src, dst, refs.load[k])
        for k, (src, dst) in enumerate(
            [
                (refs.w_att.at[:, pl.ds(pl.multiple_of(QC * t, LANES), QC)], w_qkv.at[:, pl.ds(0, QC)]),
                (refs.w_att.at[:, pl.ds(AQ, 2 * QC)], w_qkv.at[:, pl.ds(QC, 2 * QC)]),
                (refs.w_mix_in, w_mix),
                (refs.joint.at[pl.ds(pl.multiple_of(QC * t, QC), QC)], w_joint.at[pl.ds(0, QC)]),
                (refs.joint.at[pl.ds(pl.multiple_of(AQ + C * t, LANES), C)], w_joint.at[pl.ds(QC, C)]),
                (refs.g, grad),
                (refs.down_in, down),
                (refs.w_gu_in.at[:, :, pl.ds(0, F // 2)], refs.w_gu_raw),
                (refs.w_gu_in.at[:, :, pl.ds(F // 2, F // 2)], refs.w_gu_raw),
            ]
        )
    ]
    for load in loads[:-1]:
        load.start()
    lanes_row = iota((1, LANES), 1)
    blank = jnp.zeros((1, LANES), F32)
    met = greet(n, ns, s, t)
    bias_row, rate_row = blank, blank
    skip_row = jnp.zeros((1, C), F32)
    heads_row = iota((1, C), 1) // HDM
    for h in range(HL):
        bias_row = jnp.where(lanes_row == h, refs.step_bias[HL * t + h], bias_row)
        rate_row = jnp.where(lanes_row == h, refs.decay_rate[HL * t + h], rate_row)
        skip_row = jnp.where(heads_row == h, refs.skip_gain[HL * t + h], skip_row)
    taps_mix = refs.conv_mixer[:, own_c]
    ggain_row = jnp.concatenate(
        [refs.ggain[pl.ds(C // LANES * t + k, 1), :] for k in range(C // LANES)], axis=1
    )
    pick = (iota((NH, LANES), 0) == HL * t + iota((NH, LANES), 1)) & (iota((NH, LANES), 1) < HL)
    pick = pick.astype(F32)
    refs.taps8[...] = jnp.zeros(refs.taps8.shape, F32)
    for c in range(2):
        refs.taps8[:KC, NW * c : NW * (c + 1)] = refs.conv_state[:, c, :]
    eye8 = (iota((8, LANES), 0) == iota((8, LANES), 1)).astype(F32)
    taps_cols = tn(refs.taps8[...], eye8, HI)
    for c in range(2):
        refs.taps_st[c] = taps_cols[NW * c : NW * (c + 1)]
    sent = []
    mine = pl.ds(pl.multiple_of(NW * t, NW), NW)
    refs.st_all[:, mine, :] = refs.st_own[...]
    refs.taps_all[:, mine, :] = refs.taps_st[...]

    first_row = s * T
    starts = [refs.doc_starts[k] for k in range(refs.doc_starts.shape[0])]
    doc, masks = masks_of(starts, first_row, T)
    tiles = T // LANES

    def code_turn(j, carried):
        for i in range(tiles):
            real = refs.real[pl.ds(tiles * j + i, 1), :]
            ids = doc_of(starts, j * T + i * LANES + iota((1, LANES), 1))
            refs.codes[pl.ds(tiles * j + i, 1), :] = jnp.where(real > 0, ids, -7)
        return carried

    lax.fori_loop(0, n, code_turn, 0)

    def code_of(j):
        return jnp.concatenate([refs.codes[pl.ds(tiles * j + i, 1), :] for i in range(tiles)], axis=1)

    real_col = as_column(jnp.broadcast_to((code_of(s) >= 0).astype(F32), (8, T)))
    firsts = jnp.zeros((T, 1), jnp.int32)
    places = first_row + iota((T, 1), 0)
    for start in starts:
        firsts = jnp.where(places >= start, start, firsts)
    powers = (iota((1, LANES), 1) % (HEAD_SIZE // 2)).astype(F32) * (2.0 / HEAD_SIZE)
    angles = (places - firsts).astype(F32) * jnp.exp(-math.log(ROPE_BASE) * powers)
    cosine, sine = jnp.cos(angles), jnp.sin(angles)
    doc_row = doc_of(starts, first_row + iota((1, T), 1))
    lane = iota((T, LANES), 1)
    low = lane < HEAD_SIZE
    ngain = refs.ngain[...]

    met()
    halo_copy = pltpu.make_async_remote_copy(
        src_ref=x.at[pl.ds(T - HALO, HALO)],
        dst_ref=refs.halo_rx,
        send_sem=refs.halo[0].at[0],
        recv_sem=refs.halo[1].at[0],
        device_id={SEQ: lax.rem(s + 1, n)},
        device_id_type=MESH,
    )

    @pl.when(s + 1 < n)
    def _():
        halo_copy.start()

    columns = lambda every: lambda i: every.at[:, pl.ds(pl.multiple_of(NW * i, NW), NW), :]
    st_gather = Gather(columns(refs.st_all), refs.st, t)
    taps_gather = Gather(columns(refs.taps_all), refs.taps, t)
    xf = x[...].astype(F32)
    inv = lax.rsqrt(jnp.mean(xf * xf, axis=1, keepdims=True) + EPSILON)
    inv1[...] = inv
    normed[HALO:, :] = (xf * inv * ngain).astype(BF16)
    main = normed[HALO:, :]
    loads[0].wait()
    loads[1].wait()
    qkv = nn(main, w_qkv[...])
    q = (rope(qkv[:, :QC], cosine, sine, 1.0).astype(BF16) * scale).astype(F32)
    kcos, ksin = jnp.where(low, cosine, 1.0), jnp.where(low, sine, 0.0)
    kv_all = refs.kv_all
    group = t // 2
    both_k, both_v = qkv[:, QC : 2 * QC], qkv[:, 2 * QC :]
    own_kv = jnp.where(
        low,
        jnp.where(group == 0, both_k, roll(both_k, HEAD_SIZE)),
        jnp.where(group == 0, roll(both_v, HEAD_SIZE), both_v),
    )
    kv_all[s] = rope(own_kv, kcos, ksin, 1.0).astype(BF16)

    core = lax.rem(t, 2)
    H2 = T // 2
    own_half = pl.ds(pl.multiple_of(H2 * core, H2), H2)
    other_half = pl.ds(pl.multiple_of(H2 * (1 - core), H2), H2)

    def kv_copy(k):
        return pltpu.make_async_remote_copy(
            src_ref=kv_all.at[s, own_half],
            dst_ref=kv_all.at[s, own_half],
            send_sem=refs.kv[0].at[k - 1],
            recv_sem=refs.kv[1].at[k - 1],
            device_id={SEQ: lax.rem(s + k, n)},
            device_id_type=MESH,
        )

    def kv_pair(k):
        block = kv_all.at[s - k, own_half]
        return pltpu.make_async_remote_copy(
            src_ref=block,
            dst_ref=block,
            send_sem=refs.kv_fwd[0].at[k - 1],
            recv_sem=refs.kv_fwd[1].at[k - 1],
            device_id={STATE: sibling(t)},
            device_id_type=MESH,
        )

    def kv_turn(k, carried):
        kv_copy(k).start()
        return carried

    lax.fori_loop(1, n - s, kv_turn, 0)
    refs.q2[:T, :] = jnp.where(low, q, 0.0).astype(BF16)
    refs.q2[T:, :] = jnp.where(low, roll(q, HEAD_SIZE), 0.0).astype(BF16)
    loads[2].wait()
    refs.z[...] = nn(main, w_mix[0])
    raw = nn(nt(main, w_step[...]), pick, HI) + bias_row

    doc2 = jnp.concatenate([doc, doc], axis=0)
    m_ref, l_ref, acc_ref = refs.m_acc, refs.l_acc, refs.o_acc
    m_ref[...] = jnp.full(m_ref.shape, FAR, F32)
    l_ref[...] = jnp.zeros(l_ref.shape, F32)
    acc_ref[...] = jnp.zeros(acc_ref.shape, F32)

    def allowed_at(j, diagonal):
        allowed = code_of(j) == doc2
        if diagonal:
            rows2 = jnp.concatenate([iota((T, T), 0)] * 2, axis=0)
            cols2 = iota((2 * T, T), 1)
            allowed = (allowed & (cols2 <= rows2)) | (cols2 == rows2)
        return allowed

    def attend(j, diagonal):
        block = kv_all[j]
        scores = jnp.where(allowed_at(j, diagonal), nt(refs.q2[...], block), FAR)
        m = m_ref[...]
        m_new = jnp.maximum(m, jnp.max(scores, axis=1, keepdims=True))
        shrink = jnp.exp(m - m_new)
        p = jnp.exp(scores - m_new)
        l_ref[...] = l_ref[...] * shrink + jnp.sum(p, axis=1, keepdims=True)
        acc_ref[...] = acc_ref[...] * shrink + nn(p.astype(BF16), block)
        m_ref[...] = m_new

    def attend_turn(k, carried):
        @pl.when(k < s)
        def _():
            kv_copy(k + 1).wait_recv()
            kv_pair(k + 1).start()

        kv_pair(k).wait_recv()
        attend(s - k, False)
        return carried

    def attend_some(first, stop):
        lax.fori_loop(first, stop, attend_turn, 0)

    cut1, cut2 = 1 + (s + 1) // 3, 1 + (2 * s + 1) // 3
    attend(s, True)
    taps_gather.middle()
    st_gather.middle()

    @pl.when(s > 0)
    def _():
        halo_copy.wait_recv()

    @pl.when(s == 0)
    def _():
        refs.halo_rx[...] = jnp.zeros(refs.halo_rx.shape, BF16)

    hf = refs.halo_rx[...].astype(F32)
    inv_h = lax.rsqrt(jnp.mean(hf * hf, axis=1, keepdims=True) + EPSILON)
    normed[:HALO, :] = (hf * inv_h * ngain).astype(BF16)
    ext_f, ext_s, ext_o = refs.ext_f, refs.ext_s, refs.ext_o
    ext_f[...] = nn(normed[...], w_mix[1]).astype(BF16).astype(F32)
    inner_lin = conv_ref(ext_f, taps_mix, masks, T)
    inner = silu(inner_lin)
    taps_gather.finish()
    st_gather.finish()
    for c in range(2):
        ext_s[...] = nt(normed[...], refs.st_all[c]).astype(BF16).astype(F32)
        taps = refs.taps_all[c].T
        refs.wr[c] = silu(conv_ref(ext_s, taps, masks, T))
    write, read = refs.wr[0], refs.wr[1]
    step = softplus(raw)
    causal = iota((T, T), 0) >= iota((T, T), 1)
    tri = causal.astype(F32)
    cum = nn(tri, -step * rate_row, HI)
    cum_t = cum.T
    linked = (doc == doc_row) & causal
    E = expander(C)
    rows_e = expand_rows(C)
    inflow = step * real_col
    inflow_e = nn(inflow, E, HI)
    in_x = inner * inflow_e
    cum_last = cum[T - 1 : T]
    last = first_row + T - 1
    doc_last = doc_of(starts, jnp.full((T, 1), last, jnp.int32))
    prior = doc_of(starts, jnp.full((T, 1), first_row - 1, jnp.int32))
    tail = jnp.where(doc == doc_last, jnp.exp(cum_last - cum), 0.0)
    refs.tail_e[...] = nn(tail, E, HI)
    state_part = tn(refs.tail_e[...] * in_x, write, HI)
    alive = (doc == prior).astype(F32)
    alive_last = (doc_last == prior).astype(F32)[:8]
    thr = alive_last * jnp.exp(jnp.broadcast_to(cum_last, (8, LANES)))
    steps = carry_steps(n)

    carry = Carry(refs.fc, (refs.window, refs.window_thr), n, s, 1, rows_e)
    carry.begin(state_part, thr)

    g_mat = nt(read, write, HI)
    for p in range(pairs):
        cols = slice(LANES * p, LANES * (p + 1))
        ys = []
        for h in (2 * p, 2 * p + 1):
            link = link_of(linked, cum, cum_t, h)
            ys.append(nn(link * g_mat, in_x[:, cols], HI))
        refs.ssd[:, cols] = jnp.where(low, ys[0], ys[1])

    for slot in range(min(2, steps)):
        carry.advance(slot)

    @pl.when(s > 0)
    def _():
        kv_copy(1).wait_recv()
        kv_pair(1).start()

    attend_some(1, cut1)
    if steps > 2:
        carry.advance(2)
    attend_some(cut1, cut2)
    carry.rest(3)
    s_in = refs.window[...]
    refs.reach_e[...] = nn(alive * jnp.exp(cum), E, HI)
    ssd = refs.ssd[...] + refs.reach_e[...] * nt(read, s_in, HI)
    refs.ssd[...] = ssd
    z = refs.z[...]
    full_mix = ssd + skip_row * inner
    gated = full_mix * silu(z)
    copies, wait = share_rows(refs.sq, ns, t, row_sums(gated * gated))
    sent += copies
    attend_some(cut2, s + 1)
    out = acc_ref[...] / l_ref[...]
    acc_ref[...] = out
    m_ref[...] = m_ref[...] + jnp.log(l_ref[...])
    joined[:, :QC] = jnp.where(low, roll(out[:T], HEAD_SIZE), out[T:]).astype(BF16)
    loads[3].wait()
    loads[4].wait()
    loads[5].wait()
    loads[6].wait()
    dh = nn(grad[...], down[...])
    inv_g = as_column(lax.rsqrt(wait() / DM + EPSILON))
    joined[:, QC:] = (gated * inv_g * ggain_row).astype(BF16)
    rs1 = RowScatter(refs.rs1, refs.rs1_sem, t)
    rs1.start(nn(joined[...], w_joint[...]))
    own_rows = pl.ds(pl.multiple_of(TO * t, TO), TO)
    x_own = x[own_rows, :].astype(F32)
    rs1.middle()
    loads[7].wait()

    def split_columns(half):
        columns = slice(F // 2 * half, F // 2 * (half + 1))

        def turn(k, carried):
            rows = pl.ds(pl.multiple_of(64 * k, 64), 64)
            for c in range(2):
                w_gu[c, rows, columns] = refs.w_gu_raw[rows, c, :]
            return carried

        lax.fori_loop(0, D // 64, turn, 0)

    split_columns(0)
    loads[8].start()
    res = x_own + rs1.finish()
    inv2 = lax.rsqrt(jnp.mean(res * res, axis=1, keepdims=True) + EPSILON)
    mgain = refs.mgain[...]
    ag1 = gather(refs.ag1_all, refs.ag1_sem, t, (res * inv2 * mgain).astype(BF16))
    loads[8].wait()
    split_columns(1)
    ag1.middle()
    jall = Gather(lambda index: refs.jall_all.at[index], refs.jall, t)
    ag1.finish()

    n2 = jnp.concatenate([refs.ag1_all[k] for k in range(ns)], axis=0)
    gate, up = nn(n2, w_gu[0]), nn(n2, w_gu[1])
    sig = sigmoid(gate)
    act = gate * sig
    hidden = (act * up).astype(BF16)
    d_gate = (dh * up * (sig * (1.0 + gate * (1.0 - sig)))).astype(BF16)
    d_up = (dh * act).astype(BF16)
    rs2 = RowScatter(refs.rs2, refs.rs2_sem, t)
    rs2.start(nt(d_gate, w_gu[0]) + nt(d_up, w_gu[1]))
    for copy in rs1.copies + ag1.copies:
        copy.wait_send()
    rs3 = RowScatter(refs.rs1, refs.rs3_sem, t)
    rs3.start(nt(hidden, down[...]))
    rs2.middle()

    def weight_sum(stream, parts, swapped=False):
        total = HalvingSum(stream, n, s, swapped)
        column = 0
        for lhs, rhs in parts:
            width = rhs.shape[1]
            for c in range(0, width, 256):
                piece = rhs[:, c : min(c + 256, width)]
                total.fill(column + c, tn(lhs, piece).astype(BF16))
            column += width
        return total

    sum_gate = weight_sum(refs.gate_g, [(n2, d_gate)], True)
    sum_gate.start()
    rs3.middle()
    sum_down = weight_sum(refs.down_g, [(grad[...], hidden)])
    sum_down.start()
    sum_up = weight_sum(refs.up_g, [(n2, d_up)])
    dn2 = rs2.finish()
    scaled = dn2 * mgain
    d_res = (
        grad[own_rows, :].astype(F32)
        + inv2 * scaled
        - res * inv2 * inv2 * inv2 * jnp.mean(scaled * res, axis=1, keepdims=True)
    )
    ag2 = gather(refs.ag2_all, refs.ag2_sem, t, d_res.astype(BF16))

    def put_small(row, values):
        for k in range(0, values.shape[1], LANES):
            piece = values[:, k : k + LANES]
            refs.small_tx[row : row + 1, : piece.shape[1]] = piece
            row += 1

    refs.small_tx[...] = jnp.zeros(refs.small_tx.shape, F32)
    refs.small_src[...] = jnp.zeros(refs.small_src.shape, F32)
    put_small(8, jnp.sum(dn2 * res * inv2, axis=0, keepdims=True))
    ag2.middle()
    ag3 = gather(refs.ag1_all, refs.ag3_sem, t, (res + rs3.finish()).astype(BF16))
    ag2.finish()
    d_branch = jnp.concatenate([refs.ag2_all[k] for k in range(ns)], axis=0)
    d_joined = nt(d_branch, w_joint[...])
    d_gn = d_joined[:, QC:]
    scaled = d_gn * ggain_row
    copies, wait = share_rows(refs.dot, ns, t, row_sums(scaled * gated))
    sent += copies
    put_small(16, jnp.sum(d_gn * gated * inv_g, axis=0, keepdims=True))
    d_att = d_joined[:, :QC].astype(BF16).astype(F32)
    dout2 = jnp.concatenate(
        [jnp.where(low, 0.0, roll(d_att, HEAD_SIZE)), jnp.where(low, 0.0, d_att)], axis=0
    )
    delta = jnp.sum(dout2 * acc_ref[...], axis=1, keepdims=True)
    l_ref[...] = delta
    refs.dout2[...] = dout2.astype(BF16)
    jall.middle()
    sum_down.step(0)
    sum_gate.step(0)
    jall.finish()
    own_d = pl.ds(pl.multiple_of((D // ns) * t, LANES), D // ns)
    d_cols = jnp.concatenate([refs.ag2_all[k, :, own_d] for k in range(ns)], axis=0)
    sum_joint = joint = HalvingSum(refs.joint_g, n, s)
    rows_j = joint.src.shape[1]
    piece = min(rows_j, LANES)
    for k in range(ns):
        values = tn(refs.jall_all[k], d_cols).astype(BF16)
        for at in range(0, QC + C, piece):
            row = QC * k + at if at < QC else AQ + C * k + at - QC
            offset = row % rows_j
            joint.src[joint.block_of(row // rows_j), offset : offset + piece, :] = values[at : at + piece]
    dot = as_column(wait() / DM)
    d_gated = inv_g * scaled - gated * (inv_g * inv_g * inv_g * dot)
    sig = sigmoid(z)
    dy = d_gated * z * sig
    refs.d_z[...] = (d_gated * full_mix * (sig * (1.0 + z * (1.0 - sig)))).astype(BF16)
    put_small(19, nt(jnp.broadcast_to(jnp.sum(dy * inner, axis=0, keepdims=True), (8, C)), E, HI)[:1])
    reach_dy = refs.reach_e[...] * dy
    carry_b = Carry(refs.bc, (refs.window, refs.window_thr), n, s, -1, rows_e)
    carry_b.begin(tn(reach_dy, read, HI), thr)
    sum_up.start()
    joint.start()
    sum_z = weight_sum(refs.z_g, [(main, refs.d_z[...])], True)
    ag3.middle()
    d_g = jnp.zeros((T, T), F32)
    for p in range(pairs):
        cols = slice(LANES * p, LANES * (p + 1))
        xp, dyp = in_x[:, cols], dy[:, cols]
        halves = []
        for k in range(2):
            link = link_of(linked, cum, cum_t, 2 * p + k)
            halves.append(tn(link * g_mat, dyp, HI))
            own = low if k == 0 else jnp.logical_not(low)
            d_g = d_g + link * nt(jnp.where(own, dyp, 0.0), xp, HI)
        refs.w_tot[:, cols] = jnp.where(low, halves[0], halves[1])

    refs.dq2[...] = jnp.zeros(refs.dq2.shape, F32)

    def attend_back(j, diagonal):
        block = kv_all[j]
        q2, dout2 = refs.q2[...], refs.dout2[...]
        scores = jnp.where(allowed_at(j, diagonal), nt(q2, block), FAR)
        p = jnp.exp(scores - m_ref[...])
        ds = (p * (nt(dout2, block) - l_ref[...])).astype(BF16)
        refs.dq2[...] += nn(ds, block)
        return tn(ds, q2) + tn(p.astype(BF16), dout2)

    def dkv_copy(k):
        return pltpu.make_async_remote_copy(
            src_ref=refs.dkv_mid.at[k - 1],
            dst_ref=refs.dkv_rx.at[k - 1],
            send_sem=refs.dkv[0].at[k - 1],
            recv_sem=refs.dkv[1].at[k - 1],
            device_id={SEQ: lax.rem(s - k + n, n)},
            device_id_type=MESH,
        )

    def dkv_pair(k):
        return pltpu.make_async_remote_copy(
            src_ref=kv_all.at[s - k, other_half],
            dst_ref=refs.dkv_mid.at[lax.rem(k + n - 1, n)],
            send_sem=refs.dkv_fwd[0].at[k],
            recv_sem=refs.dkv_fwd[1].at[k],
            device_id={STATE: sibling(t)},
            device_id_type=MESH,
        )

    def dkv_on(k):
        dkv_pair(k).wait_recv()
        both = refs.dkv_mid[k - 1].astype(F32) + kv_all[s - k, own_half].astype(F32)
        refs.dkv_mid[k - 1] = both.astype(BF16)
        dkv_copy(k).start()

    def back_turn(k, carried):
        kv_all[s - k] = attend_back(s - k, False).astype(BF16)
        dkv_pair(k).start()

        @pl.when(k > 1)
        def _():
            dkv_on(k - 1)

        return carried

    def back_some(first, stop):
        lax.fori_loop(first, stop, back_turn, 0)

    def kv_end(k, carried):
        kv_copy(k).wait_send()
        return carried

    def pair_end(k, carried):
        kv_pair(k).wait_send()
        return carried

    lax.fori_loop(1, n - s, kv_end, 0)
    lax.fori_loop(1, s + 1, pair_end, 0)
    for slot in range(min(2, steps)):
        carry_b.advance(slot)
    back_some(1, cut1)
    if steps > 2:
        carry_b.advance(2)
    back_some(cut1, cut2)
    carry_b.rest(3)
    sum_z.start()
    back_some(cut2, s + 1)
    diagonal = attend_back(s, True)
    refs.dkv_sum[...] = diagonal
    kv_all[s] = diagonal.astype(BF16)
    dkv_pair(0).start()

    @pl.when(s > 0)
    def _():
        dkv_on(s)

    ag3.finish()
    for k in range(ns):
        refs.layer_output[TO * k : TO * (k + 1), :] = refs.ag1_all[k]
    sum_down.step(1)
    sum_gate.step(1)
    sum_up.step(0)
    later = refs.window[...]
    tail_e = refs.tail_e[...]
    tail_r = tail_e * nt(write, later, HI)
    w_tot = refs.w_tot[...] + tail_r
    d_write = tn(d_g, read, HI) + nn(tail_e * in_x, later, HI)
    d_read = nn(d_g, write, HI) + nn(reach_dy, s_in, HI)
    refs.dwr_tx[0] = d_write.T.astype(BF16)
    refs.dwr_tx[1] = d_read.T.astype(BF16)
    dwr = []
    for k in range(1, ns):
        p = lax.rem(t + k, ns)
        theirs = pl.ds(pl.multiple_of(NW * p, NW), NW)
        dwr.append(
            send_to(refs.dwr, k - 1, refs.dwr_tx.at[:, theirs, :], refs.dwr_rx.at[k - 1], {STATE: p})
        )
    sent += dwr
    u = nt(inner * w_tot, E, HI)
    tl = nt(in_x * tail_r, E, HI)
    thr_s = jnp.sum(tn(later * s_in, rows_e, HI), axis=0, keepdims=True) * thr[:1]
    d_cum = nt(dy * ssd, E, HI) - inflow * u
    at_last = iota((T, LANES), 0) == T - 1
    d_cum = d_cum + jnp.where(at_last, jnp.sum(tl, axis=0, keepdims=True) + thr_s, 0.0)
    d_ld = tn(tri, d_cum, HI)
    d_step = real_col * u - rate_row * d_ld
    put_small(20, -jnp.sum(step * d_ld, axis=0, keepdims=True))
    d_step = d_step * sigmoid(raw)
    put_small(21, jnp.sum(d_step, axis=0, keepdims=True))
    d_step = d_step.astype(BF16)
    d_lin = (inflow_e * w_tot + skip_row * dy) * silu_slope(inner_lin)

    def conv_back(ext, grad, taps, up, row, rows):
        grad[...] = jnp.zeros(grad.shape, F32)
        for k in range(KC):
            at = HALO - KC + 1 + k
            masked = up * masks[k]
            put_small(row + rows * k, jnp.sum(masked * ext[at : at + T, :], axis=0, keepdims=True))
            grad[at : at + T, :] += masked * taps[k : k + 1]
        return grad[...].astype(BF16)

    d_ext = conv_back(ext_f, refs.grad_f, taps_mix, d_lin, 22, C // LANES)
    st64 = refs.st_own[...].reshape(2 * NW, D)
    taps_own = refs.taps_st[...].reshape(2 * NW, LANES).T
    ext_o[...] = nt(normed[...], st64).astype(BF16).astype(F32)
    slope_o = silu_slope(conv_ref(ext_o, taps_own, masks, T))
    for copy in dwr:
        copy.wait_recv()
    d_wr = refs.dwr_tx[:, mine, :].astype(F32)
    for k in range(1, ns):
        d_wr = d_wr + refs.dwr_rx[k - 1].astype(F32)
    row_st = 22 + KC * (C // LANES)
    d_st = conv_back(ext_o, refs.grad_o, taps_own, d_wr.reshape(2 * NW, T).T * slope_o, row_st, 1)
    sum_z.step(0)
    refs.back_tx[...] = (nt(d_ext[:HALO], w_mix[1]) + nn(d_st[:HALO], st64)).astype(BF16)
    back = pltpu.make_async_remote_copy(
        src_ref=refs.back_tx,
        dst_ref=refs.back_rx,
        send_sem=refs.back[0].at[0],
        recv_sem=refs.back[1].at[0],
        device_id={SEQ: lax.rem(s + n - 1, n)},
        device_id_type=MESH,
    )

    @pl.when(s > 0)
    def _():
        back.start()

    sum_inner = weight_sum(refs.inner_g, [(normed[...], d_ext)])
    sum_inner.start()
    d_z = refs.d_z[...]
    dq2 = refs.dq2[...]
    dq = jnp.where(low, dq2[:T], roll(dq2[T:], HEAD_SIZE)) * scale
    d_q = rope(dq, cosine, sine, -1.0).astype(BF16)
    d_n = (
        nt(d_z, w_mix[0])
        + nt(d_ext[HALO:], w_mix[1])
        + nn(d_st[HALO:], st64)
        + nn(nt(d_step, pick.astype(BF16)).astype(BF16), w_step[...])
    )
    def dkv_turn(k, carried):
        dkv_copy(k).wait_recv()
        refs.dkv_half[...] += refs.dkv_rx[k - 1].astype(F32)
        return carried

    dkv_pair(0).wait_recv()
    refs.dkv_half[...] = refs.dkv_sum[own_half, :] + refs.dkv_mid[n - 1].astype(F32)
    lax.fori_loop(1, n - s, dkv_turn, 0)
    refs.pair_tx[...] = refs.dkv_half[...].astype(BF16)
    odd = core
    pair = send_to(refs.pair, 0, refs.pair_tx, refs.pair_rx, {STATE: sibling(t)})
    sent.append(pair)
    pair.wait_recv()
    refs.dkv_sum[own_half, :] = refs.pair_tx[...].astype(F32)
    refs.dkv_sum[other_half, :] = refs.pair_rx[...].astype(F32)
    d_kv = rope(refs.dkv_sum[...], kcos, ksin, -1.0)
    d_kv = jnp.where(low == (odd == 0), d_kv, 0.0)
    other = roll(d_kv, HEAD_SIZE)
    d_k = jnp.where(low, jnp.where(group == 0, d_kv, 0.0), jnp.where(group == 0, 0.0, other))
    d_v = jnp.where(low, jnp.where(group == 0, other, 0.0), jnp.where(group == 0, 0.0, d_kv))
    d_kv_b = d_kv.astype(BF16)
    d_qkv = jnp.concatenate([d_q, jnp.where(odd == 0, d_k, d_v).astype(BF16)], axis=1)
    mine_kv = jnp.where(odd == 0, d_kv, other).astype(BF16)
    pad_st = jnp.concatenate([jnp.zeros((T + HALO, HEAD_SIZE), F32), d_st.astype(F32)], axis=1)
    mine_kv = jnp.concatenate([jnp.zeros((HALO, LANES), F32), mine_kv.astype(F32)], axis=0)
    mixed = jnp.where(iota((T + HALO, LANES), 1) < HEAD_SIZE, mine_kv, pad_st).astype(BF16)
    sum_rest = weight_sum(refs.rest_g, [(main, d_q), (normed[...], mixed)])
    sum_rest.start()
    w_kv = jnp.where(odd == 0, w_qkv[:, QC : 2 * QC], w_qkv[:, 2 * QC :])
    d_n = d_n + nt(d_qkv, jnp.concatenate([w_qkv[:, :QC], w_kv], axis=1))
    @pl.when(s + 1 < n)
    def _():
        back.wait_recv()

    @pl.when(s + 1 == n)
    def _():
        refs.back_rx[...] = jnp.zeros(refs.back_rx.shape, BF16)

    tail_rows = d_n[T - HALO :] + refs.back_rx[...].astype(F32)
    d_n = jnp.concatenate([d_n[: T - HALO], tail_rows], axis=0)
    for copy in rs2.copies + ag3.copies:
        copy.wait_send()
    rs4 = RowScatter(refs.rs2, refs.rs4_sem, t)
    rs4.start(d_n)
    sum_joint.step(0)
    rs4.middle()
    sum_up.step(1)
    inv_own = inv1[own_rows, :]
    d_n = rs4.finish()
    scaled = d_n * ngain
    in_g = (
        d_res
        + inv_own * scaled
        - x_own * inv_own * inv_own * inv_own * jnp.mean(scaled * x_own, axis=1, keepdims=True)
    )
    ag4 = gather(refs.ag1_all, refs.ag4_sem, t, in_g.astype(BF16))
    put_small(0, jnp.sum(d_n * x_own * inv_own, axis=0, keepdims=True))

    def small_copy(k):
        return pltpu.make_async_remote_copy(
            src_ref=refs.small_src.at[lax.rem(s + k, n)],
            dst_ref=refs.small_rx.at[s],
            send_sem=refs.small[0].at[k - 1],
            recv_sem=refs.small[1].at[k - 1],
            device_id={SEQ: lax.rem(s + k, n)},
            device_id_type=MESH,
        )

    step_rows = tn(d_step, main)[:8]
    common = refs.small_tx[...]
    rows_c, rows_d = common.shape[0], D // n
    for k in range(n):
        refs.small_src[k, :rows_c, :] = common
        refs.small_src[k, rows_c:, :rows_d] = step_rows[:, rows_d * k : rows_d * (k + 1)]
    refs.small_rx[s] = refs.small_src[s]

    def small_turn(k, carried):
        small_copy(k).start()
        return carried

    lax.fori_loop(1, n, small_turn, 0)
    last_level = len(bits_of(n, False)) - 1

    def steps_of(total, first, stop):
        for level in range(first, stop):
            total.step(level)

    sum_inner.step(0)
    sum_z.step(1)
    ag4.middle()
    sum_joint.step(1)
    sum_rest.step(0)
    steps_of(sum_down, 2, last_level + 1)
    steps_of(sum_gate, 2, last_level + 1)
    ag4.finish()
    for k in range(ns):
        refs.input_grad[TO * k : TO * (k + 1), :] = refs.ag1_all[k]
    steps_of(sum_up, 2, last_level + 1)
    steps_of(sum_z, 2, last_level + 1)
    gz = gather(refs.gz_all, refs.gz_sem, t, sum_z.result())
    sum_inner.step(1)
    steps_of(sum_joint, 2, last_level + 1)
    gj = gather(refs.gj_all, refs.gj_sem, t, sum_joint.result())
    sum_rest.step(1)
    gz.middle()
    steps_of(sum_inner, 2, last_level + 1)
    gi = gather(refs.gi_all, refs.gi_sem, t, sum_inner.result())
    gj.middle()
    steps_of(sum_rest, 2, last_level + 1)
    gr = gather(refs.gr_all, refs.gr_sem, t, sum_rest.result())

    def small_end(k, carried):
        small_copy(k).wait_recv()
        return carried

    lax.fori_loop(1, n, small_end, 0)

    def small_sum(j, total):
        return total + refs.small_rx[j]

    small = gather(
        refs.sm_all, refs.sm_sem, t,
        lax.fori_loop(0, n, small_sum, jnp.zeros(refs.small_rx.shape[1:], F32)),
    )
    gi.middle()
    small.middle()
    refs.o_gu[0] = sum_gate.result()
    refs.o_gu[1] = sum_up.result()
    refs.o_down[...] = sum_down.result()
    gz.finish()
    gj.finish()
    gi.finish()
    gr.middle()
    for k in range(ns):
        refs.o_mix[0, :, C * k : C * (k + 1)] = refs.gz_all[k]
        refs.o_mix[1, :, C * k : C * (k + 1)] = refs.gi_all[k]
        refs.o_joint[:, (D // ns) * k : (D // ns) * (k + 1)] = refs.gj_all[k]
    small.finish()
    total = refs.sm_all[0, :16, :]
    for k in range(1, ns):
        total = total + refs.sm_all[k, :16, :]
    refs.o_gains[...] = total
    refs.o_small[...] = refs.sm_all[:, 16:rows_c, :]
    gr.finish()
    rows = refs.gr_all.shape[1]
    half = iota((rows, LANES), 1) < HEAD_SIZE
    g_step = 0.0
    for k in range(ns):
        refs.o_att[:, QC * k : QC * (k + 1)] = refs.gr_all[k, :, :QC]
        chosen = (iota((8, NH), 1) == HL * k + iota((8, NH), 0)) & (iota((8, NH), 0) < HL)
        g_step = g_step + tn(refs.sm_all[k, rows_c:, :], chosen.astype(F32), HI)
    refs.o_step[...] = g_step[:rows]
    for c in range(2):
        first = refs.gr_all[c, :, QC : 2 * QC].astype(F32)
        second = refs.gr_all[2 + c, :, QC : 2 * QC].astype(F32)
        refs.o_att[:, AQ + QC * c : AQ + QC * (c + 1)] = jnp.where(
            half, first, roll(second, HEAD_SIZE)
        ).astype(BF16)
    refs.o_st[...] = refs.gr_all[t, :, QC : 2 * QC]

    def small_sent(k, carried):
        small_copy(k).wait_send()
        return carried

    lax.fori_loop(1, n, small_sent, 0)
    for group_of in (
        st_gather, taps_gather, jall, rs3, rs4, ag2, ag4, gz, gj, gi, gr, small,
        sum_gate, sum_up, sum_down, sum_z, sum_joint, sum_inner, sum_rest,
    ):
        sent += group_of.copies
    for copy in sent:
        copy.wait_send()

    @pl.when(s + 1 < n)
    def _():
        halo_copy.wait_send()

    @pl.when(s > 0)
    def _():
        back.wait_send()

    carry.finish()
    carry_b.finish()

    def dkv_end(k, carried):
        dkv_copy(k).wait_send()
        return carried

    def dkv_pair_end(k, carried):
        dkv_pair(k).wait_send()
        return carried

    lax.fori_loop(1, s + 1, dkv_end, 0)
    lax.fori_loop(0, s + 1, dkv_pair_end, 0)


def layer(n, ns, arrays):
    inputs = types.SimpleNamespace(**arrays)
    T, D = inputs.x.shape
    C = inputs.w_mix_in.shape[2]
    NW = inputs.st_own.shape[1]
    F = inputs.down_in.shape[1]
    N, TO, H = NW * ns, T // ns, NH // ns
    KJ = inputs.joint.shape[0]
    QC = 2 * HEAD_SIZE
    R, RJ = D // n, KJ // n
    steps = carry_steps(n)
    levels = levels_of(n)
    sd = jax.ShapeDtypeStruct
    J = QC + C
    SMALL = -(-(22 + KC * (C // LANES) + KC) // 8) * 8
    outs = dict(
        layer_output=sd((T, D), BF16),
        input_grad=sd((T, D), BF16),
        o_down=sd((R, F), BF16),
        o_gu=sd((2, R, F), BF16),
        o_mix=sd((2, R, ns * C), BF16),
        o_joint=sd((RJ, D), BF16),
        o_att=sd((R, inputs.w_att.shape[1]), BF16),
        o_step=sd((R, NH), F32),
        o_st=sd((R, LANES), BF16),
        o_gains=sd((16, LANES), F32),
        o_small=sd((ns, SMALL - 16, LANES), F32),
    )
    vm = pltpu.VMEM
    dma = lambda k: (pltpu.SemaphoreType.DMA((k,)), pltpu.SemaphoreType.DMA((k,)))
    blocks = lambda *shape: vm((ns,) + shape, BF16)

    def scan():
        return dict(
            tx=vm((max(1, steps - 1), C, N), BF16),
            rx=vm((steps, C, N), BF16),
            thr_tx=vm((max(1, steps - 1), 8, LANES), F32),
            thr_rx=vm((steps, 8, LANES), F32),
            sem=dma(steps),
            thr_sem=dma(steps),
        )

    def rows():
        return dict(tx=vm((8, T), F32), rx=vm((ns - 1, 8, T), F32), sem=dma(ns - 1))

    def scatter():
        return dict(tx=blocks(TO, D), rx=vm((3, TO, D), BF16), mid=vm((TO, D), BF16))

    def stream(*shape):
        return dict(src=vm((n,) + shape, BF16), rx=vm((n - 1,) + shape, BF16), sem=dma(levels))

    scratch = dict(
        w_qkv=vm((D, 3 * QC), BF16),
        w_joint=vm((J, D), BF16),
        w_mix=vm((2, D, C), BF16),
        w_gu=vm((2, D, F), BF16),
        w_gu_raw=vm((D, 2, F // 2), BF16),
        down=vm((D, F), BF16),
        grad=vm((T, D), BF16),
        load=tuple(pltpu.SemaphoreType.DMA for _ in range(9)),
        taps8=vm((8, LANES), F32),
        taps_st=vm((2, NW, LANES), F32),
        codes=vm((n * T // LANES, LANES), jnp.int32),
        halo_rx=vm((HALO, D), BF16),
        st_all=vm((2, N, D), BF16),
        taps_all=vm((2, N, LANES), F32),
        kv_all=vm((n, T, LANES), BF16),
        normed=vm((T + HALO, D), BF16),
        inv1=vm((T, 1), F32),
        q2=vm((2 * T, LANES), BF16),
        z=vm((T, C), F32),
        ext_f=vm((T + HALO, C), F32),
        ext_s=vm((T + HALO, N), F32),
        ext_o=vm((T + HALO, 2 * NW), F32),
        grad_f=vm((T + HALO, C), F32),
        grad_o=vm((T + HALO, 2 * NW), F32),
        wr=vm((2, T, N), F32),
        tail_e=vm((T, C), F32),
        reach_e=vm((T, C), F32),
        ssd=vm((T, C), F32),
        w_tot=vm((T, C), F32),
        d_z=vm((T, C), BF16),
        jall_all=vm((ns, T, J), BF16),
        window=vm((C, N), F32),
        window_thr=vm((8, LANES), F32),
        m_acc=vm((2 * T, 1), F32),
        l_acc=vm((2 * T, 1), F32),
        o_acc=vm((2 * T, LANES), F32),
        dout2=vm((2 * T, LANES), BF16),
        dq2=vm((2 * T, LANES), F32),
        dkv_rx=vm((n, T // 2, LANES), BF16),
        dkv_mid=vm((n, T // 2, LANES), BF16),
        dkv_half=vm((T // 2, LANES), F32),
        dkv_sum=vm((T, LANES), F32),
        pair_tx=vm((T // 2, LANES), BF16),
        pair_rx=vm((T // 2, LANES), BF16),
        back_tx=vm((HALO, D), BF16),
        back_rx=vm((HALO, D), BF16),
        dwr_tx=vm((2, N, T), BF16),
        dwr_rx=vm((ns - 1, 2, NW, T), BF16),
        small_tx=vm((SMALL, LANES), F32),
        small_src=vm((n, SMALL + 8, LANES), F32),
        small_rx=vm((n, SMALL + 8, LANES), F32),
        halo=dma(1),
        st=dma(3),
        taps=dma(3),
        kv=dma(n - 1),
        kv_fwd=dma(n - 1),
        dkv=dma(n - 1),
        dkv_fwd=dma(n),
        jall=dma(3),
        pair=dma(1),
        back=dma(1),
        dwr=dma(ns - 1),
        small=dma(n - 1),
        sm_all=vm((ns, SMALL + 8, LANES), F32),
        fc=scan(),
        bc=scan(),
        sq=rows(),
        dot=rows(),
        rs1=scatter(),
        rs2=scatter(),
        rs1_sem=dma(2),
        rs2_sem=dma(2),
        rs3_sem=dma(2),
        rs4_sem=dma(2),
        ag1_all=blocks(TO, D),
        ag2_all=blocks(TO, D),
        gz_all=blocks(R, C),
        gi_all=blocks(R, C),
        gr_all=blocks(R, 2 * LANES),
        gj_all=blocks(RJ, D // ns),
        ag1_sem=dma(3),
        ag2_sem=dma(3),
        ag3_sem=dma(3),
        ag4_sem=dma(3),
        gz_sem=dma(3),
        gi_sem=dma(3),
        gr_sem=dma(3),
        gj_sem=dma(3),
        sm_sem=dma(3),
        gate_g=stream(R, F),
        up_g=stream(R, F),
        down_g=stream(R, F),
        z_g=stream(R, C),
        inner_g=stream(R, C),
        rest_g=stream(R, 2 * LANES),
        joint_g=stream(RJ, D // ns),
    )
    whole = pl.BlockSpec(memory_space=pltpu.VMEM)
    small = pl.BlockSpec(memory_space=pltpu.SMEM)
    far = pl.BlockSpec(memory_space=pl.ANY)
    specs = {key: whole for key in arrays}
    specs.update(doc_starts=small, step_bias=small, decay_rate=small, skip_gain=small)
    specs.update(w_att=far, joint=far, g=far, w_mix_in=far, w_gu_in=far, down_in=far)
    flat = [jax.tree.flatten(group) for group in (arrays, outs, scratch)]
    got = pl.pallas_call(
        functools.partial(layer_kernel, n, ns, [tree for _, tree in flat]),
        out_shape=flat[1][0],
        in_specs=jax.tree.flatten(specs)[0],
        out_specs=[whole] * len(outs),
        scratch_shapes=flat[2][0],
        name="layer",
        compiler_params=pltpu.CompilerParams(
            collective_id=1, has_side_effects=True, vmem_limit_bytes=VMEM_LIMIT
        ),
    )(*flat[0][0])
    return types.SimpleNamespace(**jax.tree.unflatten(flat[1][1], got))


def finish_kernel(n, ns, tree_in, tree_out, *flat):
    split = tree_in.num_leaves
    o = named(jax.tree.unflatten(tree_in, flat[:split]))
    out = named(jax.tree.unflatten(tree_out, flat[split:]))
    t, s = lax.axis_index(STATE), lax.axis_index(SEQ)
    HL, C = NH // ns, NH * HDM // ns
    per = C // LANES
    NW = out.taps_st.shape[2]
    R = out.down.shape[0]
    out.layer_output[...] = o.layer_output[...]
    out.input_grad[...] = o.input_grad[...].astype(F32)
    out.att[...] = o.o_att[...].astype(F32)
    out.joint[...] = o.o_joint[...].astype(F32)
    out.down[...] = o.o_down[...].astype(F32)
    out.step[...] = o.o_step[...]
    for c in range(2):
        out.mix[:, c, :] = o.o_mix[c].astype(F32)
        out.gu[:, c, :] = o.o_gu[c].astype(F32)
        at = HEAD_SIZE + NW * c
        out.st[:, c, :] = o.o_st[:, at : at + NW].astype(F32)
    small = o.o_small

    def part(row, width, count):
        at = s * width
        first = at // LANES
        lanes = jnp.concatenate([row(first + k) for k in range(count)], axis=1)
        return roll(lanes, lax.rem(count * LANES - (at - first * LANES), count * LANES))[:, :width]

    for at, dst in ((0, out.ngain), (8, out.mgain)):
        dst[...] = part(lambda k: o.o_gains[pl.ds(at + k, 1), :], R, 1)
    for k in range(ns):
        for i in range(per):
            out.gains[per * k + i : per * k + i + 1, :] = small[k, i : i + 1, :]
    width = out.ggain.shape[1]
    last = ns * per - 1
    out.ggain[...] = part(lambda k: out.gains[pl.ds(jnp.minimum(k, last), 1), :], width, 3)
    heads = 0.0
    for k in range(ns):
        into = (iota((LANES, LANES), 1) == HL * k + iota((LANES, LANES), 0)) & (
            iota((LANES, LANES), 0) < HL
        )
        heads = heads + nn(small[k, :8, :], into.astype(F32), HI)
        for j in range(KC):
            for i in range(per):
                row = 6 + per * j + i
                at = C * k + LANES * i
                out.taps[j : j + 1, at : at + LANES] = small[k, row : row + 1, :]
    out.skip[...], out.rate[...], out.bias[...] = (heads[k : k + 1, :NH] for k in (3, 4, 5))
    for j in range(KC):
        row = small[t, 6 + KC * per + j : 7 + KC * per + j, :]
        for c in range(2):
            out.taps_st[j, c : c + 1, :] = row[:, NW * c : NW * (c + 1)]


def finish(n, ns, o, shapes):
    sd = lambda *shape: jax.ShapeDtypeStruct(shape, F32)
    R, F = o.o_down.shape
    T, D = o.layer_output.shape
    NW = shapes.NW
    outs = dict(
        layer_output=jax.ShapeDtypeStruct((T, D), BF16),
        input_grad=sd(T, D),
        att=sd(*o.o_att.shape),
        joint=sd(*o.o_joint.shape),
        down=sd(R, F),
        step=sd(R, NH),
        mix=sd(R, 2, NH * HDM),
        gu=sd(R, 2, F),
        st=sd(R, 2, NW),
        ngain=sd(1, R),
        mgain=sd(1, R),
        ggain=sd(1, NH * HDM // n),
        gains=sd(NH * HDM // LANES, LANES),
        taps=sd(KC, NH * HDM),
        taps_st=sd(KC, 2, NW),
        skip=sd(1, NH),
        rate=sd(1, NH),
        bias=sd(1, NH),
    )
    arrays = dict(o.__dict__)
    flat = [jax.tree.flatten(group) for group in (arrays, outs)]
    whole = pl.BlockSpec(memory_space=pltpu.VMEM)
    got = pl.pallas_call(
        functools.partial(finish_kernel, n, ns, flat[0][1], flat[1][1]),
        out_shape=flat[1][0],
        in_specs=[whole] * len(arrays),
        out_specs=[whole] * len(outs),
        name="finish",
        compiler_params=pltpu.CompilerParams(vmem_limit_bytes=VMEM_LIMIT),
    )(*flat[0][0])
    return types.SimpleNamespace(**jax.tree.unflatten(flat[1][1], got))


def local(
    layer_input,
    out_grad,
    doc_starts,
    real_mask,
    norm_gain,
    attention_input_rows,
    mixer_in,
    state_in,
    step_in,
    conv_mixer,
    conv_state,
    step_bias,
    decay_rate,
    skip_gain,
    gated_gain,
    joint_out,
    mlp_gain,
    gate_up,
    down_weight,
):
    T, D = layer_input.shape
    NS, n = lax.axis_size(STATE), lax.axis_size(SEQ)
    t, s = lax.axis_index(STATE), lax.axis_index(SEQ)
    HL = NH // NS
    C = HL * HDM
    DM = NH * HDM
    NW = state_in.shape[2]
    F = gate_up.shape[2]
    w_mix = jnp.transpose(lax.dynamic_slice_in_dim(mixer_in, C * t, C, 2), (1, 0, 2))
    o = layer(
        n,
        NS,
        dict(
            x=layer_input,
            g=out_grad,
            w_att=attention_input_rows,
            w_mix_in=w_mix,
            w_step=step_in.T,
            st_own=jnp.transpose(state_in, (1, 2, 0)),
            conv_state=conv_state,
            conv_mixer=conv_mixer,
            ngain=norm_gain[None, :],
            ggain=gated_gain.reshape(-1, LANES),
            mgain=mlp_gain[None, :],
            joint=joint_out,
            w_gu_in=gate_up,
            down_in=down_weight,
            real=real_mask.reshape(-1, LANES),
            step_bias=step_bias,
            decay_rate=decay_rate,
            skip_gain=skip_gain,
            doc_starts=doc_starts,
        ),
    )
    e = finish(n, NS, o, types.SimpleNamespace(NW=NW))
    return (
        e.layer_output,
        e.input_grad,
        e.ngain.reshape(-1),
        e.att,
        e.mix,
        e.st,
        e.step,
        e.taps,
        e.taps_st,
        e.bias.reshape(-1),
        e.rate.reshape(-1),
        e.skip.reshape(-1),
        e.ggain.reshape(-1),
        e.joint,
        e.mgain.reshape(-1),
        e.gu,
        e.down,
    )


def solution(mesh):
    rep = P()
    in_specs = (
        P(SEQ, None),
        P(SEQ, None),
        rep,
        rep,
        rep,
        rep,
        rep,
        P(None, None, STATE),
        rep,
        rep,
        P(None, None, STATE),
        rep,
        rep,
        rep,
        rep,
        rep,
        rep,
        P(None, None, STATE),
        P(None, STATE),
    )
    out_specs = (
        P(SEQ, None),
        P(SEQ, None),
        P(SEQ),
        P(SEQ, None),
        P(SEQ, None, None),
        P(SEQ, None, STATE),
        P(SEQ, None),
        rep,
        P(None, None, STATE),
        rep,
        rep,
        rep,
        P(SEQ),
        P(SEQ, None),
        P(SEQ),
        P(SEQ, None, STATE),
        P(SEQ, STATE),
    )
    return jax.shard_map(local, mesh=mesh, in_specs=in_specs, out_specs=out_specs, check_vma=False)
```

```python
import functools
import math
import types

import jax
import jax.numpy as jnp
from jax import lax
from jax.experimental import pallas as pl
from jax.experimental.pallas import tpu as pltpu
from jax.sharding import PartitionSpec as P

QUERY_HEADS = 8
KEY_VALUE_HEADS = 2
HEAD_SIZE = 64
NH = 24
HDM = 64
KC = 4
EPSILON = 1e-05
ROPE_BASE = 10000.0
HI = lax.Precision.HIGHEST
F32 = jnp.float32
BF16 = jnp.bfloat16
LANES = 128
HALO = 16
FAR = -1e30
MESH = pl.DeviceIdType.MESH
SEQ, STATE = "seq", "state"
VMEM_LIMIT = 63 << 20


def nn(a, b, p=None):
    return lax.dot_general(a, b, (((1,), (0,)), ((), ())), precision=p, preferred_element_type=F32)


def nt(a, b, p=None):
    return lax.dot_general(a, b, (((1,), (1,)), ((), ())), precision=p, preferred_element_type=F32)


def tn(a, b, p=None):
    return lax.dot_general(a, b, (((0,), (0,)), ((), ())), precision=p, preferred_element_type=F32)


def sigmoid(v):
    return 1.0 / (1.0 + jnp.exp(-v))


def silu(v):
    return v * sigmoid(v)


def silu_slope(v):
    s = sigmoid(v)
    return s * (1.0 + v * (1.0 - s))


def softplus(v):
    return jnp.maximum(v, 0.0) + jnp.log1p(jnp.exp(-jnp.abs(v)))


def iota(shape, dim):
    return lax.broadcasted_iota(jnp.int32, shape, dim)


def doc_of(starts, pos):
    found = jnp.full(pos.shape, -1, jnp.int32)
    for start in starts:
        found = found + (pos >= start).astype(jnp.int32)
    return found


def roll(v, shift):
    return pltpu.roll(v, shift, 1)


def rope(v, cosine, sine, direction):
    first = (iota(v.shape, 1) % HEAD_SIZE) < HEAD_SIZE // 2
    half = HEAD_SIZE // 2
    partner = jnp.where(first, -roll(v, v.shape[1] - half), roll(v, half))
    return v * cosine + partner * (direction * sine)


def expander(width):
    return (iota((LANES, width), 1) // HDM == iota((LANES, width), 0)).astype(F32)


def masks_of(starts, first_row, rows):
    pos = first_row + iota((rows, 1), 0)
    doc = doc_of(starts, pos)
    masks = [(doc_of(starts, pos - (KC - 1 - k)) == doc).astype(F32) for k in range(KC)]
    return doc, masks


def push(src, dst, send_sem, recv_sem, device):
    copy = pltpu.make_async_remote_copy(
        src_ref=src,
        dst_ref=dst,
        send_sem=send_sem,
        recv_sem=recv_sem,
        device_id=device,
        device_id_type=MESH,
    )
    copy.start()
    return copy


def greet(n, ns, s, t):
    barrier = pltpu.get_barrier_semaphore()

    def seq_turn(k, carried):
        pl.semaphore_signal(barrier, inc=1, device_id={SEQ: lax.rem(s + k, n)}, device_id_type=MESH)
        return carried

    lax.fori_loop(1, n, seq_turn, 0)
    for k in range(1, ns):
        other = lax.rem(t + k, ns)
        pl.semaphore_signal(barrier, inc=1, device_id={STATE: other}, device_id_type=MESH)
        pl.semaphore_signal(
            barrier, inc=1, device_id={SEQ: lax.rem(s + 1, n), STATE: other}, device_id_type=MESH
        )
    return lambda: pl.semaphore_wait(barrier, n - 1 + 2 * (ns - 1))


def conv_ref(ext_ref, taps, masks, rows):
    total = 0.0
    for k in range(KC):
        at = HALO - KC + 1 + k
        total = total + ext_ref[at : at + rows, :] * taps[k : k + 1] * masks[k]
    return total


class Carry:
    def __init__(self, refs, window, n, s, direction, rows_e):
        self.n, self.s, self.direction, self.rows_e = n, s, direction, rows_e
        self.tx, self.rx, self.thr_tx, self.thr_rx = refs.tx, refs.rx, refs.thr_tx, refs.thr_rx
        self.send, self.recv = refs.sem
        self.thr_send, self.thr_recv = refs.thr_sem
        self.total, self.thr = window
        self.count = carry_steps(n)

    def place(self, slot):
        return (1, 0) if slot == 0 else (2, 0) if slot == 1 else (1 << (slot - 1), slot - 1)

    def copies(self, slot, d, source):
        to = lax.rem(self.s + self.direction * d + self.n, self.n)
        make = lambda src, dst, a, b: pltpu.make_async_remote_copy(
            src_ref=src,
            dst_ref=dst,
            send_sem=a,
            recv_sem=b,
            device_id={SEQ: to},
            device_id_type=MESH,
        )
        return (
            make(self.tx.at[source], self.rx.at[slot], self.send.at[slot], self.recv.at[slot]),
            make(
                self.thr_tx.at[source],
                self.thr_rx.at[slot],
                self.thr_send.at[slot],
                self.thr_recv.at[slot],
            ),
        )

    def inside(self, index):
        return (index >= 0) & (index < self.n)

    def start(self, slot, d, source):
        @pl.when(self.inside(self.s + self.direction * d))
        def _():
            for copy in self.copies(slot, d, source):
                copy.start()

    def finish(self):
        for slot in range(self.count):
            d, source = self.place(slot)

            @pl.when(self.inside(self.s + self.direction * d))
            def _():
                for copy in self.copies(slot, d, source):
                    copy.wait_send()

    def begin(self, part, thr):
        self.tx[0] = part.astype(BF16)
        self.thr_tx[0] = thr
        self.total[...] = jnp.zeros(self.total.shape, F32)
        self.thr[...] = jnp.ones(self.thr.shape, F32)
        for slot in range(min(2, self.count)):
            self.start(slot, *self.place(slot))

    def join(self, slot, d, source):
        @pl.when(self.inside(self.s - self.direction * d))
        def _():
            for copy in self.copies(slot, d, source):
                copy.wait_recv()
            column = nt(self.rows_e, self.thr[...], HI)[:, :1]
            self.total[...] += column * self.rx[slot].astype(F32)
            self.thr[...] = self.thr[...] * self.thr_rx[slot]

        @pl.when(jnp.logical_not(self.inside(self.s - self.direction * d)))
        def _():
            self.thr[...] = jnp.zeros(self.thr.shape, F32)

    def pass_on(self, slot, d):
        self.tx[slot - 1] = self.total[...].astype(BF16)
        self.thr_tx[slot - 1] = self.thr[...]
        self.start(slot, d, slot - 1)

    def advance(self, slot):
        self.join(slot, *self.place(slot))
        if 1 <= slot < self.count - 1:
            self.pass_on(slot + 1, 1 << slot)

    def rest(self, first):
        if first >= self.count:
            return
        for slot in range(first, min(2, self.count)):
            self.advance(slot)
        first = max(first, 2)

        def turn(slot, d):
            self.join(slot, d, slot - 1)
            self.pass_on(slot + 1, 2 * d)
            return 2 * d

        if first < self.count:
            lax.fori_loop(first, self.count - 1, turn, 1 << (first - 1))
            self.join(self.count - 1, 1 << (self.count - 2), self.count - 2)


def carry_steps(n):
    return 1 if n <= 2 else 1 + (n - 2).bit_length()


def expand_rows(width):
    return (iota((width, LANES), 0) // HDM == iota((width, LANES), 1)).astype(F32)


def link_of(linked, cum, cum_t, h):
    return jnp.exp(jnp.where(linked, cum[:, h : h + 1] - cum_t[h : h + 1, :], FAR))


def send_to(sems, k, src, dst, device):
    send, recv = sems
    return push(src, dst, send.at[k], recv.at[k], device)


def row_sums(values):
    return nt(jnp.ones((8, values.shape[1]), F32), values, HI)


def as_column(row):
    first = (iota((8, LANES), 0) == 0).astype(F32)
    return tn(row, first, HI)[:, :1]


def share_rows(refs, ns, t, row):
    tx, rx = refs.tx, refs.rx
    tx[...] = row
    copies = [
        send_to(refs.sem, k - 1, tx, rx.at[k - 1], {STATE: lax.rem(t + k, ns)})
        for k in range(1, ns)
    ]

    def wait():
        total = tx[...]
        for k in range(1, ns):
            copies[k - 1].wait_recv()
            total = total + rx[k - 1]
        return total

    return copies, wait


class RowScatter:
    def __init__(self, refs, sem, t):
        self.sem, self.t = sem, t
        self.tx, self.rx, self.mid = refs.tx, refs.rx, refs.mid
        self.odd, self.far = lax.rem(t, 2), t // 2
        self.copies = []

    def start(self, part):
        rows = self.tx.shape[1]
        part = part.astype(BF16)
        for k in range(4):
            self.tx[(k % 2) * 2 + k // 2] = part[rows * k : rows * (k + 1)]
        theirs = self.tx.at[pl.ds(2 - 2 * self.odd, 2)]
        self.copies.append(
            send_to(self.sem, 0, theirs, self.rx.at[pl.ds(0, 2)], {STATE: sibling(self.t)})
        )

    def middle(self):
        self.copies[0].wait_recv()
        away = 1 - self.far
        self.mid[...] = (
            self.tx[2 * self.odd + away].astype(F32) + self.rx[away].astype(F32)
        ).astype(BF16)
        self.copies.append(
            send_to(self.sem, 1, self.mid, self.rx.at[2], {STATE: lax.rem(self.t + 2, 4)})
        )

    def finish(self):
        total = self.tx[2 * self.odd + self.far].astype(F32) + self.rx[self.far].astype(F32)
        self.copies[1].wait_recv()
        return total + self.rx[2].astype(F32)


class Gather:
    def __init__(self, block, sem, t):
        self.block, self.sem, self.t = block, sem, t
        own = block(t)
        self.copies = [
            send_to(sem, 0, own, own, {STATE: sibling(t)}),
            send_to(sem, 1, own, own, {STATE: lax.rem(t + 2, 4)}),
        ]

    def middle(self):
        self.copies[1].wait_recv()
        block = self.block(lax.rem(self.t + 2, 4))
        self.copies.append(send_to(self.sem, 2, block, block, {STATE: sibling(self.t)}))

    def finish(self):
        self.copies[0].wait_recv()
        self.copies[2].wait_recv()


def gather(every, sem, t, own):
    every[t] = own
    return Gather(lambda index: every.at[index], sem, t)


def sibling(t):
    return t + 1 - 2 * lax.rem(t, 2)


def levels_of(n):
    return n.bit_length() - 1


def bits_of(n, swapped):
    order = list(range(levels_of(n)))
    if swapped and len(order) > 1:
        order[0], order[1] = order[1], order[0]
    return order


class HalvingSum:
    def __init__(self, refs, n, s, swapped=False):
        self.sem, self.n, self.s = refs.sem, n, s
        self.bits = bits_of(n, swapped)
        self.src, self.rx = refs.src, refs.rx
        self.copies = []

    def owner(self, p):
        top = len(self.bits) - 1
        return sum(((p >> (top - level)) & 1) << bit for level, bit in enumerate(self.bits))

    def block_of(self, index):
        top = len(self.bits) - 1
        return sum(((index >> bit) & 1) << (top - level) for level, bit in enumerate(self.bits))

    def fill(self, column, values):
        rows = self.src.shape[1]
        width = values.shape[1]
        for p in range(self.n):
            at = rows * self.owner(p)
            self.src[p, :, column : column + width] = values[at : at + rows]

    def parts(self, level):
        half = self.n >> (level + 1)
        mine = lax.rem(self.s // (1 << self.bits[level]), 2)
        if level == 0:
            return self.src, 0, half, mine
        return self.rx, self.n - (self.n >> (level - 1)), half, mine

    def start(self, level=0):
        buffer, base, half, mine = self.parts(level)
        to = self.s + (1 - 2 * mine) * (1 << self.bits[level])
        here = self.n - (self.n >> level)
        self.copies.append(
            send_to(
                self.sem,
                level,
                buffer.at[pl.ds(base + (1 - mine) * half, half)],
                self.rx.at[pl.ds(here, half)],
                {SEQ: to},
            )
        )

    def step(self, level):
        buffer, base, half, mine = self.parts(level)
        self.copies[level].wait_recv()
        here = self.n - (self.n >> level)

        def turn(i, carried):
            kept = buffer[base + mine * half + i].astype(F32)
            self.rx[here + i] = (kept + self.rx[here + i].astype(F32)).astype(BF16)
            return carried

        lax.fori_loop(0, half, turn, 0)
        if level + 1 < len(self.bits):
            self.start(level + 1)

    def result(self):
        return self.rx[self.n - 2]


def named(value):
    if isinstance(value, dict):
        return types.SimpleNamespace(**{key: named(item) for key, item in value.items()})
    return value


def layer_kernel(n, ns, trees, *flat):
    refs, at = types.SimpleNamespace(), 0
    for tree in trees:
        part = jax.tree.unflatten(tree, flat[at : at + tree.num_leaves])
        at += tree.num_leaves
        refs.__dict__.update(named(part).__dict__)
    x, normed, inv1 = refs.x, refs.normed, refs.inv1
    w_mix, w_qkv, w_joint, w_gu, down = refs.w_mix, refs.w_qkv, refs.w_joint, refs.w_gu, refs.down
    grad = refs.grad
    w_step = refs.w_step
    T, D = x.shape
    t, s = lax.axis_index(STATE), lax.axis_index(SEQ)
    joined = refs.jall_all.at[t]
    C = w_mix.shape[2]
    QC = 2 * HEAD_SIZE
    AQ = QUERY_HEADS * HEAD_SIZE
    NW = refs.st_own.shape[1]
    HL = NH // ns
    N = NW * ns
    TO = T // ns
    DM = C * ns
    F = down.shape[1]
    pairs = C // LANES
    scale = 1.0 / math.sqrt(HEAD_SIZE)
    state_peer = lambda k: {STATE: lax.rem(t + k, ns)}
    own_c = pl.ds(pl.multiple_of(C * t, LANES), C)
    loads = [
        pltpu.make_async_copy(src, dst, refs.load[k])
        for k, (src, dst) in enumerate(
            [
                (refs.w_att.at[:, pl.ds(pl.multiple_of(QC * t, LANES), QC)], w_qkv.at[:, pl.ds(0, QC)]),
                (refs.w_att.at[:, pl.ds(AQ, 2 * QC)], w_qkv.at[:, pl.ds(QC, 2 * QC)]),
                (refs.w_mix_in.at[:, :, own_c], refs.raw),
                (refs.joint.at[pl.ds(pl.multiple_of(QC * t, QC), QC)], w_joint.at[pl.ds(0, QC)]),
                (refs.joint.at[pl.ds(pl.multiple_of(AQ + C * t, LANES), C)], w_joint.at[pl.ds(QC, C)]),
                (refs.g, grad),
                (refs.down_in, down),
                (refs.w_gu_in.at[:, :, pl.ds(0, F // 2)], refs.raw.at[:, :, pl.ds(0, F // 2)]),
                (refs.w_gu_in.at[:, :, pl.ds(F // 2, F // 2)], refs.raw.at[:, :, pl.ds(0, F // 2)]),
            ]
        )
    ]
    for load in loads[:-2]:
        load.start()
    lanes_row = iota((1, LANES), 1)
    blank = jnp.zeros((1, LANES), F32)
    met = greet(n, ns, s, t)
    bias_row, rate_row = blank, blank
    skip_row = jnp.zeros((1, C), F32)
    heads_row = iota((1, C), 1) // HDM
    for h in range(HL):
        bias_row = jnp.where(lanes_row == h, refs.step_bias[HL * t + h], bias_row)
        rate_row = jnp.where(lanes_row == h, refs.decay_rate[HL * t + h], rate_row)
        skip_row = jnp.where(heads_row == h, refs.skip_gain[HL * t + h], skip_row)
    taps_mix = refs.conv_mixer[:, own_c]
    ggain_row = jnp.concatenate(
        [refs.ggain[pl.ds(C // LANES * t + k, 1), :] for k in range(C // LANES)], axis=1
    )
    pick = (iota((NH, LANES), 0) == HL * t + iota((NH, LANES), 1)) & (iota((NH, LANES), 1) < HL)
    pick = pick.astype(F32)
    refs.taps8[...] = jnp.zeros(refs.taps8.shape, F32)
    for c in range(2):
        refs.taps8[:KC, NW * c : NW * (c + 1)] = refs.conv_state[:, c, :]
    eye8 = (iota((8, LANES), 0) == iota((8, LANES), 1)).astype(F32)
    taps_cols = tn(refs.taps8[...], eye8, HI)
    for c in range(2):
        refs.taps_st[c] = taps_cols[NW * c : NW * (c + 1)]
    sent = []
    mine = pl.ds(pl.multiple_of(NW * t, NW), NW)
    refs.st_all[:, mine, :] = refs.st_own[...]
    refs.taps_all[:, mine, :] = refs.taps_st[...]

    first_row = s * T
    starts = [refs.doc_starts[k] for k in range(refs.doc_starts.shape[0])]
    doc, masks = masks_of(starts, first_row, T)
    tiles = T // LANES

    def code_turn(j, carried):
        for i in range(tiles):
            real = refs.real[pl.ds(tiles * j + i, 1), :]
            ids = doc_of(starts, j * T + i * LANES + iota((1, LANES), 1))
            refs.codes[pl.ds(tiles * j + i, 1), :] = jnp.where(real > 0, ids, -7)
        return carried

    lax.fori_loop(0, n, code_turn, 0)

    def code_of(j):
        return jnp.concatenate([refs.codes[pl.ds(tiles * j + i, 1), :] for i in range(tiles)], axis=1)

    real_col = as_column(jnp.broadcast_to((code_of(s) >= 0).astype(F32), (8, T)))
    firsts = jnp.zeros((T, 1), jnp.int32)
    places = first_row + iota((T, 1), 0)
    for start in starts:
        firsts = jnp.where(places >= start, start, firsts)
    powers = (iota((1, LANES), 1) % (HEAD_SIZE // 2)).astype(F32) * (2.0 / HEAD_SIZE)
    angles = (places - firsts).astype(F32) * jnp.exp(-math.log(ROPE_BASE) * powers)
    cosine, sine = jnp.cos(angles), jnp.sin(angles)
    doc_row = doc_of(starts, first_row + iota((1, T), 1))
    lane = iota((T, LANES), 1)
    low = lane < HEAD_SIZE
    ngain = refs.ngain[...]

    met()
    halo_copy = pltpu.make_async_remote_copy(
        src_ref=x.at[pl.ds(T - HALO, HALO)],
        dst_ref=refs.halo_rx,
        send_sem=refs.halo[0].at[0],
        recv_sem=refs.halo[1].at[0],
        device_id={SEQ: lax.rem(s + 1, n)},
        device_id_type=MESH,
    )

    @pl.when(s + 1 < n)
    def _():
        halo_copy.start()

    columns = lambda every: lambda i: every.at[:, pl.ds(pl.multiple_of(NW * i, NW), NW), :]
    st_gather = Gather(columns(refs.st_all), refs.st, t)
    taps_gather = Gather(columns(refs.taps_all), refs.taps, t)
    xf = x[...].astype(F32)
    inv = lax.rsqrt(jnp.mean(xf * xf, axis=1, keepdims=True) + EPSILON)
    inv1[...] = inv
    normed[HALO:, :] = (xf * inv * ngain).astype(BF16)
    main = normed[HALO:, :]
    loads[0].wait()
    loads[1].wait()
    qkv = nn(main, w_qkv[...])
    q = (rope(qkv[:, :QC], cosine, sine, 1.0).astype(BF16) * scale).astype(F32)
    kcos, ksin = jnp.where(low, cosine, 1.0), jnp.where(low, sine, 0.0)
    kv_all = refs.kv_all
    group = t // 2
    both_k, both_v = qkv[:, QC : 2 * QC], qkv[:, 2 * QC :]
    own_kv = jnp.where(
        low,
        jnp.where(group == 0, both_k, roll(both_k, HEAD_SIZE)),
        jnp.where(group == 0, roll(both_v, HEAD_SIZE), both_v),
    )
    kv_all[s] = rope(own_kv, kcos, ksin, 1.0).astype(BF16)

    core = lax.rem(t, 2)
    H2 = T // 2
    own_half = pl.ds(pl.multiple_of(H2 * core, H2), H2)
    other_half = pl.ds(pl.multiple_of(H2 * (1 - core), H2), H2)

    def kv_copy(k):
        return pltpu.make_async_remote_copy(
            src_ref=kv_all.at[s, own_half],
            dst_ref=kv_all.at[s, own_half],
            send_sem=refs.kv[0].at[k - 1],
            recv_sem=refs.kv[1].at[k - 1],
            device_id={SEQ: lax.rem(s + k, n)},
            device_id_type=MESH,
        )

    def kv_pair(k):
        block = kv_all.at[s - k, own_half]
        return pltpu.make_async_remote_copy(
            src_ref=block,
            dst_ref=block,
            send_sem=refs.kv_fwd[0].at[k - 1],
            recv_sem=refs.kv_fwd[1].at[k - 1],
            device_id={STATE: sibling(t)},
            device_id_type=MESH,
        )

    def kv_turn(k, carried):
        kv_copy(k).start()
        return carried

    lax.fori_loop(1, n - s, kv_turn, 0)
    refs.q2[:T, :] = jnp.where(low, q, 0.0).astype(BF16)
    refs.q2[T:, :] = jnp.where(low, roll(q, HEAD_SIZE), 0.0).astype(BF16)
    raw = nn(nt(main, w_step[...]), pick, HI) + bias_row

    doc2 = jnp.concatenate([doc, doc], axis=0)
    m_ref, l_ref, acc_ref = refs.m_acc, refs.l_acc, refs.o_acc
    m_ref[...] = jnp.full(m_ref.shape, FAR, F32)
    l_ref[...] = jnp.zeros(l_ref.shape, F32)
    acc_ref[...] = jnp.zeros(acc_ref.shape, F32)

    def allowed_at(j, diagonal):
        allowed = code_of(j) == doc2
        if diagonal:
            rows2 = jnp.concatenate([iota((T, T), 0)] * 2, axis=0)
            cols2 = iota((2 * T, T), 1)
            allowed = (allowed & (cols2 <= rows2)) | (cols2 == rows2)
        return allowed

    def attend(j, diagonal):
        block = kv_all[j]
        scores = jnp.where(allowed_at(j, diagonal), nt(refs.q2[...], block), FAR)
        m = m_ref[...]
        m_new = jnp.maximum(m, jnp.max(scores, axis=1, keepdims=True))
        shrink = jnp.exp(m - m_new)
        p = jnp.exp(scores - m_new)
        l_ref[...] = l_ref[...] * shrink + jnp.sum(p, axis=1, keepdims=True)
        acc_ref[...] = acc_ref[...] * shrink + nn(p.astype(BF16), block)
        m_ref[...] = m_new

    def attend_turn(k, carried):
        @pl.when(k < s)
        def _():
            kv_copy(k + 1).wait_recv()
            kv_pair(k + 1).start()

        kv_pair(k).wait_recv()
        attend(s - k, False)
        return carried

    def attend_some(first, stop):
        lax.fori_loop(first, stop, attend_turn, 0)

    cut1, cut2 = 1 + (s + 1) // 3, 1 + (2 * s + 1) // 3
    attend(s, True)
    loads[2].wait()

    def split_mixer(c):
        def turn(k, carried):
            rows = pl.ds(pl.multiple_of(64 * k, 64), 64)
            w_mix[c, rows, :] = refs.raw[rows, c, :C]
            return carried

        lax.fori_loop(0, D // 64, turn, 0)

    split_mixer(1)
    taps_gather.middle()
    st_gather.middle()

    @pl.when(s > 0)
    def _():
        halo_copy.wait_recv()

    @pl.when(s == 0)
    def _():
        refs.halo_rx[...] = jnp.zeros(refs.halo_rx.shape, BF16)

    hf = refs.halo_rx[...].astype(F32)
    inv_h = lax.rsqrt(jnp.mean(hf * hf, axis=1, keepdims=True) + EPSILON)
    normed[:HALO, :] = (hf * inv_h * ngain).astype(BF16)
    ext_f, ext_s, ext_o = refs.ext_f, refs.ext_s, refs.ext_o
    ext_f[...] = nn(normed[...], w_mix[1]).astype(BF16).astype(F32)
    inner_lin = conv_ref(ext_f, taps_mix, masks, T)
    inner = silu(inner_lin)
    taps_gather.finish()
    st_gather.finish()
    for c in range(2):
        ext_s[...] = nt(normed[...], refs.st_all[c]).astype(BF16).astype(F32)
        taps = refs.taps_all[c].T
        refs.wr[c] = silu(conv_ref(ext_s, taps, masks, T))
    write, read = refs.wr[0], refs.wr[1]
    step = softplus(raw)
    causal = iota((T, T), 0) >= iota((T, T), 1)
    tri = causal.astype(F32)
    cum = nn(tri, -step * rate_row, HI)
    cum_t = cum.T
    linked = (doc == doc_row) & causal
    E = expander(C)
    rows_e = expand_rows(C)
    inflow = step * real_col
    inflow_e = nn(inflow, E, HI)
    in_x = inner * inflow_e
    cum_last = cum[T - 1 : T]
    last = first_row + T - 1
    doc_last = doc_of(starts, jnp.full((T, 1), last, jnp.int32))
    prior = doc_of(starts, jnp.full((T, 1), first_row - 1, jnp.int32))
    tail = jnp.where(doc == doc_last, jnp.exp(cum_last - cum), 0.0)
    refs.tail_e[...] = nn(tail, E, HI)
    state_part = tn(refs.tail_e[...] * in_x, write, HI)
    alive = (doc == prior).astype(F32)
    alive_last = (doc_last == prior).astype(F32)[:8]
    thr = alive_last * jnp.exp(jnp.broadcast_to(cum_last, (8, LANES)))
    steps = carry_steps(n)

    carry = Carry(refs.fc, (refs.window, refs.window_thr), n, s, 1, rows_e)
    carry.begin(state_part, thr)

    g_mat = nt(read, write, HI)
    for p in range(pairs):
        cols = slice(LANES * p, LANES * (p + 1))
        ys = []
        for h in (2 * p, 2 * p + 1):
            link = link_of(linked, cum, cum_t, h)
            ys.append(nn(link * g_mat, in_x[:, cols], HI))
        refs.ssd[:, cols] = jnp.where(low, ys[0], ys[1])

    split_mixer(0)
    loads[7].start()
    refs.z[...] = nn(main, w_mix[0])
    for slot in range(min(2, steps)):
        carry.advance(slot)

    @pl.when(s > 0)
    def _():
        kv_copy(1).wait_recv()
        kv_pair(1).start()

    attend_some(1, cut1)
    if steps > 2:
        carry.advance(2)
    attend_some(cut1, cut2)
    carry.rest(3)
    s_in = refs.window[...]
    refs.reach_e[...] = nn(alive * jnp.exp(cum), E, HI)
    ssd = refs.ssd[...] + refs.reach_e[...] * nt(read, s_in, HI)
    refs.ssd[...] = ssd
    z = refs.z[...]
    full_mix = ssd + skip_row * inner
    gated = full_mix * silu(z)
    copies, wait = share_rows(refs.sq, ns, t, row_sums(gated * gated))
    sent += copies
    attend_some(cut2, s + 1)
    out = acc_ref[...] / l_ref[...]
    acc_ref[...] = out
    m_ref[...] = m_ref[...] + jnp.log(l_ref[...])
    joined[:, :QC] = jnp.where(low, roll(out[:T], HEAD_SIZE), out[T:]).astype(BF16)
    loads[3].wait()
    loads[4].wait()
    loads[5].wait()
    loads[6].wait()
    dh = nn(grad[...], down[...])
    inv_g = as_column(lax.rsqrt(wait() / DM + EPSILON))
    joined[:, QC:] = (gated * inv_g * ggain_row).astype(BF16)
    rs1 = RowScatter(refs.rs1, refs.rs1_sem, t)
    rs1.start(nn(joined[...], w_joint[...]))
    own_rows = pl.ds(pl.multiple_of(TO * t, TO), TO)
    x_own = x[own_rows, :].astype(F32)
    rs1.middle()
    loads[7].wait()

    def split_columns(half):
        columns = slice(F // 2 * half, F // 2 * (half + 1))

        def turn(k, carried):
            rows = pl.ds(pl.multiple_of(64 * k, 64), 64)
            for c in range(2):
                w_gu[c, rows, columns] = refs.raw[rows, c, : F // 2]
            return carried

        lax.fori_loop(0, D // 64, turn, 0)

    split_columns(0)
    loads[8].start()
    res = x_own + rs1.finish()
    inv2 = lax.rsqrt(jnp.mean(res * res, axis=1, keepdims=True) + EPSILON)
    mgain = refs.mgain[...]
    ag1 = gather(refs.ag1_all, refs.ag1_sem, t, (res * inv2 * mgain).astype(BF16))
    loads[8].wait()
    split_columns(1)
    ag1.middle()
    jall = Gather(lambda index: refs.jall_all.at[index], refs.jall, t)
    ag1.finish()

    n2 = jnp.concatenate([refs.ag1_all[k] for k in range(ns)], axis=0)
    gate, up = nn(n2, w_gu[0]), nn(n2, w_gu[1])
    sig = sigmoid(gate)
    act = gate * sig
    hidden = (act * up).astype(BF16)
    d_gate = (dh * up * (sig * (1.0 + gate * (1.0 - sig)))).astype(BF16)
    d_up = (dh * act).astype(BF16)
    rs2 = RowScatter(refs.rs2, refs.rs2_sem, t)
    rs2.start(nt(d_gate, w_gu[0]) + nt(d_up, w_gu[1]))
    for copy in rs1.copies + ag1.copies:
        copy.wait_send()
    rs3 = RowScatter(refs.rs1, refs.rs3_sem, t)
    rs3.start(nt(hidden, down[...]))
    rs2.middle()

    def weight_sum(stream, parts, swapped=False):
        total = HalvingSum(stream, n, s, swapped)
        column = 0
        for lhs, rhs in parts:
            width = rhs.shape[1]
            for c in range(0, width, 256):
                piece = rhs[:, c : min(c + 256, width)]
                total.fill(column + c, tn(lhs, piece).astype(BF16))
            column += width
        return total

    sum_gate = weight_sum(refs.gate_g, [(n2, d_gate)], True)
    sum_gate.start()
    rs3.middle()
    sum_down = weight_sum(refs.down_g, [(grad[...], hidden)])
    sum_down.start()
    sum_up = weight_sum(refs.up_g, [(n2, d_up)])
    dn2 = rs2.finish()
    scaled = dn2 * mgain
    d_res = (
        grad[own_rows, :].astype(F32)
        + inv2 * scaled
        - res * inv2 * inv2 * inv2 * jnp.mean(scaled * res, axis=1, keepdims=True)
    )
    ag2 = gather(refs.ag2_all, refs.ag2_sem, t, d_res.astype(BF16))

    def put_small(row, values):
        for k in range(0, values.shape[1], LANES):
            piece = values[:, k : k + LANES]
            refs.small_tx[row : row + 1, : piece.shape[1]] = piece
            row += 1

    refs.small_tx[...] = jnp.zeros(refs.small_tx.shape, F32)
    refs.step_src[...] = jnp.zeros(refs.step_src.shape, F32)
    put_small(8, jnp.sum(dn2 * res * inv2, axis=0, keepdims=True))
    ag2.middle()
    ag3 = gather(refs.ag1_all, refs.ag3_sem, t, (res + rs3.finish()).astype(BF16))
    ag2.finish()
    d_branch = jnp.concatenate([refs.ag2_all[k] for k in range(ns)], axis=0)
    d_joined = nt(d_branch, w_joint[...])
    d_gn = d_joined[:, QC:]
    scaled = d_gn * ggain_row
    copies, wait = share_rows(refs.dot, ns, t, row_sums(scaled * gated))
    sent += copies
    put_small(16, jnp.sum(d_gn * gated * inv_g, axis=0, keepdims=True))
    d_att = d_joined[:, :QC].astype(BF16).astype(F32)
    dout2 = jnp.concatenate(
        [jnp.where(low, 0.0, roll(d_att, HEAD_SIZE)), jnp.where(low, 0.0, d_att)], axis=0
    )
    delta = jnp.sum(dout2 * acc_ref[...], axis=1, keepdims=True)
    l_ref[...] = delta
    refs.dout2[...] = dout2.astype(BF16)
    jall.middle()
    sum_down.step(0)
    sum_gate.step(0)
    jall.finish()
    own_d = pl.ds(pl.multiple_of((D // ns) * t, LANES), D // ns)
    d_cols = jnp.concatenate([refs.ag2_all[k, :, own_d] for k in range(ns)], axis=0)
    sum_joint = joint = HalvingSum(refs.joint_g, n, s)
    rows_j = joint.src.shape[1]
    piece = min(rows_j, LANES)
    for k in range(ns):
        values = tn(refs.jall_all[k], d_cols).astype(BF16)
        for at in range(0, QC + C, piece):
            row = QC * k + at if at < QC else AQ + C * k + at - QC
            offset = row % rows_j
            joint.src[joint.block_of(row // rows_j), offset : offset + piece, :] = values[at : at + piece]
    dot = as_column(wait() / DM)
    d_gated = inv_g * scaled - gated * (inv_g * inv_g * inv_g * dot)
    sig = sigmoid(z)
    dy = d_gated * z * sig
    refs.d_z[...] = (d_gated * full_mix * (sig * (1.0 + z * (1.0 - sig)))).astype(BF16)
    put_small(19, nt(jnp.broadcast_to(jnp.sum(dy * inner, axis=0, keepdims=True), (8, C)), E, HI)[:1])
    reach_dy = refs.reach_e[...] * dy
    carry_b = Carry(refs.bc, (refs.window, refs.window_thr), n, s, -1, rows_e)
    carry_b.begin(tn(reach_dy, read, HI), thr)
    sum_up.start()
    joint.start()
    sum_z = weight_sum(refs.z_g, [(main, refs.d_z[...])], True)
    ag3.middle()
    d_g = jnp.zeros((T, T), F32)
    for p in range(pairs):
        cols = slice(LANES * p, LANES * (p + 1))
        xp, dyp = in_x[:, cols], dy[:, cols]
        halves = []
        for k in range(2):
            link = link_of(linked, cum, cum_t, 2 * p + k)
            halves.append(tn(link * g_mat, dyp, HI))
            own = low if k == 0 else jnp.logical_not(low)
            d_g = d_g + link * nt(jnp.where(own, dyp, 0.0), xp, HI)
        refs.w_tot[:, cols] = jnp.where(low, halves[0], halves[1])

    d_read = nn(d_g, write, HI) + nn(reach_dy, s_in, HI)
    refs.dwr_tx[1] = d_read.T.astype(BF16)
    refs.d_write[...] = tn(d_g, read, HI)
    refs.dq2[...] = jnp.zeros(refs.dq2.shape, F32)

    def attend_back(j, diagonal):
        block = kv_all[j]
        q2, dout2 = refs.q2[...], refs.dout2[...]
        scores = jnp.where(allowed_at(j, diagonal), nt(q2, block), FAR)
        p = jnp.exp(scores - m_ref[...])
        ds = (p * (nt(dout2, block) - l_ref[...])).astype(BF16)
        refs.dq2[...] += nn(ds, block)
        return tn(ds, q2) + tn(p.astype(BF16), dout2)

    def dkv_copy(k):
        return pltpu.make_async_remote_copy(
            src_ref=refs.dkv_mid.at[k - 1],
            dst_ref=refs.dkv_rx.at[k - 1],
            send_sem=refs.dkv[0].at[k - 1],
            recv_sem=refs.dkv[1].at[k - 1],
            device_id={SEQ: lax.rem(s - k + n, n)},
            device_id_type=MESH,
        )

    def dkv_pair(k):
        return pltpu.make_async_remote_copy(
            src_ref=kv_all.at[s - k, other_half],
            dst_ref=refs.dkv_mid.at[lax.rem(k + n - 1, n)],
            send_sem=refs.dkv_fwd[0].at[k],
            recv_sem=refs.dkv_fwd[1].at[k],
            device_id={STATE: sibling(t)},
            device_id_type=MESH,
        )

    def dkv_on(k):
        dkv_pair(k).wait_recv()
        both = refs.dkv_mid[k - 1].astype(F32) + kv_all[s - k, own_half].astype(F32)
        refs.dkv_mid[k - 1] = both.astype(BF16)
        dkv_copy(k).start()

    def back_turn(k, carried):
        kv_all[s - k] = attend_back(s - k, False).astype(BF16)
        dkv_pair(k).start()

        @pl.when(k > 1)
        def _():
            dkv_on(k - 1)

        return carried

    def back_some(first, stop):
        lax.fori_loop(first, stop, back_turn, 0)

    def kv_end(k, carried):
        kv_copy(k).wait_send()
        return carried

    def pair_end(k, carried):
        kv_pair(k).wait_send()
        return carried

    lax.fori_loop(1, n - s, kv_end, 0)
    lax.fori_loop(1, s + 1, pair_end, 0)
    for slot in range(min(2, steps)):
        carry_b.advance(slot)
    back_some(1, cut1)
    if steps > 2:
        carry_b.advance(2)
    back_some(cut1, cut2)
    carry_b.rest(3)
    back_some(cut2, s + 1)
    diagonal = attend_back(s, True)
    refs.dkv_sum[...] = diagonal
    kv_all[s] = diagonal.astype(BF16)
    dkv_pair(0).start()

    @pl.when(s > 0)
    def _():
        dkv_on(s)

    sum_z.start()
    ag3.finish()
    for k in range(ns):
        refs.layer_output[TO * k : TO * (k + 1), :] = refs.ag1_all[k]
    sum_down.step(1)
    sum_gate.step(1)
    sum_up.step(0)
    later = refs.window[...]
    tail_e = refs.tail_e[...]
    tail_r = tail_e * nt(write, later, HI)
    w_tot = refs.w_tot[...] + tail_r
    d_write = refs.d_write[...] + nn(tail_e * in_x, later, HI)
    refs.dwr_tx[0] = d_write.T.astype(BF16)
    dwr = []
    for k in range(1, ns):
        p = lax.rem(t + k, ns)
        theirs = pl.ds(pl.multiple_of(NW * p, NW), NW)
        dwr.append(
            send_to(refs.dwr, k - 1, refs.dwr_tx.at[:, theirs, :], refs.dwr_rx.at[k - 1], {STATE: p})
        )
    sent += dwr
    d_lin = (inflow_e * w_tot + skip_row * dy) * silu_slope(inner_lin)

    def conv_back(ext, grad, taps, up, row, rows):
        grad[...] = jnp.zeros(grad.shape, F32)
        for k in range(KC):
            at = HALO - KC + 1 + k
            masked = up * masks[k]
            put_small(row + rows * k, jnp.sum(masked * ext[at : at + T, :], axis=0, keepdims=True))
            grad[at : at + T, :] += masked * taps[k : k + 1]
        return grad[...].astype(BF16)

    d_ext = conv_back(ext_f, refs.grad_f, taps_mix, d_lin, 22, C // LANES)
    st64 = refs.st_own[...].reshape(2 * NW, D)
    taps_own = refs.taps_st[...].reshape(2 * NW, LANES).T
    ext_o[...] = nt(normed[...], st64).astype(BF16).astype(F32)
    slope_o = silu_slope(conv_ref(ext_o, taps_own, masks, T))
    for copy in dwr:
        copy.wait_recv()
    d_wr = refs.dwr_tx[:, mine, :].astype(F32)
    for k in range(1, ns):
        d_wr = d_wr + refs.dwr_rx[k - 1].astype(F32)
    row_st = 22 + KC * (C // LANES)
    d_st = conv_back(ext_o, refs.grad_o, taps_own, d_wr.reshape(2 * NW, T).T * slope_o, row_st, 1)
    refs.back_tx[...] = (nt(d_ext[:HALO], w_mix[1]) + nn(d_st[:HALO], st64)).astype(BF16)
    def back_copy(member):
        return pltpu.make_async_remote_copy(
            src_ref=refs.back_tx,
            dst_ref=refs.back_rx.at[member],
            send_sem=refs.back[0].at[0],
            recv_sem=refs.back[1].at[member],
            device_id={SEQ: lax.rem(s + n - 1, n), STATE: ns - 1},
            device_id_type=MESH,
        )

    @pl.when(s > 0)
    def _():
        back_copy(t).start()

    sum_inner = weight_sum(refs.inner_g, [(normed[...], d_ext)])
    sum_inner.start()
    u = nt(inner * w_tot, E, HI)
    tl = nt(in_x * tail_r, E, HI)
    thr_s = jnp.sum(tn(later * s_in, rows_e, HI), axis=0, keepdims=True) * thr[:1]
    d_cum = nt(dy * ssd, E, HI) - inflow * u
    at_last = iota((T, LANES), 0) == T - 1
    d_cum = d_cum + jnp.where(at_last, jnp.sum(tl, axis=0, keepdims=True) + thr_s, 0.0)
    d_ld = tn(tri, d_cum, HI)
    d_step = real_col * u - rate_row * d_ld
    put_small(20, -jnp.sum(step * d_ld, axis=0, keepdims=True))
    d_step = d_step * sigmoid(raw)
    put_small(21, jnp.sum(d_step, axis=0, keepdims=True))
    d_step = d_step.astype(BF16)
    d_z = refs.d_z[...]
    dq2 = refs.dq2[...]
    dq = jnp.where(low, dq2[:T], roll(dq2[T:], HEAD_SIZE)) * scale
    d_q = rope(dq, cosine, sine, -1.0).astype(BF16)
    d_n = (
        nt(d_z, w_mix[0])
        + nt(d_ext[HALO:], w_mix[1])
        + nn(d_st[HALO:], st64)
        + nn(nt(d_step, pick.astype(BF16)).astype(BF16), w_step[...])
    )
    def dkv_turn(k, carried):
        dkv_copy(k).wait_recv()
        refs.dkv_half[...] += refs.dkv_rx[k - 1].astype(F32)
        return carried

    dkv_pair(0).wait_recv()
    refs.dkv_half[...] = refs.dkv_sum[own_half, :] + refs.dkv_mid[n - 1].astype(F32)
    lax.fori_loop(1, n - s, dkv_turn, 0)
    refs.pair_tx[...] = refs.dkv_half[...].astype(BF16)
    odd = core
    pair = send_to(refs.pair, 0, refs.pair_tx, refs.pair_rx, {STATE: sibling(t)})
    sent.append(pair)
    pair.wait_recv()
    refs.dkv_sum[own_half, :] = refs.pair_tx[...].astype(F32)
    refs.dkv_sum[other_half, :] = refs.pair_rx[...].astype(F32)
    d_kv = rope(refs.dkv_sum[...], kcos, ksin, -1.0)
    d_kv = jnp.where(low == (odd == 0), d_kv, 0.0)
    other = roll(d_kv, HEAD_SIZE)
    d_k = jnp.where(low, jnp.where(group == 0, d_kv, 0.0), jnp.where(group == 0, 0.0, other))
    d_v = jnp.where(low, jnp.where(group == 0, other, 0.0), jnp.where(group == 0, 0.0, d_kv))
    d_kv_b = d_kv.astype(BF16)
    d_qkv = jnp.concatenate([d_q, jnp.where(odd == 0, d_k, d_v).astype(BF16)], axis=1)
    mine_kv = jnp.where(odd == 0, d_kv, other).astype(BF16)
    pad_st = jnp.concatenate([jnp.zeros((T + HALO, HEAD_SIZE), F32), d_st.astype(F32)], axis=1)
    mine_kv = jnp.concatenate([jnp.zeros((HALO, LANES), F32), mine_kv.astype(F32)], axis=0)
    mixed = jnp.where(iota((T + HALO, LANES), 1) < HEAD_SIZE, mine_kv, pad_st).astype(BF16)
    sum_rest = weight_sum(refs.rest_g, [(main, d_q), (normed[...], mixed)])
    sum_rest.start()
    w_kv = jnp.where(odd == 0, w_qkv[:, QC : 2 * QC], w_qkv[:, 2 * QC :])
    d_n = d_n + nt(d_qkv, jnp.concatenate([w_qkv[:, :QC], w_kv], axis=1))
    for copy in rs2.copies + ag3.copies:
        copy.wait_send()
    rs4 = RowScatter(refs.rs2, refs.rs4_sem, t)
    rs4.start(d_n)
    sum_joint.step(0)
    rs4.middle()
    sum_z.step(0)
    sum_up.step(1)
    inv_own = inv1[own_rows, :]
    d_n = rs4.finish()
    last_rows = (t == ns - 1) & (s + 1 < n)

    @pl.when(last_rows)
    def _():
        for member in range(ns):
            back_copy(member).wait_recv()

    @pl.when(jnp.logical_not(last_rows))
    def _():
        refs.back_rx[...] = jnp.zeros(refs.back_rx.shape, BF16)

    from_next = refs.back_rx[0].astype(F32)
    for member in range(1, ns):
        from_next = from_next + refs.back_rx[member].astype(F32)
    d_n = jnp.concatenate([d_n[: TO - HALO], d_n[TO - HALO :] + from_next], axis=0)
    scaled = d_n * ngain
    in_g = (
        d_res
        + inv_own * scaled
        - x_own * inv_own * inv_own * inv_own * jnp.mean(scaled * x_own, axis=1, keepdims=True)
    )
    ag4 = gather(refs.ag1_all, refs.ag4_sem, t, in_g.astype(BF16))
    put_small(0, jnp.sum(d_n * x_own * inv_own, axis=0, keepdims=True))

    def small_copy(k):
        peer = lax.rem(s + k, n)
        make = lambda src, dst, at: pltpu.make_async_remote_copy(
            src_ref=src,
            dst_ref=dst,
            send_sem=refs.small[0].at[at],
            recv_sem=refs.small[1].at[at],
            device_id={SEQ: peer},
            device_id_type=MESH,
        )
        return (
            make(refs.small_tx, refs.small_rx.at[s, pl.ds(0, rows_c)], k - 1),
            make(refs.step_src.at[peer], refs.small_rx.at[s, pl.ds(rows_c, 8)], n + k - 2),
        )

    step_rows = tn(d_step, main)[:8]
    rows_c, rows_d = refs.small_tx.shape[0], D // n
    for k in range(n):
        refs.step_src[k, :, :rows_d] = step_rows[:, rows_d * k : rows_d * (k + 1)]
    refs.small_rx[s, :rows_c, :] = refs.small_tx[...]
    refs.small_rx[s, rows_c:, :] = refs.step_src[s]

    def small_turn(k, carried):
        for copy in small_copy(k):
            copy.start()
        return carried

    lax.fori_loop(1, n, small_turn, 0)
    last_level = len(bits_of(n, False)) - 1

    def steps_of(total, first, stop):
        for level in range(first, stop):
            total.step(level)

    sum_inner.step(0)
    sum_z.step(1)
    ag4.middle()
    sum_joint.step(1)
    sum_rest.step(0)
    steps_of(sum_down, 2, last_level + 1)
    steps_of(sum_gate, 2, last_level + 1)
    ag4.finish()
    for k in range(ns):
        refs.input_grad[TO * k : TO * (k + 1), :] = refs.ag1_all[k]
    steps_of(sum_up, 2, last_level + 1)
    steps_of(sum_z, 2, last_level + 1)
    gz = gather(refs.gz_all, refs.gz_sem, t, sum_z.result())
    sum_inner.step(1)
    steps_of(sum_joint, 2, last_level + 1)
    gj = gather(refs.gj_all, refs.gj_sem, t, sum_joint.result())
    sum_rest.step(1)
    gz.middle()
    steps_of(sum_inner, 2, last_level + 1)
    gi = gather(refs.gi_all, refs.gi_sem, t, sum_inner.result())
    gj.middle()
    steps_of(sum_rest, 2, last_level + 1)
    gr = gather(refs.gr_all, refs.gr_sem, t, sum_rest.result())

    def small_end(k, carried):
        for copy in small_copy(k):
            copy.wait_recv()
        return carried

    lax.fori_loop(1, n, small_end, 0)

    def small_sum(j, total):
        return total + refs.small_rx[j]

    small = gather(
        refs.sm_all, refs.sm_sem, t,
        lax.fori_loop(0, n, small_sum, jnp.zeros(refs.small_rx.shape[1:], F32)),
    )
    gi.middle()
    small.middle()
    refs.o_gu[0] = sum_gate.result()
    refs.o_gu[1] = sum_up.result()
    refs.o_down[...] = sum_down.result()
    gz.finish()
    gj.finish()
    gi.finish()
    gr.middle()
    for k in range(ns):
        refs.o_mix[0, :, C * k : C * (k + 1)] = refs.gz_all[k]
        refs.o_mix[1, :, C * k : C * (k + 1)] = refs.gi_all[k]
        refs.o_joint[:, (D // ns) * k : (D // ns) * (k + 1)] = refs.gj_all[k]
    small.finish()
    total = refs.sm_all[0, :16, :]
    for k in range(1, ns):
        total = total + refs.sm_all[k, :16, :]
    refs.o_gains[...] = total
    refs.o_small[...] = refs.sm_all[:, 16:rows_c, :]
    gr.finish()
    rows = refs.gr_all.shape[1]
    half = iota((rows, LANES), 1) < HEAD_SIZE
    for k in range(ns):
        refs.o_att[:, QC * k : QC * (k + 1)] = refs.gr_all[k, :, :QC]
        refs.o_step[HL * k : HL * (k + 1), :] = refs.sm_all[k, rows_c : rows_c + HL, :rows]
    for c in range(2):
        first = refs.gr_all[c, :, QC : 2 * QC].astype(F32)
        second = refs.gr_all[2 + c, :, QC : 2 * QC].astype(F32)
        refs.o_att[:, AQ + QC * c : AQ + QC * (c + 1)] = jnp.where(
            half, first, roll(second, HEAD_SIZE)
        ).astype(BF16)
    refs.o_st[...] = refs.gr_all[t, :, QC : 2 * QC]

    def small_sent(k, carried):
        for copy in small_copy(k):
            copy.wait_send()
        return carried

    lax.fori_loop(1, n, small_sent, 0)
    for group_of in (
        st_gather, taps_gather, jall, rs3, rs4, ag2, ag4, gz, gj, gi, gr, small,
        sum_gate, sum_up, sum_down, sum_z, sum_joint, sum_inner, sum_rest,
    ):
        sent += group_of.copies
    for copy in sent:
        copy.wait_send()

    @pl.when(s + 1 < n)
    def _():
        halo_copy.wait_send()

    @pl.when(s > 0)
    def _():
        back_copy(t).wait_send()

    carry.finish()
    carry_b.finish()

    def dkv_end(k, carried):
        dkv_copy(k).wait_send()
        return carried

    def dkv_pair_end(k, carried):
        dkv_pair(k).wait_send()
        return carried

    lax.fori_loop(1, s + 1, dkv_end, 0)
    lax.fori_loop(0, s + 1, dkv_pair_end, 0)


def layer(n, ns, arrays):
    inputs = types.SimpleNamespace(**arrays)
    T, D = inputs.x.shape
    C = inputs.w_mix_in.shape[2] // ns
    NW = inputs.st_own.shape[1]
    F = inputs.down_in.shape[1]
    N, TO, H = NW * ns, T // ns, NH // ns
    KJ = inputs.joint.shape[0]
    QC = 2 * HEAD_SIZE
    R, RJ = D // n, KJ // n
    steps = carry_steps(n)
    levels = levels_of(n)
    sd = jax.ShapeDtypeStruct
    J = QC + C
    SMALL = -(-(22 + KC * (C // LANES) + KC) // 8) * 8
    outs = dict(
        layer_output=sd((T, D), BF16),
        input_grad=sd((T, D), BF16),
        o_down=sd((R, F), BF16),
        o_gu=sd((2, R, F), BF16),
        o_mix=sd((2, R, ns * C), BF16),
        o_joint=sd((RJ, D), BF16),
        o_att=sd((R, inputs.w_att.shape[1]), BF16),
        o_step=sd((NH, R), F32),
        o_st=sd((R, LANES), BF16),
        o_gains=sd((16, LANES), F32),
        o_small=sd((ns, SMALL - 16, LANES), F32),
    )
    vm = pltpu.VMEM
    dma = lambda k: (pltpu.SemaphoreType.DMA((k,)), pltpu.SemaphoreType.DMA((k,)))
    blocks = lambda *shape: vm((ns,) + shape, BF16)

    def scan():
        return dict(
            tx=vm((max(1, steps - 1), C, N), BF16),
            rx=vm((steps, C, N), BF16),
            thr_tx=vm((max(1, steps - 1), 8, LANES), F32),
            thr_rx=vm((steps, 8, LANES), F32),
            sem=dma(steps),
            thr_sem=dma(steps),
        )

    def rows():
        return dict(tx=vm((8, T), F32), rx=vm((ns - 1, 8, T), F32), sem=dma(ns - 1))

    def scatter():
        return dict(tx=blocks(TO, D), rx=vm((3, TO, D), BF16), mid=vm((TO, D), BF16))

    def stream(*shape):
        return dict(src=vm((n,) + shape, BF16), rx=vm((n - 1,) + shape, BF16), sem=dma(levels))

    scratch = dict(
        w_qkv=vm((D, 3 * QC), BF16),
        w_joint=vm((J, D), BF16),
        w_mix=vm((2, D, C), BF16),
        w_gu=vm((2, D, F), BF16),
        raw=vm((D, 2, max(C, F // 2)), BF16),
        down=vm((D, F), BF16),
        grad=vm((T, D), BF16),
        load=tuple(pltpu.SemaphoreType.DMA for _ in range(9)),
        taps8=vm((8, LANES), F32),
        taps_st=vm((2, NW, LANES), F32),
        codes=vm((n * T // LANES, LANES), jnp.int32),
        halo_rx=vm((HALO, D), BF16),
        st_all=vm((2, N, D), BF16),
        taps_all=vm((2, N, LANES), F32),
        kv_all=vm((n, T, LANES), BF16),
        normed=vm((T + HALO, D), BF16),
        inv1=vm((T, 1), F32),
        q2=vm((2 * T, LANES), BF16),
        z=vm((T, C), F32),
        ext_f=vm((T + HALO, C), F32),
        ext_s=vm((T + HALO, N), F32),
        ext_o=vm((T + HALO, 2 * NW), F32),
        grad_f=vm((T + HALO, C), F32),
        grad_o=vm((T + HALO, 2 * NW), F32),
        wr=vm((2, T, N), F32),
        tail_e=vm((T, C), F32),
        reach_e=vm((T, C), F32),
        ssd=vm((T, C), F32),
        w_tot=vm((T, C), F32),
        d_z=vm((T, C), BF16),
        jall_all=vm((ns, T, J), BF16),
        window=vm((C, N), F32),
        window_thr=vm((8, LANES), F32),
        m_acc=vm((2 * T, 1), F32),
        l_acc=vm((2 * T, 1), F32),
        o_acc=vm((2 * T, LANES), F32),
        dout2=vm((2 * T, LANES), BF16),
        dq2=vm((2 * T, LANES), F32),
        dkv_rx=vm((n, T // 2, LANES), BF16),
        dkv_mid=vm((n, T // 2, LANES), BF16),
        dkv_half=vm((T // 2, LANES), F32),
        dkv_sum=vm((T, LANES), F32),
        pair_tx=vm((T // 2, LANES), BF16),
        pair_rx=vm((T // 2, LANES), BF16),
        back_tx=vm((HALO, D), BF16),
        back_rx=vm((ns, HALO, D), BF16),
        dwr_tx=vm((2, N, T), BF16),
        d_write=vm((T, N), F32),
        dwr_rx=vm((ns - 1, 2, NW, T), BF16),
        small_tx=vm((SMALL, LANES), F32),
        step_src=vm((n, 8, LANES), F32),
        small_rx=vm((n, SMALL + 8, LANES), F32),
        halo=dma(1),
        st=dma(3),
        taps=dma(3),
        kv=dma(n - 1),
        kv_fwd=dma(n - 1),
        dkv=dma(n - 1),
        dkv_fwd=dma(n),
        jall=dma(3),
        pair=dma(1),
        back=dma(ns),
        dwr=dma(ns - 1),
        small=dma(2 * n - 2),
        sm_all=vm((ns, SMALL + 8, LANES), F32),
        fc=scan(),
        bc=scan(),
        sq=rows(),
        dot=rows(),
        rs1=scatter(),
        rs2=scatter(),
        rs1_sem=dma(2),
        rs2_sem=dma(2),
        rs3_sem=dma(2),
        rs4_sem=dma(2),
        ag1_all=blocks(TO, D),
        ag2_all=blocks(TO, D),
        gz_all=blocks(R, C),
        gi_all=blocks(R, C),
        gr_all=blocks(R, 2 * LANES),
        gj_all=blocks(RJ, D // ns),
        ag1_sem=dma(3),
        ag2_sem=dma(3),
        ag3_sem=dma(3),
        ag4_sem=dma(3),
        gz_sem=dma(3),
        gi_sem=dma(3),
        gr_sem=dma(3),
        gj_sem=dma(3),
        sm_sem=dma(3),
        gate_g=stream(R, F),
        up_g=stream(R, F),
        down_g=stream(R, F),
        z_g=stream(R, C),
        inner_g=stream(R, C),
        rest_g=stream(R, 2 * LANES),
        joint_g=stream(RJ, D // ns),
    )
    whole = pl.BlockSpec(memory_space=pltpu.VMEM)
    small = pl.BlockSpec(memory_space=pltpu.SMEM)
    far = pl.BlockSpec(memory_space=pl.ANY)
    specs = {key: whole for key in arrays}
    specs.update(doc_starts=small, step_bias=small, decay_rate=small, skip_gain=small)
    specs.update(w_att=far, joint=far, g=far, w_mix_in=far, w_gu_in=far, down_in=far)
    flat = [jax.tree.flatten(group) for group in (arrays, outs, scratch)]
    got = pl.pallas_call(
        functools.partial(layer_kernel, n, ns, [tree for _, tree in flat]),
        out_shape=flat[1][0],
        in_specs=jax.tree.flatten(specs)[0],
        out_specs=[whole] * len(outs),
        scratch_shapes=flat[2][0],
        name="layer",
        compiler_params=pltpu.CompilerParams(
            collective_id=1, has_side_effects=True, vmem_limit_bytes=VMEM_LIMIT
        ),
    )(*flat[0][0])
    return types.SimpleNamespace(**jax.tree.unflatten(flat[1][1], got))


def finish_kernel(n, ns, tree_in, tree_out, *flat):
    split = tree_in.num_leaves
    o = named(jax.tree.unflatten(tree_in, flat[:split]))
    out = named(jax.tree.unflatten(tree_out, flat[split:]))
    t, s = lax.axis_index(STATE), lax.axis_index(SEQ)
    HL, C = NH // ns, NH * HDM // ns
    per = C // LANES
    NW = out.taps_st.shape[2]
    R = out.down.shape[0]
    out.layer_output[...] = o.layer_output[...]
    out.input_grad[...] = o.input_grad[...].astype(F32)
    out.att[...] = o.o_att[...].astype(F32)
    out.joint[...] = o.o_joint[...].astype(F32)
    out.down[...] = o.o_down[...].astype(F32)
    out.step[...] = o.o_step[...]
    turned = o.o_st[...].astype(F32).T
    for c in range(2):
        out.mix[:, c, :] = o.o_mix[c].astype(F32)
        out.gu[:, c, :] = o.o_gu[c].astype(F32)
        at = HEAD_SIZE + NW * c
        out.st[c] = turned[at : at + NW]
    small = o.o_small

    def part(row, width, count):
        at = s * width
        first = at // LANES
        lanes = jnp.concatenate([row(first + k) for k in range(count)], axis=1)
        return roll(lanes, lax.rem(count * LANES - (at - first * LANES), count * LANES))[:, :width]

    for at, dst in ((0, out.ngain), (8, out.mgain)):
        dst[...] = part(lambda k: o.o_gains[pl.ds(at + k, 1), :], R, 1)
    for k in range(ns):
        for i in range(per):
            out.gains[per * k + i : per * k + i + 1, :] = small[k, i : i + 1, :]
    width = out.ggain.shape[1]
    last = ns * per - 1
    out.ggain[...] = part(lambda k: out.gains[pl.ds(jnp.minimum(k, last), 1), :], width, 3)
    heads = 0.0
    for k in range(ns):
        into = (iota((LANES, LANES), 1) == HL * k + iota((LANES, LANES), 0)) & (
            iota((LANES, LANES), 0) < HL
        )
        heads = heads + nn(small[k, :8, :], into.astype(F32), HI)
        for j in range(KC):
            for i in range(per):
                row = 6 + per * j + i
                at = C * k + LANES * i
                out.taps[j : j + 1, at : at + LANES] = small[k, row : row + 1, :]
    out.skip[...], out.rate[...], out.bias[...] = (heads[k : k + 1, :NH] for k in (3, 4, 5))
    for j in range(KC):
        row = small[t, 6 + KC * per + j : 7 + KC * per + j, :]
        for c in range(2):
            out.taps_st[j, c : c + 1, :] = row[:, NW * c : NW * (c + 1)]


def finish(n, ns, o, shapes):
    sd = lambda *shape: jax.ShapeDtypeStruct(shape, F32)
    R, F = o.o_down.shape
    T, D = o.layer_output.shape
    NW = shapes.NW
    outs = dict(
        layer_output=jax.ShapeDtypeStruct((T, D), BF16),
        input_grad=sd(T, D),
        att=sd(*o.o_att.shape),
        joint=sd(*o.o_joint.shape),
        down=sd(R, F),
        step=sd(NH, R),
        mix=sd(R, 2, NH * HDM),
        gu=sd(R, 2, F),
        st=sd(2, NW, R),
        ngain=sd(1, R),
        mgain=sd(1, R),
        ggain=sd(1, NH * HDM // n),
        gains=sd(NH * HDM // LANES, LANES),
        taps=sd(KC, NH * HDM),
        taps_st=sd(KC, 2, NW),
        skip=sd(1, NH),
        rate=sd(1, NH),
        bias=sd(1, NH),
    )
    arrays = dict(o.__dict__)
    flat = [jax.tree.flatten(group) for group in (arrays, outs)]
    whole = pl.BlockSpec(memory_space=pltpu.VMEM)
    got = pl.pallas_call(
        functools.partial(finish_kernel, n, ns, flat[0][1], flat[1][1]),
        out_shape=flat[1][0],
        in_specs=[whole] * len(arrays),
        out_specs=[whole] * len(outs),
        name="finish",
        compiler_params=pltpu.CompilerParams(vmem_limit_bytes=VMEM_LIMIT),
    )(*flat[0][0])
    return types.SimpleNamespace(**jax.tree.unflatten(flat[1][1], got))


def local(
    layer_input,
    out_grad,
    doc_starts,
    real_mask,
    norm_gain,
    attention_input_rows,
    mixer_in,
    state_in,
    step_in,
    conv_mixer,
    conv_state,
    step_bias,
    decay_rate,
    skip_gain,
    gated_gain,
    joint_out,
    mlp_gain,
    gate_up,
    down_weight,
):
    T, D = layer_input.shape
    NS, n = lax.axis_size(STATE), lax.axis_size(SEQ)
    NW = state_in.shape[2]
    o = layer(
        n,
        NS,
        dict(
            x=layer_input,
            g=out_grad,
            w_att=attention_input_rows,
            w_mix_in=mixer_in,
            w_step=step_in.T,
            st_own=jnp.transpose(state_in, (1, 2, 0)),
            conv_state=conv_state,
            conv_mixer=conv_mixer,
            ngain=norm_gain[None, :],
            ggain=gated_gain.reshape(-1, LANES),
            mgain=mlp_gain[None, :],
            joint=joint_out,
            w_gu_in=gate_up,
            down_in=down_weight,
            real=real_mask.reshape(-1, LANES),
            step_bias=step_bias,
            decay_rate=decay_rate,
            skip_gain=skip_gain,
            doc_starts=doc_starts,
        ),
    )
    e = finish(n, NS, o, types.SimpleNamespace(NW=NW))
    return (
        e.layer_output,
        e.input_grad,
        e.ngain.reshape(-1),
        e.att,
        e.mix,
        e.st.transpose(2, 0, 1),
        e.step.T,
        e.taps,
        e.taps_st,
        e.bias.reshape(-1),
        e.rate.reshape(-1),
        e.skip.reshape(-1),
        e.ggain.reshape(-1),
        e.joint,
        e.mgain.reshape(-1),
        e.gu,
        e.down,
    )


def solution(mesh):
    rep = P()
    in_specs = (
        P(SEQ, None),
        P(SEQ, None),
        rep,
        rep,
        rep,
        rep,
        rep,
        P(None, None, STATE),
        rep,
        rep,
        P(None, None, STATE),
        rep,
        rep,
        rep,
        rep,
        rep,
        rep,
        P(None, None, STATE),
        P(None, STATE),
    )
    out_specs = (
        P(SEQ, None),
        P(SEQ, None),
        P(SEQ),
        P(SEQ, None),
        P(SEQ, None, None),
        P(SEQ, None, STATE),
        P(SEQ, None),
        rep,
        P(None, None, STATE),
        rep,
        rep,
        rep,
        P(SEQ),
        P(SEQ, None),
        P(SEQ),
        P(SEQ, None, STATE),
        P(SEQ, STATE),
    )
    return jax.shard_map(local, mesh=mesh, in_specs=in_specs, out_specs=out_specs, check_vma=False)
```

```python
import functools
import math
import types

import jax
import jax.numpy as jnp
from jax import lax
from jax.experimental import pallas as pl
from jax.experimental.pallas import tpu as pltpu
from jax.sharding import PartitionSpec as P

QUERY_HEADS = 8
KEY_VALUE_HEADS = 2
HEAD_SIZE = 64
NH = 24
HDM = 64
KC = 4
EPSILON = 1e-05
ROPE_BASE = 10000.0
FINE, LEFT, RIGHT = 1, 2, 3
F32 = jnp.float32
BF16 = jnp.bfloat16
LANES = 128
HALO = 16
FAR = -1e30
MESH = pl.DeviceIdType.MESH
SEQ, STATE = "seq", "state"
VMEM_LIMIT = 63 << 20


def parts(v):
    high = v.astype(BF16)
    return high, (v - high.astype(F32)).astype(BF16)


def product(dims, a, b, mode):
    dot = lambda u, v: lax.dot_general(u, v, (dims, ((), ())), preferred_element_type=F32)
    if mode is None:
        return dot(a, b)
    if mode == LEFT:
        high, low = parts(b)
        a = a.astype(BF16)
        return dot(a, high) + dot(a, low)
    if mode == RIGHT:
        high, low = parts(a)
        b = b.astype(BF16)
        return dot(high, b) + dot(low, b)
    a_high, a_low = parts(a)
    b_high, b_low = parts(b)
    return dot(a_high, b_high) + (dot(a_high, b_low) + dot(a_low, b_high))


def nn(a, b, mode=None):
    return product(((1,), (0,)), a, b, mode)


def nt(a, b, mode=None):
    return product(((1,), (1,)), a, b, mode)


def tn(a, b, mode=None):
    return product(((0,), (0,)), a, b, mode)


def sigmoid(v):
    return 1.0 / (1.0 + jnp.exp(-v))


def silu(v):
    return v * sigmoid(v)


def silu_slope(v):
    s = sigmoid(v)
    return s * (1.0 + v * (1.0 - s))


def softplus(v):
    return jnp.maximum(v, 0.0) + jnp.log1p(jnp.exp(-jnp.abs(v)))


def iota(shape, dim):
    return lax.broadcasted_iota(jnp.int32, shape, dim)


def doc_of(starts, pos):
    found = jnp.full(pos.shape, -1, jnp.int32)
    for start in starts:
        found = found + (pos >= start).astype(jnp.int32)
    return found


def roll(v, shift):
    return pltpu.roll(v, shift, 1)


def rope(v, cosine, sine, direction):
    first = (iota(v.shape, 1) % HEAD_SIZE) < HEAD_SIZE // 2
    half = HEAD_SIZE // 2
    partner = jnp.where(first, -roll(v, v.shape[1] - half), roll(v, half))
    return v * cosine + partner * (direction * sine)


def expander(width):
    return (iota((LANES, width), 1) // HDM == iota((LANES, width), 0)).astype(F32)


def masks_of(starts, first_row, rows):
    pos = first_row + iota((rows, 1), 0)
    doc = doc_of(starts, pos)
    masks = [(doc_of(starts, pos - (KC - 1 - k)) == doc).astype(F32) for k in range(KC)]
    return doc, masks


def push(src, dst, send_sem, recv_sem, device):
    copy = pltpu.make_async_remote_copy(
        src_ref=src,
        dst_ref=dst,
        send_sem=send_sem,
        recv_sem=recv_sem,
        device_id=device,
        device_id_type=MESH,
    )
    copy.start()
    return copy


def greet(n, ns, s, t):
    barrier = pltpu.get_barrier_semaphore()

    def seq_turn(k, carried):
        pl.semaphore_signal(barrier, inc=1, device_id={SEQ: lax.rem(s + k, n)}, device_id_type=MESH)
        return carried

    lax.fori_loop(1, n, seq_turn, 0)
    for k in range(1, ns):
        other = lax.rem(t + k, ns)
        pl.semaphore_signal(barrier, inc=1, device_id={STATE: other}, device_id_type=MESH)
        pl.semaphore_signal(
            barrier, inc=1, device_id={SEQ: lax.rem(s + 1, n), STATE: other}, device_id_type=MESH
        )
    return lambda: pl.semaphore_wait(barrier, n - 1 + 2 * (ns - 1))


def conv_ref(ext_ref, taps, masks, rows):
    total = 0.0
    for k in range(KC):
        at = HALO - KC + 1 + k
        total = total + ext_ref[at : at + rows, :] * taps[k : k + 1] * masks[k]
    return total


class Carry:
    def __init__(self, refs, window, n, s, direction, rows_e):
        self.n, self.s, self.direction, self.rows_e = n, s, direction, rows_e
        self.tx, self.rx, self.thr_tx, self.thr_rx = refs.tx, refs.rx, refs.thr_tx, refs.thr_rx
        self.send, self.recv = refs.sem
        self.thr_send, self.thr_recv = refs.thr_sem
        self.total, self.thr = window
        self.count = carry_steps(n)

    def place(self, slot):
        return (1, 0) if slot == 0 else (2, 0) if slot == 1 else (1 << (slot - 1), slot - 1)

    def copies(self, slot, d, source):
        to = lax.rem(self.s + self.direction * d + self.n, self.n)
        make = lambda src, dst, a, b: pltpu.make_async_remote_copy(
            src_ref=src,
            dst_ref=dst,
            send_sem=a,
            recv_sem=b,
            device_id={SEQ: to},
            device_id_type=MESH,
        )
        return (
            make(self.tx.at[source], self.rx.at[slot], self.send.at[slot], self.recv.at[slot]),
            make(
                self.thr_tx.at[source],
                self.thr_rx.at[slot],
                self.thr_send.at[slot],
                self.thr_recv.at[slot],
            ),
        )

    def inside(self, index):
        return (index >= 0) & (index < self.n)

    def start(self, slot, d, source):
        @pl.when(self.inside(self.s + self.direction * d))
        def _():
            for copy in self.copies(slot, d, source):
                copy.start()

    def finish(self):
        for slot in range(self.count):
            d, source = self.place(slot)

            @pl.when(self.inside(self.s + self.direction * d))
            def _():
                for copy in self.copies(slot, d, source):
                    copy.wait_send()

    def begin(self, part, thr):
        self.tx[0] = part.astype(BF16)
        self.thr_tx[0] = thr
        self.total[...] = jnp.zeros(self.total.shape, F32)
        self.thr[...] = jnp.ones(self.thr.shape, F32)
        for slot in range(min(2, self.count)):
            self.start(slot, *self.place(slot))

    def join(self, slot, d, source):
        @pl.when(self.inside(self.s - self.direction * d))
        def _():
            for copy in self.copies(slot, d, source):
                copy.wait_recv()
            column = nt(self.rows_e, self.thr[...], LEFT)[:, :1]
            self.total[...] += column * self.rx[slot].astype(F32)
            self.thr[...] = self.thr[...] * self.thr_rx[slot]

        @pl.when(jnp.logical_not(self.inside(self.s - self.direction * d)))
        def _():
            self.thr[...] = jnp.zeros(self.thr.shape, F32)

    def pass_on(self, slot, d):
        self.tx[slot - 1] = self.total[...].astype(BF16)
        self.thr_tx[slot - 1] = self.thr[...]
        self.start(slot, d, slot - 1)

    def advance(self, slot):
        self.join(slot, *self.place(slot))
        if 1 <= slot < self.count - 1:
            self.pass_on(slot + 1, 1 << slot)

    def rest(self, first):
        if first >= self.count:
            return
        for slot in range(first, min(2, self.count)):
            self.advance(slot)
        first = max(first, 2)

        def turn(slot, d):
            self.join(slot, d, slot - 1)
            self.pass_on(slot + 1, 2 * d)
            return 2 * d

        if first < self.count:
            lax.fori_loop(first, self.count - 1, turn, 1 << (first - 1))
            self.join(self.count - 1, 1 << (self.count - 2), self.count - 2)


def carry_steps(n):
    return 1 if n <= 2 else 1 + (n - 2).bit_length()


def expand_rows(width):
    return (iota((width, LANES), 0) // HDM == iota((width, LANES), 1)).astype(F32)


def link_of(linked, cum, cum_t, h):
    return jnp.exp(jnp.where(linked, cum[:, h : h + 1] - cum_t[h : h + 1, :], FAR))


def send_to(sems, k, src, dst, device):
    send, recv = sems
    return push(src, dst, send.at[k], recv.at[k], device)


def row_sums(values):
    return nt(jnp.ones((8, values.shape[1]), F32), values, LEFT)


def as_column(row):
    first = (iota((8, LANES), 0) == 0).astype(F32)
    return tn(row, first, RIGHT)[:, :1]


def share_rows(refs, ns, t, row):
    tx, rx = refs.tx, refs.rx
    tx[...] = row
    copies = [
        send_to(refs.sem, k - 1, tx, rx.at[k - 1], {STATE: lax.rem(t + k, ns)})
        for k in range(1, ns)
    ]

    def wait():
        total = tx[...]
        for k in range(1, ns):
            copies[k - 1].wait_recv()
            total = total + rx[k - 1]
        return total

    return copies, wait


class RowScatter:
    def __init__(self, refs, sem, t):
        self.sem, self.t = sem, t
        self.tx, self.rx, self.mid = refs.tx, refs.rx, refs.mid
        self.odd, self.far = lax.rem(t, 2), t // 2
        self.copies = []

    def start(self, part):
        rows = self.tx.shape[1]
        part = part.astype(BF16)
        for k in range(4):
            self.tx[(k % 2) * 2 + k // 2] = part[rows * k : rows * (k + 1)]
        theirs = self.tx.at[pl.ds(2 - 2 * self.odd, 2)]
        self.copies.append(
            send_to(self.sem, 0, theirs, self.rx.at[pl.ds(0, 2)], {STATE: sibling(self.t)})
        )

    def middle(self):
        self.copies[0].wait_recv()
        away = 1 - self.far
        self.mid[...] = (
            self.tx[2 * self.odd + away].astype(F32) + self.rx[away].astype(F32)
        ).astype(BF16)
        self.copies.append(
            send_to(self.sem, 1, self.mid, self.rx.at[2], {STATE: lax.rem(self.t + 2, 4)})
        )

    def finish(self):
        total = self.tx[2 * self.odd + self.far].astype(F32) + self.rx[self.far].astype(F32)
        self.copies[1].wait_recv()
        return total + self.rx[2].astype(F32)


class Gather:
    def __init__(self, block, sem, t):
        self.block, self.sem, self.t = block, sem, t
        own = block(t)
        self.copies = [
            send_to(sem, 0, own, own, {STATE: sibling(t)}),
            send_to(sem, 1, own, own, {STATE: lax.rem(t + 2, 4)}),
        ]

    def middle(self):
        self.copies[1].wait_recv()
        block = self.block(lax.rem(self.t + 2, 4))
        self.copies.append(send_to(self.sem, 2, block, block, {STATE: sibling(self.t)}))

    def finish(self):
        self.copies[0].wait_recv()
        self.copies[2].wait_recv()


def gather(every, sem, t, own):
    every[t] = own
    return Gather(lambda index: every.at[index], sem, t)


def sibling(t):
    return t + 1 - 2 * lax.rem(t, 2)


def levels_of(n):
    return n.bit_length() - 1


def bits_of(n, swapped):
    order = list(range(levels_of(n)))
    if swapped and len(order) > 1:
        order[0], order[1] = order[1], order[0]
    return order


class HalvingSum:
    def __init__(self, refs, n, s, swapped=False):
        self.sem, self.n, self.s = refs.sem, n, s
        self.bits = bits_of(n, swapped)
        self.src, self.rx = refs.src, refs.rx
        self.copies = []

    def owner(self, p):
        top = len(self.bits) - 1
        return sum(((p >> (top - level)) & 1) << bit for level, bit in enumerate(self.bits))

    def block_of(self, index):
        top = len(self.bits) - 1
        return sum(((index >> bit) & 1) << (top - level) for level, bit in enumerate(self.bits))

    def fill(self, column, values):
        rows = self.src.shape[1]
        width = values.shape[1]
        for p in range(self.n):
            at = rows * self.owner(p)
            self.src[p, :, column : column + width] = values[at : at + rows]

    def parts(self, level):
        half = self.n >> (level + 1)
        mine = lax.rem(self.s // (1 << self.bits[level]), 2)
        if level == 0:
            return self.src, 0, half, mine
        return self.rx, self.n - (self.n >> (level - 1)), half, mine

    def start(self, level=0):
        buffer, base, half, mine = self.parts(level)
        to = self.s + (1 - 2 * mine) * (1 << self.bits[level])
        here = self.n - (self.n >> level)
        self.copies.append(
            send_to(
                self.sem,
                level,
                buffer.at[pl.ds(base + (1 - mine) * half, half)],
                self.rx.at[pl.ds(here, half)],
                {SEQ: to},
            )
        )

    def step(self, level):
        buffer, base, half, mine = self.parts(level)
        self.copies[level].wait_recv()
        here = self.n - (self.n >> level)

        def turn(i, carried):
            kept = buffer[base + mine * half + i].astype(F32)
            self.rx[here + i] = (kept + self.rx[here + i].astype(F32)).astype(BF16)
            return carried

        lax.fori_loop(0, half, turn, 0)
        if level + 1 < len(self.bits):
            self.start(level + 1)

    def result(self):
        return self.rx[self.n - 2]


def named(value):
    if isinstance(value, dict):
        return types.SimpleNamespace(**{key: named(item) for key, item in value.items()})
    return value


def layer_kernel(n, ns, trees, *flat):
    refs, at = types.SimpleNamespace(), 0
    for tree in trees:
        part = jax.tree.unflatten(tree, flat[at : at + tree.num_leaves])
        at += tree.num_leaves
        refs.__dict__.update(named(part).__dict__)
    x, normed, inv1 = refs.x, refs.normed, refs.inv1
    w_mix, w_qkv, w_joint, w_gu, down = refs.w_mix, refs.w_qkv, refs.w_joint, refs.w_gu, refs.down
    grad = refs.grad
    w_step = refs.w_step
    T, D = x.shape
    t, s = lax.axis_index(STATE), lax.axis_index(SEQ)
    joined = refs.jall_all.at[t]
    C = w_mix.shape[2]
    QC = 2 * HEAD_SIZE
    AQ = QUERY_HEADS * HEAD_SIZE
    NW = refs.st_own.shape[1]
    HL = NH // ns
    N = NW * ns
    TO = T // ns
    DM = C * ns
    F = down.shape[1]
    pairs = C // LANES
    scale = 1.0 / math.sqrt(HEAD_SIZE)
    state_peer = lambda k: {STATE: lax.rem(t + k, ns)}
    own_c = pl.ds(pl.multiple_of(C * t, LANES), C)
    loads = [
        pltpu.make_async_copy(src, dst, refs.load[k])
        for k, (src, dst) in enumerate(
            [
                (refs.w_att.at[:, pl.ds(pl.multiple_of(QC * t, LANES), QC)], w_qkv.at[:, pl.ds(0, QC)]),
                (refs.w_att.at[:, pl.ds(AQ, 2 * QC)], w_qkv.at[:, pl.ds(QC, 2 * QC)]),
                (refs.w_mix_in.at[:, :, own_c], refs.raw),
                (refs.joint.at[pl.ds(pl.multiple_of(QC * t, QC), QC)], w_joint.at[pl.ds(0, QC)]),
                (refs.joint.at[pl.ds(pl.multiple_of(AQ + C * t, LANES), C)], w_joint.at[pl.ds(QC, C)]),
                (refs.g, grad),
                (refs.down_in, down),
                (refs.w_gu_in.at[:, :, pl.ds(0, F // 2)], refs.raw.at[:, :, pl.ds(0, F // 2)]),
                (refs.w_gu_in.at[:, :, pl.ds(F // 2, F // 2)], refs.raw.at[:, :, pl.ds(0, F // 2)]),
            ]
        )
    ]
    for load in loads[:-2]:
        load.start()
    lanes_row = iota((1, LANES), 1)
    blank = jnp.zeros((1, LANES), F32)
    met = greet(n, ns, s, t)
    bias_row, rate_row = blank, blank
    skip_row = jnp.zeros((1, C), F32)
    heads_row = iota((1, C), 1) // HDM
    for h in range(HL):
        bias_row = jnp.where(lanes_row == h, refs.step_bias[HL * t + h], bias_row)
        rate_row = jnp.where(lanes_row == h, refs.decay_rate[HL * t + h], rate_row)
        skip_row = jnp.where(heads_row == h, refs.skip_gain[HL * t + h], skip_row)
    taps_mix = refs.conv_mixer[:, own_c]
    ggain_row = jnp.concatenate(
        [refs.ggain[pl.ds(C // LANES * t + k, 1), :] for k in range(C // LANES)], axis=1
    )
    pick = (iota((NH, LANES), 0) == HL * t + iota((NH, LANES), 1)) & (iota((NH, LANES), 1) < HL)
    pick = pick.astype(F32)
    refs.taps8[...] = jnp.zeros(refs.taps8.shape, F32)
    for c in range(2):
        refs.taps8[:KC, NW * c : NW * (c + 1)] = refs.conv_state[:, c, :]
    eye8 = (iota((8, LANES), 0) == iota((8, LANES), 1)).astype(F32)
    taps_cols = tn(refs.taps8[...], eye8, RIGHT)
    for c in range(2):
        refs.taps_st[c] = taps_cols[NW * c : NW * (c + 1)]
    sent = []
    mine = pl.ds(pl.multiple_of(NW * t, NW), NW)
    refs.st_all[:, mine, :] = refs.st_own[...]
    refs.taps_all[:, mine, :] = refs.taps_st[...]

    first_row = s * T
    starts = [refs.doc_starts[k] for k in range(refs.doc_starts.shape[0])]
    doc, masks = masks_of(starts, first_row, T)
    tiles = T // LANES

    def code_turn(j, carried):
        for i in range(tiles):
            real = refs.real[pl.ds(tiles * j + i, 1), :]
            ids = doc_of(starts, j * T + i * LANES + iota((1, LANES), 1))
            refs.codes[pl.ds(tiles * j + i, 1), :] = jnp.where(real > 0, ids, -7)
        return carried

    lax.fori_loop(0, n, code_turn, 0)

    def code_of(j):
        return jnp.concatenate([refs.codes[pl.ds(tiles * j + i, 1), :] for i in range(tiles)], axis=1)

    real_col = as_column(jnp.broadcast_to((code_of(s) >= 0).astype(F32), (8, T)))
    firsts = jnp.zeros((T, 1), jnp.int32)
    places = first_row + iota((T, 1), 0)
    for start in starts:
        firsts = jnp.where(places >= start, start, firsts)
    powers = (iota((1, LANES), 1) % (HEAD_SIZE // 2)).astype(F32) * (2.0 / HEAD_SIZE)
    angles = (places - firsts).astype(F32) * jnp.exp(-math.log(ROPE_BASE) * powers)
    cosine, sine = jnp.cos(angles), jnp.sin(angles)
    doc_row = doc_of(starts, first_row + iota((1, T), 1))
    lane = iota((T, LANES), 1)
    low = lane < HEAD_SIZE
    ngain = refs.ngain[...]

    met()
    halo_copy = pltpu.make_async_remote_copy(
        src_ref=x.at[pl.ds(T - HALO, HALO)],
        dst_ref=refs.halo_rx,
        send_sem=refs.halo[0].at[0],
        recv_sem=refs.halo[1].at[0],
        device_id={SEQ: lax.rem(s + 1, n)},
        device_id_type=MESH,
    )

    @pl.when(s + 1 < n)
    def _():
        halo_copy.start()

    columns = lambda every: lambda i: every.at[:, pl.ds(pl.multiple_of(NW * i, NW), NW), :]
    st_gather = Gather(columns(refs.st_all), refs.st, t)
    taps_gather = Gather(columns(refs.taps_all), refs.taps, t)
    xf = x[...].astype(F32)
    inv = lax.rsqrt(jnp.mean(xf * xf, axis=1, keepdims=True) + EPSILON)
    inv1[...] = inv
    normed[HALO:, :] = (xf * inv * ngain).astype(BF16)
    main = normed[HALO:, :]
    loads[0].wait()
    loads[1].wait()
    qkv = nn(main, w_qkv[...])
    q = (rope(qkv[:, :QC], cosine, sine, 1.0).astype(BF16) * scale).astype(F32)
    kcos, ksin = jnp.where(low, cosine, 1.0), jnp.where(low, sine, 0.0)
    kv_all = refs.kv_all
    group = t // 2
    both_k, both_v = qkv[:, QC : 2 * QC], qkv[:, 2 * QC :]
    own_kv = jnp.where(
        low,
        jnp.where(group == 0, both_k, roll(both_k, HEAD_SIZE)),
        jnp.where(group == 0, roll(both_v, HEAD_SIZE), both_v),
    )
    kv_all[s] = rope(own_kv, kcos, ksin, 1.0).astype(BF16)

    core = lax.rem(t, 2)
    H2 = T // 2
    own_half = pl.ds(pl.multiple_of(H2 * core, H2), H2)
    other_half = pl.ds(pl.multiple_of(H2 * (1 - core), H2), H2)

    def kv_copy(k):
        return pltpu.make_async_remote_copy(
            src_ref=kv_all.at[s, own_half],
            dst_ref=kv_all.at[s, own_half],
            send_sem=refs.kv[0].at[k - 1],
            recv_sem=refs.kv[1].at[k - 1],
            device_id={SEQ: lax.rem(s + k, n)},
            device_id_type=MESH,
        )

    def kv_pair(k):
        block = kv_all.at[s - k, own_half]
        return pltpu.make_async_remote_copy(
            src_ref=block,
            dst_ref=block,
            send_sem=refs.kv_fwd[0].at[k - 1],
            recv_sem=refs.kv_fwd[1].at[k - 1],
            device_id={STATE: sibling(t)},
            device_id_type=MESH,
        )

    def kv_turn(k, carried):
        kv_copy(k).start()
        return carried

    lax.fori_loop(1, n - s, kv_turn, 0)
    refs.q2[:T, :] = jnp.where(low, q, 0.0).astype(BF16)
    refs.q2[T:, :] = jnp.where(low, roll(q, HEAD_SIZE), 0.0).astype(BF16)
    raw = nn(nt(main, w_step[...]), pick, RIGHT) + bias_row

    doc2 = jnp.concatenate([doc, doc], axis=0)
    m_ref, l_ref, acc_ref = refs.m_acc, refs.l_acc, refs.o_acc
    m_ref[...] = jnp.full(m_ref.shape, FAR, F32)
    l_ref[...] = jnp.zeros(l_ref.shape, F32)
    acc_ref[...] = jnp.zeros(acc_ref.shape, F32)

    def allowed_at(j, diagonal):
        allowed = code_of(j) == doc2
        if diagonal:
            rows2 = jnp.concatenate([iota((T, T), 0)] * 2, axis=0)
            cols2 = iota((2 * T, T), 1)
            allowed = (allowed & (cols2 <= rows2)) | (cols2 == rows2)
        return allowed

    def attend(j, diagonal):
        block = kv_all[j]
        scores = jnp.where(allowed_at(j, diagonal), nt(refs.q2[...], block), FAR)
        m = m_ref[...]
        m_new = jnp.maximum(m, jnp.max(scores, axis=1, keepdims=True))
        shrink = jnp.exp(m - m_new)
        p = jnp.exp(scores - m_new)
        l_ref[...] = l_ref[...] * shrink + jnp.sum(p, axis=1, keepdims=True)
        acc_ref[...] = acc_ref[...] * shrink + nn(p.astype(BF16), block)
        m_ref[...] = m_new

    def attend_turn(k, carried):
        @pl.when(k < s)
        def _():
            kv_copy(k + 1).wait_recv()
            kv_pair(k + 1).start()

        kv_pair(k).wait_recv()
        attend(s - k, False)
        return carried

    def attend_some(first, stop):
        lax.fori_loop(first, stop, attend_turn, 0)

    cut1, cut2 = 1 + (s + 1) // 3, 1 + (2 * s + 1) // 3
    attend(s, True)
    loads[2].wait()

    def split_mixer(c):
        def turn(k, carried):
            rows = pl.ds(pl.multiple_of(64 * k, 64), 64)
            w_mix[c, rows, :] = refs.raw[rows, c, :C]
            return carried

        lax.fori_loop(0, D // 64, turn, 0)

    split_mixer(1)
    taps_gather.middle()
    st_gather.middle()

    @pl.when(s > 0)
    def _():
        halo_copy.wait_recv()

    @pl.when(s == 0)
    def _():
        refs.halo_rx[...] = jnp.zeros(refs.halo_rx.shape, BF16)

    hf = refs.halo_rx[...].astype(F32)
    inv_h = lax.rsqrt(jnp.mean(hf * hf, axis=1, keepdims=True) + EPSILON)
    normed[:HALO, :] = (hf * inv_h * ngain).astype(BF16)
    ext_f, ext_s, ext_o = refs.ext_f, refs.ext_s, refs.ext_o
    ext_f[...] = nn(normed[...], w_mix[1]).astype(BF16).astype(F32)
    inner_lin = conv_ref(ext_f, taps_mix, masks, T)
    inner = silu(inner_lin)
    taps_gather.finish()
    st_gather.finish()
    for c in range(2):
        ext_s[...] = nt(normed[...], refs.st_all[c]).astype(BF16).astype(F32)
        taps = refs.taps_all[c].T
        refs.wr[c] = silu(conv_ref(ext_s, taps, masks, T))
    write, read = refs.wr[0], refs.wr[1]
    step = softplus(raw)
    causal = iota((T, T), 0) >= iota((T, T), 1)
    tri = causal.astype(F32)
    cum = nn(tri, -step * rate_row, LEFT)
    cum_t = cum.T
    linked = (doc == doc_row) & causal
    E = expander(C)
    rows_e = expand_rows(C)
    inflow = step * real_col
    inflow_e = nn(inflow, E, RIGHT)
    in_x = inner * inflow_e
    cum_last = cum[T - 1 : T]
    last = first_row + T - 1
    doc_last = doc_of(starts, jnp.full((T, 1), last, jnp.int32))
    prior = doc_of(starts, jnp.full((T, 1), first_row - 1, jnp.int32))
    tail = jnp.where(doc == doc_last, jnp.exp(cum_last - cum), 0.0)
    refs.tail_e[...] = nn(tail, E, RIGHT)
    state_part = tn(refs.tail_e[...] * in_x, write, FINE)
    alive = (doc == prior).astype(F32)
    alive_last = (doc_last == prior).astype(F32)[:8]
    thr = alive_last * jnp.exp(jnp.broadcast_to(cum_last, (8, LANES)))
    steps = carry_steps(n)

    carry = Carry(refs.fc, (refs.window, refs.window_thr), n, s, 1, rows_e)
    carry.begin(state_part, thr)

    g_mat = nt(read, write, FINE)
    for p in range(pairs):
        cols = slice(LANES * p, LANES * (p + 1))
        ys = []
        for h in (2 * p, 2 * p + 1):
            link = link_of(linked, cum, cum_t, h)
            ys.append(nn(link * g_mat, in_x[:, cols], FINE))
        refs.ssd[:, cols] = jnp.where(low, ys[0], ys[1])

    split_mixer(0)
    loads[7].start()
    refs.z[...] = nn(main, w_mix[0])
    for slot in range(min(2, steps)):
        carry.advance(slot)

    @pl.when(s > 0)
    def _():
        kv_copy(1).wait_recv()
        kv_pair(1).start()

    attend_some(1, cut1)
    if steps > 2:
        carry.advance(2)
    attend_some(cut1, cut2)
    carry.rest(3)
    s_in = refs.window[...]
    refs.reach_e[...] = nn(alive * jnp.exp(cum), E, RIGHT)
    ssd = refs.ssd[...] + refs.reach_e[...] * nt(read, s_in, FINE)
    refs.ssd[...] = ssd
    z = refs.z[...]
    full_mix = ssd + skip_row * inner
    gated = full_mix * silu(z)
    copies, wait = share_rows(refs.sq, ns, t, row_sums(gated * gated))
    sent += copies
    attend_some(cut2, s + 1)
    out = acc_ref[...] / l_ref[...]
    acc_ref[...] = out
    m_ref[...] = m_ref[...] + jnp.log(l_ref[...])
    joined[:, :QC] = jnp.where(low, roll(out[:T], HEAD_SIZE), out[T:]).astype(BF16)
    loads[3].wait()
    loads[4].wait()
    loads[5].wait()
    loads[6].wait()
    dh = nn(grad[...], down[...])
    inv_g = as_column(lax.rsqrt(wait() / DM + EPSILON))
    joined[:, QC:] = (gated * inv_g * ggain_row).astype(BF16)
    rs1 = RowScatter(refs.rs1, refs.rs1_sem, t)
    rs1.start(nn(joined[...], w_joint[...]))
    own_rows = pl.ds(pl.multiple_of(TO * t, TO), TO)
    x_own = x[own_rows, :].astype(F32)
    rs1.middle()
    loads[7].wait()

    def split_columns(half):
        columns = slice(F // 2 * half, F // 2 * (half + 1))

        def turn(k, carried):
            rows = pl.ds(pl.multiple_of(64 * k, 64), 64)
            for c in range(2):
                w_gu[c, rows, columns] = refs.raw[rows, c, : F // 2]
            return carried

        lax.fori_loop(0, D // 64, turn, 0)

    split_columns(0)
    loads[8].start()
    res = x_own + rs1.finish()
    inv2 = lax.rsqrt(jnp.mean(res * res, axis=1, keepdims=True) + EPSILON)
    mgain = refs.mgain[...]
    ag1 = gather(refs.ag1_all, refs.ag1_sem, t, (res * inv2 * mgain).astype(BF16))
    loads[8].wait()
    split_columns(1)
    ag1.middle()
    jall = Gather(lambda index: refs.jall_all.at[index], refs.jall, t)
    ag1.finish()

    n2 = jnp.concatenate([refs.ag1_all[k] for k in range(ns)], axis=0)
    gate, up = nn(n2, w_gu[0]), nn(n2, w_gu[1])
    sig = sigmoid(gate)
    act = gate * sig
    hidden = (act * up).astype(BF16)
    d_gate = (dh * up * (sig * (1.0 + gate * (1.0 - sig)))).astype(BF16)
    d_up = (dh * act).astype(BF16)
    rs2 = RowScatter(refs.rs2, refs.rs2_sem, t)
    rs2.start(nt(d_gate, w_gu[0]) + nt(d_up, w_gu[1]))
    for copy in rs1.copies + ag1.copies:
        copy.wait_send()
    rs3 = RowScatter(refs.rs1, refs.rs3_sem, t)
    rs3.start(nt(hidden, down[...]))
    rs2.middle()

    def weight_sum(stream, parts, swapped=False):
        total = HalvingSum(stream, n, s, swapped)
        column = 0
        for lhs, rhs in parts:
            width = rhs.shape[1]
            for c in range(0, width, 256):
                piece = rhs[:, c : min(c + 256, width)]
                total.fill(column + c, tn(lhs, piece).astype(BF16))
            column += width
        return total

    sum_gate = weight_sum(refs.gate_g, [(n2, d_gate)], True)
    sum_gate.start()
    rs3.middle()
    sum_down = weight_sum(refs.down_g, [(grad[...], hidden)])
    sum_down.start()
    sum_up = weight_sum(refs.up_g, [(n2, d_up)])
    dn2 = rs2.finish()
    scaled = dn2 * mgain
    d_res = (
        grad[own_rows, :].astype(F32)
        + inv2 * scaled
        - res * inv2 * inv2 * inv2 * jnp.mean(scaled * res, axis=1, keepdims=True)
    )
    ag2 = gather(refs.ag2_all, refs.ag2_sem, t, d_res.astype(BF16))

    def put_small(row, values):
        for k in range(0, values.shape[1], LANES):
            piece = values[:, k : k + LANES]
            refs.small_tx[row : row + 1, : piece.shape[1]] = piece
            row += 1

    refs.small_tx[...] = jnp.zeros(refs.small_tx.shape, F32)
    refs.step_src[...] = jnp.zeros(refs.step_src.shape, F32)
    put_small(8, jnp.sum(dn2 * res * inv2, axis=0, keepdims=True))
    ag2.middle()
    ag3 = gather(refs.ag1_all, refs.ag3_sem, t, (res + rs3.finish()).astype(BF16))
    ag2.finish()
    d_branch = jnp.concatenate([refs.ag2_all[k] for k in range(ns)], axis=0)
    d_joined = nt(d_branch, w_joint[...])
    d_gn = d_joined[:, QC:]
    scaled = d_gn * ggain_row
    copies, wait = share_rows(refs.dot, ns, t, row_sums(scaled * gated))
    sent += copies
    put_small(16, jnp.sum(d_gn * gated * inv_g, axis=0, keepdims=True))
    d_att = d_joined[:, :QC].astype(BF16).astype(F32)
    dout2 = jnp.concatenate(
        [jnp.where(low, 0.0, roll(d_att, HEAD_SIZE)), jnp.where(low, 0.0, d_att)], axis=0
    )
    delta = jnp.sum(dout2 * acc_ref[...], axis=1, keepdims=True)
    l_ref[...] = delta
    refs.dout2[...] = dout2.astype(BF16)
    jall.middle()
    sum_down.step(0)
    sum_gate.step(0)
    jall.finish()
    own_d = pl.ds(pl.multiple_of((D // ns) * t, LANES), D // ns)
    d_cols = jnp.concatenate([refs.ag2_all[k, :, own_d] for k in range(ns)], axis=0)
    sum_joint = joint = HalvingSum(refs.joint_g, n, s)
    rows_j = joint.src.shape[1]
    piece = min(rows_j, LANES)
    for k in range(ns):
        values = tn(refs.jall_all[k], d_cols).astype(BF16)
        for at in range(0, QC + C, piece):
            row = QC * k + at if at < QC else AQ + C * k + at - QC
            offset = row % rows_j
            joint.src[joint.block_of(row // rows_j), offset : offset + piece, :] = values[at : at + piece]
    dot = as_column(wait() / DM)
    d_gated = inv_g * scaled - gated * (inv_g * inv_g * inv_g * dot)
    sig = sigmoid(z)
    dy = d_gated * z * sig
    refs.d_z[...] = (d_gated * full_mix * (sig * (1.0 + z * (1.0 - sig)))).astype(BF16)
    put_small(19, nt(jnp.broadcast_to(jnp.sum(dy * inner, axis=0, keepdims=True), (8, C)), E, RIGHT)[:1])
    reach_dy = refs.reach_e[...] * dy
    carry_b = Carry(refs.bc, (refs.window, refs.window_thr), n, s, -1, rows_e)
    carry_b.begin(tn(reach_dy, read, FINE), thr)
    sum_up.start()
    joint.start()
    sum_z = weight_sum(refs.z_g, [(main, refs.d_z[...])], True)
    ag3.middle()
    d_g = jnp.zeros((T, T), F32)
    for p in range(pairs):
        cols = slice(LANES * p, LANES * (p + 1))
        xp, dyp = in_x[:, cols], dy[:, cols]
        halves = []
        for k in range(2):
            link = link_of(linked, cum, cum_t, 2 * p + k)
            halves.append(tn(link * g_mat, dyp, FINE))
            own = low if k == 0 else jnp.logical_not(low)
            d_g = d_g + link * nt(jnp.where(own, dyp, 0.0), xp, FINE)
        refs.w_tot[:, cols] = jnp.where(low, halves[0], halves[1])

    d_read = nn(d_g, write, FINE) + nn(reach_dy, s_in, FINE)
    refs.dwr_tx[1] = d_read.T.astype(BF16)
    refs.d_write[...] = tn(d_g, read, FINE)
    refs.dq2[...] = jnp.zeros(refs.dq2.shape, F32)

    def attend_back(j, diagonal):
        block = kv_all[j]
        q2, dout2 = refs.q2[...], refs.dout2[...]
        scores = jnp.where(allowed_at(j, diagonal), nt(q2, block), FAR)
        p = jnp.exp(scores - m_ref[...])
        ds = (p * (nt(dout2, block) - l_ref[...])).astype(BF16)
        refs.dq2[...] += nn(ds, block)
        return tn(ds, q2) + tn(p.astype(BF16), dout2)

    def dkv_copy(k):
        return pltpu.make_async_remote_copy(
            src_ref=refs.dkv_mid.at[k - 1],
            dst_ref=refs.dkv_rx.at[k - 1],
            send_sem=refs.dkv[0].at[k - 1],
            recv_sem=refs.dkv[1].at[k - 1],
            device_id={SEQ: lax.rem(s - k + n, n)},
            device_id_type=MESH,
        )

    def dkv_pair(k):
        return pltpu.make_async_remote_copy(
            src_ref=kv_all.at[s - k, other_half],
            dst_ref=refs.dkv_mid.at[lax.rem(k + n - 1, n)],
            send_sem=refs.dkv_fwd[0].at[k],
            recv_sem=refs.dkv_fwd[1].at[k],
            device_id={STATE: sibling(t)},
            device_id_type=MESH,
        )

    def dkv_on(k):
        dkv_pair(k).wait_recv()
        both = refs.dkv_mid[k - 1].astype(F32) + kv_all[s - k, own_half].astype(F32)
        refs.dkv_mid[k - 1] = both.astype(BF16)
        dkv_copy(k).start()

    def back_turn(k, carried):
        kv_all[s - k] = attend_back(s - k, False).astype(BF16)
        dkv_pair(k).start()

        @pl.when(k > 1)
        def _():
            dkv_on(k - 1)

        return carried

    def back_some(first, stop):
        lax.fori_loop(first, stop, back_turn, 0)

    def kv_end(k, carried):
        kv_copy(k).wait_send()
        return carried

    def pair_end(k, carried):
        kv_pair(k).wait_send()
        return carried

    lax.fori_loop(1, n - s, kv_end, 0)
    lax.fori_loop(1, s + 1, pair_end, 0)
    for slot in range(min(2, steps)):
        carry_b.advance(slot)
    back_some(1, cut1)
    if steps > 2:
        carry_b.advance(2)
    back_some(cut1, cut2)
    carry_b.rest(3)
    back_some(cut2, s + 1)
    diagonal = attend_back(s, True)
    refs.dkv_sum[...] = diagonal
    kv_all[s] = diagonal.astype(BF16)
    dkv_pair(0).start()

    @pl.when(s > 0)
    def _():
        dkv_on(s)

    sum_z.start()
    ag3.finish()
    for k in range(ns):
        refs.layer_output[TO * k : TO * (k + 1), :] = refs.ag1_all[k]
    sum_down.step(1)
    sum_gate.step(1)
    sum_up.step(0)
    later = refs.window[...]
    tail_e = refs.tail_e[...]
    tail_r = tail_e * nt(write, later, FINE)
    w_tot = refs.w_tot[...] + tail_r
    d_write = refs.d_write[...] + nn(tail_e * in_x, later, FINE)
    refs.dwr_tx[0] = d_write.T.astype(BF16)
    dwr = []
    for k in range(1, ns):
        p = lax.rem(t + k, ns)
        theirs = pl.ds(pl.multiple_of(NW * p, NW), NW)
        dwr.append(
            send_to(refs.dwr, k - 1, refs.dwr_tx.at[:, theirs, :], refs.dwr_rx.at[k - 1], {STATE: p})
        )
    sent += dwr
    d_lin = (inflow_e * w_tot + skip_row * dy) * silu_slope(inner_lin)

    def conv_back(ext, grad, taps, up, row, rows):
        grad[...] = jnp.zeros(grad.shape, F32)
        for k in range(KC):
            at = HALO - KC + 1 + k
            masked = up * masks[k]
            put_small(row + rows * k, jnp.sum(masked * ext[at : at + T, :], axis=0, keepdims=True))
            grad[at : at + T, :] += masked * taps[k : k + 1]
        return grad[...].astype(BF16)

    d_ext = conv_back(ext_f, refs.grad_f, taps_mix, d_lin, 22, C // LANES)
    st64 = refs.st_own[...].reshape(2 * NW, D)
    taps_own = refs.taps_st[...].reshape(2 * NW, LANES).T
    ext_o[...] = nt(normed[...], st64).astype(BF16).astype(F32)
    slope_o = silu_slope(conv_ref(ext_o, taps_own, masks, T))
    for copy in dwr:
        copy.wait_recv()
    d_wr = refs.dwr_tx[:, mine, :].astype(F32)
    for k in range(1, ns):
        d_wr = d_wr + refs.dwr_rx[k - 1].astype(F32)
    row_st = 22 + KC * (C // LANES)
    d_st = conv_back(ext_o, refs.grad_o, taps_own, d_wr.reshape(2 * NW, T).T * slope_o, row_st, 1)
    refs.back_tx[...] = (nt(d_ext[:HALO], w_mix[1]) + nn(d_st[:HALO], st64)).astype(BF16)
    def back_copy(member):
        return pltpu.make_async_remote_copy(
            src_ref=refs.back_tx,
            dst_ref=refs.back_rx.at[member],
            send_sem=refs.back[0].at[0],
            recv_sem=refs.back[1].at[member],
            device_id={SEQ: lax.rem(s + n - 1, n), STATE: ns - 1},
            device_id_type=MESH,
        )

    @pl.when(s > 0)
    def _():
        back_copy(t).start()

    sum_inner = weight_sum(refs.inner_g, [(normed[...], d_ext)])
    sum_inner.start()
    u = nt(inner * w_tot, E, RIGHT)
    tl = nt(in_x * tail_r, E, RIGHT)
    thr_s = jnp.sum(tn(later * s_in, rows_e, RIGHT), axis=0, keepdims=True) * thr[:1]
    d_cum = nt(dy * ssd, E, RIGHT) - inflow * u
    at_last = iota((T, LANES), 0) == T - 1
    d_cum = d_cum + jnp.where(at_last, jnp.sum(tl, axis=0, keepdims=True) + thr_s, 0.0)
    d_ld = tn(tri, d_cum, LEFT)
    d_step = real_col * u - rate_row * d_ld
    put_small(20, -jnp.sum(step * d_ld, axis=0, keepdims=True))
    d_step = d_step * sigmoid(raw)
    put_small(21, jnp.sum(d_step, axis=0, keepdims=True))
    d_step = d_step.astype(BF16)
    d_z = refs.d_z[...]
    dq2 = refs.dq2[...]
    dq = jnp.where(low, dq2[:T], roll(dq2[T:], HEAD_SIZE)) * scale
    d_q = rope(dq, cosine, sine, -1.0).astype(BF16)
    d_n = (
        nt(d_z, w_mix[0])
        + nt(d_ext[HALO:], w_mix[1])
        + nn(d_st[HALO:], st64)
        + nn(nt(d_step, pick.astype(BF16)).astype(BF16), w_step[...])
    )
    def dkv_turn(k, carried):
        dkv_copy(k).wait_recv()
        refs.dkv_half[...] += refs.dkv_rx[k - 1].astype(F32)
        return carried

    dkv_pair(0).wait_recv()
    refs.dkv_half[...] = refs.dkv_sum[own_half, :] + refs.dkv_mid[n - 1].astype(F32)
    lax.fori_loop(1, n - s, dkv_turn, 0)
    refs.pair_tx[...] = refs.dkv_half[...].astype(BF16)
    odd = core
    pair = send_to(refs.pair, 0, refs.pair_tx, refs.pair_rx, {STATE: sibling(t)})
    sent.append(pair)
    pair.wait_recv()
    refs.dkv_sum[own_half, :] = refs.pair_tx[...].astype(F32)
    refs.dkv_sum[other_half, :] = refs.pair_rx[...].astype(F32)
    d_kv = rope(refs.dkv_sum[...], kcos, ksin, -1.0)
    d_kv = jnp.where(low == (odd == 0), d_kv, 0.0)
    other = roll(d_kv, HEAD_SIZE)
    d_k = jnp.where(low, jnp.where(group == 0, d_kv, 0.0), jnp.where(group == 0, 0.0, other))
    d_v = jnp.where(low, jnp.where(group == 0, other, 0.0), jnp.where(group == 0, 0.0, d_kv))
    d_kv_b = d_kv.astype(BF16)
    d_qkv = jnp.concatenate([d_q, jnp.where(odd == 0, d_k, d_v).astype(BF16)], axis=1)
    mine_kv = jnp.where(odd == 0, d_kv, other).astype(BF16)
    pad_st = jnp.concatenate([jnp.zeros((T + HALO, HEAD_SIZE), F32), d_st.astype(F32)], axis=1)
    mine_kv = jnp.concatenate([jnp.zeros((HALO, LANES), F32), mine_kv.astype(F32)], axis=0)
    mixed = jnp.where(iota((T + HALO, LANES), 1) < HEAD_SIZE, mine_kv, pad_st).astype(BF16)
    sum_rest = weight_sum(refs.rest_g, [(main, d_q), (normed[...], mixed)])
    sum_rest.start()
    w_kv = jnp.where(odd == 0, w_qkv[:, QC : 2 * QC], w_qkv[:, 2 * QC :])
    d_n = d_n + nt(d_qkv, jnp.concatenate([w_qkv[:, :QC], w_kv], axis=1))
    for copy in rs2.copies + ag3.copies:
        copy.wait_send()
    rs4 = RowScatter(refs.rs2, refs.rs4_sem, t)
    rs4.start(d_n)
    sum_joint.step(0)
    rs4.middle()
    sum_z.step(0)
    sum_up.step(1)
    inv_own = inv1[own_rows, :]
    d_n = rs4.finish()
    last_rows = (t == ns - 1) & (s + 1 < n)

    @pl.when(last_rows)
    def _():
        for member in range(ns):
            back_copy(member).wait_recv()

    @pl.when(jnp.logical_not(last_rows))
    def _():
        refs.back_rx[...] = jnp.zeros(refs.back_rx.shape, BF16)

    from_next = refs.back_rx[0].astype(F32)
    for member in range(1, ns):
        from_next = from_next + refs.back_rx[member].astype(F32)
    d_n = jnp.concatenate([d_n[: TO - HALO], d_n[TO - HALO :] + from_next], axis=0)
    scaled = d_n * ngain
    in_g = (
        d_res
        + inv_own * scaled
        - x_own * inv_own * inv_own * inv_own * jnp.mean(scaled * x_own, axis=1, keepdims=True)
    )
    ag4 = gather(refs.ag1_all, refs.ag4_sem, t, in_g.astype(BF16))
    put_small(0, jnp.sum(d_n * x_own * inv_own, axis=0, keepdims=True))

    def small_copy(k):
        peer = lax.rem(s + k, n)
        make = lambda src, dst, at: pltpu.make_async_remote_copy(
            src_ref=src,
            dst_ref=dst,
            send_sem=refs.small[0].at[at],
            recv_sem=refs.small[1].at[at],
            device_id={SEQ: peer},
            device_id_type=MESH,
        )
        return (
            make(refs.small_tx, refs.small_rx.at[s, pl.ds(0, rows_c)], k - 1),
            make(refs.step_src.at[peer], refs.small_rx.at[s, pl.ds(rows_c, 8)], n + k - 2),
        )

    step_rows = tn(d_step, main)[:8]
    rows_c, rows_d = refs.small_tx.shape[0], D // n
    for k in range(n):
        refs.step_src[k, :, :rows_d] = step_rows[:, rows_d * k : rows_d * (k + 1)]
    refs.small_rx[s, :rows_c, :] = refs.small_tx[...]
    refs.small_rx[s, rows_c:, :] = refs.step_src[s]

    def small_turn(k, carried):
        for copy in small_copy(k):
            copy.start()
        return carried

    lax.fori_loop(1, n, small_turn, 0)
    last_level = len(bits_of(n, False)) - 1

    def steps_of(total, first, stop):
        for level in range(first, stop):
            total.step(level)

    sum_inner.step(0)
    sum_z.step(1)
    ag4.middle()
    sum_joint.step(1)
    sum_rest.step(0)
    steps_of(sum_down, 2, last_level + 1)
    steps_of(sum_gate, 2, last_level + 1)
    ag4.finish()
    for k in range(ns):
        refs.input_grad[TO * k : TO * (k + 1), :] = refs.ag1_all[k]
    steps_of(sum_up, 2, last_level + 1)
    steps_of(sum_z, 2, last_level + 1)
    gz = gather(refs.gz_all, refs.gz_sem, t, sum_z.result())
    sum_inner.step(1)
    steps_of(sum_joint, 2, last_level + 1)
    gj = gather(refs.gj_all, refs.gj_sem, t, sum_joint.result())
    sum_rest.step(1)
    gz.middle()
    steps_of(sum_inner, 2, last_level + 1)
    gi = gather(refs.gi_all, refs.gi_sem, t, sum_inner.result())
    gj.middle()
    steps_of(sum_rest, 2, last_level + 1)
    gr = gather(refs.gr_all, refs.gr_sem, t, sum_rest.result())

    def small_end(k, carried):
        for copy in small_copy(k):
            copy.wait_recv()
        return carried

    lax.fori_loop(1, n, small_end, 0)

    def small_sum(j, total):
        return total + refs.small_rx[j]

    small = gather(
        refs.sm_all, refs.sm_sem, t,
        lax.fori_loop(0, n, small_sum, jnp.zeros(refs.small_rx.shape[1:], F32)),
    )
    gi.middle()
    small.middle()
    refs.o_gu[0] = sum_gate.result()
    refs.o_gu[1] = sum_up.result()
    refs.o_down[...] = sum_down.result()
    gz.finish()
    gj.finish()
    gi.finish()
    gr.middle()
    for k in range(ns):
        refs.o_mix[0, :, C * k : C * (k + 1)] = refs.gz_all[k]
        refs.o_mix[1, :, C * k : C * (k + 1)] = refs.gi_all[k]
        refs.o_joint[:, (D // ns) * k : (D // ns) * (k + 1)] = refs.gj_all[k]
    small.finish()
    total = refs.sm_all[0, :16, :]
    for k in range(1, ns):
        total = total + refs.sm_all[k, :16, :]
    refs.o_gains[...] = total
    refs.o_small[...] = refs.sm_all[:, 16:rows_c, :]
    gr.finish()
    rows = refs.gr_all.shape[1]
    half = iota((rows, LANES), 1) < HEAD_SIZE
    for k in range(ns):
        refs.o_att[:, QC * k : QC * (k + 1)] = refs.gr_all[k, :, :QC]
        refs.o_step[HL * k : HL * (k + 1), :] = refs.sm_all[k, rows_c : rows_c + HL, :rows]
    for c in range(2):
        first = refs.gr_all[c, :, QC : 2 * QC].astype(F32)
        second = refs.gr_all[2 + c, :, QC : 2 * QC].astype(F32)
        refs.o_att[:, AQ + QC * c : AQ + QC * (c + 1)] = jnp.where(
            half, first, roll(second, HEAD_SIZE)
        ).astype(BF16)
    refs.o_st[...] = refs.gr_all[t, :, QC : 2 * QC]

    def small_sent(k, carried):
        for copy in small_copy(k):
            copy.wait_send()
        return carried

    lax.fori_loop(1, n, small_sent, 0)
    for group_of in (
        st_gather, taps_gather, jall, rs3, rs4, ag2, ag4, gz, gj, gi, gr, small,
        sum_gate, sum_up, sum_down, sum_z, sum_joint, sum_inner, sum_rest,
    ):
        sent += group_of.copies
    for copy in sent:
        copy.wait_send()

    @pl.when(s + 1 < n)
    def _():
        halo_copy.wait_send()

    @pl.when(s > 0)
    def _():
        back_copy(t).wait_send()

    carry.finish()
    carry_b.finish()

    def dkv_end(k, carried):
        dkv_copy(k).wait_send()
        return carried

    def dkv_pair_end(k, carried):
        dkv_pair(k).wait_send()
        return carried

    lax.fori_loop(1, s + 1, dkv_end, 0)
    lax.fori_loop(0, s + 1, dkv_pair_end, 0)


def layer(n, ns, arrays):
    inputs = types.SimpleNamespace(**arrays)
    T, D = inputs.x.shape
    C = inputs.w_mix_in.shape[2] // ns
    NW = inputs.st_own.shape[1]
    F = inputs.down_in.shape[1]
    N, TO, H = NW * ns, T // ns, NH // ns
    KJ = inputs.joint.shape[0]
    QC = 2 * HEAD_SIZE
    R, RJ = D // n, KJ // n
    steps = carry_steps(n)
    levels = levels_of(n)
    sd = jax.ShapeDtypeStruct
    J = QC + C
    SMALL = -(-(22 + KC * (C // LANES) + KC) // 8) * 8
    outs = dict(
        layer_output=sd((T, D), BF16),
        input_grad=sd((T, D), BF16),
        o_down=sd((R, F), BF16),
        o_gu=sd((2, R, F), BF16),
        o_mix=sd((2, R, ns * C), BF16),
        o_joint=sd((RJ, D), BF16),
        o_att=sd((R, inputs.w_att.shape[1]), BF16),
        o_step=sd((NH, R), F32),
        o_st=sd((R, LANES), BF16),
        o_gains=sd((16, LANES), F32),
        o_small=sd((ns, SMALL - 16, LANES), F32),
    )
    vm = pltpu.VMEM
    dma = lambda k: (pltpu.SemaphoreType.DMA((k,)), pltpu.SemaphoreType.DMA((k,)))
    blocks = lambda *shape: vm((ns,) + shape, BF16)

    def scan():
        return dict(
            tx=vm((max(1, steps - 1), C, N), BF16),
            rx=vm((steps, C, N), BF16),
            thr_tx=vm((max(1, steps - 1), 8, LANES), F32),
            thr_rx=vm((steps, 8, LANES), F32),
            sem=dma(steps),
            thr_sem=dma(steps),
        )

    def rows():
        return dict(tx=vm((8, T), F32), rx=vm((ns - 1, 8, T), F32), sem=dma(ns - 1))

    def scatter():
        return dict(tx=blocks(TO, D), rx=vm((3, TO, D), BF16), mid=vm((TO, D), BF16))

    def stream(*shape):
        return dict(src=vm((n,) + shape, BF16), rx=vm((n - 1,) + shape, BF16), sem=dma(levels))

    scratch = dict(
        w_qkv=vm((D, 3 * QC), BF16),
        w_joint=vm((J, D), BF16),
        w_mix=vm((2, D, C), BF16),
        w_gu=vm((2, D, F), BF16),
        raw=vm((D, 2, max(C, F // 2)), BF16),
        down=vm((D, F), BF16),
        grad=vm((T, D), BF16),
        load=tuple(pltpu.SemaphoreType.DMA for _ in range(9)),
        taps8=vm((8, LANES), F32),
        taps_st=vm((2, NW, LANES), F32),
        codes=vm((n * T // LANES, LANES), jnp.int32),
        halo_rx=vm((HALO, D), BF16),
        st_all=vm((2, N, D), BF16),
        taps_all=vm((2, N, LANES), F32),
        kv_all=vm((n, T, LANES), BF16),
        normed=vm((T + HALO, D), BF16),
        inv1=vm((T, 1), F32),
        q2=vm((2 * T, LANES), BF16),
        z=vm((T, C), F32),
        ext_f=vm((T + HALO, C), F32),
        ext_s=vm((T + HALO, N), F32),
        ext_o=vm((T + HALO, 2 * NW), F32),
        grad_f=vm((T + HALO, C), F32),
        grad_o=vm((T + HALO, 2 * NW), F32),
        wr=vm((2, T, N), F32),
        tail_e=vm((T, C), F32),
        reach_e=vm((T, C), F32),
        ssd=vm((T, C), F32),
        w_tot=vm((T, C), F32),
        d_z=vm((T, C), BF16),
        jall_all=vm((ns, T, J), BF16),
        window=vm((C, N), F32),
        window_thr=vm((8, LANES), F32),
        m_acc=vm((2 * T, 1), F32),
        l_acc=vm((2 * T, 1), F32),
        o_acc=vm((2 * T, LANES), F32),
        dout2=vm((2 * T, LANES), BF16),
        dq2=vm((2 * T, LANES), F32),
        dkv_rx=vm((n, T // 2, LANES), BF16),
        dkv_mid=vm((n, T // 2, LANES), BF16),
        dkv_half=vm((T // 2, LANES), F32),
        dkv_sum=vm((T, LANES), F32),
        pair_tx=vm((T // 2, LANES), BF16),
        pair_rx=vm((T // 2, LANES), BF16),
        back_tx=vm((HALO, D), BF16),
        back_rx=vm((ns, HALO, D), BF16),
        dwr_tx=vm((2, N, T), BF16),
        d_write=vm((T, N), F32),
        dwr_rx=vm((ns - 1, 2, NW, T), BF16),
        small_tx=vm((SMALL, LANES), F32),
        step_src=vm((n, 8, LANES), F32),
        small_rx=vm((n, SMALL + 8, LANES), F32),
        halo=dma(1),
        st=dma(3),
        taps=dma(3),
        kv=dma(n - 1),
        kv_fwd=dma(n - 1),
        dkv=dma(n - 1),
        dkv_fwd=dma(n),
        jall=dma(3),
        pair=dma(1),
        back=dma(ns),
        dwr=dma(ns - 1),
        small=dma(2 * n - 2),
        sm_all=vm((ns, SMALL + 8, LANES), F32),
        fc=scan(),
        bc=scan(),
        sq=rows(),
        dot=rows(),
        rs1=scatter(),
        rs2=scatter(),
        rs1_sem=dma(2),
        rs2_sem=dma(2),
        rs3_sem=dma(2),
        rs4_sem=dma(2),
        ag1_all=blocks(TO, D),
        ag2_all=blocks(TO, D),
        gz_all=blocks(R, C),
        gi_all=blocks(R, C),
        gr_all=blocks(R, 2 * LANES),
        gj_all=blocks(RJ, D // ns),
        ag1_sem=dma(3),
        ag2_sem=dma(3),
        ag3_sem=dma(3),
        ag4_sem=dma(3),
        gz_sem=dma(3),
        gi_sem=dma(3),
        gr_sem=dma(3),
        gj_sem=dma(3),
        sm_sem=dma(3),
        gate_g=stream(R, F),
        up_g=stream(R, F),
        down_g=stream(R, F),
        z_g=stream(R, C),
        inner_g=stream(R, C),
        rest_g=stream(R, 2 * LANES),
        joint_g=stream(RJ, D // ns),
    )
    whole = pl.BlockSpec(memory_space=pltpu.VMEM)
    small = pl.BlockSpec(memory_space=pltpu.SMEM)
    far = pl.BlockSpec(memory_space=pl.ANY)
    specs = {key: whole for key in arrays}
    specs.update(doc_starts=small, step_bias=small, decay_rate=small, skip_gain=small)
    specs.update(w_att=far, joint=far, g=far, w_mix_in=far, w_gu_in=far, down_in=far)
    flat = [jax.tree.flatten(group) for group in (arrays, outs, scratch)]
    got = pl.pallas_call(
        functools.partial(layer_kernel, n, ns, [tree for _, tree in flat]),
        out_shape=flat[1][0],
        in_specs=jax.tree.flatten(specs)[0],
        out_specs=[whole] * len(outs),
        scratch_shapes=flat[2][0],
        name="layer",
        compiler_params=pltpu.CompilerParams(
            collective_id=1, has_side_effects=True, vmem_limit_bytes=VMEM_LIMIT
        ),
    )(*flat[0][0])
    return types.SimpleNamespace(**jax.tree.unflatten(flat[1][1], got))


def finish_kernel(n, ns, tree_in, tree_out, *flat):
    split = tree_in.num_leaves
    o = named(jax.tree.unflatten(tree_in, flat[:split]))
    out = named(jax.tree.unflatten(tree_out, flat[split:]))
    t, s = lax.axis_index(STATE), lax.axis_index(SEQ)
    HL, C = NH // ns, NH * HDM // ns
    per = C // LANES
    NW = out.taps_st.shape[2]
    R = out.down.shape[0]
    out.layer_output[...] = o.layer_output[...]
    out.input_grad[...] = o.input_grad[...].astype(F32)
    out.att[...] = o.o_att[...].astype(F32)
    out.joint[...] = o.o_joint[...].astype(F32)
    out.down[...] = o.o_down[...].astype(F32)
    out.step[...] = o.o_step[...]
    turned = o.o_st[...].astype(F32).T
    for c in range(2):
        out.mix[:, c, :] = o.o_mix[c].astype(F32)
        out.gu[:, c, :] = o.o_gu[c].astype(F32)
        at = HEAD_SIZE + NW * c
        out.st[c] = turned[at : at + NW]
    small = o.o_small

    def part(row, width, count):
        at = s * width
        first = at // LANES
        lanes = jnp.concatenate([row(first + k) for k in range(count)], axis=1)
        return roll(lanes, lax.rem(count * LANES - (at - first * LANES), count * LANES))[:, :width]

    for at, dst in ((0, out.ngain), (8, out.mgain)):
        dst[...] = part(lambda k: o.o_gains[pl.ds(at + k, 1), :], R, 1)
    for k in range(ns):
        for i in range(per):
            out.gains[per * k + i : per * k + i + 1, :] = small[k, i : i + 1, :]
    width = out.ggain.shape[1]
    last = ns * per - 1
    out.ggain[...] = part(lambda k: out.gains[pl.ds(jnp.minimum(k, last), 1), :], width, 3)
    heads = 0.0
    for k in range(ns):
        into = (iota((LANES, LANES), 1) == HL * k + iota((LANES, LANES), 0)) & (
            iota((LANES, LANES), 0) < HL
        )
        heads = heads + nn(small[k, :8, :], into.astype(F32), RIGHT)
        for j in range(KC):
            for i in range(per):
                row = 6 + per * j + i
                at = C * k + LANES * i
                out.taps[j : j + 1, at : at + LANES] = small[k, row : row + 1, :]
    out.skip[...], out.rate[...], out.bias[...] = (heads[k : k + 1, :NH] for k in (3, 4, 5))
    for j in range(KC):
        row = small[t, 6 + KC * per + j : 7 + KC * per + j, :]
        for c in range(2):
            out.taps_st[j, c : c + 1, :] = row[:, NW * c : NW * (c + 1)]


def finish(n, ns, o, shapes):
    sd = lambda *shape: jax.ShapeDtypeStruct(shape, F32)
    R, F = o.o_down.shape
    T, D = o.layer_output.shape
    NW = shapes.NW
    outs = dict(
        layer_output=jax.ShapeDtypeStruct((T, D), BF16),
        input_grad=sd(T, D),
        att=sd(*o.o_att.shape),
        joint=sd(*o.o_joint.shape),
        down=sd(R, F),
        step=sd(NH, R),
        mix=sd(R, 2, NH * HDM),
        gu=sd(R, 2, F),
        st=sd(2, NW, R),
        ngain=sd(1, R),
        mgain=sd(1, R),
        ggain=sd(1, NH * HDM // n),
        gains=sd(NH * HDM // LANES, LANES),
        taps=sd(KC, NH * HDM),
        taps_st=sd(KC, 2, NW),
        skip=sd(1, NH),
        rate=sd(1, NH),
        bias=sd(1, NH),
    )
    arrays = dict(o.__dict__)
    flat = [jax.tree.flatten(group) for group in (arrays, outs)]
    whole = pl.BlockSpec(memory_space=pltpu.VMEM)
    got = pl.pallas_call(
        functools.partial(finish_kernel, n, ns, flat[0][1], flat[1][1]),
        out_shape=flat[1][0],
        in_specs=[whole] * len(arrays),
        out_specs=[whole] * len(outs),
        name="finish",
        compiler_params=pltpu.CompilerParams(vmem_limit_bytes=VMEM_LIMIT),
    )(*flat[0][0])
    return types.SimpleNamespace(**jax.tree.unflatten(flat[1][1], got))


def local(
    layer_input,
    out_grad,
    doc_starts,
    real_mask,
    norm_gain,
    attention_input_rows,
    mixer_in,
    state_in,
    step_in,
    conv_mixer,
    conv_state,
    step_bias,
    decay_rate,
    skip_gain,
    gated_gain,
    joint_out,
    mlp_gain,
    gate_up,
    down_weight,
):
    T, D = layer_input.shape
    NS, n = lax.axis_size(STATE), lax.axis_size(SEQ)
    NW = state_in.shape[2]
    o = layer(
        n,
        NS,
        dict(
            x=layer_input,
            g=out_grad,
            w_att=attention_input_rows,
            w_mix_in=mixer_in,
            w_step=step_in.T,
            st_own=jnp.transpose(state_in, (1, 2, 0)),
            conv_state=conv_state,
            conv_mixer=conv_mixer,
            ngain=norm_gain[None, :],
            ggain=gated_gain.reshape(-1, LANES),
            mgain=mlp_gain[None, :],
            joint=joint_out,
            w_gu_in=gate_up,
            down_in=down_weight,
            real=real_mask.reshape(-1, LANES),
            step_bias=step_bias,
            decay_rate=decay_rate,
            skip_gain=skip_gain,
            doc_starts=doc_starts,
        ),
    )
    e = finish(n, NS, o, types.SimpleNamespace(NW=NW))
    return (
        e.layer_output,
        e.input_grad,
        e.ngain.reshape(-1),
        e.att,
        e.mix,
        e.st.transpose(2, 0, 1),
        e.step.T,
        e.taps,
        e.taps_st,
        e.bias.reshape(-1),
        e.rate.reshape(-1),
        e.skip.reshape(-1),
        e.ggain.reshape(-1),
        e.joint,
        e.mgain.reshape(-1),
        e.gu,
        e.down,
    )


def solution(mesh):
    rep = P()
    in_specs = (
        P(SEQ, None),
        P(SEQ, None),
        rep,
        rep,
        rep,
        rep,
        rep,
        P(None, None, STATE),
        rep,
        rep,
        P(None, None, STATE),
        rep,
        rep,
        rep,
        rep,
        rep,
        rep,
        P(None, None, STATE),
        P(None, STATE),
    )
    out_specs = (
        P(SEQ, None),
        P(SEQ, None),
        P(SEQ),
        P(SEQ, None),
        P(SEQ, None, None),
        P(SEQ, None, STATE),
        P(SEQ, None),
        rep,
        P(None, None, STATE),
        rep,
        rep,
        rep,
        P(SEQ),
        P(SEQ, None),
        P(SEQ),
        P(SEQ, None, STATE),
        P(SEQ, STATE),
    )
    return jax.shard_map(local, mesh=mesh, in_specs=in_specs, out_specs=out_specs, check_vma=False)
```

```python
import functools
import math
import types

import jax
import jax.numpy as jnp
from jax import lax
from jax.experimental import pallas as pl
from jax.experimental.pallas import tpu as pltpu
from jax.sharding import PartitionSpec as P

QUERY_HEADS = 8
KEY_VALUE_HEADS = 2
HEAD_SIZE = 64
NH = 24
HDM = 64
KC = 4
EPSILON = 1e-05
ROPE_BASE = 10000.0
FINE, LEFT, RIGHT = 1, 2, 3
F32 = jnp.float32
BF16 = jnp.bfloat16
LANES = 128
HALO = 16
FAR = -1e30
MESH = pl.DeviceIdType.MESH
SEQ, STATE = "seq", "state"
VMEM_LIMIT = 63 << 20


def parts(v):
    high = v.astype(BF16)
    return high, (v - high.astype(F32)).astype(BF16)


def product(dims, a, b, mode):
    dot = lambda u, v: lax.dot_general(u, v, (dims, ((), ())), preferred_element_type=F32)
    if mode is None:
        return dot(a, b)
    if mode == LEFT:
        high, low = parts(b)
        a = a.astype(BF16)
        return dot(a, high) + dot(a, low)
    if mode == RIGHT:
        high, low = parts(a)
        b = b.astype(BF16)
        return dot(high, b) + dot(low, b)
    a_high, a_low = parts(a)
    b_high, b_low = parts(b)
    return dot(a_high, b_high) + (dot(a_high, b_low) + dot(a_low, b_high))


def nn(a, b, mode=None):
    return product(((1,), (0,)), a, b, mode)


def nt(a, b, mode=None):
    return product(((1,), (1,)), a, b, mode)


def tn(a, b, mode=None):
    return product(((0,), (0,)), a, b, mode)


def sigmoid(v):
    return 1.0 / (1.0 + jnp.exp(-v))


def silu(v):
    return v * sigmoid(v)


def silu_slope(v):
    s = sigmoid(v)
    return s * (1.0 + v * (1.0 - s))


def softplus(v):
    return jnp.maximum(v, 0.0) + jnp.log1p(jnp.exp(-jnp.abs(v)))


def iota(shape, dim):
    return lax.broadcasted_iota(jnp.int32, shape, dim)


def doc_of(starts, pos):
    found = jnp.full(pos.shape, -1, jnp.int32)
    for start in starts:
        found = found + (pos >= start).astype(jnp.int32)
    return found


def roll(v, shift):
    return pltpu.roll(v, shift, 1)


def rope(v, cosine, sine, direction):
    first = (iota(v.shape, 1) % HEAD_SIZE) < HEAD_SIZE // 2
    half = HEAD_SIZE // 2
    partner = jnp.where(first, -roll(v, v.shape[1] - half), roll(v, half))
    return v * cosine + partner * (direction * sine)


def expander(width):
    return (iota((LANES, width), 1) // HDM == iota((LANES, width), 0)).astype(F32)


def masks_of(starts, first_row, rows):
    pos = first_row + iota((rows, 1), 0)
    doc = doc_of(starts, pos)
    masks = [(doc_of(starts, pos - (KC - 1 - k)) == doc).astype(F32) for k in range(KC)]
    return doc, masks


def push(src, dst, send_sem, recv_sem, device):
    copy = pltpu.make_async_remote_copy(
        src_ref=src,
        dst_ref=dst,
        send_sem=send_sem,
        recv_sem=recv_sem,
        device_id=device,
        device_id_type=MESH,
    )
    copy.start()
    return copy


def greet(n, ns, s, t):
    barrier = pltpu.get_barrier_semaphore()

    def seq_turn(k, carried):
        pl.semaphore_signal(barrier, inc=1, device_id={SEQ: lax.rem(s + k, n)}, device_id_type=MESH)
        return carried

    lax.fori_loop(1, n, seq_turn, 0)
    for k in range(1, ns):
        other = lax.rem(t + k, ns)
        pl.semaphore_signal(barrier, inc=1, device_id={STATE: other}, device_id_type=MESH)
        pl.semaphore_signal(
            barrier, inc=1, device_id={SEQ: lax.rem(s + 1, n), STATE: other}, device_id_type=MESH
        )
    return lambda: pl.semaphore_wait(barrier, n - 1 + 2 * (ns - 1))


def conv_ref(ext_ref, taps, masks, rows):
    total = 0.0
    for k in range(KC):
        at = HALO - KC + 1 + k
        total = total + ext_ref[at : at + rows, :] * taps[k : k + 1] * masks[k]
    return total


class Carry:
    def __init__(self, refs, window, n, s, direction, rows_e):
        self.n, self.s, self.direction, self.rows_e = n, s, direction, rows_e
        self.tx, self.rx, self.thr_tx, self.thr_rx = refs.tx, refs.rx, refs.thr_tx, refs.thr_rx
        self.send, self.recv = refs.sem
        self.thr_send, self.thr_recv = refs.thr_sem
        self.total, self.thr = window
        self.count = carry_steps(n)

    def place(self, slot):
        return (1, 0) if slot == 0 else (2, 0) if slot == 1 else (1 << (slot - 1), slot - 1)

    def copies(self, slot, d, source):
        to = lax.rem(self.s + self.direction * d + self.n, self.n)
        make = lambda src, dst, a, b: pltpu.make_async_remote_copy(
            src_ref=src,
            dst_ref=dst,
            send_sem=a,
            recv_sem=b,
            device_id={SEQ: to},
            device_id_type=MESH,
        )
        return (
            make(self.tx.at[source], self.rx.at[slot], self.send.at[slot], self.recv.at[slot]),
            make(
                self.thr_tx.at[source],
                self.thr_rx.at[slot],
                self.thr_send.at[slot],
                self.thr_recv.at[slot],
            ),
        )

    def inside(self, index):
        return (index >= 0) & (index < self.n)

    def start(self, slot, d, source):
        @pl.when(self.inside(self.s + self.direction * d))
        def _():
            for copy in self.copies(slot, d, source):
                copy.start()

    def finish(self):
        for slot in range(self.count):
            d, source = self.place(slot)

            @pl.when(self.inside(self.s + self.direction * d))
            def _():
                for copy in self.copies(slot, d, source):
                    copy.wait_send()

    def begin(self, part, thr):
        self.tx[0] = part.astype(BF16)
        self.thr_tx[0] = thr
        self.total[...] = jnp.zeros(self.total.shape, F32)
        self.thr[...] = jnp.ones(self.thr.shape, F32)
        for slot in range(min(2, self.count)):
            self.start(slot, *self.place(slot))

    def join(self, slot, d, source):
        @pl.when(self.inside(self.s - self.direction * d))
        def _():
            for copy in self.copies(slot, d, source):
                copy.wait_recv()
            column = nt(self.rows_e, self.thr[...], LEFT)[:, :1]
            self.total[...] += column * self.rx[slot].astype(F32)
            self.thr[...] = self.thr[...] * self.thr_rx[slot]

        @pl.when(jnp.logical_not(self.inside(self.s - self.direction * d)))
        def _():
            self.thr[...] = jnp.zeros(self.thr.shape, F32)

    def pass_on(self, slot, d):
        self.tx[slot - 1] = self.total[...].astype(BF16)
        self.thr_tx[slot - 1] = self.thr[...]
        self.start(slot, d, slot - 1)

    def advance(self, slot):
        self.join(slot, *self.place(slot))
        if 1 <= slot < self.count - 1:
            self.pass_on(slot + 1, 1 << slot)

    def rest(self, first):
        if first >= self.count:
            return
        for slot in range(first, min(2, self.count)):
            self.advance(slot)
        first = max(first, 2)

        def turn(slot, d):
            self.join(slot, d, slot - 1)
            self.pass_on(slot + 1, 2 * d)
            return 2 * d

        if first < self.count:
            lax.fori_loop(first, self.count - 1, turn, 1 << (first - 1))
            self.join(self.count - 1, 1 << (self.count - 2), self.count - 2)


def carry_steps(n):
    return 1 if n <= 2 else 1 + (n - 2).bit_length()


def expand_rows(width):
    return (iota((width, LANES), 0) // HDM == iota((width, LANES), 1)).astype(F32)


def link_of(linked, cum, cum_t, h):
    return jnp.exp(jnp.where(linked, cum[:, h : h + 1] - cum_t[h : h + 1, :], FAR))


def send_to(sems, k, src, dst, device):
    send, recv = sems
    return push(src, dst, send.at[k], recv.at[k], device)


def row_sums(values):
    return nt(jnp.ones((8, values.shape[1]), F32), values, LEFT)


def as_column(row):
    first = (iota((8, LANES), 0) == 0).astype(F32)
    return tn(row, first, RIGHT)[:, :1]


def share_rows(refs, ns, t, row):
    tx, rx = refs.tx, refs.rx
    tx[...] = row
    copies = [
        send_to(refs.sem, k - 1, tx, rx.at[k - 1], {STATE: lax.rem(t + k, ns)})
        for k in range(1, ns)
    ]

    def wait():
        total = tx[...]
        for k in range(1, ns):
            copies[k - 1].wait_recv()
            total = total + rx[k - 1]
        return total

    return copies, wait


class RowScatter:
    def __init__(self, refs, sem, t):
        self.sem, self.t = sem, t
        self.tx, self.rx, self.mid = refs.tx, refs.rx, refs.mid
        self.odd, self.far = lax.rem(t, 2), t // 2
        self.copies = []

    def start(self, part):
        rows = self.tx.shape[1]
        part = part.astype(BF16)
        for k in range(4):
            self.tx[(k % 2) * 2 + k // 2] = part[rows * k : rows * (k + 1)]
        theirs = self.tx.at[pl.ds(2 - 2 * self.odd, 2)]
        self.copies.append(
            send_to(self.sem, 0, theirs, self.rx.at[pl.ds(0, 2)], {STATE: sibling(self.t)})
        )

    def middle(self):
        self.copies[0].wait_recv()
        away = 1 - self.far
        self.mid[...] = (
            self.tx[2 * self.odd + away].astype(F32) + self.rx[away].astype(F32)
        ).astype(BF16)
        self.copies.append(
            send_to(self.sem, 1, self.mid, self.rx.at[2], {STATE: lax.rem(self.t + 2, 4)})
        )

    def finish(self):
        total = self.tx[2 * self.odd + self.far].astype(F32) + self.rx[self.far].astype(F32)
        self.copies[1].wait_recv()
        return total + self.rx[2].astype(F32)


class Gather:
    def __init__(self, block, sem, t):
        self.block, self.sem, self.t = block, sem, t
        own = block(t)
        self.copies = [
            send_to(sem, 0, own, own, {STATE: sibling(t)}),
            send_to(sem, 1, own, own, {STATE: lax.rem(t + 2, 4)}),
        ]

    def middle(self):
        self.copies[1].wait_recv()
        block = self.block(lax.rem(self.t + 2, 4))
        self.copies.append(send_to(self.sem, 2, block, block, {STATE: sibling(self.t)}))

    def finish(self):
        self.copies[0].wait_recv()
        self.copies[2].wait_recv()


def gather(every, sem, t, own):
    every[t] = own
    return Gather(lambda index: every.at[index], sem, t)


def sibling(t):
    return t + 1 - 2 * lax.rem(t, 2)


def levels_of(n):
    return n.bit_length() - 1


def bits_of(n, swapped):
    order = list(range(levels_of(n)))
    if swapped and len(order) > 1:
        order[0], order[1] = order[1], order[0]
    return order


class HalvingSum:
    def __init__(self, refs, n, s, swapped=False):
        self.sem, self.n, self.s = refs.sem, n, s
        self.bits = bits_of(n, swapped)
        self.src, self.rx = refs.src, refs.rx
        self.copies = []

    def owner(self, p):
        top = len(self.bits) - 1
        return sum(((p >> (top - level)) & 1) << bit for level, bit in enumerate(self.bits))

    def block_of(self, index):
        top = len(self.bits) - 1
        return sum(((index >> bit) & 1) << (top - level) for level, bit in enumerate(self.bits))

    def fill(self, column, values):
        rows = self.src.shape[1]
        width = values.shape[1]
        for p in range(self.n):
            at = rows * self.owner(p)
            self.src[p, :, column : column + width] = values[at : at + rows]

    def parts(self, level):
        half = self.n >> (level + 1)
        mine = lax.rem(self.s // (1 << self.bits[level]), 2)
        if level == 0:
            return self.src, 0, half, mine
        return self.rx, self.n - (self.n >> (level - 1)), half, mine

    def start(self, level=0):
        buffer, base, half, mine = self.parts(level)
        to = self.s + (1 - 2 * mine) * (1 << self.bits[level])
        here = self.n - (self.n >> level)
        self.copies.append(
            send_to(
                self.sem,
                level,
                buffer.at[pl.ds(base + (1 - mine) * half, half)],
                self.rx.at[pl.ds(here, half)],
                {SEQ: to},
            )
        )

    def step(self, level):
        buffer, base, half, mine = self.parts(level)
        self.copies[level].wait_recv()
        here = self.n - (self.n >> level)

        def turn(i, carried):
            kept = buffer[base + mine * half + i].astype(F32)
            self.rx[here + i] = (kept + self.rx[here + i].astype(F32)).astype(BF16)
            return carried

        lax.fori_loop(0, half, turn, 0)
        if level + 1 < len(self.bits):
            self.start(level + 1)

    def result(self):
        return self.rx[self.n - 2]


def named(value):
    if isinstance(value, dict):
        return types.SimpleNamespace(**{key: named(item) for key, item in value.items()})
    return value


def layer_kernel(n, ns, trees, *flat):
    refs, at = types.SimpleNamespace(), 0
    for tree in trees:
        part = jax.tree.unflatten(tree, flat[at : at + tree.num_leaves])
        at += tree.num_leaves
        refs.__dict__.update(named(part).__dict__)
    x, normed, inv1 = refs.x, refs.normed, refs.inv1
    w_mix, w_qkv, w_joint, w_gu, down = refs.w_mix, refs.w_qkv, refs.w_joint, refs.w_gu, refs.down
    grad = refs.grad
    w_step = refs.w_step
    T, D = x.shape
    t, s = lax.axis_index(STATE), lax.axis_index(SEQ)
    joined = refs.jall_all.at[t]
    C = w_mix.shape[2]
    QC = 2 * HEAD_SIZE
    AQ = QUERY_HEADS * HEAD_SIZE
    NW = refs.st_own.shape[1]
    HL = NH // ns
    N = NW * ns
    TO = T // ns
    DM = C * ns
    F = down.shape[1]
    pairs = C // LANES
    scale = 1.0 / math.sqrt(HEAD_SIZE)
    state_peer = lambda k: {STATE: lax.rem(t + k, ns)}
    own_c = pl.ds(pl.multiple_of(C * t, LANES), C)
    loads = [
        pltpu.make_async_copy(src, dst, refs.load[k])
        for k, (src, dst) in enumerate(
            [
                (refs.w_att.at[:, pl.ds(pl.multiple_of(QC * t, LANES), QC)], w_qkv.at[:, pl.ds(0, QC)]),
                (refs.w_att.at[:, pl.ds(AQ, 2 * QC)], w_qkv.at[:, pl.ds(QC, 2 * QC)]),
                (refs.w_mix_in.at[:, :, own_c], refs.raw),
                (refs.joint.at[pl.ds(pl.multiple_of(QC * t, QC), QC)], w_joint.at[pl.ds(0, QC)]),
                (refs.joint.at[pl.ds(pl.multiple_of(AQ + C * t, LANES), C)], w_joint.at[pl.ds(QC, C)]),
                (refs.g, grad),
                (refs.down_in, down),
                (refs.w_gu_in.at[:, :, pl.ds(0, F // 2)], refs.raw.at[:, :, pl.ds(0, F // 2)]),
                (refs.w_gu_in.at[:, :, pl.ds(F // 2, F // 2)], refs.raw.at[:, :, pl.ds(0, F // 2)]),
            ]
        )
    ]
    for load in loads[:-2]:
        load.start()
    lanes_row = iota((1, LANES), 1)
    blank = jnp.zeros((1, LANES), F32)
    met = greet(n, ns, s, t)
    bias_row, rate_row = blank, blank
    skip_row = jnp.zeros((1, C), F32)
    heads_row = iota((1, C), 1) // HDM
    for h in range(HL):
        bias_row = jnp.where(lanes_row == h, refs.step_bias[HL * t + h], bias_row)
        rate_row = jnp.where(lanes_row == h, refs.decay_rate[HL * t + h], rate_row)
        skip_row = jnp.where(heads_row == h, refs.skip_gain[HL * t + h], skip_row)
    taps_mix = refs.conv_mixer[:, own_c]
    ggain_row = jnp.concatenate(
        [refs.ggain[pl.ds(C // LANES * t + k, 1), :] for k in range(C // LANES)], axis=1
    )
    pick = (iota((NH, LANES), 0) == HL * t + iota((NH, LANES), 1)) & (iota((NH, LANES), 1) < HL)
    pick = pick.astype(F32)
    refs.taps8[...] = jnp.zeros(refs.taps8.shape, F32)
    for c in range(2):
        refs.taps8[:KC, NW * c : NW * (c + 1)] = refs.conv_state[:, c, :]
    eye8 = (iota((8, LANES), 0) == iota((8, LANES), 1)).astype(F32)
    taps_cols = tn(refs.taps8[...], eye8, RIGHT)
    for c in range(2):
        refs.taps_st[c] = taps_cols[NW * c : NW * (c + 1)]
    sent = []
    mine = pl.ds(pl.multiple_of(NW * t, NW), NW)
    refs.st_all[:, mine, :] = refs.st_own[...]
    refs.taps_all[:, mine, :] = refs.taps_st[...]

    first_row = s * T
    starts = [refs.doc_starts[k] for k in range(refs.doc_starts.shape[0])]
    doc, masks = masks_of(starts, first_row, T)
    tiles = T // LANES

    def code_turn(j, carried):
        for i in range(tiles):
            real = refs.real[pl.ds(tiles * j + i, 1), :]
            ids = doc_of(starts, j * T + i * LANES + iota((1, LANES), 1))
            refs.codes[pl.ds(tiles * j + i, 1), :] = jnp.where(real > 0, ids, -7)
        return carried

    lax.fori_loop(0, n, code_turn, 0)

    def code_of(j):
        return jnp.concatenate([refs.codes[pl.ds(tiles * j + i, 1), :] for i in range(tiles)], axis=1)

    real_col = as_column(jnp.broadcast_to((code_of(s) >= 0).astype(F32), (8, T)))
    firsts = jnp.zeros((T, 1), jnp.int32)
    places = first_row + iota((T, 1), 0)
    for start in starts:
        firsts = jnp.where(places >= start, start, firsts)
    powers = (iota((1, LANES), 1) % (HEAD_SIZE // 2)).astype(F32) * (2.0 / HEAD_SIZE)
    angles = (places - firsts).astype(F32) * jnp.exp(-math.log(ROPE_BASE) * powers)
    cosine, sine = jnp.cos(angles), jnp.sin(angles)
    doc_row = doc_of(starts, first_row + iota((1, T), 1))
    lane = iota((T, LANES), 1)
    low = lane < HEAD_SIZE
    ngain = refs.ngain[...]

    met()
    halo_copy = pltpu.make_async_remote_copy(
        src_ref=x.at[pl.ds(T - HALO, HALO)],
        dst_ref=refs.halo_rx,
        send_sem=refs.halo[0].at[0],
        recv_sem=refs.halo[1].at[0],
        device_id={SEQ: lax.rem(s + 1, n)},
        device_id_type=MESH,
    )

    @pl.when(s + 1 < n)
    def _():
        halo_copy.start()

    columns = lambda every: lambda i: every.at[:, pl.ds(pl.multiple_of(NW * i, NW), NW), :]
    st_gather = Gather(columns(refs.st_all), refs.st, t)
    taps_gather = Gather(columns(refs.taps_all), refs.taps, t)
    xf = x[...].astype(F32)
    inv = lax.rsqrt(jnp.mean(xf * xf, axis=1, keepdims=True) + EPSILON)
    inv1[...] = inv
    normed[HALO:, :] = (xf * inv * ngain).astype(BF16)
    main = normed[HALO:, :]
    loads[0].wait()
    loads[1].wait()
    qkv = nn(main, w_qkv[...])
    q = (rope(qkv[:, :QC], cosine, sine, 1.0).astype(BF16) * scale).astype(F32)
    kcos, ksin = jnp.where(low, cosine, 1.0), jnp.where(low, sine, 0.0)
    kv_all = refs.kv_all
    group = t // 2
    both_k, both_v = qkv[:, QC : 2 * QC], qkv[:, 2 * QC :]
    own_kv = jnp.where(
        low,
        jnp.where(group == 0, both_k, roll(both_k, HEAD_SIZE)),
        jnp.where(group == 0, roll(both_v, HEAD_SIZE), both_v),
    )
    kv_all[s] = rope(own_kv, kcos, ksin, 1.0).astype(BF16)

    core = lax.rem(t, 2)
    H2 = T // 2
    own_half = pl.ds(pl.multiple_of(H2 * core, H2), H2)
    other_half = pl.ds(pl.multiple_of(H2 * (1 - core), H2), H2)

    def kv_copy(k):
        return pltpu.make_async_remote_copy(
            src_ref=kv_all.at[s, own_half],
            dst_ref=kv_all.at[s, own_half],
            send_sem=refs.kv[0].at[k - 1],
            recv_sem=refs.kv[1].at[k - 1],
            device_id={SEQ: lax.rem(s + k, n)},
            device_id_type=MESH,
        )

    def kv_pair(k):
        block = kv_all.at[s - k, own_half]
        return pltpu.make_async_remote_copy(
            src_ref=block,
            dst_ref=block,
            send_sem=refs.kv_fwd[0].at[k - 1],
            recv_sem=refs.kv_fwd[1].at[k - 1],
            device_id={STATE: sibling(t)},
            device_id_type=MESH,
        )

    def kv_turn(k, carried):
        kv_copy(k).start()
        return carried

    lax.fori_loop(1, n - s, kv_turn, 0)
    refs.q2[:T, :] = jnp.where(low, q, 0.0).astype(BF16)
    refs.q2[T:, :] = jnp.where(low, roll(q, HEAD_SIZE), 0.0).astype(BF16)
    raw = nn(nt(main, w_step[...]), pick, RIGHT) + bias_row

    doc2 = jnp.concatenate([doc, doc], axis=0)
    m_ref, l_ref, acc_ref = refs.m_acc, refs.l_acc, refs.o_acc
    m_ref[...] = jnp.full(m_ref.shape, FAR, F32)
    l_ref[...] = jnp.zeros(l_ref.shape, F32)
    acc_ref[...] = jnp.zeros(acc_ref.shape, F32)

    def allowed_at(j, diagonal):
        allowed = code_of(j) == doc2
        if diagonal:
            rows2 = jnp.concatenate([iota((T, T), 0)] * 2, axis=0)
            cols2 = iota((2 * T, T), 1)
            allowed = (allowed & (cols2 <= rows2)) | (cols2 == rows2)
        return allowed

    def attend(j, diagonal):
        block = kv_all[j]
        scores = jnp.where(allowed_at(j, diagonal), nt(refs.q2[...], block), FAR)
        m = m_ref[...]
        m_new = jnp.maximum(m, jnp.max(scores, axis=1, keepdims=True))
        shrink = jnp.exp(m - m_new)
        p = jnp.exp(scores - m_new)
        l_ref[...] = l_ref[...] * shrink + jnp.sum(p, axis=1, keepdims=True)
        acc_ref[...] = acc_ref[...] * shrink + nn(p.astype(BF16), block)
        m_ref[...] = m_new

    def attend_turn(k, carried):
        @pl.when(k < s)
        def _():
            kv_copy(k + 1).wait_recv()
            kv_pair(k + 1).start()

        kv_pair(k).wait_recv()
        attend(s - k, False)
        return carried

    def attend_some(first, stop):
        lax.fori_loop(first, stop, attend_turn, 0)

    cut1, cut2 = 1 + (s + 1) // 3, 1 + (2 * s + 1) // 3
    attend(s, True)
    loads[2].wait()

    def split_mixer(c):
        def turn(k, carried):
            rows = pl.ds(pl.multiple_of(64 * k, 64), 64)
            w_mix[c, rows, :] = refs.raw[rows, c, :C]
            return carried

        lax.fori_loop(0, D // 64, turn, 0)

    split_mixer(1)
    taps_gather.middle()
    st_gather.middle()

    @pl.when(s > 0)
    def _():
        halo_copy.wait_recv()

    @pl.when(s == 0)
    def _():
        refs.halo_rx[...] = jnp.zeros(refs.halo_rx.shape, BF16)

    hf = refs.halo_rx[...].astype(F32)
    inv_h = lax.rsqrt(jnp.mean(hf * hf, axis=1, keepdims=True) + EPSILON)
    normed[:HALO, :] = (hf * inv_h * ngain).astype(BF16)
    ext_f, ext_s, ext_o = refs.ext_f, refs.ext_s, refs.ext_o
    ext_f[...] = nn(normed[...], w_mix[1]).astype(BF16).astype(F32)
    inner_lin = conv_ref(ext_f, taps_mix, masks, T)
    inner = silu(inner_lin)
    taps_gather.finish()
    st_gather.finish()
    for c in range(2):
        ext_s[...] = nt(normed[...], refs.st_all[c]).astype(BF16).astype(F32)
        taps = refs.taps_all[c].T
        refs.wr[c] = silu(conv_ref(ext_s, taps, masks, T))
    write, read = refs.wr[0], refs.wr[1]
    step = softplus(raw)
    causal = iota((T, T), 0) >= iota((T, T), 1)
    tri = causal.astype(F32)
    cum = nn(tri, -step * rate_row, LEFT)
    cum_t = cum.T
    linked = (doc == doc_row) & causal
    E = expander(C)
    rows_e = expand_rows(C)
    inflow = step * real_col
    inflow_e = nn(inflow, E, RIGHT)
    in_x = inner * inflow_e
    cum_last = cum[T - 1 : T]
    last = first_row + T - 1
    doc_last = doc_of(starts, jnp.full((T, 1), last, jnp.int32))
    prior = doc_of(starts, jnp.full((T, 1), first_row - 1, jnp.int32))
    tail = jnp.where(doc == doc_last, jnp.exp(cum_last - cum), 0.0)
    refs.tail_e[...] = nn(tail, E, RIGHT)
    state_part = tn(refs.tail_e[...] * in_x, write, FINE)
    alive = (doc == prior).astype(F32)
    alive_last = (doc_last == prior).astype(F32)[:8]
    thr = alive_last * jnp.exp(jnp.broadcast_to(cum_last, (8, LANES)))
    steps = carry_steps(n)

    carry = Carry(refs.fc, (refs.window, refs.window_thr), n, s, 1, rows_e)
    carry.begin(state_part, thr)

    g_mat = nt(read, write, FINE)
    for p in range(pairs):
        cols = slice(LANES * p, LANES * (p + 1))
        ys = []
        for h in (2 * p, 2 * p + 1):
            link = link_of(linked, cum, cum_t, h)
            ys.append(nn(link * g_mat, in_x[:, cols], FINE))
        refs.ssd[:, cols] = jnp.where(low, ys[0], ys[1])

    split_mixer(0)
    loads[7].start()
    refs.z[...] = nn(main, w_mix[0])
    for slot in range(min(2, steps)):
        carry.advance(slot)

    @pl.when(s > 0)
    def _():
        kv_copy(1).wait_recv()
        kv_pair(1).start()

    attend_some(1, cut1)
    if steps > 2:
        carry.advance(2)
    attend_some(cut1, cut2)
    carry.rest(3)
    s_in = refs.window[...]
    refs.reach_e[...] = nn(alive * jnp.exp(cum), E, RIGHT)
    ssd = refs.ssd[...] + refs.reach_e[...] * nt(read, s_in, FINE)
    refs.ssd[...] = ssd
    z = refs.z[...]
    full_mix = ssd + skip_row * inner
    gated = full_mix * silu(z)
    copies, wait = share_rows(refs.sq, ns, t, row_sums(gated * gated))
    sent += copies
    attend_some(cut2, s + 1)
    out = acc_ref[...] / l_ref[...]
    acc_ref[...] = out
    m_ref[...] = m_ref[...] + jnp.log(l_ref[...])
    joined[:, :QC] = jnp.where(low, roll(out[:T], HEAD_SIZE), out[T:]).astype(BF16)
    loads[3].wait()
    loads[4].wait()
    loads[5].wait()
    loads[6].wait()
    dh = nn(grad[...], down[...])
    inv_g = as_column(lax.rsqrt(wait() / DM + EPSILON))
    joined[:, QC:] = (gated * inv_g * ggain_row).astype(BF16)
    rs1 = RowScatter(refs.rs1, refs.rs1_sem, t)
    rs1.start(nn(joined[...], w_joint[...]))
    own_rows = pl.ds(pl.multiple_of(TO * t, TO), TO)
    x_own = x[own_rows, :].astype(F32)
    rs1.middle()
    loads[7].wait()

    def split_columns(half):
        columns = slice(F // 2 * half, F // 2 * (half + 1))

        def turn(k, carried):
            rows = pl.ds(pl.multiple_of(64 * k, 64), 64)
            for c in range(2):
                w_gu[c, rows, columns] = refs.raw[rows, c, : F // 2]
            return carried

        lax.fori_loop(0, D // 64, turn, 0)

    split_columns(0)
    loads[8].start()
    res = x_own + rs1.finish()
    inv2 = lax.rsqrt(jnp.mean(res * res, axis=1, keepdims=True) + EPSILON)
    mgain = refs.mgain[...]
    ag1 = gather(refs.ag1_all, refs.ag1_sem, t, (res * inv2 * mgain).astype(BF16))
    loads[8].wait()
    split_columns(1)
    ag1.middle()
    jall = Gather(lambda index: refs.jall_all.at[index], refs.jall, t)
    ag1.finish()

    n2 = jnp.concatenate([refs.ag1_all[k] for k in range(ns)], axis=0)
    gate, up = nn(n2, w_gu[0]), nn(n2, w_gu[1])
    sig = sigmoid(gate)
    act = gate * sig
    hidden = (act * up).astype(BF16)
    d_gate = (dh * up * (sig * (1.0 + gate * (1.0 - sig)))).astype(BF16)
    d_up = (dh * act).astype(BF16)
    rs2 = RowScatter(refs.rs2, refs.rs2_sem, t)
    rs2.start(nt(d_gate, w_gu[0]) + nt(d_up, w_gu[1]))
    for copy in rs1.copies + ag1.copies:
        copy.wait_send()
    rs3 = RowScatter(refs.rs1, refs.rs3_sem, t)
    rs3.start(nt(hidden, down[...]))
    rs2.middle()

    def weight_sum(stream, parts, swapped=False):
        total = HalvingSum(stream, n, s, swapped)
        column = 0
        for lhs, rhs in parts:
            width = rhs.shape[1]
            for c in range(0, width, 256):
                piece = rhs[:, c : min(c + 256, width)]
                total.fill(column + c, tn(lhs, piece).astype(BF16))
            column += width
        return total

    sum_gate = weight_sum(refs.gate_g, [(n2, d_gate)], True)
    sum_gate.start()
    rs3.middle()
    sum_down = weight_sum(refs.down_g, [(grad[...], hidden)])
    sum_down.start()
    sum_up = weight_sum(refs.up_g, [(n2, d_up)])
    dn2 = rs2.finish()
    scaled = dn2 * mgain
    d_res = (
        grad[own_rows, :].astype(F32)
        + inv2 * scaled
        - res * inv2 * inv2 * inv2 * jnp.mean(scaled * res, axis=1, keepdims=True)
    )
    ag2 = gather(refs.ag2_all, refs.ag2_sem, t, d_res.astype(BF16))

    def put_small(row, values):
        for k in range(0, values.shape[1], LANES):
            piece = values[:, k : k + LANES]
            refs.small_tx[row : row + 1, : piece.shape[1]] = piece
            row += 1

    refs.small_tx[...] = jnp.zeros(refs.small_tx.shape, F32)
    refs.step_src[...] = jnp.zeros(refs.step_src.shape, F32)
    put_small(8, jnp.sum(dn2 * res * inv2, axis=0, keepdims=True))
    ag2.middle()
    ag3 = gather(refs.ag1_all, refs.ag3_sem, t, (res + rs3.finish()).astype(BF16))
    ag2.finish()
    d_branch = jnp.concatenate([refs.ag2_all[k] for k in range(ns)], axis=0)
    d_joined = nt(d_branch, w_joint[...])
    d_gn = d_joined[:, QC:]
    scaled = d_gn * ggain_row
    copies, wait = share_rows(refs.dot, ns, t, row_sums(scaled * gated))
    sent += copies
    put_small(16, jnp.sum(d_gn * gated * inv_g, axis=0, keepdims=True))
    d_att = d_joined[:, :QC].astype(BF16).astype(F32)
    dout2 = jnp.concatenate(
        [jnp.where(low, 0.0, roll(d_att, HEAD_SIZE)), jnp.where(low, 0.0, d_att)], axis=0
    )
    delta = jnp.sum(dout2 * acc_ref[...], axis=1, keepdims=True)
    l_ref[...] = delta
    refs.dout2[...] = dout2.astype(BF16)
    jall.middle()
    sum_down.step(0)
    sum_gate.step(0)
    jall.finish()
    own_d = pl.ds(pl.multiple_of((D // ns) * t, LANES), D // ns)
    d_cols = jnp.concatenate([refs.ag2_all[k, :, own_d] for k in range(ns)], axis=0)
    sum_joint = joint = HalvingSum(refs.joint_g, n, s)
    rows_j = joint.src.shape[1]
    piece = min(rows_j, LANES)
    for k in range(ns):
        values = tn(refs.jall_all[k], d_cols).astype(BF16)
        for at in range(0, QC + C, piece):
            row = QC * k + at if at < QC else AQ + C * k + at - QC
            offset = row % rows_j
            joint.src[joint.block_of(row // rows_j), offset : offset + piece, :] = values[at : at + piece]
    dot = as_column(wait() / DM)
    d_gated = inv_g * scaled - gated * (inv_g * inv_g * inv_g * dot)
    sig = sigmoid(z)
    dy = d_gated * z * sig
    refs.d_z[...] = (d_gated * full_mix * (sig * (1.0 + z * (1.0 - sig)))).astype(BF16)
    put_small(19, nt(jnp.broadcast_to(jnp.sum(dy * inner, axis=0, keepdims=True), (8, C)), E, RIGHT)[:1])
    reach_dy = refs.reach_e[...] * dy
    carry_b = Carry(refs.bc, (refs.window, refs.window_thr), n, s, -1, rows_e)
    carry_b.begin(tn(reach_dy, read, FINE), thr)
    sum_up.start()
    joint.start()
    sum_z = weight_sum(refs.z_g, [(main, refs.d_z[...])], True)
    ag3.middle()
    d_g = jnp.zeros((T, T), F32)
    for p in range(pairs):
        cols = slice(LANES * p, LANES * (p + 1))
        xp, dyp = in_x[:, cols], dy[:, cols]
        halves = []
        for k in range(2):
            link = link_of(linked, cum, cum_t, 2 * p + k)
            halves.append(tn(link * g_mat, dyp, FINE))
            own = low if k == 0 else jnp.logical_not(low)
            d_g = d_g + link * nt(jnp.where(own, dyp, 0.0), xp, FINE)
        refs.w_tot[:, cols] = jnp.where(low, halves[0], halves[1])

    d_read = nn(d_g, write) + nn(reach_dy, s_in)
    refs.dwr_tx[1] = d_read.T.astype(BF16)
    refs.d_write[...] = tn(d_g, read)
    refs.dq2[...] = jnp.zeros(refs.dq2.shape, F32)

    def attend_back(j, diagonal):
        block = kv_all[j]
        q2, dout2 = refs.q2[...], refs.dout2[...]
        scores = jnp.where(allowed_at(j, diagonal), nt(q2, block), FAR)
        p = jnp.exp(scores - m_ref[...])
        ds = (p * (nt(dout2, block) - l_ref[...])).astype(BF16)
        refs.dq2[...] += nn(ds, block)
        return tn(ds, q2) + tn(p.astype(BF16), dout2)

    def dkv_copy(k):
        return pltpu.make_async_remote_copy(
            src_ref=refs.dkv_mid.at[k - 1],
            dst_ref=refs.dkv_rx.at[k - 1],
            send_sem=refs.dkv[0].at[k - 1],
            recv_sem=refs.dkv[1].at[k - 1],
            device_id={SEQ: lax.rem(s - k + n, n)},
            device_id_type=MESH,
        )

    def dkv_pair(k):
        return pltpu.make_async_remote_copy(
            src_ref=kv_all.at[s - k, other_half],
            dst_ref=refs.dkv_mid.at[lax.rem(k + n - 1, n)],
            send_sem=refs.dkv_fwd[0].at[k],
            recv_sem=refs.dkv_fwd[1].at[k],
            device_id={STATE: sibling(t)},
            device_id_type=MESH,
        )

    def dkv_on(k):
        dkv_pair(k).wait_recv()
        both = refs.dkv_mid[k - 1].astype(F32) + kv_all[s - k, own_half].astype(F32)
        refs.dkv_mid[k - 1] = both.astype(BF16)
        dkv_copy(k).start()

    def back_turn(k, carried):
        kv_all[s - k] = attend_back(s - k, False).astype(BF16)
        dkv_pair(k).start()

        @pl.when(k > 1)
        def _():
            dkv_on(k - 1)

        return carried

    def back_some(first, stop):
        lax.fori_loop(first, stop, back_turn, 0)

    def kv_end(k, carried):
        kv_copy(k).wait_send()
        return carried

    def pair_end(k, carried):
        kv_pair(k).wait_send()
        return carried

    lax.fori_loop(1, n - s, kv_end, 0)
    lax.fori_loop(1, s + 1, pair_end, 0)
    for slot in range(min(2, steps)):
        carry_b.advance(slot)
    back_some(1, cut1)
    if steps > 2:
        carry_b.advance(2)
    back_some(cut1, cut2)
    carry_b.rest(3)
    back_some(cut2, s + 1)
    diagonal = attend_back(s, True)
    refs.dkv_sum[...] = diagonal
    kv_all[s] = diagonal.astype(BF16)
    dkv_pair(0).start()

    @pl.when(s > 0)
    def _():
        dkv_on(s)

    sum_z.start()
    ag3.finish()
    for k in range(ns):
        refs.layer_output[TO * k : TO * (k + 1), :] = refs.ag1_all[k]
    sum_down.step(1)
    sum_gate.step(1)
    sum_up.step(0)
    later = refs.window[...]
    tail_e = refs.tail_e[...]
    tail_r = tail_e * nt(write, later, FINE)
    w_tot = refs.w_tot[...] + tail_r
    d_write = refs.d_write[...] + nn(tail_e * in_x, later)
    refs.dwr_tx[0] = d_write.T.astype(BF16)
    dwr = []
    for k in range(1, ns):
        p = lax.rem(t + k, ns)
        theirs = pl.ds(pl.multiple_of(NW * p, NW), NW)
        dwr.append(
            send_to(refs.dwr, k - 1, refs.dwr_tx.at[:, theirs, :], refs.dwr_rx.at[k - 1], {STATE: p})
        )
    sent += dwr
    d_lin = (inflow_e * w_tot + skip_row * dy) * silu_slope(inner_lin)

    def conv_back(ext, grad, taps, up, row, rows):
        grad[...] = jnp.zeros(grad.shape, F32)
        for k in range(KC):
            at = HALO - KC + 1 + k
            masked = up * masks[k]
            put_small(row + rows * k, jnp.sum(masked * ext[at : at + T, :], axis=0, keepdims=True))
            grad[at : at + T, :] += masked * taps[k : k + 1]
        return grad[...].astype(BF16)

    d_ext = conv_back(ext_f, refs.grad_f, taps_mix, d_lin, 22, C // LANES)
    st64 = refs.st_own[...].reshape(2 * NW, D)
    taps_own = refs.taps_st[...].reshape(2 * NW, LANES).T
    ext_o[...] = nt(normed[...], st64).astype(BF16).astype(F32)
    slope_o = silu_slope(conv_ref(ext_o, taps_own, masks, T))
    for copy in dwr:
        copy.wait_recv()
    d_wr = refs.dwr_tx[:, mine, :].astype(F32)
    for k in range(1, ns):
        d_wr = d_wr + refs.dwr_rx[k - 1].astype(F32)
    row_st = 22 + KC * (C // LANES)
    d_st = conv_back(ext_o, refs.grad_o, taps_own, d_wr.reshape(2 * NW, T).T * slope_o, row_st, 1)
    refs.back_tx[...] = (nt(d_ext[:HALO], w_mix[1]) + nn(d_st[:HALO], st64)).astype(BF16)
    def back_copy(member):
        return pltpu.make_async_remote_copy(
            src_ref=refs.back_tx,
            dst_ref=refs.back_rx.at[member],
            send_sem=refs.back[0].at[0],
            recv_sem=refs.back[1].at[member],
            device_id={SEQ: lax.rem(s + n - 1, n), STATE: ns - 1},
            device_id_type=MESH,
        )

    @pl.when(s > 0)
    def _():
        back_copy(t).start()

    sum_inner = weight_sum(refs.inner_g, [(normed[...], d_ext)])
    sum_inner.start()
    u = nt(inner * w_tot, E, RIGHT)
    tl = nt(in_x * tail_r, E, RIGHT)
    thr_s = jnp.sum(tn(later * s_in, rows_e, RIGHT), axis=0, keepdims=True) * thr[:1]
    d_cum = nt(dy * ssd, E, RIGHT) - inflow * u
    at_last = iota((T, LANES), 0) == T - 1
    d_cum = d_cum + jnp.where(at_last, jnp.sum(tl, axis=0, keepdims=True) + thr_s, 0.0)
    d_ld = tn(tri, d_cum, LEFT)
    d_step = real_col * u - rate_row * d_ld
    put_small(20, -jnp.sum(step * d_ld, axis=0, keepdims=True))
    d_step = d_step * sigmoid(raw)
    put_small(21, jnp.sum(d_step, axis=0, keepdims=True))
    d_step = d_step.astype(BF16)
    d_z = refs.d_z[...]
    dq2 = refs.dq2[...]
    dq = jnp.where(low, dq2[:T], roll(dq2[T:], HEAD_SIZE)) * scale
    d_q = rope(dq, cosine, sine, -1.0).astype(BF16)
    d_n = (
        nt(d_z, w_mix[0])
        + nt(d_ext[HALO:], w_mix[1])
        + nn(d_st[HALO:], st64)
        + nn(nt(d_step, pick.astype(BF16)).astype(BF16), w_step[...])
    )
    def dkv_turn(k, carried):
        dkv_copy(k).wait_recv()
        refs.dkv_half[...] += refs.dkv_rx[k - 1].astype(F32)
        return carried

    dkv_pair(0).wait_recv()
    refs.dkv_half[...] = refs.dkv_sum[own_half, :] + refs.dkv_mid[n - 1].astype(F32)
    lax.fori_loop(1, n - s, dkv_turn, 0)
    refs.pair_tx[...] = refs.dkv_half[...].astype(BF16)
    odd = core
    pair = send_to(refs.pair, 0, refs.pair_tx, refs.pair_rx, {STATE: sibling(t)})
    sent.append(pair)
    pair.wait_recv()
    refs.dkv_sum[own_half, :] = refs.pair_tx[...].astype(F32)
    refs.dkv_sum[other_half, :] = refs.pair_rx[...].astype(F32)
    d_kv = rope(refs.dkv_sum[...], kcos, ksin, -1.0)
    d_kv = jnp.where(low == (odd == 0), d_kv, 0.0)
    other = roll(d_kv, HEAD_SIZE)
    d_k = jnp.where(low, jnp.where(group == 0, d_kv, 0.0), jnp.where(group == 0, 0.0, other))
    d_v = jnp.where(low, jnp.where(group == 0, other, 0.0), jnp.where(group == 0, 0.0, d_kv))
    d_kv_b = d_kv.astype(BF16)
    d_qkv = jnp.concatenate([d_q, jnp.where(odd == 0, d_k, d_v).astype(BF16)], axis=1)
    mine_kv = jnp.where(odd == 0, d_kv, other).astype(BF16)
    pad_st = jnp.concatenate([jnp.zeros((T + HALO, HEAD_SIZE), F32), d_st.astype(F32)], axis=1)
    mine_kv = jnp.concatenate([jnp.zeros((HALO, LANES), F32), mine_kv.astype(F32)], axis=0)
    mixed = jnp.where(iota((T + HALO, LANES), 1) < HEAD_SIZE, mine_kv, pad_st).astype(BF16)
    sum_rest = weight_sum(refs.rest_g, [(main, d_q), (normed[...], mixed)])
    sum_rest.start()
    w_kv = jnp.where(odd == 0, w_qkv[:, QC : 2 * QC], w_qkv[:, 2 * QC :])
    d_n = d_n + nt(d_qkv, jnp.concatenate([w_qkv[:, :QC], w_kv], axis=1))
    for copy in rs2.copies + ag3.copies:
        copy.wait_send()
    rs4 = RowScatter(refs.rs2, refs.rs4_sem, t)
    rs4.start(d_n)
    sum_joint.step(0)
    rs4.middle()
    sum_z.step(0)
    sum_up.step(1)
    inv_own = inv1[own_rows, :]
    d_n = rs4.finish()
    last_rows = (t == ns - 1) & (s + 1 < n)

    @pl.when(last_rows)
    def _():
        for member in range(ns):
            back_copy(member).wait_recv()

    @pl.when(jnp.logical_not(last_rows))
    def _():
        refs.back_rx[...] = jnp.zeros(refs.back_rx.shape, BF16)

    from_next = refs.back_rx[0].astype(F32)
    for member in range(1, ns):
        from_next = from_next + refs.back_rx[member].astype(F32)
    d_n = jnp.concatenate([d_n[: TO - HALO], d_n[TO - HALO :] + from_next], axis=0)
    scaled = d_n * ngain
    in_g = (
        d_res
        + inv_own * scaled
        - x_own * inv_own * inv_own * inv_own * jnp.mean(scaled * x_own, axis=1, keepdims=True)
    )
    ag4 = gather(refs.ag1_all, refs.ag4_sem, t, in_g.astype(BF16))
    put_small(0, jnp.sum(d_n * x_own * inv_own, axis=0, keepdims=True))

    def small_copy(k):
        peer = lax.rem(s + k, n)
        make = lambda src, dst, at: pltpu.make_async_remote_copy(
            src_ref=src,
            dst_ref=dst,
            send_sem=refs.small[0].at[at],
            recv_sem=refs.small[1].at[at],
            device_id={SEQ: peer},
            device_id_type=MESH,
        )
        return (
            make(refs.small_tx, refs.small_rx.at[s, pl.ds(0, rows_c)], k - 1),
            make(refs.step_src.at[peer], refs.small_rx.at[s, pl.ds(rows_c, 8)], n + k - 2),
        )

    step_rows = tn(d_step, main)[:8]
    rows_c, rows_d = refs.small_tx.shape[0], D // n
    for k in range(n):
        refs.step_src[k, :, :rows_d] = step_rows[:, rows_d * k : rows_d * (k + 1)]
    refs.small_rx[s, :rows_c, :] = refs.small_tx[...]
    refs.small_rx[s, rows_c:, :] = refs.step_src[s]

    def small_turn(k, carried):
        for copy in small_copy(k):
            copy.start()
        return carried

    lax.fori_loop(1, n, small_turn, 0)
    last_level = len(bits_of(n, False)) - 1

    def steps_of(total, first, stop):
        for level in range(first, stop):
            total.step(level)

    sum_inner.step(0)
    sum_z.step(1)
    ag4.middle()
    sum_joint.step(1)
    sum_rest.step(0)
    steps_of(sum_down, 2, last_level + 1)
    steps_of(sum_gate, 2, last_level + 1)
    ag4.finish()
    for k in range(ns):
        refs.input_grad[TO * k : TO * (k + 1), :] = refs.ag1_all[k]
    steps_of(sum_up, 2, last_level + 1)
    steps_of(sum_z, 2, last_level + 1)
    gz = gather(refs.gz_all, refs.gz_sem, t, sum_z.result())
    sum_inner.step(1)
    steps_of(sum_joint, 2, last_level + 1)
    gj = gather(refs.gj_all, refs.gj_sem, t, sum_joint.result())
    sum_rest.step(1)
    gz.middle()
    steps_of(sum_inner, 2, last_level + 1)
    gi = gather(refs.gi_all, refs.gi_sem, t, sum_inner.result())
    gj.middle()
    steps_of(sum_rest, 2, last_level + 1)
    gr = gather(refs.gr_all, refs.gr_sem, t, sum_rest.result())

    def small_end(k, carried):
        for copy in small_copy(k):
            copy.wait_recv()
        return carried

    lax.fori_loop(1, n, small_end, 0)

    def small_sum(j, total):
        return total + refs.small_rx[j]

    small = gather(
        refs.sm_all, refs.sm_sem, t,
        lax.fori_loop(0, n, small_sum, jnp.zeros(refs.small_rx.shape[1:], F32)),
    )
    gi.middle()
    small.middle()
    refs.o_gu[0] = sum_gate.result()
    refs.o_gu[1] = sum_up.result()
    refs.o_down[...] = sum_down.result()
    gz.finish()
    gj.finish()
    gi.finish()
    gr.middle()
    for k in range(ns):
        refs.o_mix[0, :, C * k : C * (k + 1)] = refs.gz_all[k]
        refs.o_mix[1, :, C * k : C * (k + 1)] = refs.gi_all[k]
        refs.o_joint[:, (D // ns) * k : (D // ns) * (k + 1)] = refs.gj_all[k]
    small.finish()
    total = refs.sm_all[0, :16, :]
    for k in range(1, ns):
        total = total + refs.sm_all[k, :16, :]
    refs.o_gains[...] = total
    refs.o_small[...] = refs.sm_all[:, 16:rows_c, :]
    gr.finish()
    rows = refs.gr_all.shape[1]
    half = iota((rows, LANES), 1) < HEAD_SIZE
    for k in range(ns):
        refs.o_att[:, QC * k : QC * (k + 1)] = refs.gr_all[k, :, :QC]
        refs.o_step[HL * k : HL * (k + 1), :] = refs.sm_all[k, rows_c : rows_c + HL, :rows]
    for c in range(2):
        first = refs.gr_all[c, :, QC : 2 * QC].astype(F32)
        second = refs.gr_all[2 + c, :, QC : 2 * QC].astype(F32)
        refs.o_att[:, AQ + QC * c : AQ + QC * (c + 1)] = jnp.where(
            half, first, roll(second, HEAD_SIZE)
        ).astype(BF16)
    refs.o_st[...] = refs.gr_all[t, :, QC : 2 * QC]

    def small_sent(k, carried):
        for copy in small_copy(k):
            copy.wait_send()
        return carried

    lax.fori_loop(1, n, small_sent, 0)
    for group_of in (
        st_gather, taps_gather, jall, rs3, rs4, ag2, ag4, gz, gj, gi, gr, small,
        sum_gate, sum_up, sum_down, sum_z, sum_joint, sum_inner, sum_rest,
    ):
        sent += group_of.copies
    for copy in sent:
        copy.wait_send()

    @pl.when(s + 1 < n)
    def _():
        halo_copy.wait_send()

    @pl.when(s > 0)
    def _():
        back_copy(t).wait_send()

    carry.finish()
    carry_b.finish()

    def dkv_end(k, carried):
        dkv_copy(k).wait_send()
        return carried

    def dkv_pair_end(k, carried):
        dkv_pair(k).wait_send()
        return carried

    lax.fori_loop(1, s + 1, dkv_end, 0)
    lax.fori_loop(0, s + 1, dkv_pair_end, 0)


def layer(n, ns, arrays):
    inputs = types.SimpleNamespace(**arrays)
    T, D = inputs.x.shape
    C = inputs.w_mix_in.shape[2] // ns
    NW = inputs.st_own.shape[1]
    F = inputs.down_in.shape[1]
    N, TO, H = NW * ns, T // ns, NH // ns
    KJ = inputs.joint.shape[0]
    QC = 2 * HEAD_SIZE
    R, RJ = D // n, KJ // n
    steps = carry_steps(n)
    levels = levels_of(n)
    sd = jax.ShapeDtypeStruct
    J = QC + C
    SMALL = -(-(22 + KC * (C // LANES) + KC) // 8) * 8
    outs = dict(
        layer_output=sd((T, D), BF16),
        input_grad=sd((T, D), BF16),
        o_down=sd((R, F), BF16),
        o_gu=sd((2, R, F), BF16),
        o_mix=sd((2, R, ns * C), BF16),
        o_joint=sd((RJ, D), BF16),
        o_att=sd((R, inputs.w_att.shape[1]), BF16),
        o_step=sd((NH, R), F32),
        o_st=sd((R, LANES), BF16),
        o_gains=sd((16, LANES), F32),
        o_small=sd((ns, SMALL - 16, LANES), F32),
    )
    vm = pltpu.VMEM
    dma = lambda k: (pltpu.SemaphoreType.DMA((k,)), pltpu.SemaphoreType.DMA((k,)))
    blocks = lambda *shape: vm((ns,) + shape, BF16)

    def scan():
        return dict(
            tx=vm((max(1, steps - 1), C, N), BF16),
            rx=vm((steps, C, N), BF16),
            thr_tx=vm((max(1, steps - 1), 8, LANES), F32),
            thr_rx=vm((steps, 8, LANES), F32),
            sem=dma(steps),
            thr_sem=dma(steps),
        )

    def rows():
        return dict(tx=vm((8, T), F32), rx=vm((ns - 1, 8, T), F32), sem=dma(ns - 1))

    def scatter():
        return dict(tx=blocks(TO, D), rx=vm((3, TO, D), BF16), mid=vm((TO, D), BF16))

    def stream(*shape):
        return dict(src=vm((n,) + shape, BF16), rx=vm((n - 1,) + shape, BF16), sem=dma(levels))

    scratch = dict(
        w_qkv=vm((D, 3 * QC), BF16),
        w_joint=vm((J, D), BF16),
        w_mix=vm((2, D, C), BF16),
        w_gu=vm((2, D, F), BF16),
        raw=vm((D, 2, max(C, F // 2)), BF16),
        down=vm((D, F), BF16),
        grad=vm((T, D), BF16),
        load=tuple(pltpu.SemaphoreType.DMA for _ in range(9)),
        taps8=vm((8, LANES), F32),
        taps_st=vm((2, NW, LANES), F32),
        codes=vm((n * T // LANES, LANES), jnp.int32),
        halo_rx=vm((HALO, D), BF16),
        st_all=vm((2, N, D), BF16),
        taps_all=vm((2, N, LANES), F32),
        kv_all=vm((n, T, LANES), BF16),
        normed=vm((T + HALO, D), BF16),
        inv1=vm((T, 1), F32),
        q2=vm((2 * T, LANES), BF16),
        z=vm((T, C), F32),
        ext_f=vm((T + HALO, C), F32),
        ext_s=vm((T + HALO, N), F32),
        ext_o=vm((T + HALO, 2 * NW), F32),
        grad_f=vm((T + HALO, C), F32),
        grad_o=vm((T + HALO, 2 * NW), F32),
        wr=vm((2, T, N), F32),
        tail_e=vm((T, C), F32),
        reach_e=vm((T, C), F32),
        ssd=vm((T, C), F32),
        w_tot=vm((T, C), F32),
        d_z=vm((T, C), BF16),
        jall_all=vm((ns, T, J), BF16),
        window=vm((C, N), F32),
        window_thr=vm((8, LANES), F32),
        m_acc=vm((2 * T, 1), F32),
        l_acc=vm((2 * T, 1), F32),
        o_acc=vm((2 * T, LANES), F32),
        dout2=vm((2 * T, LANES), BF16),
        dq2=vm((2 * T, LANES), F32),
        dkv_rx=vm((n, T // 2, LANES), BF16),
        dkv_mid=vm((n, T // 2, LANES), BF16),
        dkv_half=vm((T // 2, LANES), F32),
        dkv_sum=vm((T, LANES), F32),
        pair_tx=vm((T // 2, LANES), BF16),
        pair_rx=vm((T // 2, LANES), BF16),
        back_tx=vm((HALO, D), BF16),
        back_rx=vm((ns, HALO, D), BF16),
        dwr_tx=vm((2, N, T), BF16),
        d_write=vm((T, N), F32),
        dwr_rx=vm((ns - 1, 2, NW, T), BF16),
        small_tx=vm((SMALL, LANES), F32),
        step_src=vm((n, 8, LANES), F32),
        small_rx=vm((n, SMALL + 8, LANES), F32),
        halo=dma(1),
        st=dma(3),
        taps=dma(3),
        kv=dma(n - 1),
        kv_fwd=dma(n - 1),
        dkv=dma(n - 1),
        dkv_fwd=dma(n),
        jall=dma(3),
        pair=dma(1),
        back=dma(ns),
        dwr=dma(ns - 1),
        small=dma(2 * n - 2),
        sm_all=vm((ns, SMALL + 8, LANES), F32),
        fc=scan(),
        bc=scan(),
        sq=rows(),
        dot=rows(),
        rs1=scatter(),
        rs2=scatter(),
        rs1_sem=dma(2),
        rs2_sem=dma(2),
        rs3_sem=dma(2),
        rs4_sem=dma(2),
        ag1_all=blocks(TO, D),
        ag2_all=blocks(TO, D),
        gz_all=blocks(R, C),
        gi_all=blocks(R, C),
        gr_all=blocks(R, 2 * LANES),
        gj_all=blocks(RJ, D // ns),
        ag1_sem=dma(3),
        ag2_sem=dma(3),
        ag3_sem=dma(3),
        ag4_sem=dma(3),
        gz_sem=dma(3),
        gi_sem=dma(3),
        gr_sem=dma(3),
        gj_sem=dma(3),
        sm_sem=dma(3),
        gate_g=stream(R, F),
        up_g=stream(R, F),
        down_g=stream(R, F),
        z_g=stream(R, C),
        inner_g=stream(R, C),
        rest_g=stream(R, 2 * LANES),
        joint_g=stream(RJ, D // ns),
    )
    whole = pl.BlockSpec(memory_space=pltpu.VMEM)
    small = pl.BlockSpec(memory_space=pltpu.SMEM)
    far = pl.BlockSpec(memory_space=pl.ANY)
    specs = {key: whole for key in arrays}
    specs.update(doc_starts=small, step_bias=small, decay_rate=small, skip_gain=small)
    specs.update(w_att=far, joint=far, g=far, w_mix_in=far, w_gu_in=far, down_in=far)
    flat = [jax.tree.flatten(group) for group in (arrays, outs, scratch)]
    got = pl.pallas_call(
        functools.partial(layer_kernel, n, ns, [tree for _, tree in flat]),
        out_shape=flat[1][0],
        in_specs=jax.tree.flatten(specs)[0],
        out_specs=[whole] * len(outs),
        scratch_shapes=flat[2][0],
        name="layer",
        compiler_params=pltpu.CompilerParams(
            collective_id=1, has_side_effects=True, vmem_limit_bytes=VMEM_LIMIT
        ),
    )(*flat[0][0])
    return types.SimpleNamespace(**jax.tree.unflatten(flat[1][1], got))


def finish_kernel(n, ns, tree_in, tree_out, tree_big, *flat):
    split = tree_in.num_leaves
    o = named(jax.tree.unflatten(tree_in, flat[:split]))
    last = split + tree_out.num_leaves
    out = named(jax.tree.unflatten(tree_out, flat[split:last]))
    held = named(jax.tree.unflatten(tree_big, flat[last:-1]))
    copies = []

    def leave(src, dst):
        copies.append(pltpu.make_async_copy(src, dst, flat[-1].at[len(copies)]))
        copies[-1].start()

    t, s = lax.axis_index(STATE), lax.axis_index(SEQ)
    HL, C = NH // ns, NH * HDM // ns
    per = C // LANES
    NW = out.taps_st.shape[2]
    R = out.down.shape[0]
    for c in range(2):
        held.mix[:, c, :] = o.o_mix[c].astype(F32)
    leave(held.mix, out.mix)
    held.input_grad[...] = o.input_grad[...].astype(F32)
    leave(held.input_grad, out.input_grad)
    held.joint[...] = o.o_joint[...].astype(F32)
    leave(held.joint, out.joint)
    for c in range(2):
        held.gu[:, c, :] = o.o_gu[c].astype(F32)
    leave(held.gu, out.gu)
    held.att[...] = o.o_att[...].astype(F32)
    leave(held.att, out.att)
    held.down[...] = o.o_down[...].astype(F32)
    leave(held.down, out.down)
    out.layer_output[...] = o.layer_output[...]
    out.step[...] = o.o_step[...]
    turned = o.o_st[...].astype(F32).T
    for c in range(2):
        at = HEAD_SIZE + NW * c
        out.st[c] = turned[at : at + NW]
    small = o.o_small

    def part(row, width, count):
        at = s * width
        first = at // LANES
        lanes = jnp.concatenate([row(first + k) for k in range(count)], axis=1)
        return roll(lanes, lax.rem(count * LANES - (at - first * LANES), count * LANES))[:, :width]

    for at, dst in ((0, out.ngain), (8, out.mgain)):
        dst[...] = part(lambda k: o.o_gains[pl.ds(at + k, 1), :], R, 1)
    for k in range(ns):
        for i in range(per):
            out.gains[per * k + i : per * k + i + 1, :] = small[k, i : i + 1, :]
    width = out.ggain.shape[1]
    last = ns * per - 1
    out.ggain[...] = part(lambda k: out.gains[pl.ds(jnp.minimum(k, last), 1), :], width, 3)
    heads = 0.0
    for k in range(ns):
        into = (iota((LANES, LANES), 1) == HL * k + iota((LANES, LANES), 0)) & (
            iota((LANES, LANES), 0) < HL
        )
        heads = heads + nn(small[k, :8, :], into.astype(F32), RIGHT)
        for j in range(KC):
            for i in range(per):
                row = 6 + per * j + i
                at = C * k + LANES * i
                out.taps[j : j + 1, at : at + LANES] = small[k, row : row + 1, :]
    out.skip[...], out.rate[...], out.bias[...] = (heads[k : k + 1, :NH] for k in (3, 4, 5))
    for j in range(KC):
        row = small[t, 6 + KC * per + j : 7 + KC * per + j, :]
        for c in range(2):
            out.taps_st[j, c : c + 1, :] = row[:, NW * c : NW * (c + 1)]
    for copy in copies:
        copy.wait()


def finish(n, ns, o, shapes):
    sd = lambda *shape: jax.ShapeDtypeStruct(shape, F32)
    R, F = o.o_down.shape
    T, D = o.layer_output.shape
    NW = shapes.NW
    outs = dict(
        layer_output=jax.ShapeDtypeStruct((T, D), BF16),
        input_grad=sd(T, D),
        att=sd(*o.o_att.shape),
        joint=sd(*o.o_joint.shape),
        down=sd(R, F),
        step=sd(NH, R),
        mix=sd(R, 2, NH * HDM),
        gu=sd(R, 2, F),
        st=sd(2, NW, R),
        ngain=sd(1, R),
        mgain=sd(1, R),
        ggain=sd(1, NH * HDM // n),
        gains=sd(NH * HDM // LANES, LANES),
        taps=sd(KC, NH * HDM),
        taps_st=sd(KC, 2, NW),
        skip=sd(1, NH),
        rate=sd(1, NH),
        bias=sd(1, NH),
    )
    arrays = dict(o.__dict__)
    big = dict(
        input_grad=outs["input_grad"], att=outs["att"], joint=outs["joint"], down=outs["down"],
        mix=outs["mix"], gu=outs["gu"],
    )
    held = {key: pltpu.VMEM(value.shape, F32) for key, value in big.items()}
    flat = [jax.tree.flatten(group) for group in (arrays, outs, held)]
    whole = pl.BlockSpec(memory_space=pltpu.VMEM)
    far = pl.BlockSpec(memory_space=pl.ANY)
    specs = {key: far if key in big else whole for key in outs}
    got = pl.pallas_call(
        functools.partial(finish_kernel, n, ns, flat[0][1], flat[1][1], flat[2][1]),
        out_shape=flat[1][0],
        in_specs=[whole] * len(arrays),
        out_specs=jax.tree.flatten(specs)[0],
        scratch_shapes=flat[2][0] + [pltpu.SemaphoreType.DMA((len(big),))],
        name="finish",
        compiler_params=pltpu.CompilerParams(vmem_limit_bytes=VMEM_LIMIT),
    )(*flat[0][0])
    return types.SimpleNamespace(**jax.tree.unflatten(flat[1][1], got))


def local(
    layer_input,
    out_grad,
    doc_starts,
    real_mask,
    norm_gain,
    attention_input_rows,
    mixer_in,
    state_in,
    step_in,
    conv_mixer,
    conv_state,
    step_bias,
    decay_rate,
    skip_gain,
    gated_gain,
    joint_out,
    mlp_gain,
    gate_up,
    down_weight,
):
    T, D = layer_input.shape
    NS, n = lax.axis_size(STATE), lax.axis_size(SEQ)
    NW = state_in.shape[2]
    o = layer(
        n,
        NS,
        dict(
            x=layer_input,
            g=out_grad,
            w_att=attention_input_rows,
            w_mix_in=mixer_in,
            w_step=step_in.T,
            st_own=jnp.transpose(state_in, (1, 2, 0)),
            conv_state=conv_state,
            conv_mixer=conv_mixer,
            ngain=norm_gain[None, :],
            ggain=gated_gain.reshape(-1, LANES),
            mgain=mlp_gain[None, :],
            joint=joint_out,
            w_gu_in=gate_up,
            down_in=down_weight,
            real=real_mask.reshape(-1, LANES),
            step_bias=step_bias,
            decay_rate=decay_rate,
            skip_gain=skip_gain,
            doc_starts=doc_starts,
        ),
    )
    e = finish(n, NS, o, types.SimpleNamespace(NW=NW))
    return (
        e.layer_output,
        e.input_grad,
        e.ngain.reshape(-1),
        e.att,
        e.mix,
        e.st.transpose(2, 0, 1),
        e.step.T,
        e.taps,
        e.taps_st,
        e.bias.reshape(-1),
        e.rate.reshape(-1),
        e.skip.reshape(-1),
        e.ggain.reshape(-1),
        e.joint,
        e.mgain.reshape(-1),
        e.gu,
        e.down,
    )


def solution(mesh):
    rep = P()
    in_specs = (
        P(SEQ, None),
        P(SEQ, None),
        rep,
        rep,
        rep,
        rep,
        rep,
        P(None, None, STATE),
        rep,
        rep,
        P(None, None, STATE),
        rep,
        rep,
        rep,
        rep,
        rep,
        rep,
        P(None, None, STATE),
        P(None, STATE),
    )
    out_specs = (
        P(SEQ, None),
        P(SEQ, None),
        P(SEQ),
        P(SEQ, None),
        P(SEQ, None, None),
        P(SEQ, None, STATE),
        P(SEQ, None),
        rep,
        P(None, None, STATE),
        rep,
        rep,
        rep,
        P(SEQ),
        P(SEQ, None),
        P(SEQ),
        P(SEQ, None, STATE),
        P(SEQ, STATE),
    )
    return jax.shard_map(local, mesh=mesh, in_specs=in_specs, out_specs=out_specs, check_vma=False)
```
